32 devices in a mesh: bucket: 8 (over z, x), seq: 4 (over y, core).
Axes of the slice: x: 2, y: 2, z: 4, core: 2. Of those that a mesh axis runs over, the one named last changes fastest.
Arguments:
- tokens: bfloat16 [16384, 1152], P(('bucket', 'seq')), may hold values from -6 to 6
- condition: float32 [8, 1152], P('bucket'), may hold values from -6 to 6
- cotangent: bfloat16 [16384, 1152], P(('bucket', 'seq')), may hold values from -6 to 6
- lengths: int32 [8, 8], P('bucket'), may hold values from 0 to 1024, as said below
- bucket_ids: int32 [8], P('bucket'), may hold values from 0 to 9
- keep_flags: int32 [16384], P(('bucket', 'seq')), may hold values 0 or 1
- head_table: int32 [10, 16], replicated, may hold values 0 or 1
- chan_table: int32 [10, 4608], replicated, may hold values 0 or 1
- ada_master: float32 [1152, 6912], P('bucket', 'seq'), may hold values from -0.1875 to 0.1875
- ada_first: float32 [1152, 6912], P('bucket', 'seq'), may hold values from -224 to 224
- ada_second: float32 [1152, 6912], P('bucket', 'seq'), may hold values from 1474.56 to 5898.24
- ada_average: float32 [1152, 6912], P('bucket', 'seq'), may hold values from -0.1875 to 0.1875
- qkv_master: float32 [1152, 3456], P('bucket', 'seq'), may hold values from -0.1875 to 0.1875
- qkv_first: float32 [1152, 3456], P('bucket', 'seq'), may hold values from -320 to 320
- qkv_second: float32 [1152, 3456], P('bucket', 'seq'), may hold values from 2621.44 to 10485.76
- qkv_average: float32 [1152, 3456], P('bucket', 'seq'), may hold values from -0.1875 to 0.1875
- out_master: float32 [1152, 1152], P('bucket', 'seq'), may hold values from -2 to 2
- out_first: float32 [1152, 1152], P('bucket', 'seq'), may hold values from -64 to 64
- out_second: float32 [1152, 1152], P('bucket', 'seq'), may hold values from 64 to 256
- out_average: float32 [1152, 1152], P('bucket', 'seq'), may hold values from -2 to 2
- up_master: float32 [1152, 4608], P('bucket', 'seq'), may hold values from -0.1875 to 0.1875
- up_first: float32 [1152, 4608], P('bucket', 'seq'), may hold values from -192 to 192
- up_second: float32 [1152, 4608], P('bucket', 'seq'), may hold values from 1024 to 4096
- up_average: float32 [1152, 4608], P('bucket', 'seq'), may hold values from -0.1875 to 0.1875
- down_master: float32 [4608, 1152], P('bucket', 'seq'), may hold values from -0.09375 to 0.09375
- down_first: float32 [4608, 1152], P('bucket', 'seq'), may hold values from -384 to 384
- down_second: float32 [4608, 1152], P('bucket', 'seq'), may hold values from 4096 to 16384
- down_average: float32 [4608, 1152], P('bucket', 'seq'), may hold values from -0.09375 to 0.09375
- bias_master: float32 [16128], P(('bucket', 'seq')), may hold values from -2 to 2
- bias_first: float32 [16128], P(('bucket', 'seq')), may hold values from -320 to 320
- bias_second: float32 [16128], P(('bucket', 'seq')), may hold values from 2621.44 to 10485.76
- bias_average: float32 [16128], P(('bucket', 'seq')), may hold values from -2 to 2
Outputs:
- output: bfloat16 [16384, 1152], P(('bucket', 'seq'))
- token_grad: float32 [16384, 1152], P(('bucket', 'seq'))
- condition_grad: float32 [8, 1152], P('bucket')
- ada_master_new: float32 [1152, 6912], P('bucket', 'seq')
- ada_first_new: float32 [1152, 6912], P('bucket', 'seq')
- ada_second_new: float32 [1152, 6912], P('bucket', 'seq')
- ada_average_new: float32 [1152, 6912], P('bucket', 'seq')
- qkv_master_new: float32 [1152, 3456], P('bucket', 'seq')
- qkv_first_new: float32 [1152, 3456], P('bucket', 'seq')
- qkv_second_new: float32 [1152, 3456], P('bucket', 'seq')
- qkv_average_new: float32 [1152, 3456], P('bucket', 'seq')
- out_master_new: float32 [1152, 1152], P('bucket', 'seq')
- out_first_new: float32 [1152, 1152], P('bucket', 'seq')
- out_second_new: float32 [1152, 1152], P('bucket', 'seq')
- out_average_new: float32 [1152, 1152], P('bucket', 'seq')
- up_master_new: float32 [1152, 4608], P('bucket', 'seq')
- up_first_new: float32 [1152, 4608], P('bucket', 'seq')
- up_second_new: float32 [1152, 4608], P('bucket', 'seq')
- up_average_new: float32 [1152, 4608], P('bucket', 'seq')
- down_master_new: float32 [4608, 1152], P('bucket', 'seq')
- down_first_new: float32 [4608, 1152], P('bucket', 'seq')
- down_second_new: float32 [4608, 1152], P('bucket', 'seq')
- down_average_new: float32 [4608, 1152], P('bucket', 'seq')
- bias_master_new: float32 [16128], P(('bucket', 'seq'))
- bias_first_new: float32 [16128], P(('bucket', 'seq'))
- bias_second_new: float32 [16128], P(('bucket', 'seq'))
- bias_average_new: float32 [16128], P(('bucket', 'seq'))
The draws below stay inside these ranges and needn't reach their ends.
Inputs may be any that keep to these rules, and one draw needn't show every extreme that they name: `lengths`: each group's images have 256 or 1024 tokens, stand first in its row with zeros after them, and fill its 2048 tokens; every draw holds an image of 1024 tokens.
All inputs are finite; a program needn't handle non-finite values. No bound on the sum of `keep_flags` on one device may be relied on, other than what follows from the above.
Results may differ from the reference program's by a relative error of at most 0.02.
Values may be sent and summed in bfloat16 or wider, within the bound.
A program may use at most 256 MiB of HBM per device.

```python
import math
import jax
import jax.numpy as jnp
from jax import lax

D = 1152
HEADS = 16
FF = 4608
IMG_GROUP = 8
TBUCKETS = 10
STEP = 10
GROUPS = 8
GROUP_TOK = 2048
TOKENS = 16384
LONGEST = 1024
SHORTEST = 256
BIAS_LEN = 16128


def draw_lengths(key, part):
    key = jax.random.fold_in(key, 11)
    kind_key, place_key, chosen_key, odd_key = jax.random.split(key, 4)
    group_ids = jnp.arange(GROUPS, dtype=jnp.int32)
    slots = jnp.arange(IMG_GROUP, dtype=jnp.int32)[None, :]
    kinds = jax.random.randint(kind_key, (GROUPS,), 0, 4, dtype=jnp.int32)
    places = jax.random.randint(place_key, (GROUPS,), 0, 5, dtype=jnp.int32)
    chosen = jax.random.randint(chosen_key, (), 0, GROUPS, dtype=jnp.int32)
    odd_place = 1 + 2 * jax.random.randint(odd_key, (), 0, 2, dtype=jnp.int32)
    forced = group_ids == chosen
    kinds = jnp.where(forced, 1, kinds)
    places = jnp.where(forced, odd_place, places)
    two_long = jnp.where(slots < 2, LONGEST, 0) * jnp.ones((GROUPS, 1), jnp.int32)
    mixed = jnp.where(slots < 5, jnp.where(slots == places[:, None], LONGEST, SHORTEST), 0)
    all_short = jnp.full((GROUPS, IMG_GROUP), SHORTEST, jnp.int32)
    kind_col = kinds[:, None]
    result = jnp.where(kind_col == 0, two_long, jnp.where(kind_col == 3, all_short, mixed))
    return result.astype(jnp.int32)


def plant(entries, stream_key, low, top_value):
    shape = entries.shape
    spot = [jax.random.randint(jax.random.fold_in(stream_key, axis), (), 0, shape[axis]) for axis in range(len(shape))]
    entries = entries.at[tuple(spot)].set(low)
    longest = shape.index(max(shape))
    spot[longest] = (spot[longest] + 1) % shape[longest]
    return entries.at[tuple(spot)].set(top_value)


def steps_of(key, dims, shards, least, top_value):
    factor_of = 1.0
    for position, blocks in shards:
        steps = jax.random.uniform(jax.random.fold_in(jax.random.fold_in(key, 6), position), (blocks,), jnp.float32, least / len(shards), top_value / len(shards))
        factor_of = factor_of * jnp.repeat(jnp.exp(steps), dims[position] // blocks).reshape((-1,) + (1,) * (len(dims) - 1 - position))
    return factor_of


def gaussian(own_key, dims, scale, bound, cuts=(), kind=jnp.bfloat16):
    values = jax.random.normal(own_key, dims, jnp.float32) * scale
    if len(cuts) > 0:
        values = steps_of(own_key, dims, cuts, -0.22, 0.18) * values
    return jnp.clip(values, min=-bound, max=bound).astype(kind)


def setup_inputs(seed: int = 0) -> dict:
    splits = jax.random.split(jax.random.key(seed), 33)
    return {
        "tokens": gaussian(splits[0], (TOKENS, D), 1.0, 6.0, ((0, 32),)),
        "condition": gaussian(splits[1], (GROUPS, D), 1.0, 6.0, ((0, 8),), jnp.float32),
        "cotangent": gaussian(splits[2], (TOKENS, D), 1.0, 6.0, ((0, 32),)),
        "lengths": draw_lengths(jax.random.fold_in(splits[32], 71), 0),
        "bucket_ids": plant(jax.random.randint(splits[4], (GROUPS,), 0, TBUCKETS), jax.random.fold_in(splits[4], 1), 0, TBUCKETS - 1).astype(jnp.int32),
        "keep_flags": plant((jax.random.randint(splits[5], (TOKENS,), 0, 4) < 3).astype(jnp.int32), jax.random.fold_in(splits[5], 1), 0, 1),
        "head_table": plant((jax.random.randint(splits[6], (TBUCKETS, HEADS), 0, 4) < 3).astype(jnp.int32), jax.random.fold_in(splits[6], 1), 0, 1),
        "chan_table": plant((jax.random.randint(splits[7], (TBUCKETS, FF), 0, 4) < 3).astype(jnp.int32), jax.random.fold_in(splits[7], 1), 0, 1),
        "ada_master": gaussian(splits[8], (D, 6 * D), D ** -0.5, 0.1875, ((0, 8), (1, 4)), jnp.float32),
        "ada_first": gaussian(splits[9], (D, 6 * D), (0.3 * TOKENS ** 0.5), 224.0, ((0, 8), (1, 4)), jnp.float32),
        "ada_second": jnp.clip(jnp.exp(math.log(5898.24) - 1.3862944 * jax.random.uniform(splits[10], (D, 6 * D), jnp.float32) ** steps_of(splits[10], (D, 6 * D), ((0, 8), (1, 4)), -0.2, 0.2)), 1474.56, 5898.24),
        "ada_average": gaussian(splits[11], (D, 6 * D), D ** -0.5, 0.1875, ((0, 8), (1, 4)), jnp.float32),
        "qkv_master": gaussian(splits[12], (D, 3 * D), D ** -0.5, 0.1875, ((0, 8), (1, 4)), jnp.float32),
        "qkv_first": gaussian(splits[13], (D, 3 * D), (0.4 * TOKENS ** 0.5), 320.0, ((0, 8), (1, 4)), jnp.float32),
        "qkv_second": jnp.clip(jnp.exp(math.log(10485.76) - 1.3862944 * jax.random.uniform(splits[14], (D, 3 * D), jnp.float32) ** steps_of(splits[14], (D, 3 * D), ((0, 8), (1, 4)), -0.2, 0.2)), 2621.44, 10485.76),
        "qkv_average": gaussian(splits[15], (D, 3 * D), D ** -0.5, 0.1875, ((0, 8), (1, 4)), jnp.float32),
        "out_master": gaussian(splits[16], (D, D), (16 * D // GROUP_TOK) ** -0.5, 2.0, ((0, 8), (1, 4)), jnp.float32),
        "out_first": gaussian(splits[17], (D, D), (4.0 * (TOKENS / GROUP_TOK) ** 0.5), 64.0, ((0, 8), (1, 4)), jnp.float32),
        "out_second": jnp.clip(jnp.exp(math.log(256.0) - 1.3862944 * jax.random.uniform(splits[18], (D, D), jnp.float32) ** steps_of(splits[18], (D, D), ((0, 8), (1, 4)), -0.2, 0.2)), 64.0, 256.0),
        "out_average": gaussian(splits[19], (D, D), (16 * D // GROUP_TOK) ** -0.5, 2.0, ((0, 8), (1, 4)), jnp.float32),
        "up_master": gaussian(splits[20], (D, FF), D ** -0.5, 0.1875, ((0, 8), (1, 4)), jnp.float32),
        "up_first": gaussian(splits[21], (D, FF), (0.25 * TOKENS ** 0.5), 192.0, ((0, 8), (1, 4)), jnp.float32),
        "up_second": jnp.clip(jnp.exp(math.log(4096.0) - 1.3862944 * jax.random.uniform(splits[22], (D, FF), jnp.float32) ** steps_of(splits[22], (D, FF), ((0, 8), (1, 4)), -0.2, 0.2)), 1024.0, 4096.0),
        "up_average": gaussian(splits[23], (D, FF), D ** -0.5, 0.1875, ((0, 8), (1, 4)), jnp.float32),
        "down_master": gaussian(splits[24], (FF, D), FF ** -0.5, 0.09375, ((0, 8), (1, 4)), jnp.float32),
        "down_first": gaussian(splits[25], (FF, D), (0.5 * TOKENS ** 0.5), 384.0, ((0, 8), (1, 4)), jnp.float32),
        "down_second": jnp.clip(jnp.exp(math.log(16384.0) - 1.3862944 * jax.random.uniform(splits[26], (FF, D), jnp.float32) ** steps_of(splits[26], (FF, D), ((0, 8), (1, 4)), -0.2, 0.2)), 4096.0, 16384.0),
        "down_average": gaussian(splits[27], (FF, D), FF ** -0.5, 0.09375, ((0, 8), (1, 4)), jnp.float32),
        "bias_master": gaussian(splits[28], (BIAS_LEN,), 0.3, 2.0, ((0, 32),), jnp.float32),
        "bias_first": gaussian(splits[29], (BIAS_LEN,), (0.4 * TOKENS ** 0.5), 320.0, ((0, 32),), jnp.float32),
        "bias_second": jnp.clip(jnp.exp(math.log(10485.76) - 1.3862944 * jax.random.uniform(splits[30], (BIAS_LEN,), jnp.float32) ** steps_of(splits[30], (BIAS_LEN,), ((0, 32),), -0.2, 0.2)), 2621.44, 10485.76),
        "bias_average": gaussian(splits[31], (BIAS_LEN,), 0.3, 2.0, ((0, 32),), jnp.float32),
    }


EPSILON = 1e-06
BETA_FIRST = 0.5
BETA_SECOND = 0.5
ADAM_EPSILON = 1e-08
MATRIX_DECAY = 0.01
EMA_DECAY = 0.9999
HIGHEST = lax.Precision.HIGHEST

@jax.custom_vjp
def low(v):
    return lax.optimization_barrier(v.astype(jnp.bfloat16)).astype(jnp.float32)

@jax.custom_vjp
def low_back(v):
    return v

def low_keep(v):
    return (low(v), None)

def low_pass(kept, grad):
    return (grad,)

def back_keep(v):
    return (v, None)

def back_low(kept, grad):
    return (low(grad),)
low.defvjp(low_keep, low_pass)
low_back.defvjp(back_keep, back_low)

def multiply(left, right):
    return jnp.dot(left, right, precision=HIGHEST)

def layer_norm(values):
    centre = values - lax.optimization_barrier(jnp.mean(values, axis=-1, keepdims=True))
    spread = lax.optimization_barrier(jnp.mean(centre * centre, axis=-1, keepdims=True))
    return centre * lax.rsqrt(spread + EPSILON)

def modulate(values, shift_row, scale_row):
    return layer_norm(values) * (1.0 + scale_row) + shift_row

def gelu_tanh(values):
    return jax.nn.gelu(values, approximate=True)

def segment_of(positions, lengths_row):
    image_ends = jnp.cumsum(lengths_row)
    return lax.optimization_barrier(jnp.sum((positions[:, None] >= image_ends[None, :]).astype(jnp.int32), axis=1))

def group_forward(params, head_table, chan_table, inputs):
    ada_weight, qkv_weight, out_weight, up_weight, down_weight, bias_all = params
    tokens_group, condition_row, bucket, lengths_row, keep_row = inputs
    width = D
    head_size = D // HEADS
    columns = 10 + FF // D
    table = bias_all.reshape(D, columns)
    ada_bias = table[:, :6].T.reshape(6 * width)
    query_bias = table[:, 6]
    value_bias = table[:, 7]
    out_bias = table[:, 8]
    up_bias = table[:, 9:columns - 1].reshape(FF)
    down_bias = table[:, columns - 1]
    silu_low = low(jax.nn.silu(condition_row))
    modulation = multiply(silu_low[None, :], ada_weight)[0] + ada_bias
    shift_one, scale_one, gate_one, shift_two, scale_two, gate_two = jnp.split(modulation, 6)
    head_keep = head_table[bucket].astype(jnp.float32)
    chan_keep = chan_table[bucket].astype(jnp.float32)
    head_wide = jnp.repeat(head_keep, head_size)
    first_in = low(modulate(tokens_group, shift_one, scale_one))
    qkv_bias = jnp.concatenate([query_bias, jnp.zeros_like(query_bias), value_bias])
    projected = low(low_back(multiply(first_in, qkv_weight) + qkv_bias))
    query_heads = projected[:, :width].reshape(GROUP_TOK, HEADS, head_size)
    key_heads = projected[:, width:2 * width].reshape(GROUP_TOK, HEADS, head_size)
    value_heads = projected[:, 2 * width:].reshape(GROUP_TOK, HEADS, head_size)
    scores = jnp.einsum('qhd,khd->hqk', query_heads, key_heads, precision=HIGHEST) * head_size ** (-0.5)
    scores = low_back(scores)
    positions = jnp.arange(GROUP_TOK, dtype=jnp.int32)
    segment = segment_of(positions, lengths_row)
    same_image = segment[:, None] == segment[None, :]
    scores = jnp.where(same_image[None], scores, -1e+30)
    top_score = lax.optimization_barrier(jnp.max(scores, axis=-1, keepdims=True))
    expo = jnp.exp(scores - top_score)
    probs = expo / lax.optimization_barrier(jnp.sum(expo, axis=-1, keepdims=True))
    attended = jnp.einsum('hqk,khd->qhd', low(probs), value_heads, precision=HIGHEST).reshape(GROUP_TOK, width)
    attended = low_back(attended)
    branch_in = low(attended * head_wide)
    attn_out = low_back(multiply(branch_in, out_weight) + out_bias)
    middle = tokens_group + gate_one * attn_out
    second_in = low(modulate(middle, shift_two, scale_two))
    hidden_pre = low_back(multiply(second_in, up_weight) + up_bias)
    hidden_act = low(gelu_tanh(hidden_pre) * chan_keep)
    mlp_out = low_back(multiply(hidden_act, down_weight) + down_bias)
    return middle + gate_two * keep_row[:, None] * mlp_out

def layer_forward(tokens_all, condition_all, ada_m, qkv_m, out_m, up_m, down_m, bias_m, lengths, bucket_ids, keep_flags, head_table, chan_table):
    params = (low(ada_m), low(qkv_m), low(out_m), low(up_m), low(down_m), low(bias_m))

    def one_group(carry, inputs):
        result = jax.checkpoint(lambda items: group_forward(params, head_table, chan_table, items))(inputs)
        return (carry, result)
    inputs = (tokens_all.reshape(GROUPS, GROUP_TOK, D), condition_all, bucket_ids, lengths, keep_flags.reshape(GROUPS, GROUP_TOK).astype(jnp.float32))
    _, outputs = lax.scan(one_group, (), inputs)
    return outputs.reshape(TOKENS, D)

def adam_update(master, moment_one, moment_two, average, gradient, step_rate, decay_rate):
    one_new = BETA_FIRST * moment_one + (1.0 - BETA_FIRST) * gradient
    two_new = BETA_SECOND * moment_two + (1.0 - BETA_SECOND) * gradient * gradient
    one_hat = one_new / (1.0 - BETA_FIRST ** STEP)
    two_hat = two_new / (1.0 - BETA_SECOND ** STEP)
    master_new = master - step_rate * (one_hat / (jnp.sqrt(two_hat) + ADAM_EPSILON) + decay_rate * master)
    average_decay = min(EMA_DECAY, (1.0 + STEP) / (10.0 + STEP))
    average_new = average_decay * average + (1.0 - average_decay) * master_new
    return (master_new, one_new, two_new, average_new)

def reference(tokens, condition, cotangent, lengths, bucket_ids, keep_flags, head_table, chan_table, ada_master, ada_first, ada_second, ada_average, qkv_master, qkv_first, qkv_second, qkv_average, out_master, out_first, out_second, out_average, up_master, up_first, up_second, up_average, down_master, down_first, down_second, down_average, bias_master, bias_first, bias_second, bias_average):

    def forward(tokens_in, condition_in, ada_m, qkv_m, out_m, up_m, down_m, bias_m):
        return layer_forward(tokens_in, condition_in, ada_m, qkv_m, out_m, up_m, down_m, bias_m, lengths, bucket_ids, keep_flags, head_table, chan_table)
    result, pullback = jax.vjp(forward, tokens.astype(jnp.float32), condition, ada_master, qkv_master, out_master, up_master, down_master, bias_master)
    grads = pullback(cotangent.astype(jnp.float32))
    token_grad, condition_grad, ada_grad, qkv_grad, out_grad, up_grad, down_grad, bias_grad = grads
    ada_new = adam_update(ada_master, ada_first, ada_second, ada_average, ada_grad, D ** (-0.5), MATRIX_DECAY)
    qkv_new = adam_update(qkv_master, qkv_first, qkv_second, qkv_average, qkv_grad, D ** (-0.5), MATRIX_DECAY)
    out_new = adam_update(out_master, out_first, out_second, out_average, out_grad, (GROUP_TOK / (16.0 * D)) ** 0.5, MATRIX_DECAY)
    up_new = adam_update(up_master, up_first, up_second, up_average, up_grad, D ** (-0.5), MATRIX_DECAY)
    down_new = adam_update(down_master, down_first, down_second, down_average, down_grad, FF ** (-0.5), MATRIX_DECAY)
    bias_new = adam_update(bias_master, bias_first, bias_second, bias_average, bias_grad, 0.3, 0.0)
    return (result.astype(jnp.bfloat16), token_grad, condition_grad, ada_new[0], ada_new[1], ada_new[2], ada_new[3], qkv_new[0], qkv_new[1], qkv_new[2], qkv_new[3], out_new[0], out_new[1], out_new[2], out_new[3], up_new[0], up_new[1], up_new[2], up_new[3], down_new[0], down_new[1], down_new[2], down_new[3], bias_new[0], bias_new[1], bias_new[2], bias_new[3])
```

```python
import functools
import math

import jax
import jax.numpy as jnp
from jax import lax
from jax.experimental import pallas as pl
from jax.experimental.pallas import tpu as pltpu
from jax.sharding import PartitionSpec as P

STEP = 10


EPSILON = 1e-06
BETA_FIRST = 0.5
BETA_SECOND = 0.5
ADAM_EPSILON = 1e-08
MATRIX_DECAY = 0.01
EMA_DECAY = 0.9999
HIGHEST = lax.Precision.HIGHEST
LOG2E = math.log2(math.e)
LANES = 128
TILE = 256
VMEM_LIMIT = 60 * 1024 * 1024
bfloat = jnp.bfloat16
single = jnp.float32


def layer_norm(values):
    centre = values - jnp.mean(values, axis=-1, keepdims=True)
    spread = jnp.mean(centre * centre, axis=-1, keepdims=True)
    return centre * lax.rsqrt(spread + EPSILON)


def modulate(values, shift_row, scale_row):
    return layer_norm(values) * (1.0 + scale_row) + shift_row


def dot_nn(left, right):
    return lax.dot_general(left, right, (((1,), (0,)), ((), ())), preferred_element_type=single)


def dot_nt(left, right):
    return lax.dot_general(left, right, (((1,), (1,)), ((), ())), preferred_element_type=single)


def dot_tn(left, right):
    return lax.dot_general(left, right, (((0,), (0,)), ((), ())), preferred_element_type=single)


def adam_update(master, moment_one, moment_two, average, gradient, step_rate, decay_rate):
    one_new = BETA_FIRST * moment_one + (1.0 - BETA_FIRST) * gradient
    two_new = BETA_SECOND * moment_two + (1.0 - BETA_SECOND) * gradient * gradient
    one_hat = one_new / (1.0 - BETA_FIRST**STEP)
    two_hat = two_new / (1.0 - BETA_SECOND**STEP)
    master_new = master - step_rate * (
        one_hat / (jnp.sqrt(two_hat) + ADAM_EPSILON) + decay_rate * master
    )
    average_decay = min(EMA_DECAY, (1.0 + STEP) / (10.0 + STEP))
    average_new = average_decay * average + (1.0 - average_decay) * master_new
    return (master_new, one_new, two_new, average_new)


def params(*semantics):
    return pltpu.CompilerParams(
        dimension_semantics=semantics or None, vmem_limit_bytes=VMEM_LIMIT
    )


def cost(flops, moved, exps=0):
    return pl.CostEstimate(flops=int(flops), bytes_accessed=int(moved), transcendentals=int(exps))


def exchange(values, axis, bit):
    count = lax.axis_size(axis)
    return lax.ppermute(values, axis, [(i, i ^ bit) for i in range(count)])


def pick(values, index, axis):
    return lax.dynamic_index_in_dim(values, index, axis, keepdims=False)


IN_VMEM = pl.BlockSpec(memory_space=pltpu.VMEM)
IN_HBM = pl.BlockSpec(memory_space=pl.ANY)


def cube_path():
    return lax.axis_size("bucket") == 8 and lax.axis_size("seq") == 4


BLOCKS, PLANES = 8, 4
X, Z0, Z1, CORE, Y = ("bucket", 1), ("bucket", 2), ("bucket", 4), ("seq", 1), ("seq", 2)


def gather_all(block, layout):
    width = block.shape[1]
    if layout == "rows":
        return lax.all_gather(block, ("bucket", "seq"), axis=0, tiled=True)
    tall = lax.all_gather(block, "bucket", axis=0, tiled=True)
    return lax.all_gather(tall, "seq", axis=0)


def place_in_kernel():
    if cube_path():
        return lax.axis_index("bucket"), lax.axis_index("seq")
    return 0, 0


DIMS = {"planes": (Y, CORE, Z1, Z0, X), "rows": (Z1, Z0, X, Y, CORE)}
MESH = pl.DeviceIdType.MESH


def my_coords():
    bucket, seq = lax.axis_index("bucket"), lax.axis_index("seq")
    return {
        (axis, amount): ((bucket if axis == "bucket" else seq) // amount) % 2
        for axis, amount in (X, Z0, Z1, CORE, Y)
    }


def partner(bit):
    bucket, seq = lax.axis_index("bucket"), lax.axis_index("seq")
    axis, amount = bit
    return (bucket ^ amount, seq) if axis == "bucket" else (bucket, seq ^ amount)


def peer_at(distance):
    bucket, seq = lax.axis_index("bucket"), lax.axis_index("seq")
    return bucket ^ (distance >> 2), seq ^ (distance & 3)


def greet(peers):
    barrier = pltpu.get_barrier_semaphore()
    for peer in peers:
        pl.semaphore_signal(barrier, inc=1, device_id=peer, device_id_type=MESH)
    pl.semaphore_wait(barrier, len(peers))


class Gathering:
    def __init__(self, own, out, layout, order, first, rows, send, recv, base):
        self.own, self.out, self.dims, self.order = own, out, DIMS[layout], order
        self.first, self.rows, self.send, self.recv, self.base = first, rows, send, recv, base
        self.me = my_coords()

    def view(self, free, flipped=None):
        index = tuple(
            slice(None)
            if dim in free
            else (1 - self.me[dim] if dim == flipped else self.me[dim])
            for dim in self.dims
        )
        return self.out.at[index + (pl.ds(self.first, self.rows), slice(None))]

    def copy(self, source, place, slot, bit):
        return pltpu.make_async_remote_copy(
            src_ref=source,
            dst_ref=place,
            send_sem=self.send.at[self.base + slot],
            recv_sem=self.recv.at[self.base + slot],
            device_id=partner(bit),
            device_id_type=MESH,
        )

    def hop(self, phase):
        place = self.view(self.order[:phase])
        source = self.own if phase == 0 else place
        return self.copy(source, place, phase, self.order[phase])

    def across(self, phase):
        if phase == 0:
            return self.copy(self.own, self.view(()), 4, CORE)
        place = self.view(self.order[: phase - 1], self.order[phase - 1])
        return self.copy(place, place, 4 + phase, CORE)

    def keep(self):
        return pltpu.make_async_copy(self.own, self.view(()), self.send.at[self.base + 9])

    def begin(self):
        self.hop(0).start()
        self.across(0).start()
        self.keep().start()

    def advance(self, phase):
        if phase == 0:
            self.keep().wait()
        self.hop(phase).wait_recv()
        if phase < 3:
            self.hop(phase + 1).start()
        self.across(phase + 1).start()

    def finish(self):
        for phase in range(5):
            self.across(phase).wait_recv()
        for phase in range(4):
            self.hop(phase).wait_send()
        for phase in range(5):
            self.across(phase).wait_send()


GATHER_SEMS = 10
PAIR_SHARES = (32, 32, 32, 32, 16)
REST_SHARES = (48, 48, 48)
PAIR_PARTS = (
    (Z1, Y, X, Z0),
    (Z1, X, Y, Z0),
    (Z1, Z0, X, Y),
    (Z1, Z0, Y, X),
    (Z1, Z0, X, Y),
)
PAIR_EVENTS = (
    (0, 0), (1, 0), (2, 0), (0, 1), (3, 0), (1, 1), (4, 0), (2, 1), (0, 2), (3, 1),
    (1, 2), (2, 2), (4, 1), (3, 2), (4, 2), (2, 3), (0, 3), (3, 3), (4, 3), (1, 3),
)
UP_PARTS = (
    (Z1, Y, Z0, X),
    (Z1, Y, X, Z0),
    (Z1, X, Z0, Y),
)
DOWN_PARTS = (
    (Z1, Z0, Y, X),
    (Z0, Z1, Y, X),
    (Y, Z1, X, Z0),
)
REST_EVENTS = (
    (5, 0), (0, 0), (1, 0), (0, 1), (2, 0), (1, 1), (3, 0), (4, 0), (2, 1), (5, 1),
    (1, 2), (0, 2), (5, 2), (3, 1), (4, 1), (3, 2), (0, 3), (2, 2), (4, 2), (3, 3),
    (1, 3), (2, 3), (4, 3), (5, 3),
)
PAIR_SUM_PARTS = (
    (Y, X, Z0, Z1),
    (X, Z0, Y, Z1),
    (Z0, X, Y, Z1),
    (Y, Z0, X, Z1),
    (Y, X, Z0, Z1),
)
PAIR_SUM_EVENTS = (
    (0, -1), (1, -1), (2, -1), (3, -1), (4, -1), (0, 0), (1, 0), (2, 0), (0, 1), (1, 1),
    (3, 0), (2, 1), (0, 2), (4, 0), (1, 2), (3, 1), (4, 1), (2, 2), (0, 3), (1, 3),
    (3, 2), (4, 2), (2, 3), (3, 3), (4, 3),
)
UP_SUM_PARTS = (
    (X, Y, Z0, Z1),
    (Z0, X, Y, Z1),
    (X, Y, Z0, Z1),
)
DOWN_SUM_PARTS = (
    (Z0, X, Y, Z1),
    (Z0, X, Y, Z1),
    (X, Y, Z0, Z1),
)
REST_SUM_EVENTS = (
    (0, -1), (1, -1), (2, -1), (3, -1), (4, -1), (5, -1), (0, 0), (1, 0), (0, 1), (2, 0),
    (3, 0), (2, 1), (5, 0), (4, 0), (0, 2), (1, 1), (2, 2), (5, 1), (0, 3), (1, 2),
    (3, 1), (2, 3), (5, 2), (3, 2), (4, 1), (1, 3), (5, 3), (4, 2), (3, 3), (4, 3),
)
NOTE_EVENT = 5
KV_EVENTS = (2, 6, 10, 14)


def split_gatherings(block_ref, out_ref, layout, shares, orders, send, recv, base):
    moving, first = [], 0
    for index, (count, order) in enumerate(zip(shares, orders)):
        own = block_ref.at[pl.ds(first, count), :]
        slot = base + GATHER_SEMS * index
        moving.append(Gathering(own, out_ref, layout, order, first, count, send, recv, slot))
        first += count
    return moving


def first_gather_kernel(
    note_ref,
    ada_ref,
    block_ref,
    out_ref,
    inbox_ref,
    silu_ref,
    mod_ref,
    parts,
    returns,
    note_send,
    note_recv,
    mod_send,
    mod_recv,
    send,
    recv,
):
    bucket, seq = lax.axis_index("bucket"), lax.axis_index("seq")
    me = bucket * PLANES + seq
    count = BLOCKS * PLANES
    barrier = pltpu.get_barrier_semaphore()

    @pl.loop(1, count)
    def _(distance):
        pl.semaphore_signal(barrier, inc=1, device_id=peer_at(distance), device_id_type=MESH)

    pl.semaphore_wait(barrier, count - 1)

    def note(distance):
        peer = peer_at(distance)
        return pltpu.make_async_remote_copy(
            src_ref=note_ref.at[peer[0] * PLANES + peer[1]],
            dst_ref=inbox_ref.at[me],
            send_sem=note_send.at[distance],
            recv_sem=note_recv.at[distance],
            device_id=peer,
            device_id_type=MESH,
        )

    def answer(distance):
        peer = peer_at(distance)
        return pltpu.make_async_remote_copy(
            src_ref=parts.at[peer[0]],
            dst_ref=returns.at[me],
            send_sem=mod_send.at[distance],
            recv_sem=mod_recv.at[distance],
            device_id=peer,
            device_id_type=MESH,
        )

    @pl.loop(1, count)
    def _(distance):
        note(distance).start()

    inbox_ref[me] = note_ref[me]
    moving = split_gatherings(
        block_ref, out_ref, "planes", PAIR_SHARES, PAIR_PARTS, send, recv, 0
    )
    for part in moving:
        part.begin()

    for part, phase in PAIR_EVENTS[:NOTE_EVENT]:
        moving[part].advance(phase)

    @pl.loop(1, count)
    def _(distance):
        note(distance).wait_recv()

    rows = ada_ref.shape[0]
    heard = jnp.concatenate([inbox_ref[PLANES * g, :, :] for g in range(BLOCKS)])
    silu = jax.nn.silu(heard[:, :rows]).astype(bfloat)
    silu_ref[...] = silu
    mods = dot_nn(silu, ada_ref[...])
    for group in range(BLOCKS):
        parts[group] = mods[group : group + 1, :]
    returns[me] = parts[bucket]

    @pl.loop(1, count)
    def _(distance):
        answer(distance).start()

    for part, phase in PAIR_EVENTS[NOTE_EVENT:]:
        moving[part].advance(phase)

    @pl.loop(1, count)
    def _(distance):
        answer(distance).wait_recv()

    for plane in range(PLANES):
        mod_ref[plane] = sum(returns[PLANES * g + plane] for g in range(BLOCKS))
    for part in moving:
        part.finish()

    @pl.loop(1, count)
    def _(distance):
        note(distance).wait_send()
        answer(distance).wait_send()


def first_gather(notes, ada_low, block):
    rows, width = block.shape
    count = BLOCKS * PLANES
    cols = ada_low.shape[1]
    out, inbox, silu, mods = pl.pallas_call(
        first_gather_kernel,
        out_shape=(
            jax.ShapeDtypeStruct((2, 2, 2, 2, 2, rows, width), bfloat),
            jax.ShapeDtypeStruct(notes.shape, single),
            jax.ShapeDtypeStruct((BLOCKS, rows), bfloat),
            jax.ShapeDtypeStruct((PLANES, 1, cols), single),
        ),
        in_specs=[IN_VMEM] * 3,
        out_specs=(IN_HBM, IN_VMEM, IN_VMEM, IN_VMEM),
        scratch_shapes=[
            pltpu.VMEM((BLOCKS, 1, cols), single),
            pltpu.VMEM((count, 1, cols), single),
        ]
        + [pltpu.SemaphoreType.DMA((count,))] * 4
        + [pltpu.SemaphoreType.DMA((len(PAIR_PARTS) * GATHER_SEMS,))] * 2,
        compiler_params=pltpu.CompilerParams(
            collective_id=1, has_side_effects=True, vmem_limit_bytes=VMEM_LIMIT
        ),
        cost_estimate=cost(0, 64 * rows * width),
        name="first_gather",
    )(notes, ada_low, block)
    return out.reshape(PLANES, BLOCKS * rows, width), inbox, silu, mods


def second_gather_kernel(
    up_ref, down_ref, kv_ref, up_out, down_out, kv_out, send, recv
):
    me = my_coords()
    greet([partner(bit) for bit in (X, Z0, Z1, CORE, Y)])
    base = len(UP_PARTS) * GATHER_SEMS
    moving = split_gatherings(
        up_ref, up_out, "planes", REST_SHARES, UP_PARTS, send, recv, 0
    )
    moving += split_gatherings(
        down_ref, down_out, "rows", REST_SHARES, DOWN_PARTS, send, recv, base
    )
    base = len(moving) * GATHER_SEMS

    def kv_copy(source, place, slot, bit):
        return pltpu.make_async_remote_copy(
            src_ref=source,
            dst_ref=place,
            send_sem=send.at[base + slot],
            recv_sem=recv.at[base + slot],
            device_id=partner(bit),
            device_id_type=MESH,
        )

    count = kv_ref.shape[0] // len(KV_EVENTS)
    overs, nears, fars, keeps = [], [], [], []
    for index in range(len(KV_EVENTS)):
        rows = pl.ds(index * count, count)
        own = kv_ref.at[rows, :]
        mine = kv_out.at[me[Y], me[CORE], rows, :]
        other = kv_out.at[1 - me[Y], me[CORE], rows, :]
        overs.append(kv_copy(own, mine, 4 * index, Y))
        nears.append(kv_copy(own, mine, 4 * index + 1, CORE))
        fars.append(kv_copy(other, other, 4 * index + 2, CORE))
        keeps.append(pltpu.make_async_copy(own, mine, send.at[base + 4 * index + 3]))
    for part in moving:
        part.begin()
    for copy in nears + keeps:
        copy.start()
    for index, (part, phase) in enumerate(REST_EVENTS):
        for piece, event in enumerate(KV_EVENTS):
            if index == event:
                overs[piece].start()
        moving[part].advance(phase)
    for over, far in zip(overs, fars):
        over.wait_recv()
        far.start()
    for part in moving:
        part.finish()
    for over, near, far, keep in zip(overs, nears, fars, keeps):
        near.wait_recv()
        far.wait_recv()
        keep.wait()
        for copy in (over, near, far):
            copy.wait_send()


def second_gather(up_block, down_block, key_value):
    rows, width = up_block.shape
    local, wide = key_value.shape
    blocks = jax.ShapeDtypeStruct((2, 2, 2, 2, 2, rows, width), bfloat)
    up, down, kv = pl.pallas_call(
        second_gather_kernel,
        out_shape=(blocks, blocks, jax.ShapeDtypeStruct((2, 2, local, wide), bfloat)),
        in_specs=[IN_VMEM] * 3,
        out_specs=(IN_HBM,) * 3,
        scratch_shapes=[pltpu.SemaphoreType.DMA(((len(UP_PARTS) + len(DOWN_PARTS)) * GATHER_SEMS + 4 * len(KV_EVENTS),))] * 2,
        compiler_params=pltpu.CompilerParams(
            collective_id=2, has_side_effects=True, vmem_limit_bytes=VMEM_LIMIT
        ),
        cost_estimate=cost(0, 128 * rows * width),
        name="second_gather",
    )(up_block, down_block, key_value)
    count = BLOCKS * PLANES * rows
    return (
        up.reshape(PLANES, BLOCKS * rows, width),
        down.reshape(count, width),
        kv.reshape(PLANES * local, wide),
    )


def slot_of(bucket_bits, seq_bits):
    slot = 0
    for axis, amount in SLOT_DIMS:
        bits = bucket_bits if axis == "bucket" else seq_bits
        slot = slot * 2 + ((bits >> amount.bit_length() - 1) & 1)
    return slot


def natural_sum(far, near, layout):
    width = far.shape[2]
    both = jnp.concatenate([near, far])
    index = {
        (b, s): slot_of(b, s) + near.shape[0] * (s % 2)
        for b in range(BLOCKS)
        for s in range(PLANES)
    }
    if layout == "rows":
        picked = [index[b, s] for b in range(BLOCKS) for s in range(PLANES)]
        gradient = jnp.stack([both[k] for k in picked]).reshape(-1, width)
        part = lax.psum_scatter(gradient, ("bucket", "seq"), scatter_dimension=0, tiled=True)
        return part.astype(single)
    picked = [index[b, s] for s in range(PLANES) for b in range(BLOCKS)]
    gradient = jnp.stack([both[k] for k in picked]).reshape(PLANES, -1, width)
    part = lax.psum_scatter(gradient, "seq", scatter_dimension=0)
    return lax.psum_scatter(part, "bucket", scatter_dimension=0, tiled=True).astype(single)


SLOT_DIMS = (Y, X, Z1, Z0)


class Scattering:
    def __init__(self, far, near, total, arrivals, out, order, first, rows, send, recv, base):
        self.far, self.near, self.total, self.arrivals = far, near, total, arrivals
        self.out, self.order, self.first, self.rows = out, order, first, rows
        self.send, self.recv, self.base = send, recv, base
        self.span = (pl.ds(first, rows), slice(None))

    def copy(self, source, place, slot, bit):
        return pltpu.make_async_remote_copy(
            src_ref=source,
            dst_ref=place,
            send_sem=self.send.at[self.base + slot],
            recv_sem=self.recv.at[self.base + slot],
            device_id=partner(bit),
            device_id_type=MESH,
        )

    def across(self):
        index = (slice(None),) * 4 + self.span
        return self.copy(self.far.at[index], self.total.at[index], 4, CORE)

    def place(self, fixed):
        return tuple(fixed.get(dim, slice(None)) for dim in SLOT_DIMS)

    def hop(self, phase):
        fixed = {dim: 0 for dim in self.order[:phase]} | {self.order[phase]: 1}
        source = self.total.at[self.place(fixed) + self.span]
        place = self.arrivals[phase].at[(slice(None),) * (3 - phase) + self.span]
        return self.copy(source, place, phase, self.order[phase])

    def add(self, fixed, source, source_dims):
        free = [dim for dim in SLOT_DIMS if dim not in fixed]

        def one(step):
            index = dict(fixed)
            for place, dim in enumerate(free):
                index[dim] = (step >> place) & 1
            spot = tuple(index[dim] for dim in SLOT_DIMS) + self.span
            term = source[tuple(index[dim] for dim in source_dims) + self.span]
            self.total[spot] = (self.total[spot].astype(single) + term.astype(single)).astype(
                bfloat
            )

        if free:
            pl.loop(0, 2 ** len(free))(one)
        else:
            one(0)

    def advance(self, phase):
        if phase < 0:
            self.across().wait_recv()
            source, dims, fixed = self.near, SLOT_DIMS, {}
        else:
            self.hop(phase).wait_recv()
            done = self.order[: phase + 1]
            dims = tuple(dim for dim in SLOT_DIMS if dim not in done)
            source, fixed = self.arrivals[phase], {dim: 0 for dim in done}
        if phase == 3:
            spot = (0,) * 4 + self.span
            self.out[self.span] = self.total[spot].astype(single) + source[self.span].astype(
                single
            )
            return
        ahead = self.order[phase + 1]
        self.add(fixed | {ahead: 1}, source, dims)
        self.hop(phase + 1).start()
        self.add(fixed | {ahead: 0}, source, dims)

    def finish(self):
        self.across().wait_send()
        for phase in range(4):
            self.hop(phase).wait_send()


SCATTER_SEMS = 5


def scatter_scratch(rows, width):
    return [
        pltpu.VMEM((2,) * free + (rows, width), bfloat) for free in (4, 3, 2, 1, 0)
    ]


def split_scatterings(far, near, scratch, out, shares, orders, send, recv, base):
    moving, first = [], 0
    for index, (count, order) in enumerate(zip(shares, orders)):
        slot = base + SCATTER_SEMS * index
        moving.append(
            Scattering(
                far, near, scratch[0], scratch[1:], out, order, first, count, send, recv, slot
            )
        )
        first += count
    return moving


def first_scatter_kernel(
    kv_far, kv_near, up_far, up_near, down_far, down_near, kv_out, up_out, down_out, *refs
):
    up_scratch, down_scratch, (kv_total, kv_arrival, send, recv) = refs[:5], refs[5:10], refs[10:]
    greet([partner(bit) for bit in (X, Z0, Z1, CORE, Y)])
    base = len(UP_SUM_PARTS) * SCATTER_SEMS
    moving = split_scatterings(
        up_far, up_near, up_scratch, up_out, REST_SHARES, UP_SUM_PARTS, send, recv, 0
    ) + split_scatterings(
        down_far, down_near, down_scratch, down_out, REST_SHARES, DOWN_SUM_PARTS, send, recv, base
    )
    base = len(moving) * SCATTER_SEMS
    local = kv_out.shape[0]
    count = local // len(KV_EVENTS)

    def kv_copy(source, place, slot, bit):
        return pltpu.make_async_remote_copy(
            src_ref=source,
            dst_ref=place,
            send_sem=send.at[base + slot],
            recv_sem=recv.at[base + slot],
            device_id=partner(bit),
            device_id_type=MESH,
        )

    nears, overs = [], []
    for index in range(len(KV_EVENTS)):
        rows = pl.ds(index * count, count)
        nears.append(
            kv_copy(kv_far.at[:, rows, :], kv_total.at[:, rows, :], 2 * index, CORE)
        )
        overs.append(
            kv_copy(kv_total.at[1, rows, :], kv_arrival.at[rows, :], 2 * index + 1, Y)
        )
    nears[0].start()
    for part in moving:
        part.across().start()
    for near in nears[1:]:
        near.start()

    def kv_add(index, side):
        rows = pl.ds(index * count, count)
        kv_total[side, rows, :] = (
            kv_total[side, rows, :].astype(single) + kv_near[side, rows, :].astype(single)
        ).astype(bfloat)

    for index, (part, phase) in enumerate(REST_SUM_EVENTS):
        for piece, event in enumerate(KV_SUM_EVENTS):
            if index == event:
                nears[piece].wait_recv()
                kv_add(piece, 1)
                overs[piece].start()
                kv_add(piece, 0)
        moving[part].advance(phase)
    for index, over in enumerate(overs):
        over.wait_recv()
        rows = pl.ds(index * count, count)
        kv_out[rows, :] = (
            kv_total[0, rows, :].astype(single) + kv_arrival[rows, :].astype(single)
        ).astype(bfloat)
    for part in moving:
        part.finish()
    for copy in nears + overs:
        copy.wait_send()


KV_SUM_EVENTS = (2, 9, 13, 17)


def first_scatter(kv_far, kv_near, up_far, up_near, down_far, down_near):
    rows, width = up_far.shape[1:]
    local, wide = kv_far.shape[1:]
    cube = (2, 2, 2, 2, rows, width)
    mine = jax.ShapeDtypeStruct((rows, width), single)
    sems = (len(UP_SUM_PARTS) + len(DOWN_SUM_PARTS)) * SCATTER_SEMS + 2 * len(KV_SUM_EVENTS)
    return pl.pallas_call(
        first_scatter_kernel,
        out_shape=(jax.ShapeDtypeStruct((local, wide), bfloat), mine, mine),
        in_specs=[IN_HBM, IN_VMEM] * 3,
        out_specs=(IN_VMEM,) * 3,
        scratch_shapes=scatter_scratch(rows, width)
        + scatter_scratch(rows, width)
        + [pltpu.VMEM((2, local, wide), bfloat), pltpu.VMEM((local, wide), bfloat)]
        + [pltpu.SemaphoreType.DMA((sems,))] * 2,
        compiler_params=pltpu.CompilerParams(
            collective_id=3, has_side_effects=True, vmem_limit_bytes=VMEM_LIMIT
        ),
        cost_estimate=cost(0, 128 * rows * width),
        name="first_scatter",
    )(
        kv_far,
        kv_near,
        up_far.reshape(cube),
        up_near.reshape(cube),
        down_far.reshape(cube),
        down_near.reshape(cube),
    )


def last_scatter_kernel(
    note_ref,
    ada_ref,
    far_ref,
    near_ref,
    out_ref,
    mod_ref,
    bias_ref,
    silu_ref,
    *refs,
):
    scratch, refs = refs[:5], refs[5:]
    inbox, parts, returns, note_send, note_recv, back_send, back_recv, send, recv = refs
    bucket, seq = lax.axis_index("bucket"), lax.axis_index("seq")
    me = bucket * PLANES + seq
    count = BLOCKS * PLANES
    barrier = pltpu.get_barrier_semaphore()

    @pl.loop(1, count)
    def _(distance):
        pl.semaphore_signal(barrier, inc=1, device_id=peer_at(distance), device_id_type=MESH)

    pl.semaphore_wait(barrier, count - 1)

    def note(distance):
        peer = peer_at(distance)
        return pltpu.make_async_remote_copy(
            src_ref=note_ref.at[peer[0] * PLANES + peer[1]],
            dst_ref=inbox.at[me],
            send_sem=note_send.at[distance],
            recv_sem=note_recv.at[distance],
            device_id=peer,
            device_id_type=MESH,
        )

    def answer(distance):
        peer = peer_at(distance)
        return pltpu.make_async_remote_copy(
            src_ref=parts.at[peer[0]],
            dst_ref=returns.at[me],
            send_sem=back_send.at[distance],
            recv_sem=back_recv.at[distance],
            device_id=peer,
            device_id_type=MESH,
        )

    moving = split_scatterings(
        far_ref, near_ref, scratch, out_ref, PAIR_SHARES, PAIR_SUM_PARTS, send, recv, 0
    )
    for part in moving:
        part.across().start()

    @pl.loop(1, count)
    def _(distance):
        note(distance).start()

    inbox[me] = note_ref[me]
    for part, phase in PAIR_SUM_EVENTS[:SUM_NOTE_EVENT]:
        moving[part].advance(phase)

    @pl.loop(1, count)
    def _(distance):
        note(distance).wait_recv()

    rows, cols = ada_ref.shape
    spot = bias_ref.shape[1]
    sums = [sum(inbox[PLANES * g + s] for s in range(PLANES)) for g in range(BLOCKS)]
    bias_ref[...] = sum(sums)[:, :spot]
    mods = jnp.concatenate(sums)[:, spot : spot + cols]
    mod_ref[...] = mods
    silu = lax.dot_general(
        mods,
        ada_ref[...].astype(single),
        (((1,), (1,)), ((), ())),
        preferred_element_type=single,
        precision=HIGHEST,
    )
    for group in range(BLOCKS):
        parts[group, :, :rows] = silu[group : group + 1, :]
        parts[group, :, rows:] = jnp.zeros((1, parts.shape[2] - rows), single)
    returns[me] = parts[bucket]

    @pl.loop(1, count)
    def _(distance):
        answer(distance).start()

    for part, phase in PAIR_SUM_EVENTS[SUM_NOTE_EVENT:]:
        moving[part].advance(phase)

    @pl.loop(1, count)
    def _(distance):
        answer(distance).wait_recv()

    for group in range(BLOCKS):
        silu_ref[group] = sum(returns[PLANES * group + s] for s in range(PLANES))
    for part in moving:
        part.finish()

    @pl.loop(1, count)
    def _(distance):
        note(distance).wait_send()
        answer(distance).wait_send()


SUM_NOTE_EVENT = 9


def last_scatter(notes, ada_low, far, near, spot):
    rows, width = far.shape[1:]
    cube = (2, 2, 2, 2, rows, width)
    count = BLOCKS * PLANES
    cols = ada_low.shape[1]
    return pl.pallas_call(
        last_scatter_kernel,
        out_shape=(
            jax.ShapeDtypeStruct((rows, width), single),
            jax.ShapeDtypeStruct((BLOCKS, cols), single),
            jax.ShapeDtypeStruct((1, spot), single),
            jax.ShapeDtypeStruct((BLOCKS, 1, 2 * LANES), single),
        ),
        in_specs=[IN_VMEM, IN_VMEM, IN_HBM, IN_VMEM],
        out_specs=(IN_VMEM,) * 4,
        scratch_shapes=scatter_scratch(rows, width)
        + [
            pltpu.VMEM(notes.shape, single),
            pltpu.VMEM((BLOCKS, 1, 2 * LANES), single),
            pltpu.VMEM((count, 1, 2 * LANES), single),
        ]
        + [pltpu.SemaphoreType.DMA((count,))] * 4
        + [pltpu.SemaphoreType.DMA((len(PAIR_SUM_PARTS) * SCATTER_SEMS,))] * 2,
        compiler_params=pltpu.CompilerParams(
            collective_id=4, has_side_effects=True, vmem_limit_bytes=VMEM_LIMIT
        ),
        cost_estimate=cost(0, 64 * rows * width),
        name="last_scatter",
    )(notes, ada_low, far.reshape(cube), near.reshape(cube))


def whole(shape):
    return pl.BlockSpec(shape, lambda *_: (0,) * len(shape))


def qkv_kernel(cols, x_ref, shift_ref, scale_ref, bias_ref, w_ref, a_ref, q_ref, kv_ref, acc):
    step = pl.program_id(0)
    width = x_ref.shape[1]

    @pl.when(step == 0)
    def _():
        values = x_ref[...].astype(single)
        a_ref[...] = modulate(values, shift_ref[...], scale_ref[...]).astype(bfloat)

    wide = -(-cols // LANES) * LANES
    part = dot_nn(a_ref[...], w_ref[0, :, :wide])[:, :cols]
    for index in range(PLANES):

        @pl.when(step == index)
        def _():
            acc[:, index * cols : (index + 1) * cols] = part

    @pl.when(step == PLANES - 1)
    def _():
        q_ref[...] = (acc[:, :width] + bias_ref[:, :width]).astype(bfloat)
        kv_ref[...] = (acc[:, width:] + bias_ref[:, width:]).astype(bfloat)


def project_qkv(tokens, shift_row, scale_row, bias_row, weight):
    rows, width = tokens.shape
    cols = 3 * width // PLANES
    return pl.pallas_call(
        functools.partial(qkv_kernel, cols),
        grid=(PLANES,),
        out_shape=(
            jax.ShapeDtypeStruct((rows, width), bfloat),
            jax.ShapeDtypeStruct((rows, width), bfloat),
            jax.ShapeDtypeStruct((rows, 2 * width), bfloat),
        ),
        in_specs=[
            whole((rows, width)),
            whole((1, width)),
            whole((1, width)),
            whole((1, 3 * width)),
            pl.BlockSpec((1,) + weight.shape[1:], lambda s: (s, 0, 0)),
        ],
        out_specs=(whole((rows, width)), whole((rows, width)), whole((rows, 2 * width))),
        scratch_shapes=[pltpu.VMEM((rows, 3 * width), single)],
        compiler_params=params("arbitrary"),
        cost_estimate=cost(6 * rows * width * width, 8 * width * width),
        name="project_qkv",
    )(tokens, shift_row, scale_row, bias_row, weight)


def image_of(len_ref, position):
    start, length, end = jnp.int32(0), jnp.int32(0), jnp.int32(0)
    for index in range(len_ref.shape[1]):
        here = len_ref[0, index]
        inside = jnp.logical_and(position >= end, position < end + here)
        start = jnp.where(inside, end, start)
        length = jnp.where(inside, here, length)
        end = end + here
    return start, length


def head_windows(heads, size):
    for head in range(heads):
        low, high = head * size, (head + 1) * size
        yield head, low // LANES * LANES, -(-high // LANES) * LANES, low, high


def head_mask(low, high, left, right):
    lane = lax.broadcasted_iota(jnp.int32, (1, high - low), 1) + low
    return jnp.logical_and(lane >= left, lane < right)


LONG, SHORT = 1024, 256


def attend_kernel(heads, len_ref, q_ref, hm_ref, kv, ob_ref, log_ref, out):
    rows, width = q_ref.shape
    size = width // heads
    my_seq = lax.axis_index("seq")
    factor = size ** (-0.5) * LOG2E

    def run(tile_start, start, span):
        tile = pl.ds(tile_start, TILE)
        keys = pl.ds(start, span)
        logs = jnp.zeros((TILE, LANES), single)
        lane = lax.broadcasted_iota(jnp.int32, (TILE, LANES), 1)
        for head, low, high, left, right in head_windows(heads, size):
            mask = head_mask(low, high, left, right)
            query = q_ref[tile, low:high] * mask.astype(single).astype(bfloat)
            scores = dot_nt(query, kv[keys, low:high])
            top = jnp.max(scores, axis=-1, keepdims=True)
            expo = jnp.exp2((scores - top) * factor)
            total = jnp.sum(expo, axis=-1, keepdims=True)
            part = dot_nn(expo.astype(bfloat), kv[keys, width + low : width + high]) / total
            out[tile, low:high] = jnp.where(mask, part, out[tile, low:high])
            logs = jnp.where(lane == head, top * factor + jnp.log2(total), logs)
        log_ref[:, tile] = logs.T[:heads, :]

    @pl.loop(0, rows // TILE)
    def _(index):
        tile_start = pl.multiple_of(index * TILE, TILE)
        start, length = image_of(len_ref, my_seq * rows + tile_start)
        start = pl.multiple_of(start, SHORT)

        @pl.when(length > SHORT)
        def _():
            run(tile_start, start, LONG)

        @pl.when(length <= SHORT)
        def _():
            run(tile_start, start, SHORT)

    ob_ref[...] = (out[...] * hm_ref[...]).astype(bfloat)


def attend(lengths, query, kv, head_row, heads):
    rows, width = query.shape
    group = kv.shape[0]
    return pl.pallas_call(
        functools.partial(attend_kernel, heads),
        out_shape=(
            jax.ShapeDtypeStruct((rows, width), bfloat),
            jax.ShapeDtypeStruct((heads, rows), single),
        ),
        in_specs=[pl.BlockSpec(memory_space=pltpu.SMEM)]
        + [IN_VMEM] * 3,
        out_specs=(IN_VMEM,) * 2,
        scratch_shapes=[pltpu.VMEM((rows, width), single)],
        compiler_params=params(),
        cost_estimate=cost(16 * rows * LONG * width, 10 * group * width, heads * rows * LONG),
        name="attend",
    )(lengths, query, head_row, kv)


def out_kernel(
    ob_ref, w_ref, bias_ref, x_ref, gate_ref, shift_ref, scale_ref, r_ref, mid_ref, a_ref
):
    step = pl.program_id(0)
    width = x_ref.shape[1]
    steps = pl.num_programs(0)
    cols = width // 4
    part = dot_nn(ob_ref[...], w_ref[0])[:, -cols:]
    for index in range(4):

        @pl.when(step == index)
        def _():
            r_ref[:, index * cols : (index + 1) * cols] = part

    @pl.when(step == steps - 1)
    def _():
        result = r_ref[...] + bias_ref[...]
        r_ref[...] = result
        middle = x_ref[...].astype(single) + gate_ref[...] * result
        mid_ref[...] = middle
        a_ref[...] = modulate(middle, shift_ref[...], scale_ref[...]).astype(bfloat)


def project_out(branch, weight, bias_row, tokens, gate_row, shift_row, scale_row):
    rows, width = tokens.shape
    planes = weight.shape[0]
    row = whole((1, width))
    return pl.pallas_call(
        out_kernel,
        grid=(planes,),
        out_shape=(
            jax.ShapeDtypeStruct((rows, width), single),
            jax.ShapeDtypeStruct((rows, width), single),
            jax.ShapeDtypeStruct((rows, width), bfloat),
        ),
        in_specs=[
            whole((rows, width)),
            pl.BlockSpec((1, width, 3 * LANES), lambda s: (s, 0, 2)),
            row,
            whole((rows, width)),
            row,
            row,
            row,
        ],
        out_specs=(whole((rows, width)),) * 3,
        compiler_params=params("arbitrary"),
        cost_estimate=cost(2 * rows * width * width, 2 * width * width + 12 * rows * width),
        name="project_out",
    )(branch, weight, bias_row, tokens, gate_row, shift_row, scale_row)


def out_copies(source, layout, plane, buffer, seq_bits, far_ref, near_ref, sem):
    my_bucket, my_seq = place_in_kernel()
    rows = far_ref.shape[1]
    copies = []
    for index in range(BLOCKS):
        if layout == "rows":
            bits, part = index % PLANES, index // PLANES
            seq = my_seq ^ bits
            bucket = plane * (BLOCKS // PLANES) + part
            start = pl.multiple_of((part * PLANES + seq) * rows, 16)
            side = bits % 2
        else:
            bits, bucket, start, side = seq_bits, index, index * rows, seq_bits_side(seq_bits)
        target = far_ref if side else near_ref
        slot = slot_of(bucket ^ my_bucket, bits if layout == "rows" else seq_bits[0])
        copies.append(
            pltpu.make_async_copy(
                source.at[buffer, pl.ds(start, rows), :], target.at[slot], sem.at[buffer, index]
            )
        )
    return copies


def seq_bits_side(seq_bits):
    return seq_bits[1]


def ffn_kernel(a_ref, df_ref, cm_ref, b_ref, up_ref, down_ref, *refs):
    f_ref, da_ref, up_far, up_near, down_far, down_near, db_ref = refs[:7]
    up, down, up_grad, down_grad, up_sem, down_sem, up_out, down_out = refs[7:]
    width = a_ref.shape[1]
    my_seq = place_in_kernel()[1]

    def loads(bits):
        plane = my_seq ^ bits
        rows = pl.ds(pl.multiple_of(plane * width, LANES), width)
        return (
            pltpu.make_async_copy(up_ref.at[plane], up.at[plane], up_sem.at[bits]),
            pltpu.make_async_copy(down_ref.at[rows, :], down.at[rows, :], down_sem.at[bits]),
        )

    for bits in (1, 3, 0, 2):
        for copy in loads(bits):
            copy.start()
    f_ref[...] = jnp.zeros_like(f_ref)
    da_ref[...] = jnp.zeros_like(da_ref)

    def one(plane, low, high, buffer):
        first, grad = a_ref[...], df_ref[...]
        hidden_rows = pl.ds(pl.multiple_of(plane * width + low, LANES), high - low)
        keep = cm_ref[plane, :, low:high]
        pre = dot_nn(first, up[plane, :, low:high]) + b_ref[plane, :, low:high]
        root = math.sqrt(2.0 / math.pi)
        square = pre * pre
        bend = jnp.tanh(root * pre * (1.0 + 0.044715 * square))
        half = 0.5 * (1.0 + bend)
        hidden = (pre * half * keep).astype(bfloat)
        slope = half + 0.5 * pre * (1.0 - bend * bend) * (root * (1.0 + 0.134145 * square))
        back = (dot_nt(grad, down[hidden_rows, :]) * keep * slope).astype(bfloat)
        f_ref[...] += dot_nn(hidden, down[hidden_rows, :])
        da_ref[...] += dot_nt(back, up[plane, :, low:high])
        up_grad[buffer, :, low:high] = dot_tn(first, back).astype(bfloat)
        down_grad[buffer, low:high, :] = dot_tn(hidden, grad).astype(bfloat)
        db_ref[plane, :, low:high] = jnp.sum(back.astype(single), axis=0, keepdims=True)

    cut = -(-width // 2 // LANES) * LANES

    def sends(plane, buffer, side_bits, far_side):
        return out_copies(
            up_grad, "planes", plane, buffer, (side_bits, far_side), up_far, up_near, up_out
        ) + out_copies(
            down_grad, "rows", plane, buffer, None, down_far, down_near, down_out
        )

    for far_side in (1, 0):

        @pl.loop(0, 2)
        def _(above):
            bits = above * 2 + far_side
            plane = my_seq ^ bits
            if not far_side:
                for copy in sends(plane, above, bits, far_side):
                    copy.wait()
            for copy in loads(bits):
                copy.wait()
            one(plane, 0, cut, above)
            one(plane, cut, width, above)
            for copy in sends(plane, above, bits, far_side):
                copy.start()

    for above in range(2):
        for copy in sends(my_seq ^ (above * 2), above, above * 2, 0):
            copy.wait()


def feed_forward(first, grad, chan_row, bias_row, up_weight, down_weight):
    rows, width = first.shape
    hidden = chan_row.shape[1]
    blocks = jax.ShapeDtypeStruct((BLOCKS * PLANES // 2, width // BLOCKS, width), bfloat)
    result = pl.pallas_call(
        ffn_kernel,
        out_shape=(
            jax.ShapeDtypeStruct((rows, width), single),
            jax.ShapeDtypeStruct((rows, width), single),
            blocks,
            blocks,
            blocks,
            blocks,
            jax.ShapeDtypeStruct((PLANES, 1, width), single),
        ),
        in_specs=[IN_VMEM] * 4 + [IN_HBM] * 2,
        out_specs=(IN_VMEM, IN_VMEM) + (IN_HBM,) * 4 + (IN_VMEM,),
        scratch_shapes=[
            pltpu.VMEM((PLANES, width, width), bfloat),
            pltpu.VMEM((hidden, width), bfloat),
            pltpu.VMEM((2, width, width), bfloat),
            pltpu.VMEM((2, width, width), bfloat),
            pltpu.SemaphoreType.DMA((PLANES,)),
            pltpu.SemaphoreType.DMA((PLANES,)),
            pltpu.SemaphoreType.DMA((2, BLOCKS)),
            pltpu.SemaphoreType.DMA((2, BLOCKS)),
        ],
        compiler_params=params(),
        cost_estimate=cost(12 * rows * width * hidden, 8 * width * hidden, rows * hidden),
        name="feed_forward",
    )(
        first,
        grad,
        chan_row.reshape(PLANES, 1, width),
        bias_row.reshape(PLANES, 1, width),
        up_weight,
        down_weight,
    )
    return result


def back_out_kernel(heads, dr_ref, w_ref, hm_ref, ob_ref, do_ref, delta_ref, acc):
    step = pl.program_id(0)
    part = dot_nt(dr_ref[0], w_ref[0])

    @pl.when(step == 0)
    def _():
        acc[...] = part

    @pl.when(step > 0)
    def _():
        acc[...] += part

    @pl.when(step == pl.num_programs(0) - 1)
    def _():
        width = acc.shape[1]
        size = width // heads
        grad = (acc[...] * hm_ref[...]).astype(bfloat)
        do_ref[...] = grad
        terms = grad.astype(single) * ob_ref[...].astype(single)
        head = lax.broadcasted_iota(jnp.int32, (heads, width), 0)
        lane = lax.broadcasted_iota(jnp.int32, (heads, width), 1)
        chosen = jnp.logical_and(lane >= head * size, lane < (head + 1) * size)
        delta_ref[...] = lax.dot_general(
            chosen.astype(single),
            terms,
            (((1,), (1,)), ((), ())),
            preferred_element_type=single,
            precision=HIGHEST,
        )


def back_out(dr_planes, weight, head_row, branch, heads):
    rows, width = branch.shape
    planes = weight.shape[0]
    return pl.pallas_call(
        functools.partial(back_out_kernel, heads),
        grid=(planes,),
        out_shape=(
            jax.ShapeDtypeStruct((rows, width), bfloat),
            jax.ShapeDtypeStruct((heads, rows), single),
        ),
        in_specs=[
            pl.BlockSpec((1, rows, 3 * LANES), lambda s: (s, 0, 0)),
            pl.BlockSpec((1, width, 3 * LANES), lambda s: (s, 0, 2)),
            whole((1, width)),
            whole((rows, width)),
        ],
        out_specs=(whole((rows, width)), whole((heads, rows))),
        scratch_shapes=[pltpu.VMEM((rows, width), single)],
        compiler_params=params("arbitrary"),
        cost_estimate=cost(2 * rows * width * width, 2 * width * width),
        name="back_out",
    )(dr_planes, weight, head_row, branch)


def attend_back_kernel(
    heads, len_ref, q_ref, do_ref, log_ref, delta_ref, kv, dq_ref, far_ref, near_ref, dq, dk, dv
):
    rows, width = q_ref.shape
    size = width // heads
    my_seq = lax.axis_index("seq")
    scale = size ** (-0.5)
    factor = scale * LOG2E
    dk[...] = jnp.zeros_like(dk)
    dv[...] = jnp.zeros_like(dv)

    def run(tile_start, start, span):
        tile = pl.ds(tile_start, TILE)
        keys = pl.ds(start, span)
        for head, low, high, left, right in head_windows(heads, size):
            mask = head_mask(low, high, left, right)
            chosen = mask.astype(single).astype(bfloat)
            query = q_ref[tile, low:high] * chosen
            grad = do_ref[tile, low:high] * chosen
            key = kv[keys, low:high]
            probs = jnp.exp2(dot_nt(key, query) * factor - log_ref[head : head + 1, tile])
            slope = dot_nt(kv[keys, width + low : width + high], grad)
            score_grad = (probs * (slope - delta_ref[head : head + 1, tile])).astype(bfloat)
            dv[keys, low:high] += dot_nn(probs.astype(bfloat), grad)
            dk[keys, low:high] += dot_nn(score_grad, query)
            part = dot_tn(score_grad, key)
            dq[tile, low:high] = jnp.where(mask, part, dq[tile, low:high])

    @pl.loop(0, rows // TILE)
    def _(index):
        tile_start = pl.multiple_of(index * TILE, TILE)
        start, length = image_of(len_ref, my_seq * rows + tile_start)
        start = pl.multiple_of(start, SHORT)

        @pl.when(length > SHORT)
        def _():
            run(tile_start, start, LONG)

        @pl.when(length <= SHORT)
        def _():
            run(tile_start, start, SHORT)

    dq_ref[...] = (dq[...] * scale).astype(bfloat)
    base = place_in_kernel()[1]
    for bits in range(PLANES):
        place = pl.ds(pl.multiple_of((base ^ bits) * rows, rows), rows)
        target = far_ref if bits % 2 else near_ref
        target[bits // 2, :, :width] = (dk[place, :] * scale).astype(bfloat)
        target[bits // 2, :, width:] = dv[place, :].astype(bfloat)


def attend_back(lengths, query, grad, logs, delta, kv, heads):
    rows, width = query.shape
    group = kv.shape[0]
    return pl.pallas_call(
        functools.partial(attend_back_kernel, heads),
        out_shape=(
            jax.ShapeDtypeStruct((rows, width), bfloat),
            jax.ShapeDtypeStruct((2, rows, 2 * width), bfloat),
            jax.ShapeDtypeStruct((2, rows, 2 * width), bfloat),
        ),
        in_specs=[pl.BlockSpec(memory_space=pltpu.SMEM)]
        + [IN_VMEM] * 5,
        out_specs=(IN_VMEM,) * 3,
        scratch_shapes=[
            pltpu.VMEM((rows, width), single),
            pltpu.VMEM((group, width), single),
            pltpu.VMEM((group, width), single),
        ],
        compiler_params=params(),
        cost_estimate=cost(40 * rows * LONG * width, 20 * group * width, heads * rows * LONG),
        name="attend_back",
    )(lengths, query, grad, logs, delta, kv)


def back_qkv_kernel(
    a_ref, ob_ref, dy_ref, dr_ref, w_ref, da_ref, far_ref, near_ref, stage, sem
):
    my_seq = place_in_kernel()[1]
    wide = dy_ref.shape[2]
    below = wide - LANES
    da_ref[...] = jnp.zeros_like(da_ref)

    def sends(plane, buffer, bits, far_side):
        return out_copies(
            stage, "planes", plane, buffer, (bits, far_side), far_ref, near_ref, sem
        )

    for far_side in (1, 0):

        @pl.loop(0, 2)
        def _(above):
            bits = above * 2 + far_side
            plane = my_seq ^ bits
            if not far_side:
                for copy in sends(plane, above, bits, far_side):
                    copy.wait()
            da_ref[...] += dot_nt(dy_ref[plane], w_ref[plane, :, :wide])
            first = dot_tn(a_ref[...], dy_ref[plane])
            second = dot_tn(ob_ref[...], dr_ref[plane])
            stage[above, :, :below] = first[:, :below].astype(bfloat)
            stage[above, :, below:wide] = (first[:, below:] + second[:, :LANES]).astype(bfloat)
            stage[above, :, wide:] = second[:, LANES:].astype(bfloat)
            for copy in sends(plane, above, bits, far_side):
                copy.start()

    for above in range(2):
        for copy in sends(my_seq ^ (above * 2), above, above * 2, 0):
            copy.wait()


def back_qkv(first_in, branch, dy_planes, dr_planes, weight):
    rows, width = first_in.shape
    blocks = jax.ShapeDtypeStruct((BLOCKS * PLANES // 2, width // BLOCKS, width), bfloat)
    return pl.pallas_call(
        back_qkv_kernel,
        out_shape=(jax.ShapeDtypeStruct((rows, width), single), blocks, blocks),
        in_specs=[IN_VMEM] * 5,
        out_specs=(IN_VMEM, IN_HBM, IN_HBM),
        scratch_shapes=[
            pltpu.VMEM((2, width, width), bfloat),
            pltpu.SemaphoreType.DMA((2, BLOCKS)),
        ],
        compiler_params=params(),
        cost_estimate=cost(14 * rows * width * width, 4 * weight.size),
        name="back_qkv",
    )(first_in, branch, dy_planes, dr_planes, weight)


def on_device(
    tokens,
    condition,
    cotangent,
    lengths,
    bucket_ids,
    keep_flags,
    head_table,
    chan_table,
    ada_master,
    ada_first,
    ada_second,
    ada_average,
    qkv_master,
    qkv_first,
    qkv_second,
    qkv_average,
    out_master,
    out_first,
    out_second,
    out_average,
    up_master,
    up_first,
    up_second,
    up_average,
    down_master,
    down_first,
    down_second,
    down_average,
    bias_master,
    bias_first,
    bias_second,
    bias_average,
):
    local_rows, width = tokens.shape
    heads = head_table.shape[1]
    head_size = width // heads
    hidden_width = chan_table.shape[1]
    hidden_ratio = hidden_width // width
    table_cols = 10 + hidden_ratio
    my_bucket, my_seq = lax.axis_index("bucket"), lax.axis_index("seq")
    buckets, seqs = lax.axis_size("bucket"), lax.axis_size("seq")
    group_rows = local_rows * seqs
    block_rows = qkv_master.shape[0]
    pair_block = jnp.concatenate([qkv_master, out_master], axis=1).astype(bfloat)
    down_block = lax.all_to_all(
        down_master.astype(bfloat), "seq", split_axis=0, concat_axis=1, tiled=True
    )
    up_block = up_master.astype(bfloat)
    ada_low = ada_master.astype(bfloat)
    if cube_path():
        count = bias_master.shape[0]
        spots = (LANES * 2, LANES * 4)
        slices = jnp.pad(condition.reshape(buckets, block_rows), ((0, 0), (0, spots[0] - block_rows)))
        told = jnp.broadcast_to(
            jnp.pad(bias_master, (0, spots[1] - count)), (buckets * seqs, spots[1])
        )
        notes = jnp.concatenate([jnp.repeat(slices, seqs, axis=0), told], axis=1)[:, None, :]
        pair_weight, inbox, silu_rows, mod_row = first_gather(notes, ada_low, pair_block)
        bias_low = inbox[:, 0, spots[0] : spots[0] + count].astype(bfloat).reshape(-1)
    else:
        pair_weight = gather_all(pair_block, "planes")
        bias_low = lax.all_gather(
            bias_master.astype(bfloat), ("bucket", "seq"), axis=0, tiled=True
        )
        silu_low = jax.nn.silu(condition).astype(bfloat)
        silu_all = lax.all_gather(silu_low, "bucket", axis=0, tiled=True)
        silu_rows = lax.dynamic_slice_in_dim(silu_all, my_bucket * block_rows, block_rows, 1)
        mod_part = lax.psum_scatter(
            dot_nn(silu_rows, ada_low), "bucket", scatter_dimension=0, tiled=True
        )
        mod_row = lax.all_gather(mod_part, "seq", axis=1, tiled=True)

    bias_table = bias_low.astype(single).reshape(width, table_cols).T
    modulation = mod_row.reshape(6, 1, width) + bias_table[:6, None, :]
    shift_one, scale_one, gate_one, shift_two, scale_two, gate_two = modulation
    value_bias = bias_table[7:8]
    qkv_bias = jnp.concatenate([bias_table[6:7], jnp.zeros_like(value_bias), value_bias], axis=1)
    out_bias = bias_table[8:9]
    up_bias = bias_table[9 : table_cols - 1].T.reshape(1, hidden_width)
    down_bias = bias_table[table_cols - 1 :]
    selector = (
        jnp.arange(head_table.shape[0], dtype=jnp.int32)[:, None] == bucket_ids[None, :]
    ).astype(single)
    head_row = jnp.repeat(jnp.sum(selector * head_table.astype(single), axis=0), head_size)[None]
    chan_row = jnp.sum(selector * chan_table.astype(single), axis=0)[None]
    keep_float = keep_flags.astype(single)[:, None]
    upstream = cotangent.astype(single)
    mlp_grad = (gate_two * keep_float * upstream).astype(bfloat)

    first_in, query, key_value = project_qkv(tokens, shift_one, scale_one, qkv_bias, pair_weight)
    if cube_path():
        up_weight, down_weight, near = second_gather(up_block, down_block, key_value)
    else:
        up_weight = gather_all(up_block, "planes")
        down_weight = gather_all(down_block, "rows")
        near = lax.all_gather(key_value, "seq", axis=0, tiled=True)
    branch_in, logs = attend(lengths, query, near, head_row, heads)
    attn_out, middle, second_in = project_out(
        branch_in, pair_weight, out_bias, tokens, gate_one, shift_two, scale_two
    )
    mlp_sum, second_grad, up_far, up_near, down_far, down_near, up_bias_grad = feed_forward(
        second_in, mlp_grad, chan_row, up_bias, up_weight, down_weight
    )
    mlp_out = mlp_sum + down_bias
    output = (middle + gate_two * keep_float * mlp_out).astype(bfloat)
    gate_two_grad = jnp.sum(keep_float * upstream * mlp_out, axis=0)
    down_bias_grad = jnp.sum(mlp_grad, axis=0, dtype=single)
    _, norm_two_back = jax.vjp(modulate, middle, shift_two[0], scale_two[0])
    middle_norm_grad, shift_two_grad, scale_two_grad = norm_two_back(second_grad)
    middle_grad = upstream + middle_norm_grad
    branch_grad = (gate_one * middle_grad).astype(bfloat)
    gate_one_grad = jnp.sum(middle_grad * attn_out, axis=0)
    out_bias_grad = jnp.sum(branch_grad, axis=0, dtype=single)
    out_cols = width // seqs
    dr_planes = jnp.pad(
        branch_grad.reshape(local_rows, seqs, out_cols).transpose(1, 0, 2),
        ((0, 0), (0, 0), (3 * LANES - out_cols, 0)),
    )
    attended_grad, delta = back_out(dr_planes, pair_weight, head_row, branch_in, heads)
    query_grad, kv_far, kv_near = attend_back(
        lengths, query, attended_grad, logs, delta, near, heads
    )
    if cube_path():
        kv_grad, up_new_grad, down_new_grad = first_scatter(
            kv_far, kv_near, up_far, up_near, down_far, down_near
        )
    else:
        terms = jnp.stack([kv_near[0], kv_far[0], kv_near[1], kv_far[1]])
        kv_grad = lax.psum_scatter(terms, "seq", scatter_dimension=0)
        up_new_grad = natural_sum(up_far, up_near, "planes")
        down_new_grad = natural_sum(down_far, down_near, "rows")
    projected_grad = jnp.concatenate([query_grad, kv_grad], axis=1)
    qkv_cols = 3 * width // seqs
    dy_planes = jnp.pad(
        projected_grad.reshape(local_rows, seqs, qkv_cols).transpose(1, 0, 2),
        ((0, 0), (0, 0), (0, -qkv_cols % LANES)),
    )
    first_grad, pair_far, pair_near = back_qkv(
        first_in, branch_in, dy_planes, dr_planes, pair_weight
    )
    query_bias_grad = jnp.sum(projected_grad[:, :width], axis=0, dtype=single)
    value_bias_grad = jnp.sum(projected_grad[:, 2 * width :], axis=0, dtype=single)
    inputs_float = tokens.astype(single)
    _, norm_one_back = jax.vjp(modulate, inputs_float, shift_one[0], scale_one[0])
    input_norm_grad, shift_one_grad, scale_one_grad = norm_one_back(first_grad)
    token_grad = middle_grad + input_norm_grad
    mod_grads = jnp.stack(
        [
            shift_one_grad,
            scale_one_grad,
            gate_one_grad,
            shift_two_grad,
            scale_two_grad,
            gate_two_grad,
        ]
    )
    bias_grad = jnp.concatenate(
        [
            mod_grads.T,
            query_bias_grad[:, None],
            value_bias_grad[:, None],
            out_bias_grad[:, None],
            up_bias_grad.reshape(width, hidden_ratio),
            down_bias_grad[:, None],
        ],
        axis=1,
    ).reshape(width * table_cols)
    mod_parts = mod_grads.reshape(seqs, 6 * width // seqs)
    if cube_path():
        count = bias_master.shape[0]
        spot = -(-count // LANES) * LANES
        notes = jnp.concatenate(
            [
                bias_grad.reshape(buckets * seqs, count),
                jnp.zeros((buckets * seqs, spot - count), single),
                jnp.tile(mod_parts, (buckets, 1)),
            ],
            axis=1,
        )
        notes = jnp.pad(notes, ((0, 0), (0, -notes.shape[1] % LANES)))[:, None, :]
        pair_new_grad, mod_all, bias_sum, silu_sum = last_scatter(
            notes, ada_low, pair_far, pair_near, spot
        )
        bias_new_grad = bias_sum[0, :count]
        silu_grad = silu_sum[:, 0, :block_rows].reshape(1, width)
    else:
        pair_new_grad = natural_sum(pair_far, pair_near, "planes")
        mod_mine = lax.psum_scatter(mod_parts, "seq", scatter_dimension=0, tiled=True)
        mod_all = lax.all_gather(mod_mine, "bucket", axis=0, tiled=True)
        silu_part = lax.dot_general(
            mod_all,
            ada_low.astype(single),
            (((1,), (1,)), ((), ())),
            preferred_element_type=single,
            precision=HIGHEST,
        )
        silu_grad = lax.all_to_all(
            lax.psum(silu_part, "seq"), "bucket", split_axis=0, concat_axis=1, tiled=True
        )
        bias_new_grad = lax.psum_scatter(
            bias_grad, ("bucket", "seq"), scatter_dimension=0, tiled=True
        )
    ada_new_grad = lax.dot_general(
        silu_rows.astype(single),
        mod_all,
        (((0,), (0,)), ((), ())),
        preferred_element_type=single,
        precision=HIGHEST,
    )
    _, silu_back = jax.vjp(jax.nn.silu, condition)
    condition_grad = silu_back(silu_grad)[0]
    down_mine = lax.all_to_all(
        down_new_grad.astype(bfloat), "seq", split_axis=1, concat_axis=0, tiled=True
    ).astype(single)
    out_rate = (group_rows / (16.0 * width)) ** 0.5
    ada_new = adam_update(
        ada_master, ada_first, ada_second, ada_average, ada_new_grad, width ** (-0.5), MATRIX_DECAY
    )
    qkv_new = adam_update(
        qkv_master,
        qkv_first,
        qkv_second,
        qkv_average,
        pair_new_grad[:, :qkv_cols],
        width ** (-0.5),
        MATRIX_DECAY,
    )
    out_new = adam_update(
        out_master,
        out_first,
        out_second,
        out_average,
        pair_new_grad[:, qkv_cols:],
        out_rate,
        MATRIX_DECAY,
    )
    up_new = adam_update(
        up_master, up_first, up_second, up_average, up_new_grad, width ** (-0.5), MATRIX_DECAY
    )
    down_new = adam_update(
        down_master,
        down_first,
        down_second,
        down_average,
        down_mine,
        hidden_width ** (-0.5),
        MATRIX_DECAY,
    )
    bias_new = adam_update(
        bias_master, bias_first, bias_second, bias_average, bias_new_grad, 0.3, 0.0
    )
    return (
        output,
        token_grad,
        condition_grad,
        *ada_new,
        *qkv_new,
        *out_new,
        *up_new,
        *down_new,
        *bias_new,
    )


def solution(mesh):
    in_specs = (
        P(("bucket", "seq"), None),
        P("bucket", None),
        P(("bucket", "seq"), None),
        P("bucket", None),
        P("bucket"),
        P(("bucket", "seq")),
        P(),
        P(),
        P("bucket", "seq"),
        P("bucket", "seq"),
        P("bucket", "seq"),
        P("bucket", "seq"),
        P("bucket", "seq"),
        P("bucket", "seq"),
        P("bucket", "seq"),
        P("bucket", "seq"),
        P("bucket", "seq"),
        P("bucket", "seq"),
        P("bucket", "seq"),
        P("bucket", "seq"),
        P("bucket", "seq"),
        P("bucket", "seq"),
        P("bucket", "seq"),
        P("bucket", "seq"),
        P("bucket", "seq"),
        P("bucket", "seq"),
        P("bucket", "seq"),
        P("bucket", "seq"),
        P(("bucket", "seq")),
        P(("bucket", "seq")),
        P(("bucket", "seq")),
        P(("bucket", "seq")),
    )
    out_specs = (
        P(("bucket", "seq"), None),
        P(("bucket", "seq"), None),
        P("bucket", None),
        P("bucket", "seq"),
        P("bucket", "seq"),
        P("bucket", "seq"),
        P("bucket", "seq"),
        P("bucket", "seq"),
        P("bucket", "seq"),
        P("bucket", "seq"),
        P("bucket", "seq"),
        P("bucket", "seq"),
        P("bucket", "seq"),
        P("bucket", "seq"),
        P("bucket", "seq"),
        P("bucket", "seq"),
        P("bucket", "seq"),
        P("bucket", "seq"),
        P("bucket", "seq"),
        P("bucket", "seq"),
        P("bucket", "seq"),
        P("bucket", "seq"),
        P("bucket", "seq"),
        P(("bucket", "seq")),
        P(("bucket", "seq")),
        P(("bucket", "seq")),
        P(("bucket", "seq")),
    )
    return jax.shard_map(
        on_device, mesh=mesh, in_specs=in_specs, out_specs=out_specs, check_vma=False
    )
```

```python
import functools
import math

import jax
import jax.numpy as jnp
from jax import lax
from jax.experimental import pallas as pl
from jax.experimental.pallas import tpu as pltpu
from jax.sharding import PartitionSpec as P

STEP = 10


EPSILON = 1e-06
BETA_FIRST = 0.5
BETA_SECOND = 0.5
ADAM_EPSILON = 1e-08
MATRIX_DECAY = 0.01
EMA_DECAY = 0.9999
HIGHEST = lax.Precision.HIGHEST
LOG2E = math.log2(math.e)
LANES = 128
TILE = 256
VMEM_LIMIT = 60 * 1024 * 1024
bfloat = jnp.bfloat16
single = jnp.float32


def layer_norm(values):
    centre = values - jnp.mean(values, axis=-1, keepdims=True)
    spread = jnp.mean(centre * centre, axis=-1, keepdims=True)
    return centre * lax.rsqrt(spread + EPSILON)


def modulate(values, shift_row, scale_row):
    return layer_norm(values) * (1.0 + scale_row) + shift_row


def dot_nn(left, right):
    return lax.dot_general(left, right, (((1,), (0,)), ((), ())), preferred_element_type=single)


def dot_nt(left, right):
    return lax.dot_general(left, right, (((1,), (1,)), ((), ())), preferred_element_type=single)


def dot_tn(left, right):
    return lax.dot_general(left, right, (((0,), (0,)), ((), ())), preferred_element_type=single)


def adam_update(master, moment_one, moment_two, average, gradient, step_rate, decay_rate):
    one_new = BETA_FIRST * moment_one + (1.0 - BETA_FIRST) * gradient
    two_new = BETA_SECOND * moment_two + (1.0 - BETA_SECOND) * gradient * gradient
    one_hat = one_new / (1.0 - BETA_FIRST**STEP)
    two_hat = two_new / (1.0 - BETA_SECOND**STEP)
    master_new = master - step_rate * (
        one_hat / (jnp.sqrt(two_hat) + ADAM_EPSILON) + decay_rate * master
    )
    average_decay = min(EMA_DECAY, (1.0 + STEP) / (10.0 + STEP))
    average_new = average_decay * average + (1.0 - average_decay) * master_new
    return (master_new, one_new, two_new, average_new)


def params(*semantics):
    return pltpu.CompilerParams(
        dimension_semantics=semantics or None, vmem_limit_bytes=VMEM_LIMIT
    )


def cost(flops, moved, exps=0):
    return pl.CostEstimate(flops=int(flops), bytes_accessed=int(moved), transcendentals=int(exps))


def exchange(values, axis, bit):
    count = lax.axis_size(axis)
    return lax.ppermute(values, axis, [(i, i ^ bit) for i in range(count)])


def pick(values, index, axis):
    return lax.dynamic_index_in_dim(values, index, axis, keepdims=False)


IN_VMEM = pl.BlockSpec(memory_space=pltpu.VMEM)
IN_HBM = pl.BlockSpec(memory_space=pl.ANY)


def cube_path():
    return lax.axis_size("bucket") == 8 and lax.axis_size("seq") == 4


BLOCKS, PLANES = 8, 4
X, Z0, Z1, CORE, Y = ("bucket", 1), ("bucket", 2), ("bucket", 4), ("seq", 1), ("seq", 2)


def gather_all(block, layout):
    width = block.shape[1]
    if layout == "rows":
        return lax.all_gather(block, ("bucket", "seq"), axis=0, tiled=True)
    tall = lax.all_gather(block, "bucket", axis=0, tiled=True)
    return lax.all_gather(tall, "seq", axis=0)


def place_in_kernel():
    if cube_path():
        return lax.axis_index("bucket"), lax.axis_index("seq")
    return 0, 0


DIMS = {"planes": (Y, CORE, Z1, Z0, X), "rows": (Z1, Z0, X, Y, CORE)}
MESH = pl.DeviceIdType.MESH


def my_coords():
    bucket, seq = lax.axis_index("bucket"), lax.axis_index("seq")
    return {
        (axis, amount): ((bucket if axis == "bucket" else seq) // amount) % 2
        for axis, amount in (X, Z0, Z1, CORE, Y)
    }


def partner(bit):
    bucket, seq = lax.axis_index("bucket"), lax.axis_index("seq")
    axis, amount = bit
    return (bucket ^ amount, seq) if axis == "bucket" else (bucket, seq ^ amount)


def peer_at(distance):
    bucket, seq = lax.axis_index("bucket"), lax.axis_index("seq")
    return bucket ^ (distance >> 2), seq ^ (distance & 3)


def greet(peers):
    barrier = pltpu.get_barrier_semaphore()
    for peer in peers:
        pl.semaphore_signal(barrier, inc=1, device_id=peer, device_id_type=MESH)
    pl.semaphore_wait(barrier, len(peers))


class Gathering:
    def __init__(self, own, out, layout, order, first, rows, send, recv, base):
        self.own, self.out, self.dims, self.order = own, out, DIMS[layout], order
        self.first, self.rows, self.send, self.recv, self.base = first, rows, send, recv, base
        self.me = my_coords()

    def view(self, free, flipped=None):
        index = tuple(
            slice(None)
            if dim in free
            else (1 - self.me[dim] if dim == flipped else self.me[dim])
            for dim in self.dims
        )
        return self.out.at[index + (pl.ds(self.first, self.rows), slice(None))]

    def copy(self, source, place, slot, bit):
        return pltpu.make_async_remote_copy(
            src_ref=source,
            dst_ref=place,
            send_sem=self.send.at[self.base + slot],
            recv_sem=self.recv.at[self.base + slot],
            device_id=partner(bit),
            device_id_type=MESH,
        )

    def hop(self, phase):
        place = self.view(self.order[:phase])
        source = self.own if phase == 0 else place
        return self.copy(source, place, phase, self.order[phase])

    def across(self, phase):
        if phase == 0:
            return self.copy(self.own, self.view(()), 4, CORE)
        place = self.view(self.order[: phase - 1], self.order[phase - 1])
        return self.copy(place, place, 4 + phase, CORE)

    def keep(self):
        return pltpu.make_async_copy(self.own, self.view(()), self.send.at[self.base + 9])

    def begin(self):
        self.hop(0).start()
        self.across(0).start()
        self.keep().start()

    def advance(self, phase):
        if phase == 0:
            self.keep().wait()
        self.hop(phase).wait_recv()
        if phase < 3:
            self.hop(phase + 1).start()
        self.across(phase + 1).start()

    def collect(self):
        for phase in range(5):
            self.across(phase).wait_recv()

    def finish(self):
        for phase in range(4):
            self.hop(phase).wait_send()
        for phase in range(5):
            self.across(phase).wait_send()


GATHER_SEMS = 10
SHARES = (32, 32, 32, 32, 16)
PAIR_PARTS = (
    (Z1, Z0, Y, X),
    (Z1, Y, X, Z0),
    (Z1, Z0, X, Y),
    (Z0, Z1, Y, X),
    (Z0, Z1, X, Y),
)
UP_PARTS = (
    (Z1, Y, Z0, X),
    (Z1, Y, Z0, X),
    (Z1, X, Y, Z0),
    (Z1, Y, Z0, X),
    (Z1, Y, Z0, X),
)
DOWN_PARTS = (
    (Z1, Y, X, Z0),
    (Z1, Y, X, Z0),
    (Z1, Z0, X, Y),
    (Z1, Y, Z0, X),
    (X, Z1, Y, Z0),
)
BEGIN, PLANE, KV = -1, -2, -3
GATHER_STEPS = (
    (0, 0), (1, 0), (2, 0), (3, 0), (4, 0), (1, 1), (0, 1), (2, 1), (1, 2), (3, 1),
    (0, 2), (4, 1), (-1, 0), (2, 2), (3, 2), (1, 3), (0, 3), (5, 0), (4, 2), (14, 0),
    (6, 0), (2, 3), (7, 0), (5, 1), (8, 0), (9, 0), (4, 3), (10, 0), (3, 3), (-2, 0),
    (6, 1), (11, 0), (7, 1), (8, 1), (-2, 1), (12, 0), (9, 1), (13, 0), (10, 1), (-2, 2),
    (14, 1), (11, 1), (-2, 3), (-3, 0), (-3, 1), (-3, 2), (-3, 3), (5, 2), (7, 2), (10, 2),
    (13, 1), (6, 2), (14, 2), (11, 2), (8, 2), (12, 1), (9, 2), (5, 3), (7, 3), (6, 3),
    (10, 3), (8, 3), (13, 2), (12, 2), (14, 3), (9, 3), (11, 3), (12, 3), (13, 3),
)
NOTE = -4
DOWN_SUM_PARTS = (
    (X, Z0, Y, Z1),
    (Z0, X, Z1, Y),
    (X, Z0, Y, Z1),
    (Z0, X, Y, Z1),
    (X, Z0, Y, Z1),
)
FIRST_SUM_STEPS = (
    (-3, 0), (-3, 1), (-3, 2), (-3, 3), (0, -1), (1, -1), (2, -1), (3, -1), (4, -1), (0, 0),
    (1, 0), (2, 0), (3, 0), (4, 0), (0, 1), (1, 1), (2, 1), (4, 1), (3, 1), (0, 2),
    (2, 2), (1, 2), (4, 2), (0, 3), (3, 2), (1, 3), (2, 3), (4, 3), (3, 3),
)
UP_SUM_PARTS = (
    (Z0, X, Z1, Y),
    (X, Z0, Z1, Y),
    (Y, X, Z0, Z1),
    (Z0, Y, X, Z1),
    (Y, X, Z1, Z0),
)
PAIR_SUM_PARTS = (
    (Y, X, Z0, Z1),
    (Y, X, Z0, Z1),
    (X, Y, Z0, Z1),
    (Y, X, Z0, Z1),
    (Z0, Y, X, Z1),
)
LAST_SUM_STEPS = (
    (-2, 0), (0, -1), (1, -1), (2, -1), (-2, 1), (3, -1), (4, -1), (-2, 2), (0, 0), (-2, 3),
    (5, -1), (6, -1), (7, -1), (1, 0), (2, 0), (8, -1), (9, -1), (4, 0), (0, 1), (3, 0),
    (-4, 0), (1, 1), (5, 0), (7, 0), (9, 0), (2, 1), (0, 2), (4, 1), (6, 0), (1, 2),
    (5, 1), (2, 2), (4, 2), (6, 1), (5, 2), (8, 0), (2, 3), (4, 3), (3, 1), (6, 2),
    (8, 1), (5, 3), (7, 1), (3, 2), (6, 3), (9, 1), (8, 2), (0, 3), (1, 3), (7, 2),
    (9, 2), (3, 3), (8, 3), (7, 3), (9, 3),
)
NOTE_STEP = 5
KV_PIECES = 4


def split_gatherings(block_ref, out_ref, layout, shares, orders, send, recv, base):
    moving, first = [], 0
    for index, (count, order) in enumerate(zip(shares, orders)):
        own = block_ref.at[pl.ds(first, count), :]
        slot = base + GATHER_SEMS * index
        moving.append(Gathering(own, out_ref, layout, order, first, count, send, recv, slot))
        first += count
    return moving


def gather_kernel(
    note_ref,
    ada_ref,
    pair_ref,
    up_ref,
    down_ref,
    x_ref,
    pair_out,
    up_out,
    down_out,
    kv_out,
    silu_ref,
    mod_ref,
    bias_ref,
    a_ref,
    q_ref,
    inbox,
    parts,
    returns,
    row,
    weights,
    acc,
    kv,
    note_send,
    note_recv,
    mod_send,
    mod_recv,
    weight_sem,
    send,
    recv,
):
    bucket, seq = lax.axis_index("bucket"), lax.axis_index("seq")
    place = my_coords()
    me = bucket * PLANES + seq
    count = BLOCKS * PLANES
    barrier = pltpu.get_barrier_semaphore()

    @pl.loop(1, count)
    def _(distance):
        pl.semaphore_signal(barrier, inc=1, device_id=peer_at(distance), device_id_type=MESH)

    pl.semaphore_wait(barrier, count - 1)

    def note(distance):
        peer = peer_at(distance)
        return pltpu.make_async_remote_copy(
            src_ref=note_ref.at[peer[0]],
            dst_ref=inbox.at[me],
            send_sem=note_send.at[distance],
            recv_sem=note_recv.at[distance],
            device_id=peer,
            device_id_type=MESH,
        )

    def answer(distance):
        peer = peer_at(distance)
        return pltpu.make_async_remote_copy(
            src_ref=parts.at[peer[0]],
            dst_ref=returns.at[me],
            send_sem=mod_send.at[distance],
            recv_sem=mod_recv.at[distance],
            device_id=peer,
            device_id_type=MESH,
        )

    @pl.loop(1, count)
    def _(distance):
        note(distance).start()

    inbox[me] = note_ref[bucket]
    base = len(PAIR_PARTS) * GATHER_SEMS
    pairs = split_gatherings(pair_ref, pair_out, "planes", SHARES, PAIR_PARTS, send, recv, 0)
    rest = split_gatherings(up_ref, up_out, "planes", SHARES, UP_PARTS, send, recv, base)
    base += len(UP_PARTS) * GATHER_SEMS
    rest += split_gatherings(down_ref, down_out, "rows", SHARES, DOWN_PARTS, send, recv, base)
    base += len(DOWN_PARTS) * GATHER_SEMS
    moving = pairs + rest
    for part in pairs:
        part.begin()

    rows, width = ada_ref.shape[0], x_ref.shape[1]
    cols = 3 * width // PLANES
    local = x_ref.shape[0] // KV_PIECES

    def kv_copy(source, target, slot, bit):
        return pltpu.make_async_remote_copy(
            src_ref=source,
            dst_ref=target,
            send_sem=send.at[base + slot],
            recv_sem=recv.at[base + slot],
            device_id=partner(bit),
            device_id_type=MESH,
        )

    def kv_step(piece, kind):
        span = pl.ds(piece * local, local)
        mine = kv_out.at[place[Y], place[CORE], span, :]
        other = kv_out.at[1 - place[Y], place[CORE], span, :]
        if kind == "over":
            return kv_copy(kv.at[span, :], mine, 4 * piece, Y)
        if kind == "near":
            return kv_copy(kv.at[span, :], mine, 4 * piece + 1, CORE)
        if kind == "far":
            return kv_copy(other, other, 4 * piece + 2, CORE)
        return pltpu.make_async_copy(kv.at[span, :], mine, send.at[base + 4 * piece + 3])

    def load(plane):
        source = pair_out.at[plane // 2, plane % 2, :, :, :, :, pl.ds(0, weights.shape[5])]
        return pltpu.make_async_copy(source, weights.at[plane % 2], weight_sem.at[plane % 2])

    def modulations():
        @pl.loop(1, count)
        def _(distance):
            note(distance).wait_recv()

        head = jnp.concatenate(
            [inbox[PLANES * g, NOTE_ROWS - 2 : NOTE_ROWS - 1, :] for g in range(BLOCKS)]
        )
        tail = jnp.concatenate(
            [inbox[PLANES * g, NOTE_ROWS - 1 : NOTE_ROWS, :] for g in range(BLOCKS)]
        )
        head, tail = jax.nn.silu(head).astype(bfloat), jax.nn.silu(tail).astype(bfloat)
        silu_ref[:, :LANES] = head
        silu_ref[:, LANES:] = tail
        mods = dot_nn(head, ada_ref[:LANES, :]) + dot_nn(
            tail[:, : rows - LANES], ada_ref[LANES:, :]
        )
        for group in range(BLOCKS):
            parts[group] = mods[group : group + 1, :]
        returns[me] = parts[bucket]

        @pl.loop(1, count)
        def _(distance):
            answer(distance).start()

    def biases():
        each = width // count
        lane = lax.broadcasted_iota(jnp.int32, (LANES, width), 1)
        entry = lax.broadcasted_iota(jnp.int32, (LANES, width), 0)
        copies = (lane % each == entry).astype(single).astype(bfloat)
        owner = lax.broadcasted_iota(jnp.int32, (NOTE_ROWS, width), 1) // each
        total = jnp.zeros((NOTE_ROWS, width), single)
        for device in range(count):
            spread = dot_nn(inbox[device].astype(bfloat), copies)
            total = jnp.where(owner == device, spread, total)
        bias_ref[...] = total

    def projection(plane):
        if plane == 0:
            for part in pairs:
                part.collect()
            load(0).start()
            load(1).start()

            @pl.loop(1, count)
            def _(distance):
                answer(distance).wait_recv()

            for index in range(PLANES):
                wide = returns.shape[2]
                row[:, index * wide : (index + 1) * wide] = sum(
                    returns[PLANES * g + index] for g in range(BLOCKS)
                )
            for index in range(6):
                mod_ref[index : index + 1, :] = (
                    row[:, index * width : (index + 1) * width] + bias_ref[index : index + 1, :]
                )
            a_ref[...] = modulate(
                x_ref[...].astype(single), mod_ref[0:1, :], mod_ref[1:2, :]
            ).astype(bfloat)
        load(plane).wait()
        weight = weights[plane % 2].reshape(width, weights.shape[5])
        acc[:, plane * cols : (plane + 1) * cols] = dot_nn(a_ref[...], weight)[:, :cols]
        if plane + 2 < PLANES:
            load(plane + 2).start()
        if plane == PLANES - 1:
            q_ref[...] = (acc[:, :width] + bias_ref[6:7, :]).astype(bfloat)
            kv[:, :width] = acc[:, width : 2 * width].astype(bfloat)
            kv[:, width:] = (acc[:, 2 * width :] + bias_ref[7:8, :]).astype(bfloat)

    for step, (part, phase) in enumerate(GATHER_STEPS):
        if step == NOTE_STEP:
            modulations()
            biases()
        if part == BEGIN:
            for moved in rest:
                moved.begin()
        elif part == PLANE:
            projection(phase)
        elif part == KV:
            for kind in ("over", "near", "keep"):
                kv_step(phase, kind).start()
        else:
            moving[part].advance(phase)
    for piece in range(KV_PIECES):
        kv_step(piece, "over").wait_recv()
        kv_step(piece, "far").start()
    for part in rest:
        part.collect()
    for part in moving:
        part.finish()
    for piece in range(KV_PIECES):
        kv_step(piece, "near").wait_recv()
        kv_step(piece, "far").wait_recv()
        kv_step(piece, "keep").wait()
        for kind in ("over", "near", "far"):
            kv_step(piece, kind).wait_send()

    @pl.loop(1, count)
    def _(distance):
        note(distance).wait_send()
        answer(distance).wait_send()


NOTE_ROWS = 16


def gather(notes, ada_low, pair_block, up_block, down_block, tokens):
    rows, width = pair_block.shape
    local = tokens.shape[0]
    count = BLOCKS * PLANES
    cols = ada_low.shape[1]
    wide = -(-3 * width // PLANES // LANES) * LANES
    blocks = jax.ShapeDtypeStruct((2, 2, 2, 2, 2, rows, width), bfloat)
    sems = 3 * len(SHARES) * GATHER_SEMS + 4 * KV_PIECES
    pair, up, down, kv, silu, mods, biases, first_in, query = pl.pallas_call(
        gather_kernel,
        out_shape=(
            blocks,
            blocks,
            blocks,
            jax.ShapeDtypeStruct((2, 2, local, 2 * width), bfloat),
            jax.ShapeDtypeStruct((BLOCKS, 2 * LANES), bfloat),
            jax.ShapeDtypeStruct((8, width), single),
            jax.ShapeDtypeStruct((NOTE_ROWS, width), single),
            jax.ShapeDtypeStruct((local, width), bfloat),
            jax.ShapeDtypeStruct((local, width), bfloat),
        ),
        in_specs=[IN_VMEM] * 6,
        out_specs=(IN_HBM,) * 4 + (IN_VMEM,) * 5,
        scratch_shapes=[
            pltpu.VMEM((count, NOTE_ROWS, LANES), single),
            pltpu.VMEM((BLOCKS, 1, cols), single),
            pltpu.VMEM((count, 1, cols), single),
            pltpu.VMEM((1, 6 * width), single),
            pltpu.VMEM((2, 2, 2, 2, rows, wide), bfloat),
            pltpu.VMEM((local, 3 * width), single),
            pltpu.VMEM((local, 2 * width), bfloat),
        ]
        + [pltpu.SemaphoreType.DMA((count,))] * 4
        + [pltpu.SemaphoreType.DMA((2,))]
        + [pltpu.SemaphoreType.DMA((sems,))] * 2,
        compiler_params=pltpu.CompilerParams(
            collective_id=1, has_side_effects=True, vmem_limit_bytes=VMEM_LIMIT
        ),
        cost_estimate=cost(6 * local * width * width, 200 * rows * width),
        name="gather",
    )(notes, ada_low, pair_block, up_block, down_block, tokens)
    tall = BLOCKS * rows
    return (
        pair.reshape(PLANES, tall, width),
        up.reshape(PLANES, tall, width),
        down.reshape(PLANES * tall, width),
        kv.reshape(PLANES * local, 2 * width),
        silu[:, :rows],
        mods,
        biases,
        first_in,
        query,
    )


def slot_of(bucket_bits, seq_bits):
    slot = 0
    for axis, amount in SLOT_DIMS:
        bits = bucket_bits if axis == "bucket" else seq_bits
        slot = slot * 2 + ((bits >> amount.bit_length() - 1) & 1)
    return slot


def natural_sum(far, near, layout):
    width = far.shape[2]
    both = jnp.concatenate([near, far])
    index = {
        (b, s): slot_of(b, s) + near.shape[0] * (s % 2)
        for b in range(BLOCKS)
        for s in range(PLANES)
    }
    if layout == "rows":
        picked = [index[b, s] for b in range(BLOCKS) for s in range(PLANES)]
        gradient = jnp.stack([both[k] for k in picked]).reshape(-1, width)
        part = lax.psum_scatter(gradient, ("bucket", "seq"), scatter_dimension=0, tiled=True)
        return part.astype(single)
    picked = [index[b, s] for s in range(PLANES) for b in range(BLOCKS)]
    gradient = jnp.stack([both[k] for k in picked]).reshape(PLANES, -1, width)
    part = lax.psum_scatter(gradient, "seq", scatter_dimension=0)
    return lax.psum_scatter(part, "bucket", scatter_dimension=0, tiled=True).astype(single)


SLOT_DIMS = (Y, X, Z1, Z0)


class Scattering:
    def __init__(self, far, near, total, arrivals, out, order, first, rows, send, recv, base):
        self.far, self.near, self.total, self.arrivals = far, near, total, arrivals
        self.out, self.order, self.first, self.rows = out, order, first, rows
        self.send, self.recv, self.base = send, recv, base
        self.span = (pl.ds(first, rows), slice(None))

    def copy(self, source, place, slot, bit):
        return pltpu.make_async_remote_copy(
            src_ref=source,
            dst_ref=place,
            send_sem=self.send.at[self.base + slot],
            recv_sem=self.recv.at[self.base + slot],
            device_id=partner(bit),
            device_id_type=MESH,
        )

    def across(self):
        index = (slice(None),) * 4 + self.span
        return self.copy(self.far.at[index], self.total.at[index], 4, CORE)

    def place(self, fixed):
        return tuple(fixed.get(dim, slice(None)) for dim in SLOT_DIMS)

    def hop(self, phase):
        fixed = {dim: 0 for dim in self.order[:phase]} | {self.order[phase]: 1}
        source = self.total.at[self.place(fixed) + self.span]
        place = self.arrivals[phase].at[(slice(None),) * (3 - phase) + self.span]
        return self.copy(source, place, phase, self.order[phase])

    def add(self, fixed, source, source_dims):
        free = [dim for dim in SLOT_DIMS if dim not in fixed]

        def one(step):
            index = dict(fixed)
            for place, dim in enumerate(free):
                index[dim] = (step >> place) & 1
            spot = tuple(index[dim] for dim in SLOT_DIMS) + self.span
            term = source[tuple(index[dim] for dim in source_dims) + self.span]
            self.total[spot] = (self.total[spot].astype(single) + term.astype(single)).astype(
                bfloat
            )

        if free:
            pl.loop(0, 2 ** len(free))(one)
        else:
            one(0)

    def advance(self, phase):
        if phase < 0:
            self.across().wait_recv()
            source, dims, fixed = self.near, SLOT_DIMS, {}
        else:
            self.hop(phase).wait_recv()
            done = self.order[: phase + 1]
            dims = tuple(dim for dim in SLOT_DIMS if dim not in done)
            source, fixed = self.arrivals[phase], {dim: 0 for dim in done}
        if phase == 3:
            spot = (0,) * 4 + self.span
            self.out[self.span] = self.total[spot].astype(single) + source[self.span].astype(
                single
            )
            return
        ahead = self.order[phase + 1]
        self.add(fixed | {ahead: 1}, source, dims)
        self.hop(phase + 1).start()
        self.add(fixed | {ahead: 0}, source, dims)

    def finish(self):
        self.across().wait_send()
        for phase in range(4):
            self.hop(phase).wait_send()


SCATTER_SEMS = 5


def scatter_scratch(rows, width):
    return [
        pltpu.VMEM((2,) * free + (rows, width), bfloat) for free in (4, 3, 2, 1, 0)
    ]


def split_scatterings(far, near, scratch, out, shares, orders, send, recv, base):
    moving, first = [], 0
    for index, (count, order) in enumerate(zip(shares, orders)):
        slot = base + SCATTER_SEMS * index
        moving.append(
            Scattering(
                far, near, scratch[0], scratch[1:], out, order, first, count, send, recv, slot
            )
        )
        first += count
    return moving


def first_scatter_kernel(kv_far, kv_near, down_far, down_near, kv_out, down_out, *refs):
    scratch, (kv_total, kv_arrival, send, recv) = refs[:5], refs[5:]
    greet([partner(bit) for bit in (X, Z0, Z1, CORE, Y)])
    moving = split_scatterings(
        down_far, down_near, scratch, down_out, SHARES, DOWN_SUM_PARTS, send, recv, 0
    )
    base = len(moving) * SCATTER_SEMS
    count = kv_out.shape[0] // KV_PIECES

    def kv_copy(source, place, slot, bit):
        return pltpu.make_async_remote_copy(
            src_ref=source,
            dst_ref=place,
            send_sem=send.at[base + slot],
            recv_sem=recv.at[base + slot],
            device_id=partner(bit),
            device_id_type=MESH,
        )

    def near(piece):
        rows = pl.ds(piece * count, count)
        return kv_copy(kv_far.at[:, rows, :], kv_total.at[:, rows, :], 2 * piece, CORE)

    def over(piece):
        rows = pl.ds(piece * count, count)
        return kv_copy(kv_total.at[1, rows, :], kv_arrival.at[rows, :], 2 * piece + 1, Y)

    def kv_add(piece, side):
        rows = pl.ds(piece * count, count)
        kv_total[side, rows, :] = (
            kv_total[side, rows, :].astype(single) + kv_near[side, rows, :].astype(single)
        ).astype(bfloat)

    for piece in range(KV_PIECES):
        near(piece).start()
    for part in moving:
        part.across().start()
    for part, phase in FIRST_SUM_STEPS:
        if part == KV:
            near(phase).wait_recv()
            kv_add(phase, 1)
            over(phase).start()
            kv_add(phase, 0)
        else:
            moving[part].advance(phase)
    for piece in range(KV_PIECES):
        over(piece).wait_recv()
        rows = pl.ds(piece * count, count)
        kv_out[rows, :] = (
            kv_total[0, rows, :].astype(single) + kv_arrival[rows, :].astype(single)
        ).astype(bfloat)
    for part in moving:
        part.finish()
    for piece in range(KV_PIECES):
        near(piece).wait_send()
        over(piece).wait_send()


def first_scatter(kv_far, kv_near, down_far, down_near):
    rows, width = down_far.shape[1:]
    local, wide = kv_far.shape[1:]
    cube = (2, 2, 2, 2, rows, width)
    sems = len(DOWN_SUM_PARTS) * SCATTER_SEMS + 2 * KV_PIECES
    return pl.pallas_call(
        first_scatter_kernel,
        out_shape=(
            jax.ShapeDtypeStruct((local, wide), bfloat),
            jax.ShapeDtypeStruct((rows, width), single),
        ),
        in_specs=[IN_HBM, IN_VMEM] * 2,
        out_specs=(IN_VMEM,) * 2,
        scratch_shapes=scatter_scratch(rows, width)
        + [pltpu.VMEM((2, local, wide), bfloat), pltpu.VMEM((local, wide), bfloat)]
        + [pltpu.SemaphoreType.DMA((sems,))] * 2,
        compiler_params=pltpu.CompilerParams(
            collective_id=3, has_side_effects=True, vmem_limit_bytes=VMEM_LIMIT
        ),
        cost_estimate=cost(0, 128 * rows * width),
        name="first_scatter",
    )(kv_far, kv_near, down_far.reshape(cube), down_near.reshape(cube))


def norm_back(values, grad, scale_row):
    centre = values - jnp.mean(values, axis=-1, keepdims=True)
    root = lax.rsqrt(jnp.mean(centre * centre, axis=-1, keepdims=True) + EPSILON)
    normed = centre * root
    scaled = grad * (1.0 + scale_row)
    inner = jnp.mean(scaled * normed, axis=-1, keepdims=True)
    return root * (scaled - jnp.mean(scaled, axis=-1, keepdims=True) - normed * inner), normed


def column_sum(values):
    return jnp.sum(values, axis=0, keepdims=True)


def last_scatter_kernel(
    up_far,
    up_near,
    a_ref,
    ob_ref,
    dq_ref,
    dkv_ref,
    dr_ref,
    w_ref,
    x_ref,
    dmid_ref,
    mod_ref,
    row_ref,
    ada_ref,
    up_out,
    pair_out,
    grad_ref,
    mods_ref,
    bias_ref,
    silu_ref,
    *refs,
):
    up_scratch, pair_scratch, refs = refs[:5], refs[5:10], refs[10:]
    far, near, weights, dy, table, line, bias_notes, mod_notes, bias_box, mod_box = refs[:10]
    parts, returns, weight_sem = refs[10:13]
    bias_send, bias_recv, mod_send, mod_recv, back_send, back_recv, send, recv = refs[13:]
    bucket, seq = lax.axis_index("bucket"), lax.axis_index("seq")
    me = bucket * PLANES + seq
    count = BLOCKS * PLANES
    barrier = pltpu.get_barrier_semaphore()

    @pl.loop(1, count)
    def _(distance):
        pl.semaphore_signal(barrier, inc=1, device_id=peer_at(distance), device_id_type=MESH)

    pl.semaphore_wait(barrier, count - 1)

    def message(source, target, out_sem, in_sem, distance):
        return pltpu.make_async_remote_copy(
            src_ref=source,
            dst_ref=target,
            send_sem=out_sem.at[distance],
            recv_sem=in_sem.at[distance],
            device_id=peer_at(distance),
            device_id_type=MESH,
        )

    def bias_note(distance):
        peer = peer_at(distance)
        source = bias_notes.at[peer[0] * PLANES + peer[1]]
        return message(source, bias_box.at[me], bias_send, bias_recv, distance)

    def mod_note(distance):
        source = mod_notes.at[peer_at(distance)[1]]
        return message(source, mod_box.at[me], mod_send, mod_recv, distance)

    def answer(distance):
        source = parts.at[peer_at(distance)[0]]
        return message(source, returns.at[me], back_send, back_recv, distance)

    base = len(UP_SUM_PARTS) * SCATTER_SEMS
    ups = split_scatterings(
        up_far, up_near, up_scratch, up_out, SHARES, UP_SUM_PARTS, send, recv, 0
    )
    pairs = split_scatterings(
        far, near, pair_scratch, pair_out, SHARES, PAIR_SUM_PARTS, send, recv, base
    )
    moving = ups + pairs
    for part in ups:
        part.across().start()

    width = x_ref.shape[1]
    rows = up_out.shape[0]
    cols = 3 * width // PLANES
    wide = dy.shape[1]
    below = wide - LANES
    order = (1, 3, 0, 2)

    def load(step):
        plane = seq ^ order[step]
        return pltpu.make_async_copy(
            w_ref.at[plane, :, pl.ds(0, wide)], weights.at[step % 2], weight_sem.at[step % 2]
        )

    def gather_dy(index):
        low, high = index * cols, (index + 1) * cols
        pieces = []
        if low < width:
            pieces.append(dq_ref[:, low : min(high, width)])
        if high > width:
            pieces.append(dkv_ref[:, max(low - width, 0) : high - width])
        first = 0
        for piece in pieces:
            dy[:, first : first + piece.shape[1]] = piece
            first += piece.shape[1]

    def project(step):
        bits = order[step]
        plane = seq ^ bits
        if step == 0:
            load(0).start()
            dy[:, cols:] = jnp.zeros((dy.shape[0], wide - cols), bfloat)
            grad_ref[...] = jnp.zeros_like(grad_ref)
        if step + 1 < PLANES:
            load(step + 1).start()
        for index in range(PLANES):

            @pl.when(plane == index)
            def _():
                gather_dy(index)

        target = far if bits % 2 else near
        place = my_coords()

        def store(values, first_col):
            for block in range(BLOCKS):
                spot = (
                    bits // 2,
                    (block % 2) ^ place[X],
                    (block // 4) ^ place[Z1],
                    (block // 2 % 2) ^ place[Z0],
                    slice(None),
                    slice(first_col, first_col + values.shape[1]),
                )
                target[spot] = values[block * rows : (block + 1) * rows, :].astype(bfloat)

        store(dot_tn(a_ref[...], dy[:, :below]), 0)
        edge = dot_tn(ob_ref[...], dr_ref[plane])
        store(dot_tn(a_ref[...], dy[:, below:]) + edge[:, :LANES], below)
        store(edge[:, LANES:], wide)
        load(step).wait()
        grad_ref[...] += dot_nt(dy[...], weights[step % 2])

    def notes():
        shift_sum, scale_sum = jnp.zeros((1, width), single), jnp.zeros((1, width), single)
        scale_row = mod_ref[1:2, :]
        for tile in range(0, x_ref.shape[0], LANES):
            span = slice(tile, tile + LANES)
            grad = grad_ref[span, :]
            back, normed = norm_back(x_ref[span, :].astype(single), grad, scale_row)
            shift_sum += column_sum(grad)
            scale_sum += column_sum(grad * normed)
            grad_ref[span, :] = dmid_ref[span, :] + back
        line[:, :width] = shift_sum
        line[:, width : 2 * width] = scale_sum
        table[0:1, :] = shift_sum
        table[1:2, :] = scale_sum
        for index in range(4):
            line[:, (2 + index) * width : (3 + index) * width] = row_ref[index : index + 1, :]
        table[2:6, :] = row_ref[0:4, :]
        table[6:7, :] = column_sum(dq_ref[...].astype(single))
        table[7:8, :] = column_sum(dkv_ref[:, width:].astype(single))
        table[8:14, :] = row_ref[4:10, :]
        table[14:16, :] = jnp.zeros((2, width), single)
        each = width // count
        lane = lax.broadcasted_iota(jnp.int32, (LANES, width), 1)
        entry = lax.broadcasted_iota(jnp.int32, (LANES, width), 0)
        copies = (lane % each == entry).astype(single)
        owner = lax.broadcasted_iota(jnp.int32, (NOTE_ROWS, width), 1) // each

        @pl.loop(0, count)
        def _(device):
            mine = jnp.where(owner == device, table[...], 0.0)
            bias_notes[device] = lax.dot_general(
                mine,
                copies,
                (((1,), (1,)), ((), ())),
                preferred_element_type=single,
                precision=HIGHEST,
            )

        part = mod_notes.shape[2]
        for index in range(PLANES):
            mod_notes[index] = line[:, index * part : (index + 1) * part]
        bias_box[me] = bias_notes[me]
        mod_box[me] = mod_notes[seq]

        @pl.loop(1, count)
        def _(distance):
            mod_note(distance).start()
            bias_note(distance).start()

    def answers():
        @pl.loop(1, count)
        def _(distance):
            mod_note(distance).wait_recv()

        sums = [sum(mod_box[PLANES * g + s] for s in range(PLANES)) for g in range(BLOCKS)]
        mods = jnp.concatenate(sums)
        mods_ref[...] = mods
        silu = lax.dot_general(
            mods,
            ada_ref[...].astype(single),
            (((1,), (1,)), ((), ())),
            preferred_element_type=single,
            precision=HIGHEST,
        )
        for group in range(BLOCKS):
            parts[group, :, :rows] = silu[group : group + 1, :]
            parts[group, :, rows:] = jnp.zeros((1, parts.shape[2] - rows), single)
        returns[me] = parts[bucket]

        @pl.loop(1, count)
        def _(distance):
            answer(distance).start()

    since = 0
    for part, phase in LAST_SUM_STEPS:
        if part == PLANE:
            project(phase)
            if phase == 1:
                for moved in pairs:
                    moved.across().start()
        elif part == NOTE:
            notes()
            since = 1
        else:
            moving[part].advance(phase)
            since += since > 0
            if since == ANSWER_AFTER:
                answers()

    @pl.loop(1, count)
    def _(distance):
        bias_note(distance).wait_recv()

    bias_ref[...] = jnp.zeros_like(bias_ref)

    @pl.loop(0, count)
    def _(device):
        bias_ref[...] += bias_box[device]

    @pl.loop(1, count)
    def _(distance):
        answer(distance).wait_recv()

    for group in range(BLOCKS):
        silu_ref[group] = sum(returns[PLANES * group + s] for s in range(PLANES))
    for part in moving:
        part.finish()

    @pl.loop(1, count)
    def _(distance):
        bias_note(distance).wait_send()
        mod_note(distance).wait_send()
        answer(distance).wait_send()


ANSWER_AFTER = 12


def last_scatter(
    up_far,
    up_near,
    first_in,
    branch,
    query_grad,
    kv_grad,
    dr_planes,
    weight,
    tokens,
    middle_grad,
    mods,
    row_grads,
    ada_low,
):
    rows, width = up_far.shape[1:]
    cube = (2, 2, 2, 2, rows, width)
    count = BLOCKS * PLANES
    cols = ada_low.shape[1]
    local = tokens.shape[0]
    wide = -(-3 * width // PLANES // LANES) * LANES
    mine = jax.ShapeDtypeStruct((rows, width), single)
    return pl.pallas_call(
        last_scatter_kernel,
        out_shape=(
            mine,
            mine,
            jax.ShapeDtypeStruct((local, width), single),
            jax.ShapeDtypeStruct((BLOCKS, cols), single),
            jax.ShapeDtypeStruct((NOTE_ROWS, LANES), single),
            jax.ShapeDtypeStruct((BLOCKS, 1, 2 * LANES), single),
        ),
        in_specs=[IN_HBM] + [IN_VMEM] * 6 + [IN_HBM] + [IN_VMEM] * 5,
        out_specs=(IN_VMEM,) * 6,
        scratch_shapes=scatter_scratch(rows, width)
        + scatter_scratch(rows, width)
        + [pltpu.VMEM(cube, bfloat)] * 2
        + [
            pltpu.VMEM((2, width, wide), bfloat),
            pltpu.VMEM((local, wide), bfloat),
            pltpu.VMEM((NOTE_ROWS, width), single),
            pltpu.VMEM((1, 6 * width), single),
            pltpu.VMEM((count, NOTE_ROWS, LANES), single),
            pltpu.VMEM((PLANES, 1, cols), single),
            pltpu.VMEM((count, NOTE_ROWS, LANES), single),
            pltpu.VMEM((count, 1, cols), single),
            pltpu.VMEM((BLOCKS, 1, 2 * LANES), single),
            pltpu.VMEM((count, 1, 2 * LANES), single),
            pltpu.SemaphoreType.DMA((2,)),
        ]
        + [pltpu.SemaphoreType.DMA((count,))] * 6
        + [pltpu.SemaphoreType.DMA((2 * len(SHARES) * SCATTER_SEMS,))] * 2,
        compiler_params=pltpu.CompilerParams(
            collective_id=4, has_side_effects=True, vmem_limit_bytes=63 * 1024 * 1024
        ),
        cost_estimate=cost(14 * local * width * width, 200 * rows * width),
        name="last_scatter",
    )(
        up_far.reshape(cube),
        up_near.reshape(cube),
        first_in,
        branch,
        query_grad,
        kv_grad,
        dr_planes,
        weight,
        tokens,
        middle_grad,
        mods,
        row_grads,
        ada_low,
    )


def whole(shape):
    return pl.BlockSpec(shape, lambda *_: (0,) * len(shape))


def qkv_kernel(cols, x_ref, shift_ref, scale_ref, bias_ref, w_ref, a_ref, q_ref, kv_ref, acc):
    step = pl.program_id(0)
    width = x_ref.shape[1]

    @pl.when(step == 0)
    def _():
        values = x_ref[...].astype(single)
        a_ref[...] = modulate(values, shift_ref[...], scale_ref[...]).astype(bfloat)

    wide = -(-cols // LANES) * LANES
    part = dot_nn(a_ref[...], w_ref[0, :, :wide])[:, :cols]
    for index in range(PLANES):

        @pl.when(step == index)
        def _():
            acc[:, index * cols : (index + 1) * cols] = part

    @pl.when(step == PLANES - 1)
    def _():
        q_ref[...] = (acc[:, :width] + bias_ref[:, :width]).astype(bfloat)
        kv_ref[...] = (acc[:, width:] + bias_ref[:, width:]).astype(bfloat)


def project_qkv(tokens, shift_row, scale_row, bias_row, weight):
    rows, width = tokens.shape
    cols = 3 * width // PLANES
    return pl.pallas_call(
        functools.partial(qkv_kernel, cols),
        grid=(PLANES,),
        out_shape=(
            jax.ShapeDtypeStruct((rows, width), bfloat),
            jax.ShapeDtypeStruct((rows, width), bfloat),
            jax.ShapeDtypeStruct((rows, 2 * width), bfloat),
        ),
        in_specs=[
            whole((rows, width)),
            whole((1, width)),
            whole((1, width)),
            whole((1, 3 * width)),
            pl.BlockSpec((1,) + weight.shape[1:], lambda s: (s, 0, 0)),
        ],
        out_specs=(whole((rows, width)), whole((rows, width)), whole((rows, 2 * width))),
        scratch_shapes=[pltpu.VMEM((rows, 3 * width), single)],
        compiler_params=params("arbitrary"),
        cost_estimate=cost(6 * rows * width * width, 8 * width * width),
        name="project_qkv",
    )(tokens, shift_row, scale_row, bias_row, weight)


def image_of(len_ref, position):
    start, length, end = jnp.int32(0), jnp.int32(0), jnp.int32(0)
    for index in range(len_ref.shape[1]):
        here = len_ref[0, index]
        inside = jnp.logical_and(position >= end, position < end + here)
        start = jnp.where(inside, end, start)
        length = jnp.where(inside, here, length)
        end = end + here
    return start, length


def head_windows(heads, size):
    for head in range(heads):
        low, high = head * size, (head + 1) * size
        yield head, low // LANES * LANES, -(-high // LANES) * LANES, low, high


def head_mask(low, high, left, right):
    lane = lax.broadcasted_iota(jnp.int32, (1, high - low), 1) + low
    return jnp.logical_and(lane >= left, lane < right)


LONG, SHORT = 1024, 256


def attend_kernel(heads, len_ref, q_ref, hm_ref, kv, ob_ref, log_ref, out):
    rows, width = q_ref.shape
    size = width // heads
    my_seq = lax.axis_index("seq")
    factor = size ** (-0.5) * LOG2E

    def run(tile_start, start, span):
        tile = pl.ds(tile_start, TILE)
        keys = pl.ds(start, span)
        logs = jnp.zeros((TILE, LANES), single)
        lane = lax.broadcasted_iota(jnp.int32, (TILE, LANES), 1)
        for head, low, high, left, right in head_windows(heads, size):
            mask = head_mask(low, high, left, right)
            query = q_ref[tile, low:high] * mask.astype(single).astype(bfloat)
            scores = dot_nt(query, kv[keys, low:high])
            top = jnp.max(scores, axis=-1, keepdims=True)
            expo = jnp.exp2((scores - top) * factor)
            total = jnp.sum(expo, axis=-1, keepdims=True)
            part = dot_nn(expo.astype(bfloat), kv[keys, width + low : width + high]) / total
            out[tile, low:high] = jnp.where(mask, part, out[tile, low:high])
            logs = jnp.where(lane == head, top * factor + jnp.log2(total), logs)
        log_ref[:, tile] = logs.T[:heads, :]

    @pl.loop(0, rows // TILE)
    def _(index):
        tile_start = pl.multiple_of(index * TILE, TILE)
        start, length = image_of(len_ref, my_seq * rows + tile_start)
        start = pl.multiple_of(start, SHORT)

        @pl.when(length > SHORT)
        def _():
            run(tile_start, start, LONG)

        @pl.when(length <= SHORT)
        def _():
            run(tile_start, start, SHORT)

    ob_ref[...] = (out[...] * hm_ref[...]).astype(bfloat)


def attend(lengths, query, kv, head_row, heads):
    rows, width = query.shape
    group = kv.shape[0]
    return pl.pallas_call(
        functools.partial(attend_kernel, heads),
        out_shape=(
            jax.ShapeDtypeStruct((rows, width), bfloat),
            jax.ShapeDtypeStruct((heads, rows), single),
        ),
        in_specs=[pl.BlockSpec(memory_space=pltpu.SMEM)]
        + [IN_VMEM] * 3,
        out_specs=(IN_VMEM,) * 2,
        scratch_shapes=[pltpu.VMEM((rows, width), single)],
        compiler_params=params(),
        cost_estimate=cost(16 * rows * LONG * width, 10 * group * width, heads * rows * LONG),
        name="attend",
    )(lengths, query, head_row, kv)


def out_kernel(ob_ref, w_ref, bias_ref, x_ref, c_ref, keep_ref, mod_ref, r_ref, mid_ref, a_ref, df_ref):
    step = pl.program_id(0)
    width = x_ref.shape[1]
    cols = width // PLANES
    part = dot_nn(ob_ref[...], w_ref[0])[:, -cols:]
    for index in range(PLANES):

        @pl.when(step == index)
        def _():
            r_ref[:, index * cols : (index + 1) * cols] = part

    @pl.when(step == PLANES - 1)
    def _():
        result = r_ref[...] + bias_ref[...]
        r_ref[...] = result
        middle = x_ref[...].astype(single) + mod_ref[2:3, :] * result
        mid_ref[...] = middle
        a_ref[...] = modulate(middle, mod_ref[3:4, :], mod_ref[4:5, :]).astype(bfloat)
        df_ref[...] = (mod_ref[5:6, :] * keep_ref[...] * c_ref[...].astype(single)).astype(bfloat)


def project_out(branch, weight, bias_row, tokens, upstream, keep, mods):
    rows, width = tokens.shape
    row, square = whole((1, width)), whole((rows, width))
    return pl.pallas_call(
        out_kernel,
        grid=(PLANES,),
        out_shape=(
            jax.ShapeDtypeStruct((rows, width), single),
            jax.ShapeDtypeStruct((rows, width), single),
            jax.ShapeDtypeStruct((rows, width), bfloat),
            jax.ShapeDtypeStruct((rows, width), bfloat),
        ),
        in_specs=[
            square,
            pl.BlockSpec((1, width, 3 * LANES), lambda s: (s, 0, 2)),
            row,
            square,
            square,
            whole((rows, 1)),
            whole(mods.shape),
        ],
        out_specs=(square,) * 4,
        compiler_params=params("arbitrary"),
        cost_estimate=cost(2 * rows * width * width, 2 * width * width + 16 * rows * width),
        name="project_out",
    )(branch, weight, bias_row, tokens, upstream, keep, mods)


def out_copies(source, layout, plane, buffer, seq_bits, far_ref, near_ref, sem):
    my_bucket, my_seq = place_in_kernel()
    rows = far_ref.shape[1]
    copies = []
    for index in range(BLOCKS):
        if layout == "rows":
            bits, part = index % PLANES, index // PLANES
            seq = my_seq ^ bits
            bucket = plane * (BLOCKS // PLANES) + part
            start = pl.multiple_of((part * PLANES + seq) * rows, 16)
            side = bits % 2
        else:
            bits, bucket, start, side = seq_bits, index, index * rows, seq_bits_side(seq_bits)
        target = far_ref if side else near_ref
        slot = slot_of(bucket ^ my_bucket, bits if layout == "rows" else seq_bits[0])
        copies.append(
            pltpu.make_async_copy(
                source.at[buffer, pl.ds(start, rows), :], target.at[slot], sem.at[buffer, index]
            )
        )
    return copies


def seq_bits_side(seq_bits):
    return seq_bits[1]


def ffn_kernel(a_ref, df_ref, cm_ref, b_ref, up_ref, down_ref, *refs):
    f_ref, da_ref, up_far, up_near, down_far, down_near, db_ref = refs[:7]
    up, down, up_grad, down_grad, up_sem, down_sem, up_out, down_out = refs[7:]
    width = a_ref.shape[1]
    my_seq = place_in_kernel()[1]

    def loads(bits):
        plane = my_seq ^ bits
        rows = pl.ds(pl.multiple_of(plane * width, LANES), width)
        return (
            pltpu.make_async_copy(up_ref.at[plane], up.at[plane], up_sem.at[bits]),
            pltpu.make_async_copy(down_ref.at[rows, :], down.at[rows, :], down_sem.at[bits]),
        )

    for bits in (1, 3, 0, 2):
        for copy in loads(bits):
            copy.start()
    f_ref[...] = jnp.zeros_like(f_ref)
    da_ref[...] = jnp.zeros_like(da_ref)

    def one(plane, low, high, buffer):
        first, grad = a_ref[...], df_ref[...]
        hidden_rows = pl.ds(pl.multiple_of(plane * width + low, LANES), high - low)
        keep = cm_ref[plane, :, low:high]
        pre = dot_nn(first, up[plane, :, low:high]) + b_ref[plane, :, low:high]
        root = math.sqrt(2.0 / math.pi)
        square = pre * pre
        bend = jnp.tanh(root * pre * (1.0 + 0.044715 * square))
        half = 0.5 * (1.0 + bend)
        hidden = (pre * half * keep).astype(bfloat)
        slope = half + 0.5 * pre * (1.0 - bend * bend) * (root * (1.0 + 0.134145 * square))
        back = (dot_nt(grad, down[hidden_rows, :]) * keep * slope).astype(bfloat)
        f_ref[...] += dot_nn(hidden, down[hidden_rows, :])
        da_ref[...] += dot_nt(back, up[plane, :, low:high])
        up_grad[buffer, :, low:high] = dot_tn(first, back).astype(bfloat)
        down_grad[buffer, low:high, :] = dot_tn(hidden, grad).astype(bfloat)
        db_ref[plane, :, low:high] = jnp.sum(back.astype(single), axis=0, keepdims=True)

    cut = -(-width // 2 // LANES) * LANES

    def sends(plane, buffer, side_bits, far_side):
        return out_copies(
            up_grad, "planes", plane, buffer, (side_bits, far_side), up_far, up_near, up_out
        ) + out_copies(
            down_grad, "rows", plane, buffer, None, down_far, down_near, down_out
        )

    for far_side in (1, 0):

        @pl.loop(0, 2)
        def _(above):
            bits = above * 2 + far_side
            plane = my_seq ^ bits
            if not far_side:
                for copy in sends(plane, above, bits, far_side):
                    copy.wait()
            for copy in loads(bits):
                copy.wait()
            one(plane, 0, cut, above)
            one(plane, cut, width, above)
            for copy in sends(plane, above, bits, far_side):
                copy.start()

    for above in range(2):
        for copy in sends(my_seq ^ (above * 2), above, above * 2, 0):
            copy.wait()


def feed_forward(first, grad, chan_row, bias_row, up_weight, down_weight):
    rows, width = first.shape
    hidden = chan_row.shape[1]
    blocks = jax.ShapeDtypeStruct((BLOCKS * PLANES // 2, width // BLOCKS, width), bfloat)
    result = pl.pallas_call(
        ffn_kernel,
        out_shape=(
            jax.ShapeDtypeStruct((rows, width), single),
            jax.ShapeDtypeStruct((rows, width), single),
            blocks,
            blocks,
            blocks,
            blocks,
            jax.ShapeDtypeStruct((PLANES, 1, width), single),
        ),
        in_specs=[IN_VMEM] * 4 + [IN_HBM] * 2,
        out_specs=(IN_VMEM, IN_VMEM) + (IN_HBM,) * 4 + (IN_VMEM,),
        scratch_shapes=[
            pltpu.VMEM((PLANES, width, width), bfloat),
            pltpu.VMEM((hidden, width), bfloat),
            pltpu.VMEM((2, width, width), bfloat),
            pltpu.VMEM((2, width, width), bfloat),
            pltpu.SemaphoreType.DMA((PLANES,)),
            pltpu.SemaphoreType.DMA((PLANES,)),
            pltpu.SemaphoreType.DMA((2, BLOCKS)),
            pltpu.SemaphoreType.DMA((2, BLOCKS)),
        ],
        compiler_params=params(),
        cost_estimate=cost(12 * rows * width * hidden, 8 * width * hidden, rows * hidden),
        name="feed_forward",
    )(
        first,
        grad,
        chan_row.reshape(PLANES, 1, width),
        bias_row.reshape(PLANES, 1, width),
        up_weight,
        down_weight,
    )
    return result


def back_out_kernel(
    heads,
    f_ref,
    da_ref,
    mid_ref,
    r_ref,
    c_ref,
    keep_ref,
    mod_ref,
    bias_ref,
    df_ref,
    w_ref,
    hm_ref,
    ob_ref,
    out_ref,
    dmid_ref,
    dr_ref,
    row_ref,
    do_ref,
    delta_ref,
    acc,
):
    step = pl.program_id(0)
    width = acc.shape[1]
    cols = width // PLANES
    edge = dr_ref.shape[2] - cols

    @pl.when(step == 0)
    def _():
        row_ref[...] = jnp.zeros_like(row_ref)
        acc[...] = jnp.zeros_like(acc)
        gate_one, scale, gate_two = mod_ref[2:3, :], mod_ref[4:5, :], mod_ref[5:6, :]

        @pl.loop(0, acc.shape[0], step=LANES)
        def _(tile):
            span = pl.ds(pl.multiple_of(tile, LANES), LANES)
            keep = keep_ref[span, :]
            upstream = c_ref[span, :].astype(single)
            middle = mid_ref[span, :]
            mlp = f_ref[span, :] + bias_ref[...]
            out_ref[span, :] = (middle + gate_two * keep * mlp).astype(bfloat)
            grad = da_ref[span, :]
            back, normed = norm_back(middle, grad, scale)
            dmid = upstream + back
            dmid_ref[span, :] = dmid
            branch = (gate_one * dmid).astype(bfloat).astype(single)
            for plane in range(PLANES):
                dr_ref[plane, span, :edge] = jnp.zeros((LANES, edge), bfloat)
                dr_ref[plane, span, edge:] = branch[:, plane * cols : (plane + 1) * cols].astype(
                    bfloat
                )
            row_ref[0:1, :] += column_sum(dmid * r_ref[span, :])
            row_ref[1:2, :] += column_sum(grad)
            row_ref[2:3, :] += column_sum(grad * normed)
            row_ref[3:4, :] += column_sum(keep * upstream * mlp)
            row_ref[4:5, :] += column_sum(branch)
            row_ref[5:6, :] += column_sum(df_ref[span, :].astype(single))

    acc[...] += dot_nt(dr_ref[step], w_ref[0])

    @pl.when(step == PLANES - 1)
    def _():
        size = width // heads
        grad = (acc[...] * hm_ref[...]).astype(bfloat)
        do_ref[...] = grad
        terms = grad.astype(single) * ob_ref[...].astype(single)
        head = lax.broadcasted_iota(jnp.int32, (heads, width), 0)
        lane = lax.broadcasted_iota(jnp.int32, (heads, width), 1)
        chosen = jnp.logical_and(lane >= head * size, lane < (head + 1) * size)
        delta_ref[...] = lax.dot_general(
            chosen.astype(single),
            terms,
            (((1,), (1,)), ((), ())),
            preferred_element_type=single,
            precision=HIGHEST,
        )


def back_out(
    mlp_sum,
    second_grad,
    middle,
    attn_out,
    upstream,
    keep,
    mods,
    bias_row,
    mlp_grad,
    weight,
    head_row,
    branch,
    heads,
):
    rows, width = branch.shape
    row, square = whole((1, width)), whole((rows, width))
    return pl.pallas_call(
        functools.partial(back_out_kernel, heads),
        grid=(PLANES,),
        out_shape=(
            jax.ShapeDtypeStruct((rows, width), bfloat),
            jax.ShapeDtypeStruct((rows, width), single),
            jax.ShapeDtypeStruct((PLANES, rows, 3 * LANES), bfloat),
            jax.ShapeDtypeStruct((8, width), single),
            jax.ShapeDtypeStruct((rows, width), bfloat),
            jax.ShapeDtypeStruct((heads, rows), single),
        ),
        in_specs=[
            square,
            square,
            square,
            square,
            square,
            whole((rows, 1)),
            whole(mods.shape),
            row,
            square,
            pl.BlockSpec((1, width, 3 * LANES), lambda s: (s, 0, 2)),
            row,
            square,
        ],
        out_specs=(
            square,
            square,
            whole((PLANES, rows, 3 * LANES)),
            whole((8, width)),
            square,
            whole((heads, rows)),
        ),
        scratch_shapes=[pltpu.VMEM((rows, width), single)],
        compiler_params=params("arbitrary"),
        cost_estimate=cost(2 * rows * width * width, 2 * width * width + 30 * rows * width),
        name="back_out",
    )(
        mlp_sum,
        second_grad,
        middle,
        attn_out,
        upstream,
        keep,
        mods,
        bias_row,
        mlp_grad,
        weight,
        head_row,
        branch,
    )


def attend_back_kernel(
    heads, len_ref, q_ref, do_ref, log_ref, delta_ref, kv, dq_ref, far_ref, near_ref, dq, dk, dv
):
    rows, width = q_ref.shape
    size = width // heads
    my_seq = lax.axis_index("seq")
    scale = size ** (-0.5)
    factor = scale * LOG2E
    dk[...] = jnp.zeros_like(dk)
    dv[...] = jnp.zeros_like(dv)

    def run(tile_start, start, span):
        tile = pl.ds(tile_start, TILE)
        keys = pl.ds(start, span)
        for head, low, high, left, right in head_windows(heads, size):
            mask = head_mask(low, high, left, right)
            chosen = mask.astype(single).astype(bfloat)
            query = q_ref[tile, low:high] * chosen
            grad = do_ref[tile, low:high] * chosen
            key = kv[keys, low:high]
            probs = jnp.exp2(dot_nt(key, query) * factor - log_ref[head : head + 1, tile])
            slope = dot_nt(kv[keys, width + low : width + high], grad)
            score_grad = (probs * (slope - delta_ref[head : head + 1, tile])).astype(bfloat)
            dv[keys, low:high] += dot_nn(probs.astype(bfloat), grad)
            dk[keys, low:high] += dot_nn(score_grad, query)
            part = dot_tn(score_grad, key)
            dq[tile, low:high] = jnp.where(mask, part, dq[tile, low:high])

    @pl.loop(0, rows // TILE)
    def _(index):
        tile_start = pl.multiple_of(index * TILE, TILE)
        start, length = image_of(len_ref, my_seq * rows + tile_start)
        start = pl.multiple_of(start, SHORT)

        @pl.when(length > SHORT)
        def _():
            run(tile_start, start, LONG)

        @pl.when(length <= SHORT)
        def _():
            run(tile_start, start, SHORT)

    dq_ref[...] = (dq[...] * scale).astype(bfloat)
    base = place_in_kernel()[1]
    for bits in range(PLANES):
        place = pl.ds(pl.multiple_of((base ^ bits) * rows, rows), rows)
        target = far_ref if bits % 2 else near_ref
        target[bits // 2, :, :width] = (dk[place, :] * scale).astype(bfloat)
        target[bits // 2, :, width:] = dv[place, :].astype(bfloat)


def attend_back(lengths, query, grad, logs, delta, kv, heads):
    rows, width = query.shape
    group = kv.shape[0]
    return pl.pallas_call(
        functools.partial(attend_back_kernel, heads),
        out_shape=(
            jax.ShapeDtypeStruct((rows, width), bfloat),
            jax.ShapeDtypeStruct((2, rows, 2 * width), bfloat),
            jax.ShapeDtypeStruct((2, rows, 2 * width), bfloat),
        ),
        in_specs=[pl.BlockSpec(memory_space=pltpu.SMEM)]
        + [IN_VMEM] * 5,
        out_specs=(IN_VMEM,) * 3,
        scratch_shapes=[
            pltpu.VMEM((rows, width), single),
            pltpu.VMEM((group, width), single),
            pltpu.VMEM((group, width), single),
        ],
        compiler_params=params(),
        cost_estimate=cost(40 * rows * LONG * width, 20 * group * width, heads * rows * LONG),
        name="attend_back",
    )(lengths, query, grad, logs, delta, kv)


def back_qkv_kernel(
    a_ref, ob_ref, dy_ref, dr_ref, w_ref, da_ref, far_ref, near_ref, stage, sem
):
    my_seq = place_in_kernel()[1]
    wide = dy_ref.shape[2]
    below = wide - LANES
    da_ref[...] = jnp.zeros_like(da_ref)

    def sends(plane, buffer, bits, far_side):
        return out_copies(
            stage, "planes", plane, buffer, (bits, far_side), far_ref, near_ref, sem
        )

    for far_side in (1, 0):

        @pl.loop(0, 2)
        def _(above):
            bits = above * 2 + far_side
            plane = my_seq ^ bits
            if not far_side:
                for copy in sends(plane, above, bits, far_side):
                    copy.wait()
            da_ref[...] += dot_nt(dy_ref[plane], w_ref[plane, :, :wide])
            first = dot_tn(a_ref[...], dy_ref[plane])
            second = dot_tn(ob_ref[...], dr_ref[plane])
            stage[above, :, :below] = first[:, :below].astype(bfloat)
            stage[above, :, below:wide] = (first[:, below:] + second[:, :LANES]).astype(bfloat)
            stage[above, :, wide:] = second[:, LANES:].astype(bfloat)
            for copy in sends(plane, above, bits, far_side):
                copy.start()

    for above in range(2):
        for copy in sends(my_seq ^ (above * 2), above, above * 2, 0):
            copy.wait()


def back_qkv(first_in, branch, dy_planes, dr_planes, weight):
    rows, width = first_in.shape
    blocks = jax.ShapeDtypeStruct((BLOCKS * PLANES // 2, width // BLOCKS, width), bfloat)
    return pl.pallas_call(
        back_qkv_kernel,
        out_shape=(jax.ShapeDtypeStruct((rows, width), single), blocks, blocks),
        in_specs=[IN_VMEM] * 5,
        out_specs=(IN_VMEM, IN_HBM, IN_HBM),
        scratch_shapes=[
            pltpu.VMEM((2, width, width), bfloat),
            pltpu.SemaphoreType.DMA((2, BLOCKS)),
        ],
        compiler_params=params(),
        cost_estimate=cost(14 * rows * width * width, 4 * weight.size),
        name="back_qkv",
    )(first_in, branch, dy_planes, dr_planes, weight)


def on_device(
    tokens,
    condition,
    cotangent,
    lengths,
    bucket_ids,
    keep_flags,
    head_table,
    chan_table,
    ada_master,
    ada_first,
    ada_second,
    ada_average,
    qkv_master,
    qkv_first,
    qkv_second,
    qkv_average,
    out_master,
    out_first,
    out_second,
    out_average,
    up_master,
    up_first,
    up_second,
    up_average,
    down_master,
    down_first,
    down_second,
    down_average,
    bias_master,
    bias_first,
    bias_second,
    bias_average,
):
    local_rows, width = tokens.shape
    heads = head_table.shape[1]
    head_size = width // heads
    hidden_width = chan_table.shape[1]
    hidden_ratio = hidden_width // width
    table_cols = 10 + hidden_ratio
    my_bucket, my_seq = lax.axis_index("bucket"), lax.axis_index("seq")
    buckets, seqs = lax.axis_size("bucket"), lax.axis_size("seq")
    group_rows = local_rows * seqs
    block_rows = qkv_master.shape[0]
    pair_block = jnp.concatenate([qkv_master, out_master], axis=1).astype(bfloat)
    down_block = lax.all_to_all(
        down_master.astype(bfloat), "seq", split_axis=0, concat_axis=1, tiled=True
    )
    up_block = up_master.astype(bfloat)
    ada_low = ada_master.astype(bfloat)
    if cube_path():
        each = width // (buckets * seqs)
        table = bias_master.reshape(each, table_cols).T
        slices = jnp.pad(
            condition.reshape(buckets, block_rows), ((0, 0), (0, 2 * LANES - block_rows))
        )
        notes = jnp.concatenate(
            [
                jnp.broadcast_to(
                    jnp.pad(table, ((0, 0), (0, LANES - each))), (buckets, table_cols, LANES)
                ),
                slices.reshape(buckets, 2, LANES),
            ],
            axis=1,
        )
        (
            pair_weight,
            up_weight,
            down_weight,
            near,
            silu_rows,
            mods,
            bias_table,
            first_in,
            query,
        ) = gather(notes, ada_low, pair_block, up_block, down_block, tokens)
    else:
        pair_weight = gather_all(pair_block, "planes")
        bias_low = lax.all_gather(
            bias_master.astype(bfloat), ("bucket", "seq"), axis=0, tiled=True
        )
        silu_low = jax.nn.silu(condition).astype(bfloat)
        silu_all = lax.all_gather(silu_low, "bucket", axis=0, tiled=True)
        silu_rows = lax.dynamic_slice_in_dim(silu_all, my_bucket * block_rows, block_rows, 1)
        mod_part = lax.psum_scatter(
            dot_nn(silu_rows, ada_low), "bucket", scatter_dimension=0, tiled=True
        )
        mod_row = lax.all_gather(mod_part, "seq", axis=1, tiled=True)
        bias_table = bias_low.astype(single).reshape(width, table_cols).T
        mods = jnp.pad(mod_row.reshape(6, width) + bias_table[:6], ((0, 2), (0, 0)))
        value_bias = bias_table[7:8]
        qkv_bias = jnp.concatenate(
            [bias_table[6:7], jnp.zeros_like(value_bias), value_bias], axis=1
        )
        first_in, query, key_value = project_qkv(
            tokens, mods[0:1], mods[1:2], qkv_bias, pair_weight
        )
        up_weight = gather_all(up_block, "planes")
        down_weight = gather_all(down_block, "rows")
        near = lax.all_gather(key_value, "seq", axis=0, tiled=True)

    out_bias = bias_table[8:9]
    up_bias = bias_table[9 : table_cols - 1].T.reshape(1, hidden_width)
    down_bias = bias_table[table_cols - 1 : table_cols]
    selector = (
        jnp.arange(head_table.shape[0], dtype=jnp.int32)[:, None] == bucket_ids[None, :]
    ).astype(single)
    head_row = jnp.repeat(jnp.sum(selector * head_table.astype(single), axis=0), head_size)[None]
    chan_row = jnp.sum(selector * chan_table.astype(single), axis=0)[None]
    keep_float = keep_flags.astype(single)[:, None]
    branch_in, logs = attend(lengths, query, near, head_row, heads)
    attn_out, middle, second_in, mlp_grad = project_out(
        branch_in, pair_weight, out_bias, tokens, cotangent, keep_float, mods
    )
    mlp_sum, second_grad, up_far, up_near, down_far, down_near, up_bias_grad = feed_forward(
        second_in, mlp_grad, chan_row, up_bias, up_weight, down_weight
    )
    output, middle_grad, dr_planes, row_grads, attended_grad, delta = back_out(
        mlp_sum,
        second_grad,
        middle,
        attn_out,
        cotangent,
        keep_float,
        mods,
        down_bias,
        mlp_grad,
        pair_weight,
        head_row,
        branch_in,
        heads,
    )
    up_bias_rows = up_bias_grad.reshape(width, hidden_ratio).T
    query_grad, kv_far, kv_near = attend_back(
        lengths, query, attended_grad, logs, delta, near, heads
    )
    qkv_cols = 3 * width // seqs
    if cube_path():
        kv_grad, down_new_grad = first_scatter(kv_far, kv_near, down_far, down_near)
        rows_all = jnp.concatenate([row_grads[:5], up_bias_rows, row_grads[5:6]])
        rows_all = jnp.pad(rows_all, ((0, 16 - rows_all.shape[0]), (0, 0)))
        up_new_grad, pair_new_grad, token_grad, mod_all, bias_sum, silu_sum = last_scatter(
            up_far,
            up_near,
            first_in,
            branch_in,
            query_grad,
            kv_grad,
            dr_planes,
            pair_weight,
            tokens,
            middle_grad,
            mods,
            rows_all,
            ada_low,
        )
        bias_new_grad = bias_sum[:table_cols, : width // (buckets * seqs)].T.reshape(-1)
        silu_grad = silu_sum[:, 0, :block_rows].reshape(1, width)
    else:
        terms = jnp.stack([kv_near[0], kv_far[0], kv_near[1], kv_far[1]])
        kv_grad = lax.psum_scatter(terms, "seq", scatter_dimension=0)
        projected_grad = jnp.concatenate([query_grad, kv_grad], axis=1)
        dy_planes = jnp.pad(
            projected_grad.reshape(local_rows, seqs, qkv_cols).transpose(1, 0, 2),
            ((0, 0), (0, 0), (0, -qkv_cols % LANES)),
        )
        first_grad, pair_far, pair_near = back_qkv(
            first_in, branch_in, dy_planes, dr_planes, pair_weight
        )
        back, normed = norm_back(tokens.astype(single), first_grad, mods[1:2])
        token_grad = middle_grad + back
        up_new_grad = natural_sum(up_far, up_near, "planes")
        down_new_grad = natural_sum(down_far, down_near, "rows")
        pair_new_grad = natural_sum(pair_far, pair_near, "planes")
        mod_grads = jnp.concatenate(
            [column_sum(first_grad), column_sum(first_grad * normed), row_grads[:4]]
        )
        bias_grad = jnp.concatenate(
            [
                mod_grads,
                column_sum(query_grad.astype(single)),
                column_sum(kv_grad[:, width:].astype(single)),
                row_grads[4:5],
                up_bias_rows,
                row_grads[5:6],
            ]
        ).T.reshape(width * table_cols)
        mod_mine = lax.psum_scatter(
            mod_grads.reshape(seqs, 6 * width // seqs), "seq", scatter_dimension=0, tiled=True
        )
        mod_all = lax.all_gather(mod_mine, "bucket", axis=0, tiled=True)
        silu_part = lax.dot_general(
            mod_all,
            ada_low.astype(single),
            (((1,), (1,)), ((), ())),
            preferred_element_type=single,
            precision=HIGHEST,
        )
        silu_grad = lax.all_to_all(
            lax.psum(silu_part, "seq"), "bucket", split_axis=0, concat_axis=1, tiled=True
        )
        bias_new_grad = lax.psum_scatter(
            bias_grad, ("bucket", "seq"), scatter_dimension=0, tiled=True
        )
    ada_new_grad = lax.dot_general(
        silu_rows.astype(single),
        mod_all,
        (((0,), (0,)), ((), ())),
        preferred_element_type=single,
        precision=HIGHEST,
    )
    _, silu_back = jax.vjp(jax.nn.silu, condition)
    condition_grad = silu_back(silu_grad)[0]
    down_mine = lax.all_to_all(
        down_new_grad.astype(bfloat), "seq", split_axis=1, concat_axis=0, tiled=True
    ).astype(single)
    out_rate = (group_rows / (16.0 * width)) ** 0.5
    ada_new = adam_update(
        ada_master, ada_first, ada_second, ada_average, ada_new_grad, width ** (-0.5), MATRIX_DECAY
    )
    qkv_new = adam_update(
        qkv_master,
        qkv_first,
        qkv_second,
        qkv_average,
        pair_new_grad[:, :qkv_cols],
        width ** (-0.5),
        MATRIX_DECAY,
    )
    out_new = adam_update(
        out_master,
        out_first,
        out_second,
        out_average,
        pair_new_grad[:, qkv_cols:],
        out_rate,
        MATRIX_DECAY,
    )
    up_new = adam_update(
        up_master, up_first, up_second, up_average, up_new_grad, width ** (-0.5), MATRIX_DECAY
    )
    down_new = adam_update(
        down_master,
        down_first,
        down_second,
        down_average,
        down_mine,
        hidden_width ** (-0.5),
        MATRIX_DECAY,
    )
    bias_new = adam_update(
        bias_master, bias_first, bias_second, bias_average, bias_new_grad, 0.3, 0.0
    )
    return (
        output,
        token_grad,
        condition_grad,
        *ada_new,
        *qkv_new,
        *out_new,
        *up_new,
        *down_new,
        *bias_new,
    )


def solution(mesh):
    in_specs = (
        P(("bucket", "seq"), None),
        P("bucket", None),
        P(("bucket", "seq"), None),
        P("bucket", None),
        P("bucket"),
        P(("bucket", "seq")),
        P(),
        P(),
        P("bucket", "seq"),
        P("bucket", "seq"),
        P("bucket", "seq"),
        P("bucket", "seq"),
        P("bucket", "seq"),
        P("bucket", "seq"),
        P("bucket", "seq"),
        P("bucket", "seq"),
        P("bucket", "seq"),
        P("bucket", "seq"),
        P("bucket", "seq"),
        P("bucket", "seq"),
        P("bucket", "seq"),
        P("bucket", "seq"),
        P("bucket", "seq"),
        P("bucket", "seq"),
        P("bucket", "seq"),
        P("bucket", "seq"),
        P("bucket", "seq"),
        P("bucket", "seq"),
        P(("bucket", "seq")),
        P(("bucket", "seq")),
        P(("bucket", "seq")),
        P(("bucket", "seq")),
    )
    out_specs = (
        P(("bucket", "seq"), None),
        P(("bucket", "seq"), None),
        P("bucket", None),
        P("bucket", "seq"),
        P("bucket", "seq"),
        P("bucket", "seq"),
        P("bucket", "seq"),
        P("bucket", "seq"),
        P("bucket", "seq"),
        P("bucket", "seq"),
        P("bucket", "seq"),
        P("bucket", "seq"),
        P("bucket", "seq"),
        P("bucket", "seq"),
        P("bucket", "seq"),
        P("bucket", "seq"),
        P("bucket", "seq"),
        P("bucket", "seq"),
        P("bucket", "seq"),
        P("bucket", "seq"),
        P("bucket", "seq"),
        P("bucket", "seq"),
        P("bucket", "seq"),
        P(("bucket", "seq")),
        P(("bucket", "seq")),
        P(("bucket", "seq")),
        P(("bucket", "seq")),
    )
    return jax.shard_map(
        on_device, mesh=mesh, in_specs=in_specs, out_specs=out_specs, check_vma=False
    )
```

```python
import functools
import math

import jax
import jax.numpy as jnp
from jax import lax
from jax.experimental import pallas as pl
from jax.experimental.pallas import tpu as pltpu
from jax.sharding import PartitionSpec as P

STEP = 10


EPSILON = 1e-06
BETA_FIRST = 0.5
BETA_SECOND = 0.5
ADAM_EPSILON = 1e-08
MATRIX_DECAY = 0.01
EMA_DECAY = 0.9999
HIGHEST = lax.Precision.HIGHEST
LOG2E = math.log2(math.e)
LANES = 128
TILE = 256
VMEM_LIMIT = 60 * 1024 * 1024
bfloat = jnp.bfloat16
single = jnp.float32


def layer_norm(values):
    centre = values - jnp.mean(values, axis=-1, keepdims=True)
    spread = jnp.mean(centre * centre, axis=-1, keepdims=True)
    return centre * lax.rsqrt(spread + EPSILON)


def modulate(values, shift_row, scale_row):
    return layer_norm(values) * (1.0 + scale_row) + shift_row


def dot_nn(left, right):
    return lax.dot_general(left, right, (((1,), (0,)), ((), ())), preferred_element_type=single)


def dot_nt(left, right):
    return lax.dot_general(left, right, (((1,), (1,)), ((), ())), preferred_element_type=single)


def dot_tn(left, right):
    return lax.dot_general(left, right, (((0,), (0,)), ((), ())), preferred_element_type=single)


def adam_update(master, moment_one, moment_two, average, gradient, step_rate, decay_rate):
    one_new = BETA_FIRST * moment_one + (1.0 - BETA_FIRST) * gradient
    two_new = BETA_SECOND * moment_two + (1.0 - BETA_SECOND) * gradient * gradient
    one_hat = one_new / (1.0 - BETA_FIRST**STEP)
    two_hat = two_new / (1.0 - BETA_SECOND**STEP)
    master_new = master - step_rate * (
        one_hat / (jnp.sqrt(two_hat) + ADAM_EPSILON) + decay_rate * master
    )
    average_decay = min(EMA_DECAY, (1.0 + STEP) / (10.0 + STEP))
    average_new = average_decay * average + (1.0 - average_decay) * master_new
    return (master_new, one_new, two_new, average_new)


def params(*semantics):
    return pltpu.CompilerParams(
        dimension_semantics=semantics or None, vmem_limit_bytes=VMEM_LIMIT
    )


def cost(flops, moved, exps=0):
    return pl.CostEstimate(flops=int(flops), bytes_accessed=int(moved), transcendentals=int(exps))


def exchange(values, axis, bit):
    count = lax.axis_size(axis)
    return lax.ppermute(values, axis, [(i, i ^ bit) for i in range(count)])


def pick(values, index, axis):
    return lax.dynamic_index_in_dim(values, index, axis, keepdims=False)


IN_VMEM = pl.BlockSpec(memory_space=pltpu.VMEM)
IN_HBM = pl.BlockSpec(memory_space=pl.ANY)
IN_SMEM = pl.BlockSpec(memory_space=pltpu.SMEM)


def cube_path():
    return lax.axis_size("bucket") == 8 and lax.axis_size("seq") == 4


BLOCKS, PLANES = 8, 4
X, Z0, Z1, CORE, Y = ("bucket", 1), ("bucket", 2), ("bucket", 4), ("seq", 1), ("seq", 2)
MIDDLE, FORWARD = ("bucket", 6), ("bucket", 2, "forward")


def gather_all(block, layout):
    width = block.shape[1]
    if layout == "rows":
        return lax.all_gather(block, ("bucket", "seq"), axis=0, tiled=True)
    tall = lax.all_gather(block, "bucket", axis=0, tiled=True)
    return lax.all_gather(tall, "seq", axis=0)


def place_in_kernel():
    if cube_path():
        return lax.axis_index("bucket"), lax.axis_index("seq")
    return 0, 0


DIMS = {"planes": (Y, CORE, Z1, Z0, X), "rows": (Z1, Z0, X, Y, CORE)}
MESH = pl.DeviceIdType.MESH


def my_coords():
    bucket, seq = lax.axis_index("bucket"), lax.axis_index("seq")
    return {
        (axis, amount): ((bucket if axis == "bucket" else seq) // amount) % 2
        for axis, amount in (X, Z0, Z1, CORE, Y)
    }


def partner(bit):
    bucket, seq = lax.axis_index("bucket"), lax.axis_index("seq")
    axis, amount = bit[:2]
    return (bucket ^ amount, seq) if axis == "bucket" else (bucket, seq ^ amount)


def peer_at(distance):
    bucket, seq = lax.axis_index("bucket"), lax.axis_index("seq")
    return bucket ^ (distance >> 2), seq ^ (distance & 3)


def greet(peers):
    barrier = pltpu.get_barrier_semaphore()
    for peer in peers:
        pl.semaphore_signal(barrier, inc=1, device_id=peer, device_id_type=MESH)
    pl.semaphore_wait(barrier, len(peers))


class Gathering:
    def __init__(self, own, out, layout, order, first, rows, send, recv, base):
        self.own, self.out, self.dims, self.order = own, out, DIMS[layout], order
        self.first, self.rows, self.send, self.recv, self.base = first, rows, send, recv, base
        self.me = my_coords()
        self.inner = self.me[Z0] != self.me[Z1]

    def view(self, free, flipped=None):
        index = tuple(
            slice(None)
            if dim in free
            else (1 - self.me[dim] if dim == flipped else self.me[dim])
            for dim in self.dims
        )
        return self.out.at[index + (pl.ds(self.first, self.rows), slice(None))]

    def copy(self, source, place, slot, bit):
        return pltpu.make_async_remote_copy(
            src_ref=source,
            dst_ref=place,
            send_sem=self.send.at[self.base + slot],
            recv_sem=self.recv.at[self.base + slot],
            device_id=partner(bit),
            device_id_type=MESH,
        )

    def dim(self, phase):
        return Z1 if self.order[phase] in (MIDDLE, FORWARD) else self.order[phase]

    def had(self, phase):
        return [self.dim(past) for past in range(phase) if self.order[past] != MIDDLE]

    def arrived(self, phase):
        return self.view(self.had(phase), self.dim(phase))

    def hop(self, phase):
        place = self.arrived(phase) if self.order[phase] == FORWARD else self.view(self.had(phase))
        source = self.own if phase == 0 else place
        return self.copy(source, place, phase, self.order[phase])

    def across(self, phase):
        if phase == 0:
            return self.copy(self.own, self.view(()), 5, CORE)
        place = self.arrived(phase - 1)
        return self.copy(place, place, 5 + phase, CORE)

    def keep(self):
        return pltpu.make_async_copy(self.own, self.view(()), self.send.at[self.base + 11])

    def begin(self):
        self.hop(0).start()
        self.across(0).start()
        self.keep().start()

    def sends(self, phase, act):
        if self.order[phase] in (MIDDLE, FORWARD):
            pl.when(self.inner)(act)
        else:
            act()

    def advance(self, phase):
        if phase == 0:
            self.keep().wait()
        kind = self.order[phase]
        if kind == MIDDLE:

            @pl.when(self.inner)
            def _():
                self.hop(phase).wait_recv()
                self.hop(phase + 1).start()

            return
        if kind == FORWARD:

            @pl.when(jnp.logical_not(self.inner))
            def _():
                self.hop(phase).wait_recv()

        else:
            self.hop(phase).wait_recv()
        if phase < 4:
            self.sends(phase + 1, lambda: self.hop(phase + 1).start())
        self.across(phase + 1).start()

    def collect(self):
        for phase in range(6):
            if phase == 0 or self.order[phase - 1] != MIDDLE:
                self.across(phase).wait_recv()

    def finish(self):
        for phase in range(5):
            self.sends(phase, lambda phase=phase: self.hop(phase).wait_send())
        for phase in range(6):
            if phase == 0 or self.order[phase - 1] != MIDDLE:
                self.across(phase).wait_send()


GATHER_SEMS = 12
SHARES = (32, 32, 32, 32, 16)
PAIR_PARTS = (
    (X, Z0, Y, MIDDLE, FORWARD),
    (Z0, MIDDLE, FORWARD, X, Y),
    (Z0, Y, MIDDLE, FORWARD, X),
    (Z0, MIDDLE, FORWARD, Y, X),
    (Z0, MIDDLE, FORWARD, Y, X),
)
UP_PARTS = (
    (Z0, X, Y, MIDDLE, FORWARD),
    (Z0, X, Y, MIDDLE, FORWARD),
    (Y, Z0, MIDDLE, FORWARD, X),
    (Y, Z0, MIDDLE, FORWARD, X),
    (Z0, X, MIDDLE, FORWARD, Y),
)
DOWN_PARTS = (
    (Z0, MIDDLE, FORWARD, Y, X),
    (Z0, Y, X, MIDDLE, FORWARD),
    (Z0, MIDDLE, FORWARD, Y, X),
    (Z0, X, Y, MIDDLE, FORWARD),
    (Z0, MIDDLE, FORWARD, X, Y),
)
BEGIN, PLANE, KV = -1, -2, -3
GATHER_STEPS = (
    (0, 0), (1, 0), (2, 0), (3, 0), (4, 0), (1, 1), (0, 1), (2, 1), (3, 1), (4, 1),
    (-1, 0), (1, 2), (3, 2), (0, 2), (2, 2), (4, 2), (7, 0), (5, 0), (8, 0), (6, 0),
    (9, 0), (1, 3), (10, 0), (11, 0), (5, 1), (3, 3), (12, 0), (13, 0), (14, 0), (6, 1),
    (4, 3), (9, 1), (0, 3), (2, 3), (10, 1), (7, 1), (12, 1), (14, 1), (8, 1), (1, 4),
    (3, 4), (9, 2), (11, 1), (13, 1), (7, 2), (5, 2), (4, 4), (0, 4), (8, 2), (10, 2),
    (6, 2), (12, 2), (14, 2), (13, 2), (9, 3), (2, 4), (-2, 0), (5, 3), (10, 3), (7, 3),
    (11, 2), (-2, 1), (14, 3), (12, 3), (-2, 2), (8, 3), (-2, 3), (-3, 0), (-3, 1), (-3, 2),
    (-3, 3), (6, 3), (9, 4), (10, 4), (14, 4), (5, 4), (13, 3), (7, 4), (6, 4), (11, 3),
    (12, 4), (13, 4), (8, 4), (11, 4),
)
NOTE = -4
DOWN_SUM_PARTS = (
    (X, Z0, Y, Z1),
    (X, Y, Z0, Z1),
    (Z0, X, Y, Z1),
    (Z0, X, Y, Z1),
    (X, Z0, Z1, Y),
)
FIRST_SUM_STEPS = (
    (-3, 0), (-3, 1), (-3, 2), (-3, 3), (0, -1), (1, -1), (2, -1), (3, -1), (4, -1), (0, 0),
    (2, 0), (1, 0), (3, 0), (4, 0), (0, 1), (1, 1), (2, 1), (4, 1), (0, 2), (1, 2),
    (3, 1), (2, 2), (4, 2), (0, 3), (3, 2), (4, 3), (1, 3), (2, 3), (3, 3),
)
UP_SUM_PARTS = (
    (Z0, X, Z1, Y),
    (X, Z0, Z1, Y),
    (Y, X, Z0, Z1),
    (Z0, Y, X, Z1),
    (Y, X, Z1, Z0),
)
PAIR_SUM_PARTS = (
    (Y, X, Z0, Z1),
    (Y, X, Z0, Z1),
    (X, Y, Z0, Z1),
    (Y, X, Z0, Z1),
    (Z0, Y, X, Z1),
)
LAST_SUM_STEPS = (
    (-2, 0), (0, -1), (1, -1), (2, -1), (-2, 1), (3, -1), (4, -1), (-2, 2), (0, 0), (-2, 3),
    (5, -1), (6, -1), (7, -1), (1, 0), (2, 0), (8, -1), (9, -1), (4, 0), (0, 1), (3, 0),
    (-4, 0), (1, 1), (5, 0), (7, 0), (9, 0), (2, 1), (0, 2), (4, 1), (6, 0), (1, 2),
    (5, 1), (2, 2), (4, 2), (6, 1), (5, 2), (8, 0), (2, 3), (4, 3), (3, 1), (6, 2),
    (8, 1), (5, 3), (7, 1), (3, 2), (6, 3), (9, 1), (8, 2), (0, 3), (1, 3), (7, 2),
    (9, 2), (3, 3), (8, 3), (7, 3), (9, 3),
)
NOTE_STEP = 5
KV_PIECES = 4


def split_gatherings(block_ref, out_ref, layout, shares, orders, send, recv, base):
    moving, first = [], 0
    for index, (count, order) in enumerate(zip(shares, orders)):
        own = block_ref.at[pl.ds(first, count), :]
        slot = base + GATHER_SEMS * index
        moving.append(Gathering(own, out_ref, layout, order, first, count, send, recv, slot))
        first += count
    return moving


def kv_needed(piece, act):
    place = my_coords()
    quarter = KV_PIECES // 2
    last = jnp.logical_and(place[Y] == 1, place[CORE] == 1)
    first = jnp.logical_and(place[Y] == 0, place[CORE] == 0)
    skipped = first if piece < quarter else last
    pl.when(jnp.logical_not(skipped))(act)


def kv_expected(piece, act):
    place = my_coords()
    quarter = KV_PIECES // 2
    last = jnp.logical_and(place[Y] == 0, place[CORE] == 1)
    first = jnp.logical_and(place[Y] == 1, place[CORE] == 0)
    skipped = first if piece < quarter else last
    pl.when(jnp.logical_not(skipped))(act)


def kv_relayed(piece, act):
    place = my_coords()
    quarter = KV_PIECES // 2
    last = jnp.logical_and(place[Y] == 0, place[CORE] == 0)
    first = jnp.logical_and(place[Y] == 1, place[CORE] == 1)
    skipped = first if piece < quarter else last
    pl.when(jnp.logical_not(skipped))(act)


def gather_kernel(
    cond_ref,
    table_ref,
    ada_ref,
    qkv_master,
    out_master,
    up_master,
    cut_ref,
    x_ref,
    pair_out,
    up_out,
    down_out,
    kv_out,
    silu_ref,
    mod_ref,
    bias_ref,
    a_ref,
    q_ref,
    note_ref,
    pair_ref,
    up_ref,
    down_ref,
    cuts,
    inbox,
    parts,
    returns,
    row,
    weights,
    acc,
    kv,
    note_send,
    note_recv,
    mod_send,
    mod_recv,
    cut_send,
    cut_recv,
    weight_sem,
    send,
    recv,
):
    bucket, seq = lax.axis_index("bucket"), lax.axis_index("seq")
    place = my_coords()
    me = bucket * PLANES + seq
    count = BLOCKS * PLANES
    barrier = pltpu.get_barrier_semaphore()

    @pl.loop(1, count)
    def _(distance):
        pl.semaphore_signal(barrier, inc=1, device_id=peer_at(distance), device_id_type=MESH)

    rows, width = ada_ref.shape[0], x_ref.shape[1]
    cols = 3 * width // PLANES
    pair_ref[:, :cols] = qkv_master[...].astype(bfloat)
    pair_ref[:, cols:] = out_master[...].astype(bfloat)
    up_ref[...] = up_master[...].astype(bfloat)
    note_ref[...] = jnp.zeros_like(note_ref)
    for index in range(BLOCKS):
        start = index * rows
        note_ref[index, : NOTE_ROWS - 2, : table_ref.shape[1]] = table_ref[...]
        note_ref[index, NOTE_ROWS - 2 : NOTE_ROWS - 1, :] = cond_ref[:, start : start + LANES]
        note_ref[index, NOTE_ROWS - 1 :, : rows - LANES] = cond_ref[
            :, start + LANES : start + rows
        ]
    pl.semaphore_wait(barrier, count - 1)

    def cut(distance):
        return pltpu.make_async_remote_copy(
            src_ref=cut_ref.at[seq ^ distance],
            dst_ref=cuts.at[seq],
            send_sem=cut_send.at[distance],
            recv_sem=cut_recv.at[distance],
            device_id=(bucket, seq ^ distance),
            device_id_type=MESH,
        )

    def note(distance):
        peer = peer_at(distance)
        return pltpu.make_async_remote_copy(
            src_ref=note_ref.at[peer[0]],
            dst_ref=inbox.at[me],
            send_sem=note_send.at[distance],
            recv_sem=note_recv.at[distance],
            device_id=peer,
            device_id_type=MESH,
        )

    def answer(distance):
        peer = peer_at(distance)
        return pltpu.make_async_remote_copy(
            src_ref=parts.at[peer[0]],
            dst_ref=returns.at[me],
            send_sem=mod_send.at[distance],
            recv_sem=mod_recv.at[distance],
            device_id=peer,
            device_id_type=MESH,
        )

    @pl.loop(1, count)
    def _(distance):
        note(distance).start()

    inbox[me] = note_ref[bucket]
    cuts[seq] = cut_ref[seq]
    base = len(PAIR_PARTS) * GATHER_SEMS
    pairs = split_gatherings(pair_ref, pair_out, "planes", SHARES, PAIR_PARTS, send, recv, 0)
    rest = split_gatherings(up_ref, up_out, "planes", SHARES, UP_PARTS, send, recv, base)
    base += len(UP_PARTS) * GATHER_SEMS
    rest += split_gatherings(down_ref, down_out, "rows", SHARES, DOWN_PARTS, send, recv, base)
    base += len(DOWN_PARTS) * GATHER_SEMS
    moving = pairs + rest
    for part in pairs:
        part.begin()
    for distance in range(1, PLANES):
        cut(distance).start()

    local = x_ref.shape[0] // KV_PIECES

    def kv_copy(source, target, slot, bit):
        return pltpu.make_async_remote_copy(
            src_ref=source,
            dst_ref=target,
            send_sem=send.at[base + slot],
            recv_sem=recv.at[base + slot],
            device_id=partner(bit),
            device_id_type=MESH,
        )

    def kv_step(piece, kind):
        span = pl.ds(piece * local, local)
        mine = kv_out.at[place[Y], place[CORE], span, :]
        other = kv_out.at[1 - place[Y], place[CORE], span, :]
        if kind == "over":
            return kv_copy(kv.at[span, :], mine, 4 * piece, Y)
        if kind == "near":
            return kv_copy(kv.at[span, :], mine, 4 * piece + 1, CORE)
        if kind == "far":
            return kv_copy(other, other, 4 * piece + 2, CORE)
        return pltpu.make_async_copy(kv.at[span, :], mine, send.at[base + 4 * piece + 3])

    def load(plane):
        source = pair_out.at[plane // 2, plane % 2, :, :, :, :, pl.ds(0, weights.shape[5])]
        return pltpu.make_async_copy(source, weights.at[plane % 2], weight_sem.at[plane % 2])

    def modulations():
        @pl.loop(1, count)
        def _(distance):
            note(distance).wait_recv()

        head = jnp.concatenate(
            [inbox[PLANES * g, NOTE_ROWS - 2 : NOTE_ROWS - 1, :] for g in range(BLOCKS)]
        )
        tail = jnp.concatenate(
            [inbox[PLANES * g, NOTE_ROWS - 1 : NOTE_ROWS, :] for g in range(BLOCKS)]
        )
        head, tail = jax.nn.silu(head).astype(bfloat), jax.nn.silu(tail).astype(bfloat)
        silu_ref[:, :LANES] = head
        silu_ref[:, LANES:] = tail
        mods = dot_nn(head, ada_ref[:LANES, :].astype(bfloat)) + dot_nn(
            tail[:, : rows - LANES], ada_ref[LANES:, :].astype(bfloat)
        )
        for group in range(BLOCKS):
            parts[group] = mods[group : group + 1, :]
        returns[me] = parts[bucket]

        @pl.loop(1, count)
        def _(distance):
            answer(distance).start()

    def biases():
        each = width // count
        lane = lax.broadcasted_iota(jnp.int32, (LANES, width), 1)
        entry = lax.broadcasted_iota(jnp.int32, (LANES, width), 0)
        copies = (lane % each == entry).astype(single).astype(bfloat)
        owner = lax.broadcasted_iota(jnp.int32, (NOTE_ROWS, width), 1) // each
        total = jnp.zeros((NOTE_ROWS, width), single)
        for device in range(count):
            spread = dot_nn(inbox[device].astype(bfloat), copies)
            total = jnp.where(owner == device, spread, total)
        bias_ref[...] = total

    def projection(plane):
        if plane == 0:
            for part in pairs:
                part.collect()
            load(0).start()
            load(1).start()

            @pl.loop(1, count)
            def _(distance):
                answer(distance).wait_recv()

            for index in range(PLANES):
                wide = returns.shape[2]
                row[:, index * wide : (index + 1) * wide] = sum(
                    returns[PLANES * g + index] for g in range(BLOCKS)
                )
            for index in range(6):
                mod_ref[index : index + 1, :] = (
                    row[:, index * width : (index + 1) * width] + bias_ref[index : index + 1, :]
                )
            a_ref[...] = modulate(
                x_ref[...].astype(single), mod_ref[0:1, :], mod_ref[1:2, :]
            ).astype(bfloat)
        load(plane).wait()
        weight = weights[plane % 2].reshape(width, weights.shape[5])
        acc[:, plane * cols : (plane + 1) * cols] = dot_nn(a_ref[...], weight)[:, :cols]
        if plane + 2 < PLANES:
            load(plane + 2).start()
        if plane == PLANES - 1:
            q_ref[...] = (acc[:, :width] + bias_ref[6:7, :]).astype(bfloat)
            kv[:, :width] = acc[:, width : 2 * width].astype(bfloat)
            kv[:, width:] = (acc[:, 2 * width :] + bias_ref[7:8, :]).astype(bfloat)

    for step, (part, phase) in enumerate(GATHER_STEPS):
        if step == NOTE_STEP:
            modulations()
            biases()
        if part == BEGIN:
            for distance in range(1, PLANES):
                cut(distance).wait_recv()
            for index in range(PLANES):
                each = cuts.shape[2]
                down_ref[:, index * each : (index + 1) * each] = cuts[index]
            for moved in rest:
                moved.begin()
        elif part == PLANE:
            projection(phase)
        elif part == KV:
            kv_needed(phase, lambda: kv_step(phase, "over").start())
            for kind in ("near", "keep"):
                kv_step(phase, kind).start()
        else:
            moving[part].advance(phase)
    def relay(piece):
        kv_step(piece, "over").wait_recv()
        kv_step(piece, "far").start()

    for piece in range(KV_PIECES):
        kv_expected(piece, functools.partial(relay, piece))
    for part in rest:
        part.collect()
    for part in moving:
        part.finish()
    for piece in range(KV_PIECES):
        kv_step(piece, "near").wait_recv()
        kv_relayed(piece, lambda piece=piece: kv_step(piece, "far").wait_recv())
        kv_step(piece, "keep").wait()
        kv_step(piece, "near").wait_send()
        kv_needed(piece, lambda piece=piece: kv_step(piece, "over").wait_send())
        kv_expected(piece, lambda piece=piece: kv_step(piece, "far").wait_send())

    for distance in range(1, PLANES):
        cut(distance).wait_send()

    @pl.loop(1, count)
    def _(distance):
        note(distance).wait_send()
        answer(distance).wait_send()


NOTE_ROWS = 16


def gather(condition, table, ada_master, qkv_master, out_master, up_master, cut, tokens):
    rows, width = up_master.shape
    local = tokens.shape[0]
    count = BLOCKS * PLANES
    cols = ada_master.shape[1]
    block = pltpu.VMEM((rows, width), bfloat)
    wide = -(-3 * width // PLANES // LANES) * LANES
    blocks = jax.ShapeDtypeStruct((2, 2, 2, 2, 2, rows, width), bfloat)
    sems = 3 * len(SHARES) * GATHER_SEMS + 4 * KV_PIECES
    pair, up, down, kv, silu, mods, biases, first_in, query = pl.pallas_call(
        gather_kernel,
        out_shape=(
            blocks,
            blocks,
            blocks,
            jax.ShapeDtypeStruct((2, 2, local, 2 * width), bfloat),
            jax.ShapeDtypeStruct((BLOCKS, 2 * LANES), bfloat),
            jax.ShapeDtypeStruct((8, width), single),
            jax.ShapeDtypeStruct((NOTE_ROWS, width), single),
            jax.ShapeDtypeStruct((local, width), bfloat),
            jax.ShapeDtypeStruct((local, width), bfloat),
        ),
        in_specs=[IN_VMEM] * 8,
        out_specs=(IN_HBM,) * 4 + (IN_VMEM,) * 5,
        scratch_shapes=[
            pltpu.VMEM((BLOCKS, NOTE_ROWS, LANES), single),
            block,
            block,
            block,
            pltpu.VMEM(cut.shape, bfloat),
            pltpu.VMEM((count, NOTE_ROWS, LANES), single),
            pltpu.VMEM((BLOCKS, 1, cols), single),
            pltpu.VMEM((count, 1, cols), single),
            pltpu.VMEM((1, 6 * width), single),
            pltpu.VMEM((2, 2, 2, 2, rows, wide), bfloat),
            pltpu.VMEM((local, 3 * width), single),
            pltpu.VMEM((local, 2 * width), bfloat),
        ]
        + [pltpu.SemaphoreType.DMA((count,))] * 4
        + [pltpu.SemaphoreType.DMA((PLANES,))] * 2
        + [pltpu.SemaphoreType.DMA((2,))]
        + [pltpu.SemaphoreType.DMA((sems,))] * 2,
        compiler_params=pltpu.CompilerParams(
            collective_id=1, has_side_effects=True, vmem_limit_bytes=VMEM_LIMIT
        ),
        cost_estimate=cost(6 * local * width * width, 200 * rows * width),
        name="gather",
    )(condition, table, ada_master, qkv_master, out_master, up_master, cut, tokens)
    tall = BLOCKS * rows
    return (
        pair.reshape(PLANES, tall, width),
        up.reshape(PLANES, tall, width),
        down.reshape(PLANES * tall, width),
        kv.reshape(PLANES * local, 2 * width),
        silu[:, :rows],
        mods,
        biases,
        first_in,
        query,
    )


def slot_of(bucket_bits, seq_bits):
    slot = 0
    for axis, amount in SLOT_DIMS:
        bits = bucket_bits if axis == "bucket" else seq_bits
        slot = slot * 2 + ((bits >> amount.bit_length() - 1) & 1)
    return slot


def natural_sum(far, near, layout):
    width = far.shape[2]
    both = jnp.concatenate([near, far])
    index = {
        (b, s): slot_of(b, s) + near.shape[0] * (s % 2)
        for b in range(BLOCKS)
        for s in range(PLANES)
    }
    if layout == "rows":
        picked = [index[b, s] for b in range(BLOCKS) for s in range(PLANES)]
        gradient = jnp.stack([both[k] for k in picked]).reshape(-1, width)
        part = lax.psum_scatter(gradient, ("bucket", "seq"), scatter_dimension=0, tiled=True)
        return part.astype(single)
    picked = [index[b, s] for s in range(PLANES) for b in range(BLOCKS)]
    gradient = jnp.stack([both[k] for k in picked]).reshape(PLANES, -1, width)
    part = lax.psum_scatter(gradient, "seq", scatter_dimension=0)
    return lax.psum_scatter(part, "bucket", scatter_dimension=0, tiled=True).astype(single)


SLOT_DIMS = (Y, X, Z1, Z0)


class Scattering:
    def __init__(self, far, near, total, arrivals, out, order, first, rows, send, recv, base):
        self.far, self.near, self.total, self.arrivals = far, near, total, arrivals
        self.out, self.order, self.first, self.rows = out, order, first, rows
        self.send, self.recv, self.base = send, recv, base
        self.span = (pl.ds(first, rows), slice(None))

    def copy(self, source, place, slot, bit):
        return pltpu.make_async_remote_copy(
            src_ref=source,
            dst_ref=place,
            send_sem=self.send.at[self.base + slot],
            recv_sem=self.recv.at[self.base + slot],
            device_id=partner(bit),
            device_id_type=MESH,
        )

    def across(self):
        index = (slice(None),) * 4 + self.span
        return self.copy(self.far.at[index], self.total.at[index], 4, CORE)

    def place(self, fixed):
        return tuple(fixed.get(dim, slice(None)) for dim in SLOT_DIMS)

    def hop(self, phase):
        fixed = {dim: 0 for dim in self.order[:phase]} | {self.order[phase]: 1}
        source = self.total.at[self.place(fixed) + self.span]
        place = self.arrivals[phase].at[(slice(None),) * (3 - phase) + self.span]
        return self.copy(source, place, phase, self.order[phase])

    def add(self, fixed, source, source_dims):
        free = [dim for dim in SLOT_DIMS if dim not in fixed]

        def one(step):
            index = dict(fixed)
            for place, dim in enumerate(free):
                index[dim] = (step >> place) & 1
            spot = tuple(index[dim] for dim in SLOT_DIMS) + self.span
            term = source[tuple(index[dim] for dim in source_dims) + self.span]
            self.total[spot] = (self.total[spot].astype(single) + term.astype(single)).astype(
                bfloat
            )

        if free:
            pl.loop(0, 2 ** len(free))(one)
        else:
            one(0)

    def advance(self, phase):
        if phase < 0:
            self.across().wait_recv()
            source, dims, fixed = self.near, SLOT_DIMS, {}
        else:
            self.hop(phase).wait_recv()
            done = self.order[: phase + 1]
            dims = tuple(dim for dim in SLOT_DIMS if dim not in done)
            source, fixed = self.arrivals[phase], {dim: 0 for dim in done}
        if phase == 3:
            spot = (0,) * 4 + self.span
            self.out[self.span] = self.total[spot].astype(single) + source[self.span].astype(
                single
            )
            return
        ahead = self.order[phase + 1]
        self.add(fixed | {ahead: 1}, source, dims)
        self.hop(phase + 1).start()
        self.add(fixed | {ahead: 0}, source, dims)

    def finish(self):
        self.across().wait_send()
        for phase in range(4):
            self.hop(phase).wait_send()


SCATTER_SEMS = 5


def scatter_scratch(rows, width):
    return [
        pltpu.VMEM((2,) * free + (rows, width), bfloat) for free in (4, 3, 2, 1, 0)
    ]


def split_scatterings(far, near, scratch, out, shares, orders, send, recv, base):
    moving, first = [], 0
    for index, (count, order) in enumerate(zip(shares, orders)):
        slot = base + SCATTER_SEMS * index
        moving.append(
            Scattering(
                far, near, scratch[0], scratch[1:], out, order, first, count, send, recv, slot
            )
        )
        first += count
    return moving


def first_scatter_kernel(kv_far, kv_near, down_far, down_near, kv_out, down_out, *refs):
    scratch, (kv_total, kv_arrival, send, recv) = refs[:5], refs[5:]
    greet([partner(bit) for bit in (X, Z0, Z1, CORE, Y)])
    moving = split_scatterings(
        down_far, down_near, scratch, down_out, SHARES, DOWN_SUM_PARTS, send, recv, 0
    )
    base = len(moving) * SCATTER_SEMS
    count = kv_out.shape[0] // KV_PIECES

    def kv_copy(source, place, slot, bit):
        return pltpu.make_async_remote_copy(
            src_ref=source,
            dst_ref=place,
            send_sem=send.at[base + slot],
            recv_sem=recv.at[base + slot],
            device_id=partner(bit),
            device_id_type=MESH,
        )

    def near(piece):
        rows = pl.ds(piece * count, count)
        return kv_copy(kv_far.at[:, rows, :], kv_total.at[:, rows, :], 2 * piece, CORE)

    def over(piece):
        rows = pl.ds(piece * count, count)
        return kv_copy(kv_total.at[1, rows, :], kv_arrival.at[rows, :], 2 * piece + 1, Y)

    def kv_add(piece, side):
        rows = pl.ds(piece * count, count)
        kv_total[side, rows, :] = (
            kv_total[side, rows, :].astype(single) + kv_near[side, rows, :].astype(single)
        ).astype(bfloat)

    def pass_over(piece):
        kv_add(piece, 1)
        over(piece).start()

    def take(piece):
        over(piece).wait_recv()
        rows = pl.ds(piece * count, count)
        kv_total[0, rows, :] = (
            kv_total[0, rows, :].astype(single) + kv_arrival[rows, :].astype(single)
        ).astype(bfloat)

    for piece in range(KV_PIECES):
        near(piece).start()
    for part in moving:
        part.across().start()
    for part, phase in FIRST_SUM_STEPS:
        if part == KV:
            near(phase).wait_recv()
            kv_expected(phase, functools.partial(pass_over, phase))
            kv_add(phase, 0)
        else:
            moving[part].advance(phase)
    for piece in range(KV_PIECES):
        kv_needed(piece, functools.partial(take, piece))
    kv_out[...] = kv_total[0]
    for part in moving:
        part.finish()
    for piece in range(KV_PIECES):
        near(piece).wait_send()
        kv_expected(piece, lambda piece=piece: over(piece).wait_send())


def first_scatter(kv_far, kv_near, down_far, down_near):
    rows, width = down_far.shape[1:]
    local, wide = kv_far.shape[1:]
    cube = (2, 2, 2, 2, rows, width)
    sems = len(DOWN_SUM_PARTS) * SCATTER_SEMS + 2 * KV_PIECES
    return pl.pallas_call(
        first_scatter_kernel,
        out_shape=(
            jax.ShapeDtypeStruct((local, wide), bfloat),
            jax.ShapeDtypeStruct((rows, width), single),
        ),
        in_specs=[IN_HBM, IN_VMEM] * 2,
        out_specs=(IN_VMEM,) * 2,
        scratch_shapes=scatter_scratch(rows, width)
        + [pltpu.VMEM((2, local, wide), bfloat), pltpu.VMEM((local, wide), bfloat)]
        + [pltpu.SemaphoreType.DMA((sems,))] * 2,
        compiler_params=pltpu.CompilerParams(
            collective_id=3, has_side_effects=True, vmem_limit_bytes=VMEM_LIMIT
        ),
        cost_estimate=cost(0, 128 * rows * width),
        name="first_scatter",
    )(kv_far, kv_near, down_far.reshape(cube), down_near.reshape(cube))


def norm_back(values, grad, scale_row):
    centre = values - jnp.mean(values, axis=-1, keepdims=True)
    root = lax.rsqrt(jnp.mean(centre * centre, axis=-1, keepdims=True) + EPSILON)
    normed = centre * root
    scaled = grad * (1.0 + scale_row)
    inner = jnp.mean(scaled * normed, axis=-1, keepdims=True)
    return root * (scaled - jnp.mean(scaled, axis=-1, keepdims=True) - normed * inner), normed


def column_sum(values):
    return jnp.sum(values, axis=0, keepdims=True)


def last_scatter_kernel(
    up_far,
    up_near,
    a_ref,
    ob_ref,
    dq_ref,
    dkv_ref,
    dr_ref,
    w_ref,
    x_ref,
    dmid_ref,
    mod_ref,
    row_ref,
    ada_ref,
    down_ref,
    up_out,
    pair_out,
    grad_ref,
    mods_ref,
    bias_ref,
    silu_ref,
    cuts,
    *refs,
):
    up_scratch, pair_scratch, refs = refs[:5], refs[5:10], refs[10:]
    cut_send, cut_recv, cut_ref, refs = refs[0], refs[1], refs[2], refs[3:]
    far, near, weights, dy, table, line, bias_notes, mod_notes, bias_box, mod_box = refs[:10]
    parts, returns, weight_sem = refs[10:13]
    bias_send, bias_recv, mod_send, mod_recv, back_send, back_recv, send, recv = refs[13:]
    bucket, seq = lax.axis_index("bucket"), lax.axis_index("seq")
    me = bucket * PLANES + seq
    count = BLOCKS * PLANES
    barrier = pltpu.get_barrier_semaphore()

    @pl.loop(1, count)
    def _(distance):
        pl.semaphore_signal(barrier, inc=1, device_id=peer_at(distance), device_id_type=MESH)

    pl.semaphore_wait(barrier, count - 1)

    def message(source, target, out_sem, in_sem, distance):
        return pltpu.make_async_remote_copy(
            src_ref=source,
            dst_ref=target,
            send_sem=out_sem.at[distance],
            recv_sem=in_sem.at[distance],
            device_id=peer_at(distance),
            device_id_type=MESH,
        )

    def bias_note(distance):
        peer = peer_at(distance)
        source = bias_notes.at[peer[0] * PLANES + peer[1]]
        return message(source, bias_box.at[me], bias_send, bias_recv, distance)

    def mod_note(distance):
        source = mod_notes.at[peer_at(distance)[1]]
        return message(source, mod_box.at[me], mod_send, mod_recv, distance)

    def answer(distance):
        source = parts.at[peer_at(distance)[0]]
        return message(source, returns.at[me], back_send, back_recv, distance)

    base = len(UP_SUM_PARTS) * SCATTER_SEMS
    ups = split_scatterings(
        up_far, up_near, up_scratch, up_out, SHARES, UP_SUM_PARTS, send, recv, 0
    )
    pairs = split_scatterings(
        far, near, pair_scratch, pair_out, SHARES, PAIR_SUM_PARTS, send, recv, base
    )
    moving = ups + pairs
    for part in ups:
        part.across().start()

    def cut(distance):
        return pltpu.make_async_remote_copy(
            src_ref=cut_ref.at[seq ^ distance],
            dst_ref=cuts.at[seq],
            send_sem=cut_send.at[distance],
            recv_sem=cut_recv.at[distance],
            device_id=(bucket, seq ^ distance),
            device_id_type=MESH,
        )

    for index in range(PLANES):
        each = cuts.shape[2]
        cut_ref[index] = down_ref[:, index * each : (index + 1) * each].astype(bfloat)
    cuts[seq] = cut_ref[seq]
    for distance in range(1, PLANES):
        cut(distance).start()

    width = x_ref.shape[1]
    rows = up_out.shape[0]
    cols = 3 * width // PLANES
    wide = dy.shape[1]
    below = wide - LANES
    order = (1, 3, 0, 2)

    def load(step):
        plane = seq ^ order[step]
        return pltpu.make_async_copy(
            w_ref.at[plane, :, pl.ds(0, wide)], weights.at[step % 2], weight_sem.at[step % 2]
        )

    def gather_dy(index):
        low, high = index * cols, (index + 1) * cols
        pieces = []
        if low < width:
            pieces.append(dq_ref[:, low : min(high, width)])
        if high > width:
            pieces.append(dkv_ref[:, max(low - width, 0) : high - width])
        first = 0
        for piece in pieces:
            dy[:, first : first + piece.shape[1]] = piece
            first += piece.shape[1]

    def project(step):
        bits = order[step]
        plane = seq ^ bits
        if step == 0:
            load(0).start()
            dy[:, cols:] = jnp.zeros((dy.shape[0], wide - cols), bfloat)
            grad_ref[...] = jnp.zeros_like(grad_ref)
        if step + 1 < PLANES:
            load(step + 1).start()
        for index in range(PLANES):

            @pl.when(plane == index)
            def _():
                gather_dy(index)

        target = far if bits % 2 else near
        place = my_coords()

        def store(values, first_col):
            for block in range(BLOCKS):
                spot = (
                    bits // 2,
                    (block % 2) ^ place[X],
                    (block // 4) ^ place[Z1],
                    (block // 2 % 2) ^ place[Z0],
                    slice(None),
                    slice(first_col, first_col + values.shape[1]),
                )
                target[spot] = values[block * rows : (block + 1) * rows, :].astype(bfloat)

        store(dot_tn(a_ref[...], dy[:, :below]), 0)
        edge = dot_tn(ob_ref[...], dr_ref[plane])
        store(dot_tn(a_ref[...], dy[:, below:]) + edge[:, :LANES], below)
        store(edge[:, LANES:], wide)
        load(step).wait()
        grad_ref[...] += dot_nt(dy[...], weights[step % 2])

    def notes():
        shift_sum, scale_sum = jnp.zeros((1, width), single), jnp.zeros((1, width), single)
        scale_row = mod_ref[1:2, :]
        for tile in range(0, x_ref.shape[0], LANES):
            span = slice(tile, tile + LANES)
            grad = grad_ref[span, :]
            back, normed = norm_back(x_ref[span, :].astype(single), grad, scale_row)
            shift_sum += column_sum(grad)
            scale_sum += column_sum(grad * normed)
            grad_ref[span, :] = dmid_ref[span, :] + back
        line[:, :width] = shift_sum
        line[:, width : 2 * width] = scale_sum
        table[0:1, :] = shift_sum
        table[1:2, :] = scale_sum
        for index in range(4):
            line[:, (2 + index) * width : (3 + index) * width] = row_ref[index : index + 1, :]
        table[2:6, :] = row_ref[0:4, :]
        table[6:7, :] = column_sum(dq_ref[...].astype(single))
        table[7:8, :] = column_sum(dkv_ref[:, width:].astype(single))
        table[8:14, :] = row_ref[4:10, :]
        table[14:16, :] = jnp.zeros((2, width), single)
        each = width // count
        lane = lax.broadcasted_iota(jnp.int32, (LANES, width), 1)
        entry = lax.broadcasted_iota(jnp.int32, (LANES, width), 0)
        copies = (lane % each == entry).astype(single)
        owner = lax.broadcasted_iota(jnp.int32, (NOTE_ROWS, width), 1) // each

        @pl.loop(0, count)
        def _(device):
            mine = jnp.where(owner == device, table[...], 0.0)
            bias_notes[device] = lax.dot_general(
                mine,
                copies,
                (((1,), (1,)), ((), ())),
                preferred_element_type=single,
                precision=HIGHEST,
            )

        part = mod_notes.shape[2]
        for index in range(PLANES):
            mod_notes[index] = line[:, index * part : (index + 1) * part]
        bias_box[me] = bias_notes[me]
        mod_box[me] = mod_notes[seq]

        @pl.loop(1, count)
        def _(distance):
            mod_note(distance).start()
            bias_note(distance).start()

    def answers():
        @pl.loop(1, count)
        def _(distance):
            mod_note(distance).wait_recv()

        sums = [sum(mod_box[PLANES * g + s] for s in range(PLANES)) for g in range(BLOCKS)]
        mods = jnp.concatenate(sums)
        mods_ref[...] = mods
        silu = lax.dot_general(
            mods,
            ada_ref[...].astype(bfloat).astype(single),
            (((1,), (1,)), ((), ())),
            preferred_element_type=single,
            precision=HIGHEST,
        )
        for group in range(BLOCKS):
            parts[group, :, :rows] = silu[group : group + 1, :]
            parts[group, :, rows:] = jnp.zeros((1, parts.shape[2] - rows), single)
        returns[me] = parts[bucket]

        @pl.loop(1, count)
        def _(distance):
            answer(distance).start()

    since = 0
    for part, phase in LAST_SUM_STEPS:
        if part == PLANE:
            project(phase)
            if phase == 1:
                for moved in pairs:
                    moved.across().start()
        elif part == NOTE:
            notes()
            since = 1
        else:
            moving[part].advance(phase)
            since += since > 0
            if since == ANSWER_AFTER:
                answers()

    @pl.loop(1, count)
    def _(distance):
        bias_note(distance).wait_recv()

    bias_ref[...] = jnp.zeros_like(bias_ref)

    @pl.loop(0, count)
    def _(device):
        bias_ref[...] += bias_box[device]

    @pl.loop(1, count)
    def _(distance):
        answer(distance).wait_recv()

    for group in range(BLOCKS):
        silu_ref[group] = sum(returns[PLANES * group + s] for s in range(PLANES))
    for part in moving:
        part.finish()
    for distance in range(1, PLANES):
        cut(distance).wait_recv()
        cut(distance).wait_send()

    @pl.loop(1, count)
    def _(distance):
        bias_note(distance).wait_send()
        mod_note(distance).wait_send()
        answer(distance).wait_send()


ANSWER_AFTER = 12


def last_scatter(
    up_far,
    up_near,
    first_in,
    branch,
    query_grad,
    kv_grad,
    dr_planes,
    weight,
    tokens,
    middle_grad,
    mods,
    row_grads,
    ada_master,
    down_grad,
):
    rows, width = up_far.shape[1:]
    cube = (2, 2, 2, 2, rows, width)
    count = BLOCKS * PLANES
    cols = ada_master.shape[1]
    cuts = (PLANES, rows, width // PLANES)
    local = tokens.shape[0]
    wide = -(-3 * width // PLANES // LANES) * LANES
    mine = jax.ShapeDtypeStruct((rows, width), single)
    return pl.pallas_call(
        last_scatter_kernel,
        out_shape=(
            mine,
            mine,
            jax.ShapeDtypeStruct((local, width), single),
            jax.ShapeDtypeStruct((BLOCKS, cols), single),
            jax.ShapeDtypeStruct((NOTE_ROWS, LANES), single),
            jax.ShapeDtypeStruct((BLOCKS, 1, 2 * LANES), single),
            jax.ShapeDtypeStruct(cuts, bfloat),
        ),
        in_specs=[IN_HBM] + [IN_VMEM] * 6 + [IN_HBM] + [IN_VMEM] * 6,
        out_specs=(IN_VMEM,) * 7,
        scratch_shapes=scatter_scratch(rows, width)
        + scatter_scratch(rows, width)
        + [pltpu.SemaphoreType.DMA((PLANES,))] * 2
        + [pltpu.VMEM(cuts, bfloat)]
        + [pltpu.VMEM(cube, bfloat)] * 2
        + [
            pltpu.VMEM((2, width, wide), bfloat),
            pltpu.VMEM((local, wide), bfloat),
            pltpu.VMEM((NOTE_ROWS, width), single),
            pltpu.VMEM((1, 6 * width), single),
            pltpu.VMEM((count, NOTE_ROWS, LANES), single),
            pltpu.VMEM((PLANES, 1, cols), single),
            pltpu.VMEM((count, NOTE_ROWS, LANES), single),
            pltpu.VMEM((count, 1, cols), single),
            pltpu.VMEM((BLOCKS, 1, 2 * LANES), single),
            pltpu.VMEM((count, 1, 2 * LANES), single),
            pltpu.SemaphoreType.DMA((2,)),
        ]
        + [pltpu.SemaphoreType.DMA((count,))] * 6
        + [pltpu.SemaphoreType.DMA((2 * len(SHARES) * SCATTER_SEMS,))] * 2,
        compiler_params=pltpu.CompilerParams(
            collective_id=4, has_side_effects=True, vmem_limit_bytes=63 * 1024 * 1024
        ),
        cost_estimate=cost(14 * local * width * width, 200 * rows * width),
        name="last_scatter",
    )(
        up_far.reshape(cube),
        up_near.reshape(cube),
        first_in,
        branch,
        query_grad,
        kv_grad,
        dr_planes,
        weight,
        tokens,
        middle_grad,
        mods,
        row_grads,
        ada_master,
        down_grad,
    )


def whole(shape):
    return pl.BlockSpec(shape, lambda *_: (0,) * len(shape))


def qkv_kernel(cols, x_ref, shift_ref, scale_ref, bias_ref, w_ref, a_ref, q_ref, kv_ref, acc):
    step = pl.program_id(0)
    width = x_ref.shape[1]

    @pl.when(step == 0)
    def _():
        values = x_ref[...].astype(single)
        a_ref[...] = modulate(values, shift_ref[...], scale_ref[...]).astype(bfloat)

    wide = -(-cols // LANES) * LANES
    part = dot_nn(a_ref[...], w_ref[0, :, :wide])[:, :cols]
    for index in range(PLANES):

        @pl.when(step == index)
        def _():
            acc[:, index * cols : (index + 1) * cols] = part

    @pl.when(step == PLANES - 1)
    def _():
        q_ref[...] = (acc[:, :width] + bias_ref[:, :width]).astype(bfloat)
        kv_ref[...] = (acc[:, width:] + bias_ref[:, width:]).astype(bfloat)


def project_qkv(tokens, shift_row, scale_row, bias_row, weight):
    rows, width = tokens.shape
    cols = 3 * width // PLANES
    return pl.pallas_call(
        functools.partial(qkv_kernel, cols),
        grid=(PLANES,),
        out_shape=(
            jax.ShapeDtypeStruct((rows, width), bfloat),
            jax.ShapeDtypeStruct((rows, width), bfloat),
            jax.ShapeDtypeStruct((rows, 2 * width), bfloat),
        ),
        in_specs=[
            whole((rows, width)),
            whole((1, width)),
            whole((1, width)),
            whole((1, 3 * width)),
            pl.BlockSpec((1,) + weight.shape[1:], lambda s: (s, 0, 0)),
        ],
        out_specs=(whole((rows, width)), whole((rows, width)), whole((rows, 2 * width))),
        scratch_shapes=[pltpu.VMEM((rows, 3 * width), single)],
        compiler_params=params("arbitrary"),
        cost_estimate=cost(6 * rows * width * width, 8 * width * width),
        name="project_qkv",
    )(tokens, shift_row, scale_row, bias_row, weight)


def image_of(len_ref, position):
    start, length, end = jnp.int32(0), jnp.int32(0), jnp.int32(0)
    for index in range(len_ref.shape[1]):
        here = len_ref[0, index]
        inside = jnp.logical_and(position >= end, position < end + here)
        start = jnp.where(inside, end, start)
        length = jnp.where(inside, here, length)
        end = end + here
    return start, length


def head_windows(heads, size):
    for head in range(heads):
        low, high = head * size, (head + 1) * size
        yield head, low // LANES * LANES, -(-high // LANES) * LANES, low, high


def head_mask(low, high, left, right):
    lane = lax.broadcasted_iota(jnp.int32, (1, high - low), 1) + low
    return jnp.logical_and(lane >= left, lane < right)


LONG, SHORT = 1024, 256


def head_row(table_ref, bucket_ref, width):
    heads = table_ref.shape[1]
    size = width // heads
    lane = lax.broadcasted_iota(jnp.int32, (1, width), 1)
    row = jnp.zeros((1, width), jnp.int32)
    for head in range(heads):
        inside = jnp.logical_and(lane >= head * size, lane < (head + 1) * size)
        row = jnp.where(inside, table_ref[bucket_ref[0], head], row)
    return row.astype(single)


def attend_kernel(heads, len_ref, table_ref, bucket_ref, q_ref, kv, ob_ref, log_ref, out):
    rows, width = q_ref.shape
    size = width // heads
    my_seq = lax.axis_index("seq")
    factor = size ** (-0.5) * LOG2E

    def run(tile_start, start, span):
        tile = pl.ds(tile_start, TILE)
        keys = pl.ds(start, span)
        logs = jnp.zeros((TILE, LANES), single)
        lane = lax.broadcasted_iota(jnp.int32, (TILE, LANES), 1)
        for head, low, high, left, right in head_windows(heads, size):
            mask = head_mask(low, high, left, right)
            query = q_ref[tile, low:high] * mask.astype(single).astype(bfloat)
            scores = dot_nt(query, kv[keys, low:high])
            top = jnp.max(scores, axis=-1, keepdims=True)
            expo = jnp.exp2((scores - top) * factor)
            total = jnp.sum(expo, axis=-1, keepdims=True)
            part = dot_nn(expo.astype(bfloat), kv[keys, width + low : width + high]) / total
            out[tile, low:high] = jnp.where(mask, part, out[tile, low:high])
            logs = jnp.where(lane == head, top * factor + jnp.log2(total), logs)
        log_ref[:, tile] = logs.T[:heads, :]

    @pl.loop(0, rows // TILE)
    def _(index):
        tile_start = pl.multiple_of(index * TILE, TILE)
        start, length = image_of(len_ref, my_seq * rows + tile_start)
        start = pl.multiple_of(start, SHORT)

        @pl.when(length > SHORT)
        def _():
            run(tile_start, start, LONG)

        @pl.when(length <= SHORT)
        def _():
            run(tile_start, start, SHORT)

    ob_ref[...] = (out[...] * head_row(table_ref, bucket_ref, width)).astype(bfloat)


def attend(lengths, head_table, bucket_ids, query, kv, heads):
    rows, width = query.shape
    group = kv.shape[0]
    return pl.pallas_call(
        functools.partial(attend_kernel, heads),
        out_shape=(
            jax.ShapeDtypeStruct((rows, width), bfloat),
            jax.ShapeDtypeStruct((heads, rows), single),
        ),
        in_specs=[IN_SMEM] * 3 + [IN_VMEM] * 2,
        out_specs=(IN_VMEM,) * 2,
        scratch_shapes=[pltpu.VMEM((rows, width), single)],
        compiler_params=params(),
        cost_estimate=cost(16 * rows * LONG * width, 10 * group * width, heads * rows * LONG),
        name="attend",
    )(lengths, head_table, bucket_ids, query, kv)


def out_kernel(ob_ref, w_ref, bias_ref, x_ref, c_ref, keep_ref, mod_ref, r_ref, mid_ref, a_ref, df_ref):
    step = pl.program_id(0)
    width = x_ref.shape[1]
    cols = width // PLANES
    part = dot_nn(ob_ref[...], w_ref[0])[:, -cols:]
    for index in range(PLANES):

        @pl.when(step == index)
        def _():
            r_ref[:, index * cols : (index + 1) * cols] = part

    @pl.when(step == PLANES - 1)
    def _():
        result = r_ref[...] + bias_ref[...]
        r_ref[...] = result
        middle = x_ref[...].astype(single) + mod_ref[2:3, :] * result
        mid_ref[...] = middle
        a_ref[...] = modulate(middle, mod_ref[3:4, :], mod_ref[4:5, :]).astype(bfloat)
        df_ref[...] = (mod_ref[5:6, :] * keep_ref[...] * c_ref[...].astype(single)).astype(bfloat)


def project_out(branch, weight, bias_row, tokens, upstream, keep, mods):
    rows, width = tokens.shape
    row, square = whole((1, width)), whole((rows, width))
    return pl.pallas_call(
        out_kernel,
        grid=(PLANES,),
        out_shape=(
            jax.ShapeDtypeStruct((rows, width), single),
            jax.ShapeDtypeStruct((rows, width), single),
            jax.ShapeDtypeStruct((rows, width), bfloat),
            jax.ShapeDtypeStruct((rows, width), bfloat),
        ),
        in_specs=[
            square,
            pl.BlockSpec((1, width, 3 * LANES), lambda s: (s, 0, 2)),
            row,
            square,
            square,
            whole((rows, 1)),
            whole(mods.shape),
        ],
        out_specs=(square,) * 4,
        compiler_params=params("arbitrary"),
        cost_estimate=cost(2 * rows * width * width, 2 * width * width + 16 * rows * width),
        name="project_out",
    )(branch, weight, bias_row, tokens, upstream, keep, mods)


def out_copies(source, layout, plane, buffer, seq_bits, far_ref, near_ref, sem):
    my_bucket, my_seq = place_in_kernel()
    rows = far_ref.shape[1]
    copies = []
    for index in range(BLOCKS):
        if layout == "rows":
            bits, part = index % PLANES, index // PLANES
            seq = my_seq ^ bits
            bucket = plane * (BLOCKS // PLANES) + part
            start = pl.multiple_of((part * PLANES + seq) * rows, 16)
            side = bits % 2
        else:
            bits, bucket, start, side = seq_bits, index, index * rows, seq_bits_side(seq_bits)
        target = far_ref if side else near_ref
        slot = slot_of(bucket ^ my_bucket, bits if layout == "rows" else seq_bits[0])
        copies.append(
            pltpu.make_async_copy(
                source.at[buffer, pl.ds(start, rows), :], target.at[slot], sem.at[buffer, index]
            )
        )
    return copies


def seq_bits_side(seq_bits):
    return seq_bits[1]


def ffn_kernel(bucket_ref, a_ref, df_ref, cm_ref, b_ref, up_ref, down_ref, *refs):
    f_ref, da_ref, up_far, up_near, down_far, down_near, db_ref = refs[:7]
    up, down, up_grad, down_grad, up_sem, down_sem, up_out, down_out = refs[7:]
    width = a_ref.shape[1]
    my_seq = place_in_kernel()[1]

    def loads(bits):
        plane = my_seq ^ bits
        rows = pl.ds(pl.multiple_of(plane * width, LANES), width)
        return (
            pltpu.make_async_copy(up_ref.at[plane], up.at[plane], up_sem.at[bits]),
            pltpu.make_async_copy(down_ref.at[rows, :], down.at[rows, :], down_sem.at[bits]),
        )

    for bits in (1, 3, 0, 2):
        for copy in loads(bits):
            copy.start()
    f_ref[...] = jnp.zeros_like(f_ref)
    da_ref[...] = jnp.zeros_like(da_ref)

    def one(plane, low, high, buffer):
        first, grad = a_ref[...], df_ref[...]
        hidden_rows = pl.ds(pl.multiple_of(plane * width + low, LANES), high - low)
        keep = cm_ref[pl.ds(bucket_ref[0], 1), hidden_rows].astype(single)
        pre = dot_nn(first, up[plane, :, low:high]) + b_ref[plane, :, low:high]
        root = math.sqrt(2.0 / math.pi)
        square = pre * pre
        bend = jnp.tanh(root * pre * (1.0 + 0.044715 * square))
        half = 0.5 * (1.0 + bend)
        hidden = (pre * half * keep).astype(bfloat)
        slope = half + 0.5 * pre * (1.0 - bend * bend) * (root * (1.0 + 0.134145 * square))
        back = (dot_nt(grad, down[hidden_rows, :]) * keep * slope).astype(bfloat)
        f_ref[...] += dot_nn(hidden, down[hidden_rows, :])
        da_ref[...] += dot_nt(back, up[plane, :, low:high])
        up_grad[buffer, :, low:high] = dot_tn(first, back).astype(bfloat)
        down_grad[buffer, low:high, :] = dot_tn(hidden, grad).astype(bfloat)
        db_ref[plane, :, low:high] = jnp.sum(back.astype(single), axis=0, keepdims=True)

    cut = -(-width // 2 // LANES) * LANES

    def sends(plane, buffer, side_bits, far_side):
        return out_copies(
            up_grad, "planes", plane, buffer, (side_bits, far_side), up_far, up_near, up_out
        ) + out_copies(
            down_grad, "rows", plane, buffer, None, down_far, down_near, down_out
        )

    for far_side in (1, 0):

        @pl.loop(0, 2)
        def _(above):
            bits = above * 2 + far_side
            plane = my_seq ^ bits
            if not far_side:
                for copy in sends(plane, above, bits, far_side):
                    copy.wait()
            for copy in loads(bits):
                copy.wait()
            one(plane, 0, cut, above)
            one(plane, cut, width, above)
            for copy in sends(plane, above, bits, far_side):
                copy.start()

    for above in range(2):
        for copy in sends(my_seq ^ (above * 2), above, above * 2, 0):
            copy.wait()


def feed_forward(bucket_ids, first, grad, chan_table, bias_row, up_weight, down_weight):
    rows, width = first.shape
    hidden = chan_table.shape[1]
    blocks = jax.ShapeDtypeStruct((BLOCKS * PLANES // 2, width // BLOCKS, width), bfloat)
    result = pl.pallas_call(
        ffn_kernel,
        out_shape=(
            jax.ShapeDtypeStruct((rows, width), single),
            jax.ShapeDtypeStruct((rows, width), single),
            blocks,
            blocks,
            blocks,
            blocks,
            jax.ShapeDtypeStruct((PLANES, 1, width), single),
        ),
        in_specs=[IN_SMEM] + [IN_VMEM] * 4 + [IN_HBM] * 2,
        out_specs=(IN_VMEM, IN_VMEM) + (IN_HBM,) * 4 + (IN_VMEM,),
        scratch_shapes=[
            pltpu.VMEM((PLANES, width, width), bfloat),
            pltpu.VMEM((hidden, width), bfloat),
            pltpu.VMEM((2, width, width), bfloat),
            pltpu.VMEM((2, width, width), bfloat),
            pltpu.SemaphoreType.DMA((PLANES,)),
            pltpu.SemaphoreType.DMA((PLANES,)),
            pltpu.SemaphoreType.DMA((2, BLOCKS)),
            pltpu.SemaphoreType.DMA((2, BLOCKS)),
        ],
        compiler_params=params(),
        cost_estimate=cost(12 * rows * width * hidden, 8 * width * hidden, rows * hidden),
        name="feed_forward",
    )(
        bucket_ids,
        first,
        grad,
        chan_table,
        bias_row.reshape(PLANES, 1, width),
        up_weight,
        down_weight,
    )
    return result


def back_out_kernel(
    heads,
    f_ref,
    da_ref,
    mid_ref,
    r_ref,
    c_ref,
    keep_ref,
    mod_ref,
    bias_ref,
    df_ref,
    w_ref,
    table_ref,
    bucket_ref,
    ob_ref,
    out_ref,
    dmid_ref,
    dr_ref,
    row_ref,
    do_ref,
    delta_ref,
    acc,
):
    step = pl.program_id(0)
    width = acc.shape[1]
    cols = width // PLANES
    edge = dr_ref.shape[2] - cols

    @pl.when(step == 0)
    def _():
        row_ref[...] = jnp.zeros_like(row_ref)
        acc[...] = jnp.zeros_like(acc)
        gate_one, scale, gate_two = mod_ref[2:3, :], mod_ref[4:5, :], mod_ref[5:6, :]

        @pl.loop(0, acc.shape[0], step=LANES)
        def _(tile):
            span = pl.ds(pl.multiple_of(tile, LANES), LANES)
            keep = keep_ref[span, :]
            upstream = c_ref[span, :].astype(single)
            middle = mid_ref[span, :]
            mlp = f_ref[span, :] + bias_ref[...]
            out_ref[span, :] = (middle + gate_two * keep * mlp).astype(bfloat)
            grad = da_ref[span, :]
            back, normed = norm_back(middle, grad, scale)
            dmid = upstream + back
            dmid_ref[span, :] = dmid
            branch = (gate_one * dmid).astype(bfloat).astype(single)
            for plane in range(PLANES):
                dr_ref[plane, span, :edge] = jnp.zeros((LANES, edge), bfloat)
                dr_ref[plane, span, edge:] = branch[:, plane * cols : (plane + 1) * cols].astype(
                    bfloat
                )
            row_ref[0:1, :] += column_sum(dmid * r_ref[span, :])
            row_ref[1:2, :] += column_sum(grad)
            row_ref[2:3, :] += column_sum(grad * normed)
            row_ref[3:4, :] += column_sum(keep * upstream * mlp)
            row_ref[4:5, :] += column_sum(branch)
            row_ref[5:6, :] += column_sum(df_ref[span, :].astype(single))

    acc[...] += dot_nt(dr_ref[step], w_ref[0])

    @pl.when(step == PLANES - 1)
    def _():
        size = width // heads
        grad = (acc[...] * head_row(table_ref, bucket_ref, width)).astype(bfloat)
        do_ref[...] = grad
        terms = grad.astype(single) * ob_ref[...].astype(single)
        head = lax.broadcasted_iota(jnp.int32, (heads, width), 0)
        lane = lax.broadcasted_iota(jnp.int32, (heads, width), 1)
        chosen = jnp.logical_and(lane >= head * size, lane < (head + 1) * size)
        delta_ref[...] = lax.dot_general(
            chosen.astype(single),
            terms,
            (((1,), (1,)), ((), ())),
            preferred_element_type=single,
            precision=HIGHEST,
        )


def back_out(
    mlp_sum,
    second_grad,
    middle,
    attn_out,
    upstream,
    keep,
    mods,
    bias_row,
    mlp_grad,
    weight,
    head_table,
    bucket_ids,
    branch,
    heads,
):
    rows, width = branch.shape
    row, square = whole((1, width)), whole((rows, width))
    return pl.pallas_call(
        functools.partial(back_out_kernel, heads),
        grid=(PLANES,),
        out_shape=(
            jax.ShapeDtypeStruct((rows, width), bfloat),
            jax.ShapeDtypeStruct((rows, width), single),
            jax.ShapeDtypeStruct((PLANES, rows, 3 * LANES), bfloat),
            jax.ShapeDtypeStruct((8, width), single),
            jax.ShapeDtypeStruct((rows, width), bfloat),
            jax.ShapeDtypeStruct((heads, rows), single),
        ),
        in_specs=[
            square,
            square,
            square,
            square,
            square,
            whole((rows, 1)),
            whole(mods.shape),
            row,
            square,
            pl.BlockSpec((1, width, 3 * LANES), lambda s: (s, 0, 2)),
            IN_SMEM,
            IN_SMEM,
            square,
        ],
        out_specs=(
            square,
            square,
            whole((PLANES, rows, 3 * LANES)),
            whole((8, width)),
            square,
            whole((heads, rows)),
        ),
        scratch_shapes=[pltpu.VMEM((rows, width), single)],
        compiler_params=params("arbitrary"),
        cost_estimate=cost(2 * rows * width * width, 2 * width * width + 30 * rows * width),
        name="back_out",
    )(
        mlp_sum,
        second_grad,
        middle,
        attn_out,
        upstream,
        keep,
        mods,
        bias_row,
        mlp_grad,
        weight,
        head_table,
        bucket_ids,
        branch,
    )


def attend_back_kernel(
    heads, len_ref, q_ref, do_ref, log_ref, delta_ref, kv, dq_ref, far_ref, near_ref, dq, dk, dv
):
    rows, width = q_ref.shape
    size = width // heads
    my_seq = lax.axis_index("seq")
    scale = size ** (-0.5)
    factor = scale * LOG2E
    dk[...] = jnp.zeros_like(dk)
    dv[...] = jnp.zeros_like(dv)

    def run(tile_start, start, span):
        tile = pl.ds(tile_start, TILE)
        keys = pl.ds(start, span)
        for head, low, high, left, right in head_windows(heads, size):
            mask = head_mask(low, high, left, right)
            chosen = mask.astype(single).astype(bfloat)
            query = q_ref[tile, low:high] * chosen
            grad = do_ref[tile, low:high] * chosen
            key = kv[keys, low:high]
            probs = jnp.exp2(dot_nt(key, query) * factor - log_ref[head : head + 1, tile])
            slope = dot_nt(kv[keys, width + low : width + high], grad)
            score_grad = (probs * (slope - delta_ref[head : head + 1, tile])).astype(bfloat)
            dv[keys, low:high] += dot_nn(probs.astype(bfloat), grad)
            dk[keys, low:high] += dot_nn(score_grad, query)
            part = dot_tn(score_grad, key)
            dq[tile, low:high] = jnp.where(mask, part, dq[tile, low:high])

    @pl.loop(0, rows // TILE)
    def _(index):
        tile_start = pl.multiple_of(index * TILE, TILE)
        start, length = image_of(len_ref, my_seq * rows + tile_start)
        start = pl.multiple_of(start, SHORT)

        @pl.when(length > SHORT)
        def _():
            run(tile_start, start, LONG)

        @pl.when(length <= SHORT)
        def _():
            run(tile_start, start, SHORT)

    dq_ref[...] = (dq[...] * scale).astype(bfloat)
    base = place_in_kernel()[1]
    for bits in range(PLANES):
        place = pl.ds(pl.multiple_of((base ^ bits) * rows, rows), rows)
        target = far_ref if bits % 2 else near_ref
        target[bits // 2, :, :width] = (dk[place, :] * scale).astype(bfloat)
        target[bits // 2, :, width:] = dv[place, :].astype(bfloat)


def attend_back(lengths, query, grad, logs, delta, kv, heads):
    rows, width = query.shape
    group = kv.shape[0]
    return pl.pallas_call(
        functools.partial(attend_back_kernel, heads),
        out_shape=(
            jax.ShapeDtypeStruct((rows, width), bfloat),
            jax.ShapeDtypeStruct((2, rows, 2 * width), bfloat),
            jax.ShapeDtypeStruct((2, rows, 2 * width), bfloat),
        ),
        in_specs=[pl.BlockSpec(memory_space=pltpu.SMEM)]
        + [IN_VMEM] * 5,
        out_specs=(IN_VMEM,) * 3,
        scratch_shapes=[
            pltpu.VMEM((rows, width), single),
            pltpu.VMEM((group, width), single),
            pltpu.VMEM((group, width), single),
        ],
        compiler_params=params(),
        cost_estimate=cost(40 * rows * LONG * width, 20 * group * width, heads * rows * LONG),
        name="attend_back",
    )(lengths, query, grad, logs, delta, kv)


def back_qkv_kernel(
    a_ref, ob_ref, dy_ref, dr_ref, w_ref, da_ref, far_ref, near_ref, stage, sem
):
    my_seq = place_in_kernel()[1]
    wide = dy_ref.shape[2]
    below = wide - LANES
    da_ref[...] = jnp.zeros_like(da_ref)

    def sends(plane, buffer, bits, far_side):
        return out_copies(
            stage, "planes", plane, buffer, (bits, far_side), far_ref, near_ref, sem
        )

    for far_side in (1, 0):

        @pl.loop(0, 2)
        def _(above):
            bits = above * 2 + far_side
            plane = my_seq ^ bits
            if not far_side:
                for copy in sends(plane, above, bits, far_side):
                    copy.wait()
            da_ref[...] += dot_nt(dy_ref[plane], w_ref[plane, :, :wide])
            first = dot_tn(a_ref[...], dy_ref[plane])
            second = dot_tn(ob_ref[...], dr_ref[plane])
            stage[above, :, :below] = first[:, :below].astype(bfloat)
            stage[above, :, below:wide] = (first[:, below:] + second[:, :LANES]).astype(bfloat)
            stage[above, :, wide:] = second[:, LANES:].astype(bfloat)
            for copy in sends(plane, above, bits, far_side):
                copy.start()

    for above in range(2):
        for copy in sends(my_seq ^ (above * 2), above, above * 2, 0):
            copy.wait()


def back_qkv(first_in, branch, dy_planes, dr_planes, weight):
    rows, width = first_in.shape
    blocks = jax.ShapeDtypeStruct((BLOCKS * PLANES // 2, width // BLOCKS, width), bfloat)
    return pl.pallas_call(
        back_qkv_kernel,
        out_shape=(jax.ShapeDtypeStruct((rows, width), single), blocks, blocks),
        in_specs=[IN_VMEM] * 5,
        out_specs=(IN_VMEM, IN_HBM, IN_HBM),
        scratch_shapes=[
            pltpu.VMEM((2, width, width), bfloat),
            pltpu.SemaphoreType.DMA((2, BLOCKS)),
        ],
        compiler_params=params(),
        cost_estimate=cost(14 * rows * width * width, 4 * weight.size),
        name="back_qkv",
    )(first_in, branch, dy_planes, dr_planes, weight)


def on_device(
    tokens,
    condition,
    cotangent,
    lengths,
    bucket_ids,
    keep_flags,
    head_table,
    chan_table,
    ada_master,
    ada_first,
    ada_second,
    ada_average,
    qkv_master,
    qkv_first,
    qkv_second,
    qkv_average,
    out_master,
    out_first,
    out_second,
    out_average,
    up_master,
    up_first,
    up_second,
    up_average,
    down_master,
    down_first,
    down_second,
    down_average,
    bias_master,
    bias_first,
    bias_second,
    bias_average,
):
    local_rows, width = tokens.shape
    heads = head_table.shape[1]
    head_size = width // heads
    hidden_width = chan_table.shape[1]
    hidden_ratio = hidden_width // width
    table_cols = 10 + hidden_ratio
    my_bucket, my_seq = lax.axis_index("bucket"), lax.axis_index("seq")
    buckets, seqs = lax.axis_size("bucket"), lax.axis_size("seq")
    group_rows = local_rows * seqs
    block_rows = qkv_master.shape[0]
    if cube_path():
        table = bias_master.reshape(-1, table_cols).T
        cut = down_master.astype(bfloat).reshape(seqs, -1, down_master.shape[1])
        (
            pair_weight,
            up_weight,
            down_weight,
            near,
            silu_rows,
            mods,
            bias_table,
            first_in,
            query,
        ) = gather(
            condition, table, ada_master, qkv_master, out_master, up_master, cut, tokens
        )
    else:
        pair_block = jnp.concatenate([qkv_master, out_master], axis=1).astype(bfloat)
        down_block = lax.all_to_all(
            down_master.astype(bfloat), "seq", split_axis=0, concat_axis=1, tiled=True
        )
        up_block = up_master.astype(bfloat)
        ada_low = ada_master.astype(bfloat)
        pair_weight = gather_all(pair_block, "planes")
        bias_low = lax.all_gather(
            bias_master.astype(bfloat), ("bucket", "seq"), axis=0, tiled=True
        )
        silu_low = jax.nn.silu(condition).astype(bfloat)
        silu_all = lax.all_gather(silu_low, "bucket", axis=0, tiled=True)
        silu_rows = lax.dynamic_slice_in_dim(silu_all, my_bucket * block_rows, block_rows, 1)
        mod_part = lax.psum_scatter(
            dot_nn(silu_rows, ada_low), "bucket", scatter_dimension=0, tiled=True
        )
        mod_row = lax.all_gather(mod_part, "seq", axis=1, tiled=True)
        bias_table = bias_low.astype(single).reshape(width, table_cols).T
        mods = jnp.pad(mod_row.reshape(6, width) + bias_table[:6], ((0, 2), (0, 0)))
        value_bias = bias_table[7:8]
        qkv_bias = jnp.concatenate(
            [bias_table[6:7], jnp.zeros_like(value_bias), value_bias], axis=1
        )
        first_in, query, key_value = project_qkv(
            tokens, mods[0:1], mods[1:2], qkv_bias, pair_weight
        )
        up_weight = gather_all(up_block, "planes")
        down_weight = gather_all(down_block, "rows")
        near = lax.all_gather(key_value, "seq", axis=0, tiled=True)

    out_bias = bias_table[8:9]
    up_bias = bias_table[9 : table_cols - 1].T.reshape(1, hidden_width)
    down_bias = bias_table[table_cols - 1 : table_cols]
    keep_float = keep_flags.astype(single)[:, None]
    branch_in, logs = attend(lengths, head_table, bucket_ids, query, near, heads)
    attn_out, middle, second_in, mlp_grad = project_out(
        branch_in, pair_weight, out_bias, tokens, cotangent, keep_float, mods
    )
    mlp_sum, second_grad, up_far, up_near, down_far, down_near, up_bias_grad = feed_forward(
        bucket_ids, second_in, mlp_grad, chan_table, up_bias, up_weight, down_weight
    )
    output, middle_grad, dr_planes, row_grads, attended_grad, delta = back_out(
        mlp_sum,
        second_grad,
        middle,
        attn_out,
        cotangent,
        keep_float,
        mods,
        down_bias,
        mlp_grad,
        pair_weight,
        head_table,
        bucket_ids,
        branch_in,
        heads,
    )
    up_bias_rows = up_bias_grad.reshape(width, hidden_ratio).T
    query_grad, kv_far, kv_near = attend_back(
        lengths, query, attended_grad, logs, delta, near, heads
    )
    qkv_cols = 3 * width // seqs
    if cube_path():
        kv_grad, down_new_grad = first_scatter(kv_far, kv_near, down_far, down_near)
        rows_all = jnp.concatenate([row_grads[:5], up_bias_rows, row_grads[5:6]])
        rows_all = jnp.pad(rows_all, ((0, 16 - rows_all.shape[0]), (0, 0)))
        (
            up_new_grad,
            pair_new_grad,
            token_grad,
            mod_all,
            bias_sum,
            silu_sum,
            down_cuts,
        ) = last_scatter(
            up_far,
            up_near,
            first_in,
            branch_in,
            query_grad,
            kv_grad,
            dr_planes,
            pair_weight,
            tokens,
            middle_grad,
            mods,
            rows_all,
            ada_master,
            down_new_grad,
        )
        down_mine = down_cuts.reshape(down_master.shape)
        bias_new_grad = bias_sum[:table_cols, : width // (buckets * seqs)].T.reshape(-1)
        silu_grad = silu_sum[:, 0, :block_rows].reshape(1, width)
    else:
        terms = jnp.stack([kv_near[0], kv_far[0], kv_near[1], kv_far[1]])
        kv_grad = lax.psum_scatter(terms, "seq", scatter_dimension=0)
        projected_grad = jnp.concatenate([query_grad, kv_grad], axis=1)
        dy_planes = jnp.pad(
            projected_grad.reshape(local_rows, seqs, qkv_cols).transpose(1, 0, 2),
            ((0, 0), (0, 0), (0, -qkv_cols % LANES)),
        )
        first_grad, pair_far, pair_near = back_qkv(
            first_in, branch_in, dy_planes, dr_planes, pair_weight
        )
        back, normed = norm_back(tokens.astype(single), first_grad, mods[1:2])
        token_grad = middle_grad + back
        up_new_grad = natural_sum(up_far, up_near, "planes")
        down_new_grad = natural_sum(down_far, down_near, "rows")
        pair_new_grad = natural_sum(pair_far, pair_near, "planes")
        mod_grads = jnp.concatenate(
            [column_sum(first_grad), column_sum(first_grad * normed), row_grads[:4]]
        )
        bias_grad = jnp.concatenate(
            [
                mod_grads,
                column_sum(query_grad.astype(single)),
                column_sum(kv_grad[:, width:].astype(single)),
                row_grads[4:5],
                up_bias_rows,
                row_grads[5:6],
            ]
        ).T.reshape(width * table_cols)
        mod_mine = lax.psum_scatter(
            mod_grads.reshape(seqs, 6 * width // seqs), "seq", scatter_dimension=0, tiled=True
        )
        mod_all = lax.all_gather(mod_mine, "bucket", axis=0, tiled=True)
        silu_part = lax.dot_general(
            mod_all,
            ada_low.astype(single),
            (((1,), (1,)), ((), ())),
            preferred_element_type=single,
            precision=HIGHEST,
        )
        silu_grad = lax.all_to_all(
            lax.psum(silu_part, "seq"), "bucket", split_axis=0, concat_axis=1, tiled=True
        )
        bias_new_grad = lax.psum_scatter(
            bias_grad, ("bucket", "seq"), scatter_dimension=0, tiled=True
        )
        down_mine = lax.all_to_all(
            down_new_grad.astype(bfloat), "seq", split_axis=1, concat_axis=0, tiled=True
        )
    ada_new_grad = lax.dot_general(
        silu_rows.astype(single),
        mod_all,
        (((0,), (0,)), ((), ())),
        preferred_element_type=single,
        precision=HIGHEST,
    )
    _, silu_back = jax.vjp(jax.nn.silu, condition)
    condition_grad = silu_back(silu_grad)[0]
    out_rate = (group_rows / (16.0 * width)) ** 0.5
    ada_new = adam_update(
        ada_master, ada_first, ada_second, ada_average, ada_new_grad, width ** (-0.5), MATRIX_DECAY
    )
    qkv_new = adam_update(
        qkv_master,
        qkv_first,
        qkv_second,
        qkv_average,
        pair_new_grad[:, :qkv_cols],
        width ** (-0.5),
        MATRIX_DECAY,
    )
    out_new = adam_update(
        out_master,
        out_first,
        out_second,
        out_average,
        pair_new_grad[:, qkv_cols:],
        out_rate,
        MATRIX_DECAY,
    )
    up_new = adam_update(
        up_master, up_first, up_second, up_average, up_new_grad, width ** (-0.5), MATRIX_DECAY
    )
    down_new = adam_update(
        down_master.T,
        down_first.T,
        down_second.T,
        down_average.T,
        down_mine.T.astype(single),
        hidden_width ** (-0.5),
        MATRIX_DECAY,
    )
    down_new = [value.T for value in down_new]
    bias_new = adam_update(
        bias_master, bias_first, bias_second, bias_average, bias_new_grad, 0.3, 0.0
    )
    return (
        output,
        token_grad,
        condition_grad,
        *ada_new,
        *qkv_new,
        *out_new,
        *up_new,
        *down_new,
        *bias_new,
    )


def solution(mesh):
    in_specs = (
        P(("bucket", "seq"), None),
        P("bucket", None),
        P(("bucket", "seq"), None),
        P("bucket", None),
        P("bucket"),
        P(("bucket", "seq")),
        P(),
        P(),
        P("bucket", "seq"),
        P("bucket", "seq"),
        P("bucket", "seq"),
        P("bucket", "seq"),
        P("bucket", "seq"),
        P("bucket", "seq"),
        P("bucket", "seq"),
        P("bucket", "seq"),
        P("bucket", "seq"),
        P("bucket", "seq"),
        P("bucket", "seq"),
        P("bucket", "seq"),
        P("bucket", "seq"),
        P("bucket", "seq"),
        P("bucket", "seq"),
        P("bucket", "seq"),
        P("bucket", "seq"),
        P("bucket", "seq"),
        P("bucket", "seq"),
        P("bucket", "seq"),
        P(("bucket", "seq")),
        P(("bucket", "seq")),
        P(("bucket", "seq")),
        P(("bucket", "seq")),
    )
    out_specs = (
        P(("bucket", "seq"), None),
        P(("bucket", "seq"), None),
        P("bucket", None),
        P("bucket", "seq"),
        P("bucket", "seq"),
        P("bucket", "seq"),
        P("bucket", "seq"),
        P("bucket", "seq"),
        P("bucket", "seq"),
        P("bucket", "seq"),
        P("bucket", "seq"),
        P("bucket", "seq"),
        P("bucket", "seq"),
        P("bucket", "seq"),
        P("bucket", "seq"),
        P("bucket", "seq"),
        P("bucket", "seq"),
        P("bucket", "seq"),
        P("bucket", "seq"),
        P("bucket", "seq"),
        P("bucket", "seq"),
        P("bucket", "seq"),
        P("bucket", "seq"),
        P(("bucket", "seq")),
        P(("bucket", "seq")),
        P(("bucket", "seq")),
        P(("bucket", "seq")),
    )
    return jax.shard_map(
        on_device, mesh=mesh, in_specs=in_specs, out_specs=out_specs, check_vma=False
    )
```

```python
import functools
import math

import jax
import jax.numpy as jnp
from jax import lax
from jax.experimental import pallas as pl
from jax.experimental.pallas import tpu as pltpu
from jax.sharding import PartitionSpec as P

STEP = 10


EPSILON = 1e-06
BETA_FIRST = 0.5
BETA_SECOND = 0.5
ADAM_EPSILON = 1e-08
MATRIX_DECAY = 0.01
EMA_DECAY = 0.9999
HIGHEST = lax.Precision.HIGHEST
LOG2E = math.log2(math.e)
LANES = 128
TILE = 256
VMEM_LIMIT = 60 * 1024 * 1024
bfloat = jnp.bfloat16
single = jnp.float32


def layer_norm(values):
    centre = values - jnp.mean(values, axis=-1, keepdims=True)
    spread = jnp.mean(centre * centre, axis=-1, keepdims=True)
    return centre * lax.rsqrt(spread + EPSILON)


def modulate(values, shift_row, scale_row):
    return layer_norm(values) * (1.0 + scale_row) + shift_row


def dot_nn(left, right):
    return lax.dot_general(left, right, (((1,), (0,)), ((), ())), preferred_element_type=single)


def dot_nt(left, right):
    return lax.dot_general(left, right, (((1,), (1,)), ((), ())), preferred_element_type=single)


def dot_tn(left, right):
    return lax.dot_general(left, right, (((0,), (0,)), ((), ())), preferred_element_type=single)


def adam_update(master, moment_one, moment_two, average, gradient, step_rate, decay_rate):
    one_new = BETA_FIRST * moment_one + (1.0 - BETA_FIRST) * gradient
    two_new = BETA_SECOND * moment_two + (1.0 - BETA_SECOND) * gradient * gradient
    one_hat = one_new / (1.0 - BETA_FIRST**STEP)
    two_hat = two_new / (1.0 - BETA_SECOND**STEP)
    master_new = master - step_rate * (
        one_hat / (jnp.sqrt(two_hat) + ADAM_EPSILON) + decay_rate * master
    )
    average_decay = min(EMA_DECAY, (1.0 + STEP) / (10.0 + STEP))
    average_new = average_decay * average + (1.0 - average_decay) * master_new
    return (master_new, one_new, two_new, average_new)


def params(*semantics):
    return pltpu.CompilerParams(
        dimension_semantics=semantics or None, vmem_limit_bytes=VMEM_LIMIT
    )


def cost(flops, moved, exps=0):
    return pl.CostEstimate(flops=int(flops), bytes_accessed=int(moved), transcendentals=int(exps))


def exchange(values, axis, bit):
    count = lax.axis_size(axis)
    return lax.ppermute(values, axis, [(i, i ^ bit) for i in range(count)])


def pick(values, index, axis):
    return lax.dynamic_index_in_dim(values, index, axis, keepdims=False)


IN_VMEM = pl.BlockSpec(memory_space=pltpu.VMEM)
IN_HBM = pl.BlockSpec(memory_space=pl.ANY)
IN_SMEM = pl.BlockSpec(memory_space=pltpu.SMEM)


def cube_path():
    return lax.axis_size("bucket") == 8 and lax.axis_size("seq") == 4


BLOCKS, PLANES = 8, 4
X, Z0, Z1, CORE, Y = ("bucket", 1), ("bucket", 2), ("bucket", 4), ("seq", 1), ("seq", 2)
MIDDLE, FORWARD = ("bucket", 6), ("bucket", 2, "forward")


def gather_all(block, layout):
    width = block.shape[1]
    if layout == "rows":
        return lax.all_gather(block, ("bucket", "seq"), axis=0, tiled=True)
    tall = lax.all_gather(block, "bucket", axis=0, tiled=True)
    return lax.all_gather(tall, "seq", axis=0)


def place_in_kernel():
    if cube_path():
        return lax.axis_index("bucket"), lax.axis_index("seq")
    return 0, 0


DIMS = {"planes": (Y, CORE, Z1, Z0, X), "rows": (Z1, Z0, X, Y, CORE)}
MESH = pl.DeviceIdType.MESH


def my_coords():
    bucket, seq = lax.axis_index("bucket"), lax.axis_index("seq")
    return {
        (axis, amount): ((bucket if axis == "bucket" else seq) // amount) % 2
        for axis, amount in (X, Z0, Z1, CORE, Y)
    }


def partner(bit):
    bucket, seq = lax.axis_index("bucket"), lax.axis_index("seq")
    axis, amount = bit[:2]
    return (bucket ^ amount, seq) if axis == "bucket" else (bucket, seq ^ amount)


def peer_at(distance):
    bucket, seq = lax.axis_index("bucket"), lax.axis_index("seq")
    return bucket ^ (distance >> 2), seq ^ (distance & 3)


def greet(peers):
    barrier = pltpu.get_barrier_semaphore()
    for peer in peers:
        pl.semaphore_signal(barrier, inc=1, device_id=peer, device_id_type=MESH)
    pl.semaphore_wait(barrier, len(peers))


class Gathering:
    def __init__(self, own, out, layout, order, first, rows, send, recv, base):
        self.own, self.out, self.dims, self.order = own, out, DIMS[layout], order
        self.first, self.rows, self.send, self.recv, self.base = first, rows, send, recv, base
        self.me = my_coords()
        self.inner = self.me[Z0] != self.me[Z1]

    def view(self, free, flipped=None):
        index = tuple(
            slice(None)
            if dim in free
            else (1 - self.me[dim] if dim == flipped else self.me[dim])
            for dim in self.dims
        )
        return self.out.at[index + (pl.ds(self.first, self.rows), slice(None))]

    def copy(self, source, place, slot, bit):
        return pltpu.make_async_remote_copy(
            src_ref=source,
            dst_ref=place,
            send_sem=self.send.at[self.base + slot],
            recv_sem=self.recv.at[self.base + slot],
            device_id=partner(bit),
            device_id_type=MESH,
        )

    def dim(self, phase):
        return Z1 if self.order[phase] in (MIDDLE, FORWARD) else self.order[phase]

    def had(self, phase):
        return [self.dim(past) for past in range(phase) if self.order[past] != MIDDLE]

    def arrived(self, phase):
        return self.view(self.had(phase), self.dim(phase))

    def hop(self, phase):
        place = self.arrived(phase) if self.order[phase] == FORWARD else self.view(self.had(phase))
        source = self.own if phase == 0 else place
        return self.copy(source, place, phase, self.order[phase])

    def across(self, phase):
        if phase == 0:
            return self.copy(self.own, self.view(()), 5, CORE)
        place = self.arrived(phase - 1)
        return self.copy(place, place, 5 + phase, CORE)

    def keep(self):
        return pltpu.make_async_copy(self.own, self.view(()), self.send.at[self.base + 11])

    def begin(self):
        self.hop(0).start()
        self.across(0).start()
        self.keep().start()

    def sends(self, phase, act):
        if self.order[phase] in (MIDDLE, FORWARD):
            pl.when(self.inner)(act)
        else:
            act()

    def advance(self, phase):
        if phase == 0:
            self.keep().wait()
        kind = self.order[phase]
        if kind == MIDDLE:

            @pl.when(self.inner)
            def _():
                self.hop(phase).wait_recv()
                self.hop(phase + 1).start()

            return
        if kind == FORWARD:

            @pl.when(jnp.logical_not(self.inner))
            def _():
                self.hop(phase).wait_recv()

        else:
            self.hop(phase).wait_recv()
        if phase < 4:
            self.sends(phase + 1, lambda: self.hop(phase + 1).start())
        self.across(phase + 1).start()

    def collect(self):
        for phase in range(6):
            if phase == 0 or self.order[phase - 1] != MIDDLE:
                self.across(phase).wait_recv()

    def finish(self):
        for phase in range(5):
            self.sends(phase, lambda phase=phase: self.hop(phase).wait_send())
        for phase in range(6):
            if phase == 0 or self.order[phase - 1] != MIDDLE:
                self.across(phase).wait_send()


GATHER_SEMS = 12
SHARES = (32, 32, 32, 32, 16)
PAIR_PARTS = (
    (X, Z0, Y, MIDDLE, FORWARD),
    (Z0, MIDDLE, FORWARD, X, Y),
    (Z0, Y, MIDDLE, FORWARD, X),
    (Z0, MIDDLE, FORWARD, Y, X),
    (Z0, MIDDLE, FORWARD, Y, X),
)
UP_PARTS = (
    (Z0, X, Y, MIDDLE, FORWARD),
    (Z0, X, Y, MIDDLE, FORWARD),
    (Y, Z0, MIDDLE, FORWARD, X),
    (Y, Z0, MIDDLE, FORWARD, X),
    (Z0, X, MIDDLE, FORWARD, Y),
)
DOWN_PARTS = (
    (Z0, MIDDLE, FORWARD, Y, X),
    (Z0, Y, X, MIDDLE, FORWARD),
    (Z0, MIDDLE, FORWARD, Y, X),
    (Z0, X, Y, MIDDLE, FORWARD),
    (Z0, MIDDLE, FORWARD, X, Y),
)
BEGIN, PLANE, KV = -1, -2, -3
GATHER_STEPS = (
    (0, 0), (1, 0), (2, 0), (3, 0), (4, 0), (1, 1), (0, 1), (2, 1), (3, 1), (4, 1),
    (-1, 0), (1, 2), (3, 2), (0, 2), (2, 2), (4, 2), (7, 0), (5, 0), (8, 0), (6, 0),
    (9, 0), (1, 3), (10, 0), (11, 0), (5, 1), (3, 3), (12, 0), (13, 0), (14, 0), (6, 1),
    (4, 3), (9, 1), (0, 3), (2, 3), (10, 1), (7, 1), (12, 1), (14, 1), (8, 1), (1, 4),
    (3, 4), (9, 2), (11, 1), (13, 1), (7, 2), (5, 2), (4, 4), (0, 4), (8, 2), (10, 2),
    (6, 2), (12, 2), (14, 2), (13, 2), (9, 3), (2, 4), (-2, 0), (5, 3), (10, 3), (7, 3),
    (11, 2), (-2, 1), (14, 3), (12, 3), (-2, 2), (8, 3), (-2, 3), (-3, 0), (-3, 1), (-3, 2),
    (-3, 3), (6, 3), (9, 4), (10, 4), (14, 4), (5, 4), (13, 3), (7, 4), (6, 4), (11, 3),
    (12, 4), (13, 4), (8, 4), (11, 4),
)
NOTE, TAKE, ALL = -4, -5, -6
DOWN_SUM_PARTS = (
    (X, Z0, Z1, Y),
    (Y, X, Z0, Z1),
    (Z0, Y, Z1, X),
    (X, Z0, Z1, Y),
    (Y, Z0, Z1, X),
)
UP_SUM_PARTS = (
    (X, Z0, Y, Z1),
    (X, Y, Z0, Z1),
    (Y, X, Z0, Z1),
    (X, Y, Z0, Z1),
    (Z0, Y, X, Z1),
)
OUT_SHARES = (80, 64)
OUT_SUM_PARTS = (
    (X, Y, Z0, Z1),
    (Z0, Y, X, Z1),
)
PAIR_SUM_PARTS = (
    (Z0, Y, X, Z1),
    (X, Y, Z0, Z1),
    (X, Y, Z0, Z1),
    (X, Y, Z0, Z1),
    (X, Y, Z0, Z1),
)
SUM_STEPS = (
    (-3, 0), (-3, 1), (-3, 2), (-3, 3), (0, -1), (1, -1), (2, -1), (-5, 0), (3, -1), (4, -1),
    (5, -1), (6, -1), (7, -1), (-5, 1), (8, -1), (0, 0), (9, -1), (10, -1), (11, -1), (2, 0),
    (-5, 2), (0, 1), (3, 0), (9, 0), (-5, 3), (-2, 0), (-2, 1), (5, 0), (11, 0), (1, 0),
    (0, 2), (4, 0), (6, 0), (3, 1), (-6, 0), (-2, 2), (5, 1), (-2, 3), (4, 1), (7, 0),
    (8, 0), (12, -1), (13, -1), (14, -1), (15, -1), (16, -1), (3, 2), (2, 1), (-4, 0), (4, 2),
    (9, 1), (10, 0), (11, 1), (0, 3), (12, 0), (1, 1), (6, 1), (2, 2), (7, 1), (5, 2),
    (1, 2), (6, 2), (8, 1), (3, 3), (7, 2), (13, 0), (5, 3), (10, 1), (1, 3), (12, 1),
    (6, 3), (14, 0), (8, 2), (13, 1), (7, 3), (10, 2), (14, 1), (15, 0), (8, 3), (13, 2),
    (16, 0), (4, 3), (10, 3), (9, 2), (15, 1), (14, 2), (11, 2), (16, 1), (2, 3), (13, 3),
    (9, 3), (12, 2), (15, 2), (14, 3), (11, 3), (16, 2), (12, 3), (15, 3), (16, 3),
)
NOTE_STEP = 5
KV_PIECES = 4


def split_gatherings(block_ref, out_ref, layout, shares, orders, send, recv, base):
    moving, first = [], 0
    for index, (count, order) in enumerate(zip(shares, orders)):
        own = block_ref.at[pl.ds(first, count), :]
        slot = base + GATHER_SEMS * index
        moving.append(Gathering(own, out_ref, layout, order, first, count, send, recv, slot))
        first += count
    return moving


def kv_needed(piece, act):
    place = my_coords()
    quarter = KV_PIECES // 2
    last = jnp.logical_and(place[Y] == 1, place[CORE] == 1)
    first = jnp.logical_and(place[Y] == 0, place[CORE] == 0)
    skipped = first if piece < quarter else last
    pl.when(jnp.logical_not(skipped))(act)


def kv_expected(piece, act):
    place = my_coords()
    quarter = KV_PIECES // 2
    last = jnp.logical_and(place[Y] == 0, place[CORE] == 1)
    first = jnp.logical_and(place[Y] == 1, place[CORE] == 0)
    skipped = first if piece < quarter else last
    pl.when(jnp.logical_not(skipped))(act)


def kv_relayed(piece, act):
    place = my_coords()
    quarter = KV_PIECES // 2
    last = jnp.logical_and(place[Y] == 0, place[CORE] == 0)
    first = jnp.logical_and(place[Y] == 1, place[CORE] == 1)
    skipped = first if piece < quarter else last
    pl.when(jnp.logical_not(skipped))(act)


def gather_kernel(
    cond_ref,
    table_ref,
    ada_ref,
    qkv_master,
    out_master,
    up_master,
    cut_ref,
    x_ref,
    pair_out,
    up_out,
    down_out,
    kv_out,
    silu_ref,
    mod_ref,
    bias_ref,
    a_ref,
    q_ref,
    note_ref,
    pair_ref,
    up_ref,
    down_ref,
    cuts,
    inbox,
    parts,
    returns,
    row,
    weights,
    acc,
    kv,
    note_send,
    note_recv,
    mod_send,
    mod_recv,
    cut_send,
    cut_recv,
    weight_sem,
    send,
    recv,
):
    bucket, seq = lax.axis_index("bucket"), lax.axis_index("seq")
    place = my_coords()
    me = bucket * PLANES + seq
    count = BLOCKS * PLANES
    barrier = pltpu.get_barrier_semaphore()

    @pl.loop(1, count)
    def _(distance):
        pl.semaphore_signal(barrier, inc=1, device_id=peer_at(distance), device_id_type=MESH)

    rows, width = ada_ref.shape[0], x_ref.shape[1]
    cols = 3 * width // PLANES
    pair_ref[:, :cols] = qkv_master[...].astype(bfloat)
    pair_ref[:, cols:] = out_master[...].astype(bfloat)
    up_ref[...] = up_master[...].astype(bfloat)
    note_ref[...] = jnp.zeros_like(note_ref)
    for index in range(BLOCKS):
        start = index * rows
        note_ref[index, : NOTE_ROWS - 2, : table_ref.shape[1]] = table_ref[...]
        note_ref[index, NOTE_ROWS - 2 : NOTE_ROWS - 1, :] = cond_ref[:, start : start + LANES]
        note_ref[index, NOTE_ROWS - 1 :, : rows - LANES] = cond_ref[
            :, start + LANES : start + rows
        ]
    pl.semaphore_wait(barrier, count - 1)

    def cut(distance):
        return pltpu.make_async_remote_copy(
            src_ref=cut_ref.at[seq ^ distance],
            dst_ref=cuts.at[seq],
            send_sem=cut_send.at[distance],
            recv_sem=cut_recv.at[distance],
            device_id=(bucket, seq ^ distance),
            device_id_type=MESH,
        )

    def note(distance):
        peer = peer_at(distance)
        return pltpu.make_async_remote_copy(
            src_ref=note_ref.at[peer[0]],
            dst_ref=inbox.at[me],
            send_sem=note_send.at[distance],
            recv_sem=note_recv.at[distance],
            device_id=peer,
            device_id_type=MESH,
        )

    def answer(distance):
        peer = peer_at(distance)
        return pltpu.make_async_remote_copy(
            src_ref=parts.at[peer[0]],
            dst_ref=returns.at[me],
            send_sem=mod_send.at[distance],
            recv_sem=mod_recv.at[distance],
            device_id=peer,
            device_id_type=MESH,
        )

    @pl.loop(1, count)
    def _(distance):
        note(distance).start()

    inbox[me] = note_ref[bucket]
    cuts[seq] = cut_ref[seq]
    base = len(PAIR_PARTS) * GATHER_SEMS
    pairs = split_gatherings(pair_ref, pair_out, "planes", SHARES, PAIR_PARTS, send, recv, 0)
    rest = split_gatherings(up_ref, up_out, "planes", SHARES, UP_PARTS, send, recv, base)
    base += len(UP_PARTS) * GATHER_SEMS
    rest += split_gatherings(down_ref, down_out, "rows", SHARES, DOWN_PARTS, send, recv, base)
    base += len(DOWN_PARTS) * GATHER_SEMS
    moving = pairs + rest
    for part in pairs:
        part.begin()
    for distance in range(1, PLANES):
        cut(distance).start()

    local = x_ref.shape[0] // KV_PIECES

    def kv_copy(source, target, slot, bit):
        return pltpu.make_async_remote_copy(
            src_ref=source,
            dst_ref=target,
            send_sem=send.at[base + slot],
            recv_sem=recv.at[base + slot],
            device_id=partner(bit),
            device_id_type=MESH,
        )

    def kv_step(piece, kind):
        span = pl.ds(piece * local, local)
        mine = kv_out.at[place[Y], place[CORE], span, :]
        other = kv_out.at[1 - place[Y], place[CORE], span, :]
        if kind == "over":
            return kv_copy(kv.at[span, :], mine, 4 * piece, Y)
        if kind == "near":
            return kv_copy(kv.at[span, :], mine, 4 * piece + 1, CORE)
        if kind == "far":
            return kv_copy(other, other, 4 * piece + 2, CORE)
        return pltpu.make_async_copy(kv.at[span, :], mine, send.at[base + 4 * piece + 3])

    def load(plane):
        source = pair_out.at[plane // 2, plane % 2, :, :, :, :, pl.ds(0, weights.shape[5])]
        return pltpu.make_async_copy(source, weights.at[plane % 2], weight_sem.at[plane % 2])

    def modulations():
        @pl.loop(1, count)
        def _(distance):
            note(distance).wait_recv()

        head = jnp.concatenate(
            [inbox[PLANES * g, NOTE_ROWS - 2 : NOTE_ROWS - 1, :] for g in range(BLOCKS)]
        )
        tail = jnp.concatenate(
            [inbox[PLANES * g, NOTE_ROWS - 1 : NOTE_ROWS, :] for g in range(BLOCKS)]
        )
        head, tail = jax.nn.silu(head).astype(bfloat), jax.nn.silu(tail).astype(bfloat)
        silu_ref[:, :LANES] = head
        silu_ref[:, LANES:] = tail
        mods = dot_nn(head, ada_ref[:LANES, :].astype(bfloat)) + dot_nn(
            tail[:, : rows - LANES], ada_ref[LANES:, :].astype(bfloat)
        )
        for group in range(BLOCKS):
            parts[group] = mods[group : group + 1, :]
        returns[me] = parts[bucket]

        @pl.loop(1, count)
        def _(distance):
            answer(distance).start()

    def biases():
        each = width // count
        for device in range(count):
            heard = inbox[device].astype(bfloat).astype(single)
            bias_ref[:, device * each : (device + 1) * each] = heard[:, :each]

    def projection(plane):
        if plane == 0:
            for part in pairs:
                part.collect()
            load(0).start()
            load(1).start()

            @pl.loop(1, count)
            def _(distance):
                answer(distance).wait_recv()

            for index in range(PLANES):
                wide = returns.shape[2]
                row[:, index * wide : (index + 1) * wide] = sum(
                    returns[PLANES * g + index] for g in range(BLOCKS)
                )
            for index in range(6):
                mod_ref[index : index + 1, :] = (
                    row[:, index * width : (index + 1) * width] + bias_ref[index : index + 1, :]
                )
            a_ref[...] = modulate(
                x_ref[...].astype(single), mod_ref[0:1, :], mod_ref[1:2, :]
            ).astype(bfloat)
        load(plane).wait()
        weight = weights[plane % 2].reshape(width, weights.shape[5])
        acc[:, plane * cols : (plane + 1) * cols] = dot_nn(a_ref[...], weight)[:, :cols]
        if plane + 2 < PLANES:
            load(plane + 2).start()
        if plane == PLANES - 1:
            q_ref[...] = (acc[:, :width] + bias_ref[6:7, :]).astype(bfloat)
            kv[:, :width] = acc[:, width : 2 * width].astype(bfloat)
            kv[:, width:] = (acc[:, 2 * width :] + bias_ref[7:8, :]).astype(bfloat)

    for step, (part, phase) in enumerate(GATHER_STEPS):
        if step == NOTE_STEP:
            modulations()
            biases()
        if part == BEGIN:
            for distance in range(1, PLANES):
                cut(distance).wait_recv()
            for index in range(PLANES):
                each = cuts.shape[2]
                down_ref[:, index * each : (index + 1) * each] = cuts[index]
            for moved in rest:
                moved.begin()
        elif part == PLANE:
            projection(phase)
        elif part == KV:
            kv_needed(phase, lambda: kv_step(phase, "over").start())
            for kind in ("near", "keep"):
                kv_step(phase, kind).start()
        else:
            moving[part].advance(phase)
    def relay(piece):
        kv_step(piece, "over").wait_recv()
        kv_step(piece, "far").start()

    for piece in range(KV_PIECES):
        kv_expected(piece, functools.partial(relay, piece))
    for part in rest:
        part.collect()
    for part in moving:
        part.finish()
    for piece in range(KV_PIECES):
        kv_step(piece, "near").wait_recv()
        kv_relayed(piece, lambda piece=piece: kv_step(piece, "far").wait_recv())
        kv_step(piece, "keep").wait()
        kv_step(piece, "near").wait_send()
        kv_needed(piece, lambda piece=piece: kv_step(piece, "over").wait_send())
        kv_expected(piece, lambda piece=piece: kv_step(piece, "far").wait_send())

    for distance in range(1, PLANES):
        cut(distance).wait_send()

    @pl.loop(1, count)
    def _(distance):
        note(distance).wait_send()
        answer(distance).wait_send()


NOTE_ROWS = 16


def gather(condition, table, ada_master, qkv_master, out_master, up_master, cut, tokens):
    rows, width = up_master.shape
    local = tokens.shape[0]
    count = BLOCKS * PLANES
    cols = ada_master.shape[1]
    block = pltpu.VMEM((rows, width), bfloat)
    wide = -(-3 * width // PLANES // LANES) * LANES
    blocks = jax.ShapeDtypeStruct((2, 2, 2, 2, 2, rows, width), bfloat)
    sems = 3 * len(SHARES) * GATHER_SEMS + 4 * KV_PIECES
    pair, up, down, kv, silu, mods, biases, first_in, query = pl.pallas_call(
        gather_kernel,
        out_shape=(
            blocks,
            blocks,
            blocks,
            jax.ShapeDtypeStruct((2, 2, local, 2 * width), bfloat),
            jax.ShapeDtypeStruct((BLOCKS, 2 * LANES), bfloat),
            jax.ShapeDtypeStruct((8, width), single),
            jax.ShapeDtypeStruct((NOTE_ROWS, width), single),
            jax.ShapeDtypeStruct((local, width), bfloat),
            jax.ShapeDtypeStruct((local, width), bfloat),
        ),
        in_specs=[IN_VMEM] * 8,
        out_specs=(IN_HBM,) * 4 + (IN_VMEM,) * 5,
        scratch_shapes=[
            pltpu.VMEM((BLOCKS, NOTE_ROWS, LANES), single),
            block,
            block,
            block,
            pltpu.VMEM(cut.shape, bfloat),
            pltpu.VMEM((count, NOTE_ROWS, LANES), single),
            pltpu.VMEM((BLOCKS, 1, cols), single),
            pltpu.VMEM((count, 1, cols), single),
            pltpu.VMEM((1, 6 * width), single),
            pltpu.VMEM((2, 2, 2, 2, rows, wide), bfloat),
            pltpu.VMEM((local, 3 * width), single),
            pltpu.VMEM((local, 2 * width), bfloat),
        ]
        + [pltpu.SemaphoreType.DMA((count,))] * 4
        + [pltpu.SemaphoreType.DMA((PLANES,))] * 2
        + [pltpu.SemaphoreType.DMA((2,))]
        + [pltpu.SemaphoreType.DMA((sems,))] * 2,
        compiler_params=pltpu.CompilerParams(
            collective_id=1, has_side_effects=True, vmem_limit_bytes=VMEM_LIMIT
        ),
        cost_estimate=cost(6 * local * width * width, 200 * rows * width),
        name="gather",
    )(condition, table, ada_master, qkv_master, out_master, up_master, cut, tokens)
    tall = BLOCKS * rows
    return (
        pair.reshape(PLANES, tall, width),
        up.reshape(PLANES, tall, width),
        down.reshape(PLANES * tall, width),
        kv.reshape(PLANES * local, 2 * width),
        silu[:, :rows],
        mods,
        biases,
        first_in,
        query,
    )


def slot_of(bucket_bits, seq_bits):
    slot = 0
    for axis, amount in SLOT_DIMS:
        bits = bucket_bits if axis == "bucket" else seq_bits
        slot = slot * 2 + ((bits >> amount.bit_length() - 1) & 1)
    return slot


def natural_sum(far, near, layout):
    width = far.shape[2]
    both = jnp.concatenate([near, far])
    index = {
        (b, s): slot_of(b, s) + near.shape[0] * (s % 2)
        for b in range(BLOCKS)
        for s in range(PLANES)
    }
    if layout == "rows":
        picked = [index[b, s] for b in range(BLOCKS) for s in range(PLANES)]
        gradient = jnp.stack([both[k] for k in picked]).reshape(-1, width)
        part = lax.psum_scatter(gradient, ("bucket", "seq"), scatter_dimension=0, tiled=True)
        return part.astype(single)
    picked = [index[b, s] for s in range(PLANES) for b in range(BLOCKS)]
    gradient = jnp.stack([both[k] for k in picked]).reshape(PLANES, -1, width)
    part = lax.psum_scatter(gradient, "seq", scatter_dimension=0)
    return lax.psum_scatter(part, "bucket", scatter_dimension=0, tiled=True).astype(single)


SLOT_DIMS = (Y, X, Z1, Z0)


class Scattering:
    def __init__(self, far, near, total, arrivals, out, order, first, rows, send, recv, base):
        self.far, self.near, self.total, self.arrivals = far, near, total, arrivals
        self.out, self.order, self.first, self.rows = out, order, first, rows
        self.send, self.recv, self.base = send, recv, base
        self.span = (pl.ds(first, rows), slice(None))
        self.near_span = None

    def copy(self, source, place, slot, bit):
        return pltpu.make_async_remote_copy(
            src_ref=source,
            dst_ref=place,
            send_sem=self.send.at[self.base + slot],
            recv_sem=self.recv.at[self.base + slot],
            device_id=partner(bit),
            device_id_type=MESH,
        )

    def across(self):
        index = (slice(None),) * 4 + self.span
        return self.copy(self.far.at[index], self.total.at[index], 4, CORE)

    def place(self, fixed):
        return tuple(fixed.get(dim, slice(None)) for dim in SLOT_DIMS)

    def hop(self, phase):
        fixed = {dim: 0 for dim in self.order[:phase]} | {self.order[phase]: 1}
        source = self.total.at[self.place(fixed) + self.span]
        place = self.arrivals[phase].at[(slice(None),) * (3 - phase) + self.span]
        return self.copy(source, place, phase, self.order[phase])

    def add(self, fixed, source, source_dims, source_span=None):
        free = [dim for dim in SLOT_DIMS if dim not in fixed]

        def one(step):
            index = dict(fixed)
            for place, dim in enumerate(free):
                index[dim] = (step >> place) & 1
            spot = tuple(index[dim] for dim in SLOT_DIMS) + self.span
            term = source[tuple(index[dim] for dim in source_dims) + (source_span or self.span)]
            self.total[spot] = (self.total[spot].astype(single) + term.astype(single)).astype(
                bfloat
            )

        if free:
            pl.loop(0, 2 ** len(free))(one)
        else:
            one(0)

    def advance(self, phase):
        span = None
        if phase < 0 and self.near is None:
            self.hop(0).start()
            return
        if phase < 0:
            self.across().wait_recv()
            source, dims, fixed, span = self.near, SLOT_DIMS, {}, self.near_span
        else:
            self.hop(phase).wait_recv()
            done = self.order[: phase + 1]
            dims = tuple(dim for dim in SLOT_DIMS if dim not in done)
            source, fixed = self.arrivals[phase], {dim: 0 for dim in done}
        if phase == 3:
            spot = (0,) * 4 + self.span
            self.out[self.span] = self.total[spot].astype(single) + source[self.span].astype(
                single
            )
            return
        ahead = self.order[phase + 1]
        self.add(fixed | {ahead: 1}, source, dims, span)
        self.hop(phase + 1).start()
        self.add(fixed | {ahead: 0}, source, dims, span)

    def finish(self):
        self.across().wait_send()
        for phase in range(4):
            self.hop(phase).wait_send()


SCATTER_SEMS = 5


def scatter_scratch(rows, width):
    return [
        pltpu.VMEM((2,) * free + (rows, width), bfloat) for free in (4, 3, 2, 1, 0)
    ]


def split_scatterings(far, near, scratch, out, shares, orders, send, recv, base):
    moving, first = [], 0
    for index, (count, order) in enumerate(zip(shares, orders)):
        slot = base + SCATTER_SEMS * index
        moving.append(
            Scattering(
                far, near, scratch[0], scratch[1:], out, order, first, count, send, recv, slot
            )
        )
        first += count
    return moving


def norm_back(values, grad, scale_row):
    centre = values - jnp.mean(values, axis=-1, keepdims=True)
    root = lax.rsqrt(jnp.mean(centre * centre, axis=-1, keepdims=True) + EPSILON)
    normed = centre * root
    scaled = grad * (1.0 + scale_row)
    inner = jnp.mean(scaled * normed, axis=-1, keepdims=True)
    return root * (scaled - jnp.mean(scaled, axis=-1, keepdims=True) - normed * inner), normed


def column_sum(values):
    return jnp.sum(values, axis=0, keepdims=True)


def scatter_kernel(
    kv_far,
    kv_near,
    down_far,
    down_near,
    up_far,
    up_near,
    wo_far,
    w_ref,
    x_ref,
    dmid_ref,
    wo_near,
    a_ref,
    dq_ref,
    mod_ref,
    row_ref,
    ada_ref,
    up_out,
    wo_sum,
    pair_out,
    grad_ref,
    mods_ref,
    bias_ref,
    silu_ref,
    cuts,
    far,
    *refs,
):
    down_scratch, up_scratch, refs = refs[:5], refs[5:10], refs[10:]
    wo_scratch, pair_scratch, refs = refs[:5], refs[5:10], refs[10:]
    kv_total, kv_arrival, kv_stage, stage, down_sum, cut_ref, plane_stage, refs = refs[:7] + (refs[7:],)
    x_tile, dmid_tile, weights, dy, table, line, bias_notes, mod_notes, bias_box, mod_box = refs[:10]
    parts, returns, cut_send, cut_recv, local_sem, far_sem = refs[10:16]
    bias_send, bias_recv, mod_send, mod_recv, back_send, back_recv, send, recv = refs[16:]
    bucket, seq = lax.axis_index("bucket"), lax.axis_index("seq")
    me = bucket * PLANES + seq
    count = BLOCKS * PLANES
    barrier = pltpu.get_barrier_semaphore()

    @pl.loop(1, count)
    def _(distance):
        pl.semaphore_signal(barrier, inc=1, device_id=peer_at(distance), device_id_type=MESH)

    pl.semaphore_wait(barrier, count - 1)

    def message(source, target, out_sem, in_sem, distance):
        return pltpu.make_async_remote_copy(
            src_ref=source,
            dst_ref=target,
            send_sem=out_sem.at[distance],
            recv_sem=in_sem.at[distance],
            device_id=peer_at(distance),
            device_id_type=MESH,
        )

    def bias_note(distance):
        peer = peer_at(distance)
        source = bias_notes.at[peer[0] * PLANES + peer[1]]
        return message(source, bias_box.at[me], bias_send, bias_recv, distance)

    def mod_note(distance):
        source = mod_notes.at[peer_at(distance)[1]]
        return message(source, mod_box.at[me], mod_send, mod_recv, distance)

    def answer(distance):
        source = parts.at[peer_at(distance)[0]]
        return message(source, returns.at[me], back_send, back_recv, distance)

    place = my_coords()
    base = 0

    def streams(far_ref, near_ref, scratch, out, shares, orders):
        nonlocal base
        start, base = base, base + len(orders) * SCATTER_SEMS
        return split_scatterings(far_ref, near_ref, scratch, out, shares, orders, send, recv, start)

    downs = streams(down_far, down_near, down_scratch, down_sum, SHARES, DOWN_SUM_PARTS)
    ups = streams(up_far, up_near, up_scratch, up_out, SHARES, UP_SUM_PARTS)
    wos = streams(wo_far, wo_near, wo_scratch, wo_sum, OUT_SHARES, OUT_SUM_PARTS)
    pairs = streams(far, None, pair_scratch, pair_out, SHARES, PAIR_SUM_PARTS)
    moving = downs + ups + wos + pairs
    piece_rows = kv_arrival.shape[0] // KV_PIECES

    def kv_copy(source, target, slot, bit):
        return pltpu.make_async_remote_copy(
            src_ref=source,
            dst_ref=target,
            send_sem=send.at[base + slot],
            recv_sem=recv.at[base + slot],
            device_id=partner(bit),
            device_id_type=MESH,
        )

    def kv_span(piece):
        return pl.ds(piece * piece_rows, piece_rows)

    def near_kv(piece):
        span = kv_span(piece)
        return kv_copy(kv_far.at[:, span, :], kv_total.at[:, span, :], 2 * piece, CORE)

    def over(piece):
        span = kv_span(piece)
        return kv_copy(kv_total.at[1, span, :], kv_arrival.at[span, :], 2 * piece + 1, Y)

    def kv_load(piece):
        return pltpu.make_async_copy(
            kv_near.at[:, kv_span(piece), :], kv_stage, local_sem.at[2]
        )

    def kv_add(piece, side):
        span = kv_span(piece)
        kv_total[side, span, :] = (
            kv_total[side, span, :].astype(single) + kv_stage[side].astype(single)
        ).astype(bfloat)

    def pass_over(piece):
        kv_add(piece, 1)
        over(piece).start()

    def take(piece):
        over(piece).wait_recv()
        span = kv_span(piece)
        kv_total[0, span, :] = (
            kv_total[0, span, :].astype(single) + kv_arrival[span, :].astype(single)
        ).astype(bfloat)

    staged = [part for part, phase in SUM_STEPS if phase < 0 and 0 <= part < len(downs + ups)]

    def stage_load(turn):
        part = moving[staged[turn]]
        spot = (slice(None),) * 4
        return pltpu.make_async_copy(
            part.near.at[spot + part.span],
            stage.at[(turn % 2,) + spot + (pl.ds(0, part.rows), slice(None))],
            local_sem.at[turn % 2],
        )

    kv_load(0).start()
    for piece in range(KV_PIECES):
        near_kv(piece).start()
    for part in downs + ups + wos:
        part.across().start()
    for turn in range(2):
        stage_load(turn).start()

    def cut(distance):
        return pltpu.make_async_remote_copy(
            src_ref=cut_ref.at[seq ^ distance],
            dst_ref=cuts.at[seq],
            send_sem=cut_send.at[distance],
            recv_sem=cut_recv.at[distance],
            device_id=(bucket, seq ^ distance),
            device_id_type=MESH,
        )

    def cut_down():
        for index in range(PLANES):
            each = cuts.shape[2]
            cut_ref[index] = down_sum[:, index * each : (index + 1) * each].astype(bfloat)
        cuts[seq] = cut_ref[seq]
        for distance in range(1, PLANES):
            cut(distance).start()

    local, width = dq_ref.shape
    rows = up_out.shape[0]
    cols = 3 * width // PLANES
    wide = dy.shape[1]
    order = (1, 3, 0, 2)

    def load(step):
        plane = seq ^ order[step]
        return pltpu.make_async_copy(
            w_ref.at[plane, :, pl.ds(0, wide)], weights, local_sem.at[3]
        )

    def gather_dy(index):
        low, high = index * cols, (index + 1) * cols
        pieces = []
        if low < width:
            pieces.append(dq_ref[:, low : min(high, width)])
        if high > width:
            pieces.append(kv_total[0, :, max(low - width, 0) : high - width])
        first = 0
        for piece in pieces:
            dy[:, first : first + piece.shape[1]] = piece
            first += piece.shape[1]

    def block_spot(block, bits):
        return (
            bits // 2,
            (block % 2) ^ place[X],
            (block // 4) ^ place[Z1],
            (block // 2 % 2) ^ place[Z0],
        )

    def far_copy(block, bits):
        return pltpu.make_async_copy(
            plane_stage.at[pl.ds(block * rows, rows), :],
            far.at[block_spot(block, bits)],
            far_sem.at[block],
        )

    def project(step):
        bits = order[step]
        plane = seq ^ bits
        if step == 0:
            load(0).start()
            dy[:, cols:] = jnp.zeros((local, wide - cols), bfloat)
            grad_ref[...] = jnp.zeros_like(grad_ref)
        for index in range(PLANES):

            @pl.when(plane == index)
            def _():
                gather_dy(index)

        if step == 1:
            for block in range(BLOCKS):
                far_copy(block, order[0]).wait()
        total = pair_scratch[0]
        for low, high in ((0, 4 * LANES), (4 * LANES, wide)):
            values = dot_tn(a_ref[...], dy[:, low:high])
            if step < 2:
                plane_stage[:, low:high] = values.astype(bfloat)
                continue
            for block in range(BLOCKS):
                spot = block_spot(block, bits) + (slice(None), slice(low, high))
                value = values[block * rows : (block + 1) * rows, :]
                total[spot] = (total[spot].astype(single) + value).astype(bfloat)
        if step < 2:
            for block in range(BLOCKS):
                far_copy(block, bits).start()
        load(step).wait()
        grad_ref[...] += dot_nt(dy[...], weights[...])
        if step + 1 < PLANES:
            load(step + 1).start()
        if step == 1:
            for block in range(BLOCKS):
                far_copy(block, bits).wait()
            for part in pairs:
                part.across().start()

    def tile_loads(tile):
        span = pl.ds(tile * LANES, LANES)
        return (
            pltpu.make_async_copy(x_ref.at[span, :], x_tile.at[tile % 2], far_sem.at[tile % 2]),
            pltpu.make_async_copy(
                dmid_ref.at[span, :], dmid_tile.at[tile % 2], far_sem.at[2 + tile % 2]
            ),
        )

    def notes():
        shift_sum, scale_sum = jnp.zeros((1, width), single), jnp.zeros((1, width), single)
        scale_row = mod_ref[1:2, :]
        tiles = local // LANES
        for copy in tile_loads(0):
            copy.start()
        for tile in range(tiles):
            if tile + 1 < tiles:
                for copy in tile_loads(tile + 1):
                    copy.start()
            for copy in tile_loads(tile):
                copy.wait()
            span = slice(tile * LANES, (tile + 1) * LANES)
            grad = grad_ref[span, :]
            back, normed = norm_back(x_tile[tile % 2].astype(single), grad, scale_row)
            shift_sum += column_sum(grad)
            scale_sum += column_sum(grad * normed)
            grad_ref[span, :] = dmid_tile[tile % 2] + back
        table[...] = jnp.zeros_like(table)
        line[:, :width] = shift_sum
        line[:, width : 2 * width] = scale_sum
        table[0:1, :width] = shift_sum
        table[1:2, :width] = scale_sum
        for index in range(4):
            line[:, (2 + index) * width : (3 + index) * width] = row_ref[index : index + 1, :]
        table[2:6, :width] = row_ref[0:4, :]
        table[6:7, :width] = column_sum(dq_ref[...].astype(single))
        table[7:8, :width] = column_sum(kv_total[0, :, width:].astype(single))
        table[8:14, :width] = row_ref[4:10, :]
        each = width // count
        for device in range(count):
            bias_notes[device] = table[:, device * each : device * each + LANES]

        part = mod_notes.shape[2]
        for index in range(PLANES):
            mod_notes[index] = line[:, index * part : (index + 1) * part]
        bias_box[me] = bias_notes[me]
        mod_box[me] = mod_notes[seq]

        @pl.loop(1, count)
        def _(distance):
            mod_note(distance).start()
            bias_note(distance).start()

    def answers():
        @pl.loop(1, count)
        def _(distance):
            mod_note(distance).wait_recv()

        sums = [sum(mod_box[PLANES * g + s] for s in range(PLANES)) for g in range(BLOCKS)]
        mods = jnp.concatenate(sums)
        mods_ref[...] = mods
        silu = lax.dot_general(
            mods,
            ada_ref[...].astype(bfloat).astype(single),
            (((1,), (1,)), ((), ())),
            preferred_element_type=single,
            precision=HIGHEST,
        )
        for group in range(BLOCKS):
            parts[group, :, :rows] = silu[group : group + 1, :]
            parts[group, :, rows:] = jnp.zeros((1, parts.shape[2] - rows), single)
        returns[me] = parts[bucket]

        @pl.loop(1, count)
        def _(distance):
            answer(distance).start()

    since, turn, left = 0, 0, len(downs)
    for part, phase in SUM_STEPS:
        if part == KV:
            near_kv(phase).wait_recv()
            kv_load(phase).wait()
            kv_expected(phase, functools.partial(pass_over, phase))
            kv_add(phase, 0)
            if phase + 1 < KV_PIECES:
                kv_load(phase + 1).start()
        elif part == TAKE:
            kv_needed(phase, functools.partial(take, phase))
        elif part == ALL:
            for moved in pairs:
                moved.across().wait_recv()
        elif part == PLANE:
            project(phase)
        elif part == NOTE:
            notes()
            since = 1
        else:
            mover = moving[part]
            if phase < 0 and part < len(downs + ups):
                stage_load(turn).wait()
                mover.near = stage.at[turn % 2]
                mover.near_span = (pl.ds(0, mover.rows), slice(None))
                mover.advance(phase)
                if turn + 2 < len(staged):
                    stage_load(turn + 2).start()
                turn += 1
            else:
                mover.advance(phase)
            if part < len(downs) and phase == 3:
                left -= 1
                if left == 0:
                    cut_down()
            since += since > 0
            if since == ANSWER_AFTER:
                answers()

    @pl.loop(1, count)
    def _(distance):
        bias_note(distance).wait_recv()

    bias_ref[...] = jnp.zeros_like(bias_ref)

    @pl.loop(0, count)
    def _(device):
        bias_ref[...] += bias_box[device]

    @pl.loop(1, count)
    def _(distance):
        answer(distance).wait_recv()

    for group in range(BLOCKS):
        silu_ref[group] = sum(returns[PLANES * group + s] for s in range(PLANES))
    for part in moving:
        part.finish()
    for piece in range(KV_PIECES):
        near_kv(piece).wait_send()
        kv_expected(piece, lambda piece=piece: over(piece).wait_send())
    for distance in range(1, PLANES):
        cut(distance).wait_recv()
        cut(distance).wait_send()

    @pl.loop(1, count)
    def _(distance):
        bias_note(distance).wait_send()
        mod_note(distance).wait_send()
        answer(distance).wait_send()


ANSWER_AFTER = 12


def scatter(
    kv_far,
    kv_near,
    down_far,
    down_near,
    up_far,
    up_near,
    wo_far,
    wo_near,
    first_in,
    query_grad,
    weight,
    tokens,
    middle_grad,
    mods,
    row_grads,
    ada_master,
):
    rows, width = up_far.shape[1:]
    edge = wo_far.shape[2]
    count = BLOCKS * PLANES
    cols = ada_master.shape[1]
    cuts = (PLANES, rows, width // PLANES)
    local, kv_wide = kv_far.shape[1:]
    wide = -(-3 * width // PLANES // LANES) * LANES
    cube, wo_cube = (2, 2, 2, 2, rows, width), (2, 2, 2, 2, rows, edge)
    sems = (3 * len(SHARES) + len(OUT_SHARES)) * SCATTER_SEMS + 2 * KV_PIECES
    return pl.pallas_call(
        scatter_kernel,
        out_shape=(
            jax.ShapeDtypeStruct((rows, width), single),
            jax.ShapeDtypeStruct((rows, edge), single),
            jax.ShapeDtypeStruct((rows, wide), single),
            jax.ShapeDtypeStruct((local, width), single),
            jax.ShapeDtypeStruct((BLOCKS, cols), single),
            jax.ShapeDtypeStruct((NOTE_ROWS, LANES), single),
            jax.ShapeDtypeStruct((BLOCKS, 1, 2 * LANES), single),
            jax.ShapeDtypeStruct(cuts, bfloat),
            jax.ShapeDtypeStruct((2, 2, 2, 2, rows, wide), bfloat),
        ),
        in_specs=[IN_HBM] * 10 + [IN_VMEM] * 6,
        out_specs=(IN_VMEM,) * 8 + (IN_HBM,),
        scratch_shapes=scatter_scratch(rows, width)
        + scatter_scratch(rows, width)
        + scatter_scratch(rows, edge)
        + scatter_scratch(rows, wide)
        + [
            pltpu.VMEM((2, local, kv_wide), bfloat),
            pltpu.VMEM((local, kv_wide), bfloat),
            pltpu.VMEM((2, local // KV_PIECES, kv_wide), bfloat),
            pltpu.VMEM((2, 2, 2, 2, 2, max(SHARES), width), bfloat),
            pltpu.VMEM((rows, width), single),
            pltpu.VMEM(cuts, bfloat),
            pltpu.VMEM((width, wide), bfloat),
            pltpu.VMEM((2, LANES, width), bfloat),
            pltpu.VMEM((2, LANES, width), single),
            pltpu.VMEM((width, wide), bfloat),
            pltpu.VMEM((local, wide), bfloat),
            pltpu.VMEM((NOTE_ROWS, width + LANES), single),
            pltpu.VMEM((1, 6 * width), single),
            pltpu.VMEM((count, NOTE_ROWS, LANES), single),
            pltpu.VMEM((PLANES, 1, cols), single),
            pltpu.VMEM((count, NOTE_ROWS, LANES), single),
            pltpu.VMEM((count, 1, cols), single),
            pltpu.VMEM((BLOCKS, 1, 2 * LANES), single),
            pltpu.VMEM((count, 1, 2 * LANES), single),
            pltpu.SemaphoreType.DMA((PLANES,)),
            pltpu.SemaphoreType.DMA((PLANES,)),
            pltpu.SemaphoreType.DMA((4,)),
            pltpu.SemaphoreType.DMA((BLOCKS,)),
        ]
        + [pltpu.SemaphoreType.DMA((count,))] * 6
        + [pltpu.SemaphoreType.DMA((sems,))] * 2,
        compiler_params=pltpu.CompilerParams(
            collective_id=4, has_side_effects=True, vmem_limit_bytes=63 * 1024 * 1024
        ),
        cost_estimate=cost(12 * local * width * width, 300 * rows * width),
        name="scatter",
    )(
        kv_far,
        kv_near,
        down_far.reshape(cube),
        down_near.reshape(cube),
        up_far.reshape(cube),
        up_near.reshape(cube),
        wo_far.reshape(wo_cube),
        weight,
        tokens,
        middle_grad,
        wo_near.reshape(wo_cube),
        first_in,
        query_grad,
        mods,
        row_grads,
        ada_master,
    )


def whole(shape):
    return pl.BlockSpec(shape, lambda *_: (0,) * len(shape))


def qkv_kernel(cols, x_ref, shift_ref, scale_ref, bias_ref, w_ref, a_ref, q_ref, kv_ref, acc):
    step = pl.program_id(0)
    width = x_ref.shape[1]

    @pl.when(step == 0)
    def _():
        values = x_ref[...].astype(single)
        a_ref[...] = modulate(values, shift_ref[...], scale_ref[...]).astype(bfloat)

    wide = -(-cols // LANES) * LANES
    part = dot_nn(a_ref[...], w_ref[0, :, :wide])[:, :cols]
    for index in range(PLANES):

        @pl.when(step == index)
        def _():
            acc[:, index * cols : (index + 1) * cols] = part

    @pl.when(step == PLANES - 1)
    def _():
        q_ref[...] = (acc[:, :width] + bias_ref[:, :width]).astype(bfloat)
        kv_ref[...] = (acc[:, width:] + bias_ref[:, width:]).astype(bfloat)


def project_qkv(tokens, shift_row, scale_row, bias_row, weight):
    rows, width = tokens.shape
    cols = 3 * width // PLANES
    return pl.pallas_call(
        functools.partial(qkv_kernel, cols),
        grid=(PLANES,),
        out_shape=(
            jax.ShapeDtypeStruct((rows, width), bfloat),
            jax.ShapeDtypeStruct((rows, width), bfloat),
            jax.ShapeDtypeStruct((rows, 2 * width), bfloat),
        ),
        in_specs=[
            whole((rows, width)),
            whole((1, width)),
            whole((1, width)),
            whole((1, 3 * width)),
            pl.BlockSpec((1,) + weight.shape[1:], lambda s: (s, 0, 0)),
        ],
        out_specs=(whole((rows, width)), whole((rows, width)), whole((rows, 2 * width))),
        scratch_shapes=[pltpu.VMEM((rows, 3 * width), single)],
        compiler_params=params("arbitrary"),
        cost_estimate=cost(6 * rows * width * width, 8 * width * width),
        name="project_qkv",
    )(tokens, shift_row, scale_row, bias_row, weight)


def image_of(len_ref, position):
    start, length, end = jnp.int32(0), jnp.int32(0), jnp.int32(0)
    for index in range(len_ref.shape[1]):
        here = len_ref[0, index]
        inside = jnp.logical_and(position >= end, position < end + here)
        start = jnp.where(inside, end, start)
        length = jnp.where(inside, here, length)
        end = end + here
    return start, length


def head_windows(heads, size):
    for head in range(heads):
        low, high = head * size, (head + 1) * size
        yield head, low // LANES * LANES, -(-high // LANES) * LANES, low, high


def head_mask(low, high, left, right):
    lane = lax.broadcasted_iota(jnp.int32, (1, high - low), 1) + low
    return jnp.logical_and(lane >= left, lane < right)


LONG, SHORT = 1024, 256


def head_row(table_ref, bucket_ref, width):
    heads = table_ref.shape[1]
    size = width // heads
    lane = lax.broadcasted_iota(jnp.int32, (1, width), 1)
    row = jnp.zeros((1, width), jnp.int32)
    for head in range(heads):
        inside = jnp.logical_and(lane >= head * size, lane < (head + 1) * size)
        row = jnp.where(inside, table_ref[bucket_ref[0], head], row)
    return row.astype(single)


def attend_kernel(heads, len_ref, table_ref, bucket_ref, q_ref, kv, ob_ref, log_ref, out):
    rows, width = q_ref.shape
    size = width // heads
    my_seq = lax.axis_index("seq")
    factor = size ** (-0.5) * LOG2E

    def run(tile_start, start, span):
        tile = pl.ds(tile_start, TILE)
        keys = pl.ds(start, span)
        logs = jnp.zeros((TILE, LANES), single)
        lane = lax.broadcasted_iota(jnp.int32, (TILE, LANES), 1)
        for head, low, high, left, right in head_windows(heads, size):
            mask = head_mask(low, high, left, right)
            query = q_ref[tile, low:high] * mask.astype(single).astype(bfloat)
            scores = dot_nt(query, kv[keys, low:high])
            top = jnp.max(scores, axis=-1, keepdims=True)
            expo = jnp.exp2((scores - top) * factor)
            total = jnp.sum(expo, axis=-1, keepdims=True)
            part = dot_nn(expo.astype(bfloat), kv[keys, width + low : width + high]) / total
            out[tile, low:high] = jnp.where(mask, part, out[tile, low:high])
            logs = jnp.where(lane == head, top * factor + jnp.log2(total), logs)
        log_ref[:, tile] = logs.T[:heads, :]

    @pl.loop(0, rows // TILE)
    def _(index):
        tile_start = pl.multiple_of(index * TILE, TILE)
        start, length = image_of(len_ref, my_seq * rows + tile_start)
        start = pl.multiple_of(start, SHORT)

        @pl.when(length > SHORT)
        def _():
            run(tile_start, start, LONG)

        @pl.when(length <= SHORT)
        def _():
            run(tile_start, start, SHORT)

    ob_ref[...] = (out[...] * head_row(table_ref, bucket_ref, width)).astype(bfloat)


def attend(lengths, head_table, bucket_ids, query, kv, heads):
    rows, width = query.shape
    group = kv.shape[0]
    return pl.pallas_call(
        functools.partial(attend_kernel, heads),
        out_shape=(
            jax.ShapeDtypeStruct((rows, width), bfloat),
            jax.ShapeDtypeStruct((heads, rows), single),
        ),
        in_specs=[IN_SMEM] * 3 + [IN_VMEM] * 2,
        out_specs=(IN_VMEM,) * 2,
        scratch_shapes=[pltpu.VMEM((rows, width), single)],
        compiler_params=params(),
        cost_estimate=cost(16 * rows * LONG * width, 10 * group * width, heads * rows * LONG),
        name="attend",
    )(lengths, head_table, bucket_ids, query, kv)


def out_copies(source, layout, plane, buffer, seq_bits, far_ref, near_ref, sem):
    my_bucket, my_seq = place_in_kernel()
    rows = far_ref.shape[1]
    copies = []
    for index in range(BLOCKS):
        if layout == "rows":
            bits, part = index % PLANES, index // PLANES
            seq = my_seq ^ bits
            bucket = plane * (BLOCKS // PLANES) + part
            start = pl.multiple_of((part * PLANES + seq) * rows, 16)
            side = bits % 2
        else:
            bits, bucket, start, side = seq_bits, index, index * rows, seq_bits_side(seq_bits)
        target = far_ref if side else near_ref
        slot = slot_of(bucket ^ my_bucket, bits if layout == "rows" else seq_bits[0])
        copies.append(
            pltpu.make_async_copy(
                source.at[buffer, pl.ds(start, rows), :], target.at[slot], sem.at[buffer, index]
            )
        )
    return copies


def seq_bits_side(seq_bits):
    return seq_bits[1]


def middle_kernel(
    heads,
    bucket_ref,
    table_ref,
    ob_ref,
    x_ref,
    c_ref,
    keep_ref,
    mod_ref,
    out_bias,
    down_bias,
    chan_ref,
    up_bias,
    pair_ref,
    up_ref,
    down_ref,
    out_ref,
    mid_ref,
    up_far,
    up_near,
    down_far,
    down_near,
    wo_far,
    wo_near,
    do_ref,
    delta_ref,
    row_ref,
    db_ref,
    up,
    down,
    up_grad,
    down_grad,
    total,
    da,
    result,
    second,
    df,
    dr,
    wo_sem,
    up_sem,
    down_sem,
    up_out,
    down_out,
    wo_out,
):
    local, width = x_ref.shape
    my_seq = place_in_kernel()[1]
    cols, edge = width // PLANES, dr.shape[2]

    def wo_load(plane, target):
        source = pair_ref.at[plane, :, pl.ds(width - edge, edge)]
        return pltpu.make_async_copy(source, target, wo_sem.at[plane])

    def wo_stage(plane):
        return up_grad.at[plane % 2, :, pl.ds(plane // 2 * edge, edge)]

    def loads(bits):
        plane = my_seq ^ bits
        rows = pl.ds(pl.multiple_of(plane * width, LANES), width)
        return (
            pltpu.make_async_copy(up_ref.at[plane], up.at[plane], up_sem.at[bits]),
            pltpu.make_async_copy(down_ref.at[rows, :], down.at[rows, :], down_sem.at[bits]),
        )

    for plane in range(PLANES):
        wo_load(plane, wo_stage(plane)).start()
    for bits in (1, 3, 0, 2):
        for copy in loads(bits):
            copy.start()
    total[...] = jnp.zeros_like(total)
    da[...] = jnp.zeros_like(da)
    row_ref[...] = jnp.zeros_like(row_ref)
    for plane in range(PLANES):
        wo_load(plane, wo_stage(plane)).wait()
        stage = up_grad[plane % 2, :, plane // 2 * edge : (plane // 2 + 1) * edge]
        result[:, plane * cols : (plane + 1) * cols] = dot_nn(ob_ref[...], stage)[:, -cols:]

    @pl.loop(0, local, step=LANES)
    def _(tile):
        span = pl.ds(pl.multiple_of(tile, LANES), LANES)
        branch = result[span, :] + out_bias[...]
        result[span, :] = branch
        middle = x_ref[span, :].astype(single) + mod_ref[2:3, :] * branch
        mid_ref[span, :] = middle
        second[span, :] = modulate(middle, mod_ref[3:4, :], mod_ref[4:5, :]).astype(bfloat)
        upstream = c_ref[span, :].astype(single)
        df[span, :] = (mod_ref[5:6, :] * keep_ref[span, :] * upstream).astype(bfloat)

    def one(plane, low, high, buffer):
        first, grad = second[...], df[...]
        hidden_rows = pl.ds(pl.multiple_of(plane * width + low, LANES), high - low)
        keep = chan_ref[pl.ds(bucket_ref[0], 1), hidden_rows].astype(single)
        pre = dot_nn(first, up[plane, :, low:high]) + up_bias[plane, :, low:high]
        root = math.sqrt(2.0 / math.pi)
        square = pre * pre
        half = 0.5 + 0.5 * jnp.tanh(pre * (root + (root * 0.044715) * square))
        kept = half * keep
        hidden = (pre * kept).astype(bfloat)
        bend = pre * (1.0 - half) * (2.0 * root + (2.0 * root * 0.134145) * square)
        back = (dot_nt(grad, down[hidden_rows, :]) * (kept + kept * bend)).astype(bfloat)
        total[...] += dot_nn(hidden, down[hidden_rows, :])
        da[...] += dot_nt(back, up[plane, :, low:high])
        up_grad[buffer, :, low:high] = dot_tn(first, back).astype(bfloat)
        down_grad[buffer, low:high, :] = dot_tn(hidden, grad).astype(bfloat)
        db_ref[plane, :, low:high] = column_sum(back.astype(single))

    cut = -(-width // 2 // LANES) * LANES

    def sends(plane, buffer, side_bits, far_side):
        return out_copies(
            up_grad, "planes", plane, buffer, (side_bits, far_side), up_far, up_near, up_out
        ) + out_copies(down_grad, "rows", plane, buffer, None, down_far, down_near, down_out)

    for far_side in (1, 0):

        @pl.loop(0, 2)
        def _(above):
            bits = above * 2 + far_side
            plane = my_seq ^ bits
            if not far_side:
                for copy in sends(plane, above, bits, far_side):
                    copy.wait()
            for copy in loads(bits):
                copy.wait()
            one(plane, 0, cut, above)
            one(plane, cut, width, above)
            for copy in sends(plane, above, bits, far_side):
                copy.start()

    def wo_end(plane):
        return down.at[pl.ds(plane * width, width), pl.ds(0, edge)]

    for plane in range(PLANES):
        wo_load(plane, wo_end(plane)).start()
    gate_one, scale, gate_two = mod_ref[2:3, :], mod_ref[4:5, :], mod_ref[5:6, :]

    @pl.loop(0, local, step=LANES)
    def _(tile):
        span = pl.ds(pl.multiple_of(tile, LANES), LANES)
        keep = keep_ref[span, :]
        upstream = c_ref[span, :].astype(single)
        middle = mid_ref[span, :]
        mlp = total[span, :] + down_bias[...]
        out_ref[span, :] = (middle + gate_two * keep * mlp).astype(bfloat)
        grad = da[span, :]
        back, normed = norm_back(middle, grad, scale)
        dmid = upstream + back
        mid_ref[span, :] = dmid
        branch = (gate_one * dmid).astype(bfloat).astype(single)
        for plane in range(PLANES):
            dr[plane, span, : edge - cols] = jnp.zeros((LANES, edge - cols), bfloat)
            dr[plane, span, edge - cols :] = branch[:, plane * cols : (plane + 1) * cols].astype(
                bfloat
            )
        row_ref[0:1, :] += column_sum(dmid * result[span, :])
        row_ref[1:2, :] += column_sum(grad)
        row_ref[2:3, :] += column_sum(grad * normed)
        row_ref[3:4, :] += column_sum(keep * upstream * mlp)
        row_ref[4:5, :] += column_sum(branch)
        row_ref[5:6, :] += column_sum(df[span, :].astype(single))

    for above in range(2):
        for copy in sends(my_seq ^ (above * 2), above, above * 2, 0):
            copy.wait()
    stage = up_grad.at[:, :, pl.ds(0, edge)]
    for far_side in (1, 0):
        for above in range(2):
            bits = above * 2 + far_side
            plane = my_seq ^ bits
            copies = out_copies(
                stage, "planes", plane, above, (bits, far_side), wo_far, wo_near, wo_out
            )
            if not far_side:
                for copy in copies:
                    copy.wait()
            up_grad[above, :, :edge] = dot_tn(ob_ref[...], dr[plane]).astype(bfloat)
            for copy in copies:
                copy.start()
    for plane in range(PLANES):
        wo_load(plane, wo_end(plane)).wait()
        part = dot_nt(dr[plane], down[plane * width : (plane + 1) * width, :edge])
        if plane == 0:
            total[...] = part
        else:
            total[...] += part
    size = width // heads
    grad = (total[...] * head_row(table_ref, bucket_ref, width)).astype(bfloat)
    do_ref[...] = grad
    terms = grad.astype(single) * ob_ref[...].astype(single)
    head = lax.broadcasted_iota(jnp.int32, (heads, width), 0)
    lane = lax.broadcasted_iota(jnp.int32, (heads, width), 1)
    chosen = jnp.logical_and(lane >= head * size, lane < (head + 1) * size)
    delta_ref[...] = lax.dot_general(
        chosen.astype(single),
        terms,
        (((1,), (1,)), ((), ())),
        preferred_element_type=single,
        precision=HIGHEST,
    )
    for above in range(2):
        for copy in out_copies(
            stage, "planes", my_seq ^ (above * 2), above, (above * 2, 0), wo_far, wo_near, wo_out
        ):
            copy.wait()


def middle(
    bucket_ids,
    head_table,
    branch,
    tokens,
    upstream,
    keep,
    mods,
    out_bias,
    down_bias,
    chan_table,
    up_bias,
    pair_weight,
    up_weight,
    down_weight,
):
    rows, width = branch.shape
    heads, hidden = head_table.shape[1], chan_table.shape[1]
    edge = 3 * LANES
    blocks = jax.ShapeDtypeStruct((BLOCKS * PLANES // 2, width // BLOCKS, width), bfloat)
    narrow = jax.ShapeDtypeStruct((BLOCKS * PLANES // 2, width // BLOCKS, edge), bfloat)
    square = pltpu.VMEM((rows, width), single)
    low_square = pltpu.VMEM((rows, width), bfloat)
    return pl.pallas_call(
        functools.partial(middle_kernel, heads),
        out_shape=(
            jax.ShapeDtypeStruct((rows, width), bfloat),
            jax.ShapeDtypeStruct((rows, width), single),
            blocks,
            blocks,
            blocks,
            blocks,
            narrow,
            narrow,
            jax.ShapeDtypeStruct((rows, width), bfloat),
            jax.ShapeDtypeStruct((heads, rows), single),
            jax.ShapeDtypeStruct((8, width), single),
            jax.ShapeDtypeStruct((PLANES, 1, width), single),
        ),
        in_specs=[IN_SMEM] * 2 + [IN_VMEM] * 9 + [IN_HBM] * 3,
        out_specs=(IN_VMEM,) * 2 + (IN_HBM,) * 6 + (IN_VMEM,) * 4,
        scratch_shapes=[
            pltpu.VMEM((PLANES, width, width), bfloat),
            pltpu.VMEM((hidden, width), bfloat),
            pltpu.VMEM((2, width, width), bfloat),
            pltpu.VMEM((2, width, width), bfloat),
            square,
            square,
            square,
            low_square,
            low_square,
            pltpu.VMEM((PLANES, rows, edge), bfloat),
            pltpu.SemaphoreType.DMA((PLANES,)),
            pltpu.SemaphoreType.DMA((PLANES,)),
            pltpu.SemaphoreType.DMA((PLANES,)),
            pltpu.SemaphoreType.DMA((2, BLOCKS)),
            pltpu.SemaphoreType.DMA((2, BLOCKS)),
            pltpu.SemaphoreType.DMA((2, BLOCKS)),
        ],
        compiler_params=pltpu.CompilerParams(vmem_limit_bytes=63 * 1024 * 1024),
        cost_estimate=cost(12 * rows * width * hidden, 8 * width * hidden, rows * hidden),
        name="middle",
    )(
        bucket_ids,
        head_table,
        branch,
        tokens,
        upstream,
        keep,
        mods,
        out_bias,
        down_bias,
        chan_table,
        up_bias.reshape(PLANES, 1, width),
        pair_weight,
        up_weight,
        down_weight,
    )


def attend_back_kernel(
    heads, len_ref, q_ref, do_ref, log_ref, delta_ref, kv, dq_ref, far_ref, near_ref, dq, dk, dv
):
    rows, width = q_ref.shape
    size = width // heads
    my_seq = lax.axis_index("seq")
    scale = size ** (-0.5)
    factor = scale * LOG2E
    dk[...] = jnp.zeros_like(dk)
    dv[...] = jnp.zeros_like(dv)

    def run(tile_start, start, span):
        tile = pl.ds(tile_start, TILE)
        keys = pl.ds(start, span)
        for head, low, high, left, right in head_windows(heads, size):
            mask = head_mask(low, high, left, right)
            chosen = mask.astype(single).astype(bfloat)
            query = q_ref[tile, low:high] * chosen
            grad = do_ref[tile, low:high] * chosen
            key = kv[keys, low:high]
            probs = jnp.exp2(dot_nt(key, query) * factor - log_ref[head : head + 1, tile])
            slope = dot_nt(kv[keys, width + low : width + high], grad)
            score_grad = (probs * (slope - delta_ref[head : head + 1, tile])).astype(bfloat)
            dv[keys, low:high] += dot_nn(probs.astype(bfloat), grad)
            dk[keys, low:high] += dot_nn(score_grad, query)
            part = dot_tn(score_grad, key)
            dq[tile, low:high] = jnp.where(mask, part, dq[tile, low:high])

    @pl.loop(0, rows // TILE)
    def _(index):
        tile_start = pl.multiple_of(index * TILE, TILE)
        start, length = image_of(len_ref, my_seq * rows + tile_start)
        start = pl.multiple_of(start, SHORT)

        @pl.when(length > SHORT)
        def _():
            run(tile_start, start, LONG)

        @pl.when(length <= SHORT)
        def _():
            run(tile_start, start, SHORT)

    dq_ref[...] = (dq[...] * scale).astype(bfloat)
    base = place_in_kernel()[1]
    for bits in range(PLANES):
        place = pl.ds(pl.multiple_of((base ^ bits) * rows, rows), rows)
        target = far_ref if bits % 2 else near_ref
        target[bits // 2, :, :width] = (dk[place, :] * scale).astype(bfloat)
        target[bits // 2, :, width:] = dv[place, :].astype(bfloat)


def attend_back(lengths, query, grad, logs, delta, kv, heads):
    rows, width = query.shape
    group = kv.shape[0]
    return pl.pallas_call(
        functools.partial(attend_back_kernel, heads),
        out_shape=(
            jax.ShapeDtypeStruct((rows, width), bfloat),
            jax.ShapeDtypeStruct((2, rows, 2 * width), bfloat),
            jax.ShapeDtypeStruct((2, rows, 2 * width), bfloat),
        ),
        in_specs=[pl.BlockSpec(memory_space=pltpu.SMEM)]
        + [IN_VMEM] * 5,
        out_specs=(IN_VMEM,) * 3,
        scratch_shapes=[
            pltpu.VMEM((rows, width), single),
            pltpu.VMEM((group, width), single),
            pltpu.VMEM((group, width), single),
        ],
        compiler_params=params(),
        cost_estimate=cost(40 * rows * LONG * width, 20 * group * width, heads * rows * LONG),
        name="attend_back",
    )(lengths, query, grad, logs, delta, kv)


def back_qkv_kernel(a_ref, dy_ref, w_ref, da_ref, far_ref, near_ref, stage, sem):
    my_seq = place_in_kernel()[1]
    wide = dy_ref.shape[2]
    da_ref[...] = jnp.zeros_like(da_ref)

    def sends(plane, buffer, bits, far_side):
        return out_copies(
            stage, "planes", plane, buffer, (bits, far_side), far_ref, near_ref, sem
        )

    for far_side in (1, 0):

        @pl.loop(0, 2)
        def _(above):
            bits = above * 2 + far_side
            plane = my_seq ^ bits
            if not far_side:
                for copy in sends(plane, above, bits, far_side):
                    copy.wait()
            da_ref[...] += dot_nt(dy_ref[plane], w_ref[plane, :, :wide])
            stage[above] = dot_tn(a_ref[...], dy_ref[plane]).astype(bfloat)
            for copy in sends(plane, above, bits, far_side):
                copy.start()

    for above in range(2):
        for copy in sends(my_seq ^ (above * 2), above, above * 2, 0):
            copy.wait()


def back_qkv(first_in, dy_planes, weight):
    rows, width = first_in.shape
    wide = dy_planes.shape[2]
    blocks = jax.ShapeDtypeStruct((BLOCKS * PLANES // 2, width // BLOCKS, wide), bfloat)
    return pl.pallas_call(
        back_qkv_kernel,
        out_shape=(jax.ShapeDtypeStruct((rows, width), single), blocks, blocks),
        in_specs=[IN_VMEM] * 3,
        out_specs=(IN_VMEM, IN_HBM, IN_HBM),
        scratch_shapes=[
            pltpu.VMEM((2, width, wide), bfloat),
            pltpu.SemaphoreType.DMA((2, BLOCKS)),
        ],
        compiler_params=params(),
        cost_estimate=cost(12 * rows * width * width, 4 * weight.size),
        name="back_qkv",
    )(first_in, dy_planes, weight)


def on_device(
    tokens,
    condition,
    cotangent,
    lengths,
    bucket_ids,
    keep_flags,
    head_table,
    chan_table,
    ada_master,
    ada_first,
    ada_second,
    ada_average,
    qkv_master,
    qkv_first,
    qkv_second,
    qkv_average,
    out_master,
    out_first,
    out_second,
    out_average,
    up_master,
    up_first,
    up_second,
    up_average,
    down_master,
    down_first,
    down_second,
    down_average,
    bias_master,
    bias_first,
    bias_second,
    bias_average,
):
    local_rows, width = tokens.shape
    heads = head_table.shape[1]
    head_size = width // heads
    hidden_width = chan_table.shape[1]
    hidden_ratio = hidden_width // width
    table_cols = 10 + hidden_ratio
    my_bucket, my_seq = lax.axis_index("bucket"), lax.axis_index("seq")
    buckets, seqs = lax.axis_size("bucket"), lax.axis_size("seq")
    group_rows = local_rows * seqs
    block_rows = qkv_master.shape[0]
    if cube_path():
        table = bias_master.reshape(-1, table_cols).T
        cut = down_master.astype(bfloat).reshape(seqs, -1, down_master.shape[1])
        (
            pair_weight,
            up_weight,
            down_weight,
            near,
            silu_rows,
            mods,
            bias_table,
            first_in,
            query,
        ) = gather(
            condition, table, ada_master, qkv_master, out_master, up_master, cut, tokens
        )
    else:
        pair_block = jnp.concatenate([qkv_master, out_master], axis=1).astype(bfloat)
        down_block = lax.all_to_all(
            down_master.astype(bfloat), "seq", split_axis=0, concat_axis=1, tiled=True
        )
        up_block = up_master.astype(bfloat)
        ada_low = ada_master.astype(bfloat)
        pair_weight = gather_all(pair_block, "planes")
        bias_low = lax.all_gather(
            bias_master.astype(bfloat), ("bucket", "seq"), axis=0, tiled=True
        )
        silu_low = jax.nn.silu(condition).astype(bfloat)
        silu_all = lax.all_gather(silu_low, "bucket", axis=0, tiled=True)
        silu_rows = lax.dynamic_slice_in_dim(silu_all, my_bucket * block_rows, block_rows, 1)
        mod_part = lax.psum_scatter(
            dot_nn(silu_rows, ada_low), "bucket", scatter_dimension=0, tiled=True
        )
        mod_row = lax.all_gather(mod_part, "seq", axis=1, tiled=True)
        bias_table = bias_low.astype(single).reshape(width, table_cols).T
        mods = jnp.pad(mod_row.reshape(6, width) + bias_table[:6], ((0, 2), (0, 0)))
        value_bias = bias_table[7:8]
        qkv_bias = jnp.concatenate(
            [bias_table[6:7], jnp.zeros_like(value_bias), value_bias], axis=1
        )
        first_in, query, key_value = project_qkv(
            tokens, mods[0:1], mods[1:2], qkv_bias, pair_weight
        )
        up_weight = gather_all(up_block, "planes")
        down_weight = gather_all(down_block, "rows")
        near = lax.all_gather(key_value, "seq", axis=0, tiled=True)

    out_bias = bias_table[8:9]
    up_bias = bias_table[9 : table_cols - 1].T.reshape(1, hidden_width)
    down_bias = bias_table[table_cols - 1 : table_cols]
    keep_float = keep_flags.astype(single)[:, None]
    branch_in, logs = attend(lengths, head_table, bucket_ids, query, near, heads)
    (
        output,
        middle_grad,
        up_far,
        up_near,
        down_far,
        down_near,
        wo_far,
        wo_near,
        attended_grad,
        delta,
        row_grads,
        up_bias_grad,
    ) = middle(
        bucket_ids,
        head_table,
        branch_in,
        tokens,
        cotangent,
        keep_float,
        mods,
        out_bias,
        down_bias,
        chan_table,
        up_bias,
        pair_weight,
        up_weight,
        down_weight,
    )
    up_bias_rows = up_bias_grad.reshape(width, hidden_ratio).T
    query_grad, kv_far, kv_near = attend_back(
        lengths, query, attended_grad, logs, delta, near, heads
    )
    qkv_cols = 3 * width // seqs
    if cube_path():
        rows_all = jnp.concatenate([row_grads[:5], up_bias_rows, row_grads[5:6]])
        rows_all = jnp.pad(rows_all, ((0, 16 - rows_all.shape[0]), (0, 0)))
        (
            up_new_grad,
            out_new_grad,
            pair_new_grad,
            token_grad,
            mod_all,
            bias_sum,
            silu_sum,
            down_cuts,
            _,
        ) = scatter(
            kv_far,
            kv_near,
            down_far,
            down_near,
            up_far,
            up_near,
            wo_far,
            wo_near,
            first_in,
            query_grad,
            pair_weight,
            tokens,
            middle_grad,
            mods,
            rows_all,
            ada_master,
        )
        down_mine = down_cuts.reshape(down_master.shape)
        bias_new_grad = bias_sum[:table_cols, : width // (buckets * seqs)].T.reshape(-1)
        silu_grad = silu_sum[:, 0, :block_rows].reshape(1, width)
    else:
        terms = jnp.stack([kv_near[0], kv_far[0], kv_near[1], kv_far[1]])
        kv_grad = lax.psum_scatter(terms, "seq", scatter_dimension=0)
        projected_grad = jnp.concatenate([query_grad, kv_grad], axis=1)
        dy_planes = jnp.pad(
            projected_grad.reshape(local_rows, seqs, qkv_cols).transpose(1, 0, 2),
            ((0, 0), (0, 0), (0, -qkv_cols % LANES)),
        )
        first_grad, pair_far, pair_near = back_qkv(first_in, dy_planes, pair_weight)
        out_new_grad = natural_sum(wo_far, wo_near, "planes")
        back, normed = norm_back(tokens.astype(single), first_grad, mods[1:2])
        token_grad = middle_grad + back
        up_new_grad = natural_sum(up_far, up_near, "planes")
        down_new_grad = natural_sum(down_far, down_near, "rows")
        pair_new_grad = natural_sum(pair_far, pair_near, "planes")
        mod_grads = jnp.concatenate(
            [column_sum(first_grad), column_sum(first_grad * normed), row_grads[:4]]
        )
        bias_grad = jnp.concatenate(
            [
                mod_grads,
                column_sum(query_grad.astype(single)),
                column_sum(kv_grad[:, width:].astype(single)),
                row_grads[4:5],
                up_bias_rows,
                row_grads[5:6],
            ]
        ).T.reshape(width * table_cols)
        mod_mine = lax.psum_scatter(
            mod_grads.reshape(seqs, 6 * width // seqs), "seq", scatter_dimension=0, tiled=True
        )
        mod_all = lax.all_gather(mod_mine, "bucket", axis=0, tiled=True)
        silu_part = lax.dot_general(
            mod_all,
            ada_low.astype(single),
            (((1,), (1,)), ((), ())),
            preferred_element_type=single,
            precision=HIGHEST,
        )
        silu_grad = lax.all_to_all(
            lax.psum(silu_part, "seq"), "bucket", split_axis=0, concat_axis=1, tiled=True
        )
        bias_new_grad = lax.psum_scatter(
            bias_grad, ("bucket", "seq"), scatter_dimension=0, tiled=True
        )
        down_mine = lax.all_to_all(
            down_new_grad.astype(bfloat), "seq", split_axis=1, concat_axis=0, tiled=True
        )
    ada_new_grad = lax.dot_general(
        silu_rows.astype(single),
        mod_all,
        (((0,), (0,)), ((), ())),
        preferred_element_type=single,
        precision=HIGHEST,
    )
    _, silu_back = jax.vjp(jax.nn.silu, condition)
    condition_grad = silu_back(silu_grad)[0]
    out_rate = (group_rows / (16.0 * width)) ** 0.5
    ada_new = adam_update(
        ada_master, ada_first, ada_second, ada_average, ada_new_grad, width ** (-0.5), MATRIX_DECAY
    )
    qkv_new = adam_update(
        qkv_master,
        qkv_first,
        qkv_second,
        qkv_average,
        pair_new_grad[:, :qkv_cols],
        width ** (-0.5),
        MATRIX_DECAY,
    )
    out_new = adam_update(
        out_master,
        out_first,
        out_second,
        out_average,
        out_new_grad[:, -out_master.shape[1] :],
        out_rate,
        MATRIX_DECAY,
    )
    up_new = adam_update(
        up_master, up_first, up_second, up_average, up_new_grad, width ** (-0.5), MATRIX_DECAY
    )
    down_new = adam_update(
        down_master.T,
        down_first.T,
        down_second.T,
        down_average.T,
        down_mine.T.astype(single),
        hidden_width ** (-0.5),
        MATRIX_DECAY,
    )
    down_new = [value.T for value in down_new]
    bias_new = adam_update(
        bias_master, bias_first, bias_second, bias_average, bias_new_grad, 0.3, 0.0
    )
    return (
        output,
        token_grad,
        condition_grad,
        *ada_new,
        *qkv_new,
        *out_new,
        *up_new,
        *down_new,
        *bias_new,
    )


def solution(mesh):
    in_specs = (
        P(("bucket", "seq"), None),
        P("bucket", None),
        P(("bucket", "seq"), None),
        P("bucket", None),
        P("bucket"),
        P(("bucket", "seq")),
        P(),
        P(),
        P("bucket", "seq"),
        P("bucket", "seq"),
        P("bucket", "seq"),
        P("bucket", "seq"),
        P("bucket", "seq"),
        P("bucket", "seq"),
        P("bucket", "seq"),
        P("bucket", "seq"),
        P("bucket", "seq"),
        P("bucket", "seq"),
        P("bucket", "seq"),
        P("bucket", "seq"),
        P("bucket", "seq"),
        P("bucket", "seq"),
        P("bucket", "seq"),
        P("bucket", "seq"),
        P("bucket", "seq"),
        P("bucket", "seq"),
        P("bucket", "seq"),
        P("bucket", "seq"),
        P(("bucket", "seq")),
        P(("bucket", "seq")),
        P(("bucket", "seq")),
        P(("bucket", "seq")),
    )
    out_specs = (
        P(("bucket", "seq"), None),
        P(("bucket", "seq"), None),
        P("bucket", None),
        P("bucket", "seq"),
        P("bucket", "seq"),
        P("bucket", "seq"),
        P("bucket", "seq"),
        P("bucket", "seq"),
        P("bucket", "seq"),
        P("bucket", "seq"),
        P("bucket", "seq"),
        P("bucket", "seq"),
        P("bucket", "seq"),
        P("bucket", "seq"),
        P("bucket", "seq"),
        P("bucket", "seq"),
        P("bucket", "seq"),
        P("bucket", "seq"),
        P("bucket", "seq"),
        P("bucket", "seq"),
        P("bucket", "seq"),
        P("bucket", "seq"),
        P("bucket", "seq"),
        P(("bucket", "seq")),
        P(("bucket", "seq")),
        P(("bucket", "seq")),
        P(("bucket", "seq")),
    )
    return jax.shard_map(
        on_device, mesh=mesh, in_specs=in_specs, out_specs=out_specs, check_vma=False
    )
```

```python
import functools
import math

import jax
import jax.numpy as jnp
from jax import lax
from jax.experimental import pallas as pl
from jax.experimental.pallas import tpu as pltpu
from jax.sharding import PartitionSpec as P

STEP = 10


EPSILON = 1e-06
BETA_FIRST = 0.5
BETA_SECOND = 0.5
ADAM_EPSILON = 1e-08
MATRIX_DECAY = 0.01
EMA_DECAY = 0.9999
HIGHEST = lax.Precision.HIGHEST
LOG2E = math.log2(math.e)
LANES = 128
TILE = 256
VMEM_LIMIT = 60 * 1024 * 1024
bfloat = jnp.bfloat16
single = jnp.float32


def layer_norm(values):
    centre = values - jnp.mean(values, axis=-1, keepdims=True)
    spread = jnp.mean(centre * centre, axis=-1, keepdims=True)
    return centre * lax.rsqrt(spread + EPSILON)


def modulate(values, shift_row, scale_row):
    return layer_norm(values) * (1.0 + scale_row) + shift_row


def dot_nn(left, right):
    return lax.dot_general(left, right, (((1,), (0,)), ((), ())), preferred_element_type=single)


def dot_nt(left, right):
    return lax.dot_general(left, right, (((1,), (1,)), ((), ())), preferred_element_type=single)


def dot_tn(left, right):
    return lax.dot_general(left, right, (((0,), (0,)), ((), ())), preferred_element_type=single)


def adam_update(master, moment_one, moment_two, average, gradient, step_rate, decay_rate):
    one_new = BETA_FIRST * moment_one + (1.0 - BETA_FIRST) * gradient
    two_new = BETA_SECOND * moment_two + (1.0 - BETA_SECOND) * gradient * gradient
    one_hat = one_new / (1.0 - BETA_FIRST**STEP)
    two_hat = two_new / (1.0 - BETA_SECOND**STEP)
    master_new = master - step_rate * (
        one_hat / (jnp.sqrt(two_hat) + ADAM_EPSILON) + decay_rate * master
    )
    average_decay = min(EMA_DECAY, (1.0 + STEP) / (10.0 + STEP))
    average_new = average_decay * average + (1.0 - average_decay) * master_new
    return (master_new, one_new, two_new, average_new)


def params(*semantics):
    return pltpu.CompilerParams(
        dimension_semantics=semantics or None, vmem_limit_bytes=VMEM_LIMIT
    )


def cost(flops, moved, exps=0):
    return pl.CostEstimate(flops=int(flops), bytes_accessed=int(moved), transcendentals=int(exps))


def exchange(values, axis, bit):
    count = lax.axis_size(axis)
    return lax.ppermute(values, axis, [(i, i ^ bit) for i in range(count)])


def pick(values, index, axis):
    return lax.dynamic_index_in_dim(values, index, axis, keepdims=False)


IN_VMEM = pl.BlockSpec(memory_space=pltpu.VMEM)
IN_HBM = pl.BlockSpec(memory_space=pl.ANY)
IN_SMEM = pl.BlockSpec(memory_space=pltpu.SMEM)


def cube_path():
    return lax.axis_size("bucket") == 8 and lax.axis_size("seq") == 4


BLOCKS, PLANES = 8, 4
X, Z0, Z1, CORE, Y = ("bucket", 1), ("bucket", 2), ("bucket", 4), ("seq", 1), ("seq", 2)
MIDDLE, FORWARD = ("bucket", 6), ("bucket", 2, "forward")


def gather_all(block, layout):
    width = block.shape[1]
    if layout == "rows":
        return lax.all_gather(block, ("bucket", "seq"), axis=0, tiled=True)
    tall = lax.all_gather(block, "bucket", axis=0, tiled=True)
    return lax.all_gather(tall, "seq", axis=0)


def place_in_kernel():
    if cube_path():
        return lax.axis_index("bucket"), lax.axis_index("seq")
    return 0, 0


DIMS = {"planes": (Y, CORE, Z1, Z0, X), "rows": (Z1, Z0, X, Y, CORE)}
MESH = pl.DeviceIdType.MESH


def my_coords():
    bucket, seq = lax.axis_index("bucket"), lax.axis_index("seq")
    return {
        (axis, amount): ((bucket if axis == "bucket" else seq) // amount) % 2
        for axis, amount in (X, Z0, Z1, CORE, Y)
    }


def partner(bit):
    bucket, seq = lax.axis_index("bucket"), lax.axis_index("seq")
    axis, amount = bit[:2]
    return (bucket ^ amount, seq) if axis == "bucket" else (bucket, seq ^ amount)


def peer_at(distance):
    bucket, seq = lax.axis_index("bucket"), lax.axis_index("seq")
    return bucket ^ (distance >> 2), seq ^ (distance & 3)


def greet(peers):
    barrier = pltpu.get_barrier_semaphore()
    for peer in peers:
        pl.semaphore_signal(barrier, inc=1, device_id=peer, device_id_type=MESH)
    pl.semaphore_wait(barrier, len(peers))


class Gathering:
    def __init__(self, own, out, layout, order, first, rows, send, recv, base):
        self.own, self.out, self.dims, self.order = own, out, DIMS[layout], order
        self.first, self.rows, self.send, self.recv, self.base = first, rows, send, recv, base
        self.me = my_coords()
        self.inner = self.me[Z0] != self.me[Z1]

    def view(self, free, flipped=None):
        index = tuple(
            slice(None)
            if dim in free
            else (1 - self.me[dim] if dim == flipped else self.me[dim])
            for dim in self.dims
        )
        return self.out.at[index + (pl.ds(self.first, self.rows), slice(None))]

    def copy(self, source, place, slot, bit):
        return pltpu.make_async_remote_copy(
            src_ref=source,
            dst_ref=place,
            send_sem=self.send.at[self.base + slot],
            recv_sem=self.recv.at[self.base + slot],
            device_id=partner(bit),
            device_id_type=MESH,
        )

    def dim(self, phase):
        return Z1 if self.order[phase] in (MIDDLE, FORWARD) else self.order[phase]

    def had(self, phase):
        return [self.dim(past) for past in range(phase) if self.order[past] != MIDDLE]

    def arrived(self, phase):
        return self.view(self.had(phase), self.dim(phase))

    def hop(self, phase):
        place = self.arrived(phase) if self.order[phase] == FORWARD else self.view(self.had(phase))
        source = self.own if phase == 0 else place
        return self.copy(source, place, phase, self.order[phase])

    def across(self, phase):
        if phase == 0:
            return self.copy(self.own, self.view(()), 5, CORE)
        place = self.arrived(phase - 1)
        return self.copy(place, place, 5 + phase, CORE)

    def keep(self):
        return pltpu.make_async_copy(self.own, self.view(()), self.send.at[self.base + 11])

    def begin(self):
        self.hop(0).start()
        self.across(0).start()
        self.keep().start()

    def sends(self, phase, act):
        if self.order[phase] in (MIDDLE, FORWARD):
            pl.when(self.inner)(act)
        else:
            act()

    def advance(self, phase):
        if phase == 0:
            self.keep().wait()
        kind = self.order[phase]
        if kind == MIDDLE:

            @pl.when(self.inner)
            def _():
                self.hop(phase).wait_recv()
                self.hop(phase + 1).start()

            return
        if kind == FORWARD:

            @pl.when(jnp.logical_not(self.inner))
            def _():
                self.hop(phase).wait_recv()

        else:
            self.hop(phase).wait_recv()
        if phase < 4:
            self.sends(phase + 1, lambda: self.hop(phase + 1).start())
        self.across(phase + 1).start()

    def collect(self):
        for phase in range(6):
            if phase == 0 or self.order[phase - 1] != MIDDLE:
                self.across(phase).wait_recv()

    def finish(self):
        for phase in range(5):
            self.sends(phase, lambda phase=phase: self.hop(phase).wait_send())
        for phase in range(6):
            if phase == 0 or self.order[phase - 1] != MIDDLE:
                self.across(phase).wait_send()


GATHER_SEMS = 12
SHARES = (32, 32, 32, 32, 16)
PAIR_PARTS = (
    (X, Z0, Y, MIDDLE, FORWARD),
    (Z0, MIDDLE, FORWARD, X, Y),
    (Z0, Y, MIDDLE, FORWARD, X),
    (Z0, MIDDLE, FORWARD, Y, X),
    (Z0, MIDDLE, FORWARD, Y, X),
)
UP_PARTS = (
    (Z0, X, Y, MIDDLE, FORWARD),
    (Z0, X, Y, MIDDLE, FORWARD),
    (Y, Z0, MIDDLE, FORWARD, X),
    (Y, Z0, MIDDLE, FORWARD, X),
    (Z0, X, MIDDLE, FORWARD, Y),
)
DOWN_PARTS = (
    (Z0, MIDDLE, FORWARD, Y, X),
    (Z0, Y, X, MIDDLE, FORWARD),
    (Z0, MIDDLE, FORWARD, Y, X),
    (Z0, X, Y, MIDDLE, FORWARD),
    (Z0, MIDDLE, FORWARD, X, Y),
)
BEGIN, PLANE, KV = -1, -2, -3
GATHER_STEPS = (
    (0, 0), (1, 0), (2, 0), (3, 0), (4, 0), (1, 1), (0, 1), (2, 1), (3, 1), (4, 1),
    (-1, 0), (1, 2), (3, 2), (0, 2), (2, 2), (4, 2), (7, 0), (5, 0), (8, 0), (6, 0),
    (9, 0), (1, 3), (10, 0), (11, 0), (5, 1), (3, 3), (12, 0), (13, 0), (14, 0), (6, 1),
    (4, 3), (9, 1), (0, 3), (2, 3), (10, 1), (7, 1), (12, 1), (14, 1), (8, 1), (1, 4),
    (3, 4), (9, 2), (11, 1), (13, 1), (7, 2), (5, 2), (4, 4), (0, 4), (8, 2), (10, 2),
    (6, 2), (12, 2), (14, 2), (13, 2), (9, 3), (2, 4), (-2, 0), (5, 3), (10, 3), (7, 3),
    (11, 2), (-2, 1), (14, 3), (12, 3), (-2, 2), (8, 3), (-2, 3), (-3, 0), (-3, 1), (-3, 2),
    (-3, 3), (6, 3), (9, 4), (10, 4), (14, 4), (5, 4), (13, 3), (7, 4), (6, 4), (11, 3),
    (12, 4), (13, 4), (8, 4), (11, 4),
)
NOTE, TAKE, ALL = -4, -5, -6
DOWN_SUM_PARTS = (
    (X, Z0, Y, Z1),
    (Z0, X, Y, Z1),
    (Z0, X, Y, Z1),
    (Y, Z0, Z1, X),
    (X, Z0, Z1, Y),
)
UP_SUM_PARTS = (
    (X, Z0, Z1, Y),
    (Y, X, Z0, Z1),
    (X, Y, Z0, Z1),
    (X, Y, Z0, Z1),
    (Z0, Y, X, Z1),
)
OUT_SHARES = (80, 64)
OUT_SUM_PARTS = (
    (Y, X, Z0, Z1),
    (X, Y, Z0, Z1),
)
PAIR_SUM_PARTS = (
    (Z0, Y, X, Z1),
    (X, Y, Z0, Z1),
    (X, Y, Z0, Z1),
    (Y, X, Z0, Z1),
    (X, Y, Z0, Z1),
)
SUM_STEPS = (
    (-3, 0), (-3, 1), (-3, 2), (-3, 3), (0, -1), (1, -1), (-5, 0), (2, -1), (3, -1), (4, -1),
    (5, -1), (-5, 1), (6, -1), (0, 0), (7, -1), (1, 0), (8, -1), (9, -1), (-5, 2), (4, 0),
    (10, -1), (11, -1), (-5, 3), (2, 0), (-2, 0), (5, 0), (0, 1), (-2, 1), (3, 0), (9, 0),
    (4, 1), (7, 0), (5, 1), (1, 1), (6, 0), (-6, 0), (-2, 2), (3, 1), (-2, 3), (4, 2),
    (8, 0), (10, 0), (12, -1), (13, -1), (14, -1), (15, -1), (16, -1), (5, 2), (0, 2), (9, 1),
    (-4, 0), (11, 0), (3, 2), (7, 1), (2, 1), (1, 2), (4, 3), (12, 0), (6, 1), (0, 3),
    (8, 1), (7, 2), (10, 1), (1, 3), (6, 2), (15, 0), (5, 3), (8, 2), (13, 0), (7, 3),
    (11, 1), (10, 2), (2, 2), (6, 3), (14, 0), (8, 3), (12, 1), (11, 2), (16, 0), (10, 3),
    (13, 1), (9, 2), (3, 3), (2, 3), (14, 1), (11, 3), (15, 1), (16, 1), (13, 2), (9, 3),
    (12, 2), (14, 2), (15, 2), (16, 2), (13, 3), (12, 3), (14, 3), (15, 3), (16, 3),
)
NOTE_STEP = 5
KV_PIECES = 4


def split_gatherings(block_ref, out_ref, layout, shares, orders, send, recv, base):
    moving, first = [], 0
    for index, (count, order) in enumerate(zip(shares, orders)):
        own = block_ref.at[pl.ds(first, count), :]
        slot = base + GATHER_SEMS * index
        moving.append(Gathering(own, out_ref, layout, order, first, count, send, recv, slot))
        first += count
    return moving


def kv_needed(piece, act):
    place = my_coords()
    quarter = KV_PIECES // 2
    last = jnp.logical_and(place[Y] == 1, place[CORE] == 1)
    first = jnp.logical_and(place[Y] == 0, place[CORE] == 0)
    skipped = first if piece < quarter else last
    pl.when(jnp.logical_not(skipped))(act)


def kv_expected(piece, act):
    place = my_coords()
    quarter = KV_PIECES // 2
    last = jnp.logical_and(place[Y] == 0, place[CORE] == 1)
    first = jnp.logical_and(place[Y] == 1, place[CORE] == 0)
    skipped = first if piece < quarter else last
    pl.when(jnp.logical_not(skipped))(act)


def kv_relayed(piece, act):
    place = my_coords()
    quarter = KV_PIECES // 2
    last = jnp.logical_and(place[Y] == 0, place[CORE] == 0)
    first = jnp.logical_and(place[Y] == 1, place[CORE] == 1)
    skipped = first if piece < quarter else last
    pl.when(jnp.logical_not(skipped))(act)


def gather_kernel(
    cond_ref,
    table_ref,
    ada_ref,
    qkv_master,
    out_master,
    up_master,
    cut_ref,
    x_ref,
    pair_out,
    up_out,
    down_out,
    kv_out,
    silu_ref,
    mod_ref,
    bias_ref,
    a_ref,
    q_ref,
    note_ref,
    pair_ref,
    up_ref,
    down_ref,
    cuts,
    inbox,
    parts,
    returns,
    row,
    weights,
    acc,
    kv,
    note_send,
    note_recv,
    mod_send,
    mod_recv,
    cut_send,
    cut_recv,
    weight_sem,
    send,
    recv,
):
    bucket, seq = lax.axis_index("bucket"), lax.axis_index("seq")
    place = my_coords()
    me = bucket * PLANES + seq
    count = BLOCKS * PLANES
    barrier = pltpu.get_barrier_semaphore()

    @pl.loop(1, count)
    def _(distance):
        pl.semaphore_signal(barrier, inc=1, device_id=peer_at(distance), device_id_type=MESH)

    rows, width = ada_ref.shape[0], x_ref.shape[1]
    cols = 3 * width // PLANES
    pair_ref[:, :cols] = qkv_master[...].astype(bfloat)
    pair_ref[:, cols:] = out_master[...].astype(bfloat)
    up_ref[...] = up_master[...].astype(bfloat)
    note_ref[...] = jnp.zeros_like(note_ref)
    for index in range(BLOCKS):
        start = index * rows
        note_ref[index, : NOTE_ROWS - 2, : table_ref.shape[1]] = table_ref[...]
        note_ref[index, NOTE_ROWS - 2 : NOTE_ROWS - 1, :] = cond_ref[:, start : start + LANES]
        note_ref[index, NOTE_ROWS - 1 :, : rows - LANES] = cond_ref[
            :, start + LANES : start + rows
        ]
    pl.semaphore_wait(barrier, count - 1)

    def cut(distance):
        return pltpu.make_async_remote_copy(
            src_ref=cut_ref.at[seq ^ distance],
            dst_ref=cuts.at[seq],
            send_sem=cut_send.at[distance],
            recv_sem=cut_recv.at[distance],
            device_id=(bucket, seq ^ distance),
            device_id_type=MESH,
        )

    def note(distance):
        peer = peer_at(distance)
        return pltpu.make_async_remote_copy(
            src_ref=note_ref.at[peer[0]],
            dst_ref=inbox.at[me],
            send_sem=note_send.at[distance],
            recv_sem=note_recv.at[distance],
            device_id=peer,
            device_id_type=MESH,
        )

    def answer(distance):
        peer = peer_at(distance)
        return pltpu.make_async_remote_copy(
            src_ref=parts.at[peer[0]],
            dst_ref=returns.at[me],
            send_sem=mod_send.at[distance],
            recv_sem=mod_recv.at[distance],
            device_id=peer,
            device_id_type=MESH,
        )

    @pl.loop(1, count)
    def _(distance):
        note(distance).start()

    inbox[me] = note_ref[bucket]
    cuts[seq] = cut_ref[seq]
    base = len(PAIR_PARTS) * GATHER_SEMS
    pairs = split_gatherings(pair_ref, pair_out, "planes", SHARES, PAIR_PARTS, send, recv, 0)
    rest = split_gatherings(up_ref, up_out, "planes", SHARES, UP_PARTS, send, recv, base)
    base += len(UP_PARTS) * GATHER_SEMS
    rest += split_gatherings(down_ref, down_out, "rows", SHARES, DOWN_PARTS, send, recv, base)
    base += len(DOWN_PARTS) * GATHER_SEMS
    moving = pairs + rest
    for part in pairs:
        part.begin()
    for distance in range(1, PLANES):
        cut(distance).start()

    local = x_ref.shape[0] // KV_PIECES

    def kv_copy(source, target, slot, bit):
        return pltpu.make_async_remote_copy(
            src_ref=source,
            dst_ref=target,
            send_sem=send.at[base + slot],
            recv_sem=recv.at[base + slot],
            device_id=partner(bit),
            device_id_type=MESH,
        )

    def kv_step(piece, kind):
        span = pl.ds(piece * local, local)
        mine = kv_out.at[place[Y], place[CORE], span, :]
        other = kv_out.at[1 - place[Y], place[CORE], span, :]
        if kind == "over":
            return kv_copy(kv.at[span, :], mine, 4 * piece, Y)
        if kind == "near":
            return kv_copy(kv.at[span, :], mine, 4 * piece + 1, CORE)
        if kind == "far":
            return kv_copy(other, other, 4 * piece + 2, CORE)
        return pltpu.make_async_copy(kv.at[span, :], mine, send.at[base + 4 * piece + 3])

    def load(plane):
        source = pair_out.at[plane // 2, plane % 2, :, :, :, :, pl.ds(0, weights.shape[5])]
        return pltpu.make_async_copy(source, weights.at[plane % 2], weight_sem.at[plane % 2])

    def modulations():
        @pl.loop(1, count)
        def _(distance):
            note(distance).wait_recv()

        head = jnp.concatenate(
            [inbox[PLANES * g, NOTE_ROWS - 2 : NOTE_ROWS - 1, :] for g in range(BLOCKS)]
        )
        tail = jnp.concatenate(
            [inbox[PLANES * g, NOTE_ROWS - 1 : NOTE_ROWS, :] for g in range(BLOCKS)]
        )
        head, tail = jax.nn.silu(head).astype(bfloat), jax.nn.silu(tail).astype(bfloat)
        silu_ref[:, :LANES] = head
        silu_ref[:, LANES:] = tail
        mods = dot_nn(head, ada_ref[:LANES, :].astype(bfloat)) + dot_nn(
            tail[:, : rows - LANES], ada_ref[LANES:, :].astype(bfloat)
        )
        for group in range(BLOCKS):
            parts[group] = mods[group : group + 1, :]
        returns[me] = parts[bucket]

        @pl.loop(1, count)
        def _(distance):
            answer(distance).start()

    def biases():
        each = width // count
        for device in range(count):
            heard = inbox[device].astype(bfloat).astype(single)
            bias_ref[:, device * each : (device + 1) * each] = heard[:, :each]

    def projection(plane):
        if plane == 0:
            for part in pairs:
                part.collect()
            load(0).start()
            load(1).start()

            @pl.loop(1, count)
            def _(distance):
                answer(distance).wait_recv()

            for index in range(PLANES):
                wide = returns.shape[2]
                row[:, index * wide : (index + 1) * wide] = sum(
                    returns[PLANES * g + index] for g in range(BLOCKS)
                )
            for index in range(6):
                mod_ref[index : index + 1, :] = (
                    row[:, index * width : (index + 1) * width] + bias_ref[index : index + 1, :]
                )
            a_ref[...] = modulate(
                x_ref[...].astype(single), mod_ref[0:1, :], mod_ref[1:2, :]
            ).astype(bfloat)
        load(plane).wait()
        weight = weights[plane % 2].reshape(width, weights.shape[5])
        acc[:, plane * cols : (plane + 1) * cols] = dot_nn(a_ref[...], weight)[:, :cols]
        if plane + 2 < PLANES:
            load(plane + 2).start()
        if plane == PLANES - 1:
            q_ref[...] = (acc[:, :width] + bias_ref[6:7, :]).astype(bfloat)
            kv[:, :width] = acc[:, width : 2 * width].astype(bfloat)
            kv[:, width:] = (acc[:, 2 * width :] + bias_ref[7:8, :]).astype(bfloat)

    for step, (part, phase) in enumerate(GATHER_STEPS):
        if step == NOTE_STEP:
            modulations()
            biases()
        if part == BEGIN:
            for distance in range(1, PLANES):
                cut(distance).wait_recv()
            for index in range(PLANES):
                each = cuts.shape[2]
                down_ref[:, index * each : (index + 1) * each] = cuts[index]
            for moved in rest:
                moved.begin()
        elif part == PLANE:
            projection(phase)
        elif part == KV:
            kv_needed(phase, lambda: kv_step(phase, "over").start())
            for kind in ("near", "keep"):
                kv_step(phase, kind).start()
        else:
            moving[part].advance(phase)
    def relay(piece):
        kv_step(piece, "over").wait_recv()
        kv_step(piece, "far").start()

    for piece in range(KV_PIECES):
        kv_expected(piece, functools.partial(relay, piece))
    for part in rest:
        part.collect()
    for part in moving:
        part.finish()
    for piece in range(KV_PIECES):
        kv_step(piece, "near").wait_recv()
        kv_relayed(piece, lambda piece=piece: kv_step(piece, "far").wait_recv())
        kv_step(piece, "keep").wait()
        kv_step(piece, "near").wait_send()
        kv_needed(piece, lambda piece=piece: kv_step(piece, "over").wait_send())
        kv_expected(piece, lambda piece=piece: kv_step(piece, "far").wait_send())

    for distance in range(1, PLANES):
        cut(distance).wait_send()

    @pl.loop(1, count)
    def _(distance):
        note(distance).wait_send()
        answer(distance).wait_send()


NOTE_ROWS = 16


def gather(condition, table, ada_master, qkv_master, out_master, up_master, cut, tokens):
    rows, width = up_master.shape
    local = tokens.shape[0]
    count = BLOCKS * PLANES
    cols = ada_master.shape[1]
    block = pltpu.VMEM((rows, width), bfloat)
    wide = -(-3 * width // PLANES // LANES) * LANES
    blocks = jax.ShapeDtypeStruct((2, 2, 2, 2, 2, rows, width), bfloat)
    sems = 3 * len(SHARES) * GATHER_SEMS + 4 * KV_PIECES
    pair, up, down, kv, silu, mods, biases, first_in, query = pl.pallas_call(
        gather_kernel,
        out_shape=(
            blocks,
            blocks,
            blocks,
            jax.ShapeDtypeStruct((2, 2, local, 2 * width), bfloat),
            jax.ShapeDtypeStruct((BLOCKS, 2 * LANES), bfloat),
            jax.ShapeDtypeStruct((8, width), single),
            jax.ShapeDtypeStruct((NOTE_ROWS, width), single),
            jax.ShapeDtypeStruct((local, width), bfloat),
            jax.ShapeDtypeStruct((local, width), bfloat),
        ),
        in_specs=[IN_VMEM] * 8,
        out_specs=(IN_HBM,) * 4 + (IN_VMEM,) * 5,
        scratch_shapes=[
            pltpu.VMEM((BLOCKS, NOTE_ROWS, LANES), single),
            block,
            block,
            block,
            pltpu.VMEM(cut.shape, bfloat),
            pltpu.VMEM((count, NOTE_ROWS, LANES), single),
            pltpu.VMEM((BLOCKS, 1, cols), single),
            pltpu.VMEM((count, 1, cols), single),
            pltpu.VMEM((1, 6 * width), single),
            pltpu.VMEM((2, 2, 2, 2, rows, wide), bfloat),
            pltpu.VMEM((local, 3 * width), single),
            pltpu.VMEM((local, 2 * width), bfloat),
        ]
        + [pltpu.SemaphoreType.DMA((count,))] * 4
        + [pltpu.SemaphoreType.DMA((PLANES,))] * 2
        + [pltpu.SemaphoreType.DMA((2,))]
        + [pltpu.SemaphoreType.DMA((sems,))] * 2,
        compiler_params=pltpu.CompilerParams(
            collective_id=1, has_side_effects=True, vmem_limit_bytes=VMEM_LIMIT
        ),
        cost_estimate=cost(6 * local * width * width, 200 * rows * width),
        name="gather",
    )(condition, table, ada_master, qkv_master, out_master, up_master, cut, tokens)
    tall = BLOCKS * rows
    return (
        pair.reshape(PLANES, tall, width),
        up.reshape(PLANES, tall, width),
        down.reshape(PLANES * tall, width),
        kv.reshape(PLANES * local, 2 * width),
        silu[:, :rows],
        mods,
        biases,
        first_in,
        query,
    )


def slot_of(bucket_bits, seq_bits):
    slot = 0
    for axis, amount in SLOT_DIMS:
        bits = bucket_bits if axis == "bucket" else seq_bits
        slot = slot * 2 + ((bits >> amount.bit_length() - 1) & 1)
    return slot


def natural_sum(far, near, layout):
    width = far.shape[2]
    both = jnp.concatenate([near, far])
    index = {
        (b, s): slot_of(b, s) + near.shape[0] * (s % 2)
        for b in range(BLOCKS)
        for s in range(PLANES)
    }
    if layout == "rows":
        picked = [index[b, s] for b in range(BLOCKS) for s in range(PLANES)]
        gradient = jnp.stack([both[k] for k in picked]).reshape(-1, width)
        part = lax.psum_scatter(gradient, ("bucket", "seq"), scatter_dimension=0, tiled=True)
        return part.astype(single)
    picked = [index[b, s] for s in range(PLANES) for b in range(BLOCKS)]
    gradient = jnp.stack([both[k] for k in picked]).reshape(PLANES, -1, width)
    part = lax.psum_scatter(gradient, "seq", scatter_dimension=0)
    return lax.psum_scatter(part, "bucket", scatter_dimension=0, tiled=True).astype(single)


SLOT_DIMS = (Y, X, Z1, Z0)


class Scattering:
    def __init__(self, far, near, total, arrivals, out, order, first, rows, send, recv, base):
        self.far, self.near, self.total, self.arrivals = far, near, total, arrivals
        self.out, self.order, self.first, self.rows = out, order, first, rows
        self.send, self.recv, self.base = send, recv, base
        self.span = (pl.ds(first, rows), slice(None))
        self.near_span = None

    def copy(self, source, place, slot, bit):
        return pltpu.make_async_remote_copy(
            src_ref=source,
            dst_ref=place,
            send_sem=self.send.at[self.base + slot],
            recv_sem=self.recv.at[self.base + slot],
            device_id=partner(bit),
            device_id_type=MESH,
        )

    def across(self):
        index = (slice(None),) * 4 + self.span
        return self.copy(self.far.at[index], self.total.at[index], 4, CORE)

    def place(self, fixed):
        return tuple(fixed.get(dim, slice(None)) for dim in SLOT_DIMS)

    def hop(self, phase):
        fixed = {dim: 0 for dim in self.order[:phase]} | {self.order[phase]: 1}
        source = self.total.at[self.place(fixed) + self.span]
        place = self.arrivals[phase].at[(slice(None),) * (3 - phase) + self.span]
        return self.copy(source, place, phase, self.order[phase])

    def add(self, fixed, source, source_dims, source_span=None):
        free = [dim for dim in SLOT_DIMS if dim not in fixed]

        def one(step):
            index = dict(fixed)
            for place, dim in enumerate(free):
                index[dim] = (step >> place) & 1
            spot = tuple(index[dim] for dim in SLOT_DIMS) + self.span
            term = source[tuple(index[dim] for dim in source_dims) + (source_span or self.span)]
            self.total[spot] = (self.total[spot].astype(single) + term.astype(single)).astype(
                bfloat
            )

        if free:
            pl.loop(0, 2 ** len(free))(one)
        else:
            one(0)

    def advance(self, phase):
        span = None
        if phase < 0 and self.near is None:
            self.hop(0).start()
            return
        if phase < 0:
            self.across().wait_recv()
            source, dims, fixed, span = self.near, SLOT_DIMS, {}, self.near_span
        else:
            self.hop(phase).wait_recv()
            done = self.order[: phase + 1]
            dims = tuple(dim for dim in SLOT_DIMS if dim not in done)
            source, fixed = self.arrivals[phase], {dim: 0 for dim in done}
        if phase == 3:
            spot = (0,) * 4 + self.span
            self.out[self.span] = self.total[spot].astype(single) + source[self.span].astype(
                single
            )
            return
        ahead = self.order[phase + 1]
        self.add(fixed | {ahead: 1}, source, dims, span)
        self.hop(phase + 1).start()
        self.add(fixed | {ahead: 0}, source, dims, span)

    def finish(self):
        self.across().wait_send()
        for phase in range(4):
            self.hop(phase).wait_send()


SCATTER_SEMS = 5


def scatter_scratch(rows, width):
    return [
        pltpu.VMEM((2,) * free + (rows, width), bfloat) for free in (4, 3, 2, 1, 0)
    ]


def split_scatterings(far, near, scratch, out, shares, orders, send, recv, base):
    moving, first = [], 0
    for index, (count, order) in enumerate(zip(shares, orders)):
        slot = base + SCATTER_SEMS * index
        moving.append(
            Scattering(
                far, near, scratch[0], scratch[1:], out, order, first, count, send, recv, slot
            )
        )
        first += count
    return moving


def norm_back(values, grad, scale_row):
    centre = values - jnp.mean(values, axis=-1, keepdims=True)
    root = lax.rsqrt(jnp.mean(centre * centre, axis=-1, keepdims=True) + EPSILON)
    normed = centre * root
    scaled = grad * (1.0 + scale_row)
    inner = jnp.mean(scaled * normed, axis=-1, keepdims=True)
    return root * (scaled - jnp.mean(scaled, axis=-1, keepdims=True) - normed * inner), normed


def column_sum(values):
    return jnp.sum(values, axis=0, keepdims=True)


def scatter_kernel(
    kv_far,
    kv_near,
    down_far,
    down_near,
    up_far,
    up_near,
    wo_far,
    w_ref,
    x_ref,
    dmid_ref,
    wo_near,
    a_ref,
    dq_ref,
    mod_ref,
    row_ref,
    ada_ref,
    up_out,
    wo_sum,
    pair_out,
    grad_ref,
    mods_ref,
    bias_ref,
    silu_ref,
    cuts,
    far,
    *refs,
):
    down_scratch, up_scratch, refs = refs[:5], refs[5:10], refs[10:]
    wo_scratch, pair_scratch, refs = refs[:5], refs[5:10], refs[10:]
    kv_total, kv_arrival, kv_stage, stage, down_sum, cut_ref, plane_stage, refs = refs[:7] + (refs[7:],)
    x_tile, dmid_tile, weights, dy, table, line, bias_notes, mod_notes, bias_box, mod_box = refs[:10]
    parts, returns, cut_send, cut_recv, local_sem, far_sem = refs[10:16]
    bias_send, bias_recv, mod_send, mod_recv, back_send, back_recv, send, recv = refs[16:]
    bucket, seq = lax.axis_index("bucket"), lax.axis_index("seq")
    me = bucket * PLANES + seq
    count = BLOCKS * PLANES
    barrier = pltpu.get_barrier_semaphore()

    @pl.loop(1, count)
    def _(distance):
        pl.semaphore_signal(barrier, inc=1, device_id=peer_at(distance), device_id_type=MESH)

    pl.semaphore_wait(barrier, count - 1)

    def message(source, target, out_sem, in_sem, distance):
        return pltpu.make_async_remote_copy(
            src_ref=source,
            dst_ref=target,
            send_sem=out_sem.at[distance],
            recv_sem=in_sem.at[distance],
            device_id=peer_at(distance),
            device_id_type=MESH,
        )

    def bias_note(distance):
        peer = peer_at(distance)
        source = bias_notes.at[peer[0] * PLANES + peer[1]]
        return message(source, bias_box.at[me], bias_send, bias_recv, distance)

    def mod_note(distance):
        source = mod_notes.at[peer_at(distance)[1]]
        return message(source, mod_box.at[me], mod_send, mod_recv, distance)

    def answer(distance):
        source = parts.at[peer_at(distance)[0]]
        return message(source, returns.at[me], back_send, back_recv, distance)

    place = my_coords()
    base = 0

    def streams(far_ref, near_ref, scratch, out, shares, orders):
        nonlocal base
        start, base = base, base + len(orders) * SCATTER_SEMS
        return split_scatterings(far_ref, near_ref, scratch, out, shares, orders, send, recv, start)

    downs = streams(down_far, down_near, down_scratch, down_sum, SHARES, DOWN_SUM_PARTS)
    ups = streams(up_far, up_near, up_scratch, up_out, SHARES, UP_SUM_PARTS)
    wos = streams(wo_far, wo_near, wo_scratch, wo_sum, OUT_SHARES, OUT_SUM_PARTS)
    pairs = streams(far, None, pair_scratch, pair_out, SHARES, PAIR_SUM_PARTS)
    moving = downs + ups + wos + pairs
    piece_rows = kv_arrival.shape[0] // KV_PIECES

    def kv_copy(source, target, slot, bit):
        return pltpu.make_async_remote_copy(
            src_ref=source,
            dst_ref=target,
            send_sem=send.at[base + slot],
            recv_sem=recv.at[base + slot],
            device_id=partner(bit),
            device_id_type=MESH,
        )

    def kv_span(piece):
        return pl.ds(piece * piece_rows, piece_rows)

    def near_kv(piece):
        span = kv_span(piece)
        return kv_copy(kv_far.at[:, span, :], kv_total.at[:, span, :], 2 * piece, CORE)

    def over(piece):
        span = kv_span(piece)
        return kv_copy(kv_total.at[1, span, :], kv_arrival.at[span, :], 2 * piece + 1, Y)

    def kv_load(piece):
        return pltpu.make_async_copy(
            kv_near.at[:, kv_span(piece), :], kv_stage, local_sem.at[2]
        )

    def kv_add(piece, side):
        span = kv_span(piece)
        kv_total[side, span, :] = (
            kv_total[side, span, :].astype(single) + kv_stage[side].astype(single)
        ).astype(bfloat)

    def pass_over(piece):
        kv_add(piece, 1)
        over(piece).start()

    def take(piece):
        over(piece).wait_recv()
        span = kv_span(piece)
        kv_total[0, span, :] = (
            kv_total[0, span, :].astype(single) + kv_arrival[span, :].astype(single)
        ).astype(bfloat)

    staged = [part for part, phase in SUM_STEPS if phase < 0 and 0 <= part < len(downs + ups)]

    def stage_load(turn):
        part = moving[staged[turn]]
        spot = (slice(None),) * 4
        return pltpu.make_async_copy(
            part.near.at[spot + part.span],
            stage.at[(turn % 2,) + spot + (pl.ds(0, part.rows), slice(None))],
            local_sem.at[turn % 2],
        )

    kv_load(0).start()
    for piece in range(KV_PIECES):
        near_kv(piece).start()
    for part in downs + ups + wos:
        part.across().start()
    for turn in range(2):
        stage_load(turn).start()

    def cut(distance):
        return pltpu.make_async_remote_copy(
            src_ref=cut_ref.at[seq ^ distance],
            dst_ref=cuts.at[seq],
            send_sem=cut_send.at[distance],
            recv_sem=cut_recv.at[distance],
            device_id=(bucket, seq ^ distance),
            device_id_type=MESH,
        )

    def cut_down():
        for index in range(PLANES):
            each = cuts.shape[2]
            cut_ref[index] = down_sum[:, index * each : (index + 1) * each].astype(bfloat)
        cuts[seq] = cut_ref[seq]
        for distance in range(1, PLANES):
            cut(distance).start()

    local, width = dq_ref.shape
    rows = up_out.shape[0]
    cols = 3 * width // PLANES
    wide = dy.shape[1]
    order = (1, 3, 0, 2)

    def load(step):
        plane = seq ^ order[step]
        return pltpu.make_async_copy(
            w_ref.at[plane, :, pl.ds(0, wide)], weights, local_sem.at[3]
        )

    def gather_dy(index):
        low, high = index * cols, (index + 1) * cols
        pieces = []
        if low < width:
            pieces.append(dq_ref[:, low : min(high, width)])
        if high > width:
            pieces.append(kv_total[0, :, max(low - width, 0) : high - width])
        first = 0
        for piece in pieces:
            dy[:, first : first + piece.shape[1]] = piece
            first += piece.shape[1]

    def block_spot(block, bits):
        return (
            bits // 2,
            (block % 2) ^ place[X],
            (block // 4) ^ place[Z1],
            (block // 2 % 2) ^ place[Z0],
        )

    def far_copy(block, bits):
        return pltpu.make_async_copy(
            plane_stage.at[pl.ds(block * rows, rows), :],
            far.at[block_spot(block, bits)],
            far_sem.at[block],
        )

    def project(step):
        bits = order[step]
        plane = seq ^ bits
        if step == 0:
            load(0).start()
            dy[:, cols:] = jnp.zeros((local, wide - cols), bfloat)
            grad_ref[...] = jnp.zeros_like(grad_ref)
        for index in range(PLANES):

            @pl.when(plane == index)
            def _():
                gather_dy(index)

        if step == 1:
            for block in range(BLOCKS):
                far_copy(block, order[0]).wait()
        total = pair_scratch[0]
        for low, high in ((0, 4 * LANES), (4 * LANES, wide)):
            values = dot_tn(a_ref[...], dy[:, low:high])
            if step < 2:
                plane_stage[:, low:high] = values.astype(bfloat)
                continue
            for block in range(BLOCKS):
                spot = block_spot(block, bits) + (slice(None), slice(low, high))
                value = values[block * rows : (block + 1) * rows, :]
                total[spot] = (total[spot].astype(single) + value).astype(bfloat)
        if step < 2:
            for block in range(BLOCKS):
                far_copy(block, bits).start()
        load(step).wait()
        grad_ref[...] += dot_nt(dy[...], weights[...])
        if step + 1 < PLANES:
            load(step + 1).start()
        if step == 1:
            for block in range(BLOCKS):
                far_copy(block, bits).wait()
            for part in pairs:
                part.across().start()

    def tile_loads(tile):
        span = pl.ds(tile * LANES, LANES)
        return (
            pltpu.make_async_copy(x_ref.at[span, :], x_tile.at[tile % 2], far_sem.at[tile % 2]),
            pltpu.make_async_copy(
                dmid_ref.at[span, :], dmid_tile.at[tile % 2], far_sem.at[2 + tile % 2]
            ),
        )

    def notes():
        shift_sum, scale_sum = jnp.zeros((1, width), single), jnp.zeros((1, width), single)
        scale_row = mod_ref[1:2, :]
        tiles = local // LANES
        for copy in tile_loads(0):
            copy.start()
        for tile in range(tiles):
            if tile + 1 < tiles:
                for copy in tile_loads(tile + 1):
                    copy.start()
            for copy in tile_loads(tile):
                copy.wait()
            span = slice(tile * LANES, (tile + 1) * LANES)
            grad = grad_ref[span, :]
            back, normed = norm_back(x_tile[tile % 2].astype(single), grad, scale_row)
            shift_sum += column_sum(grad)
            scale_sum += column_sum(grad * normed)
            grad_ref[span, :] = dmid_tile[tile % 2] + back
        table[...] = jnp.zeros_like(table)
        line[:, :width] = shift_sum
        line[:, width : 2 * width] = scale_sum
        table[0:1, :width] = shift_sum
        table[1:2, :width] = scale_sum
        for index in range(4):
            line[:, (2 + index) * width : (3 + index) * width] = row_ref[index : index + 1, :]
        table[2:6, :width] = row_ref[0:4, :]
        table[6:7, :width] = column_sum(dq_ref[...].astype(single))
        table[7:8, :width] = column_sum(kv_total[0, :, width:].astype(single))
        table[8:14, :width] = row_ref[4:10, :]
        each = width // count
        for device in range(count):
            bias_notes[device] = table[:, device * each : device * each + LANES]

        part = mod_notes.shape[2]
        for index in range(PLANES):
            mod_notes[index] = line[:, index * part : (index + 1) * part]
        bias_box[me] = bias_notes[me]
        mod_box[me] = mod_notes[seq]

        @pl.loop(1, count)
        def _(distance):
            mod_note(distance).start()
            bias_note(distance).start()

    def answers():
        @pl.loop(1, count)
        def _(distance):
            mod_note(distance).wait_recv()

        sums = [sum(mod_box[PLANES * g + s] for s in range(PLANES)) for g in range(BLOCKS)]
        mods = jnp.concatenate(sums)
        mods_ref[...] = mods
        silu = lax.dot_general(
            mods,
            ada_ref[...].astype(bfloat).astype(single),
            (((1,), (1,)), ((), ())),
            preferred_element_type=single,
            precision=HIGHEST,
        )
        for group in range(BLOCKS):
            parts[group, :, :rows] = silu[group : group + 1, :]
            parts[group, :, rows:] = jnp.zeros((1, parts.shape[2] - rows), single)
        returns[me] = parts[bucket]

        @pl.loop(1, count)
        def _(distance):
            answer(distance).start()

    since, turn, left = 0, 0, len(downs)
    for part, phase in SUM_STEPS:
        if part == KV:
            near_kv(phase).wait_recv()
            kv_load(phase).wait()
            kv_expected(phase, functools.partial(pass_over, phase))
            kv_add(phase, 0)
            if phase + 1 < KV_PIECES:
                kv_load(phase + 1).start()
        elif part == TAKE:
            kv_needed(phase, functools.partial(take, phase))
        elif part == ALL:
            for moved in pairs:
                moved.across().wait_recv()
        elif part == PLANE:
            project(phase)
        elif part == NOTE:
            notes()
            since = 1
        else:
            mover = moving[part]
            if phase < 0 and part < len(downs + ups):
                stage_load(turn).wait()
                mover.near = stage.at[turn % 2]
                mover.near_span = (pl.ds(0, mover.rows), slice(None))
                mover.advance(phase)
                if turn + 2 < len(staged):
                    stage_load(turn + 2).start()
                turn += 1
            else:
                mover.advance(phase)
            if part < len(downs) and phase == 3:
                left -= 1
                if left == 0:
                    cut_down()
            since += since > 0
            if since == ANSWER_AFTER:
                answers()

    @pl.loop(1, count)
    def _(distance):
        bias_note(distance).wait_recv()

    bias_ref[...] = jnp.zeros_like(bias_ref)

    @pl.loop(0, count)
    def _(device):
        bias_ref[...] += bias_box[device]

    @pl.loop(1, count)
    def _(distance):
        answer(distance).wait_recv()

    for group in range(BLOCKS):
        silu_ref[group] = sum(returns[PLANES * group + s] for s in range(PLANES))
    for part in moving:
        part.finish()
    for piece in range(KV_PIECES):
        near_kv(piece).wait_send()
        kv_expected(piece, lambda piece=piece: over(piece).wait_send())
    for distance in range(1, PLANES):
        cut(distance).wait_recv()
        cut(distance).wait_send()

    @pl.loop(1, count)
    def _(distance):
        bias_note(distance).wait_send()
        mod_note(distance).wait_send()
        answer(distance).wait_send()


ANSWER_AFTER = 26


def scatter(
    kv_far,
    kv_near,
    down_far,
    down_near,
    up_far,
    up_near,
    wo_far,
    wo_near,
    first_in,
    query_grad,
    weight,
    tokens,
    middle_grad,
    mods,
    row_grads,
    ada_master,
):
    rows, width = up_far.shape[1:]
    edge = wo_far.shape[2]
    count = BLOCKS * PLANES
    cols = ada_master.shape[1]
    cuts = (PLANES, rows, width // PLANES)
    local, kv_wide = kv_far.shape[1:]
    wide = -(-3 * width // PLANES // LANES) * LANES
    cube, wo_cube = (2, 2, 2, 2, rows, width), (2, 2, 2, 2, rows, edge)
    sems = (3 * len(SHARES) + len(OUT_SHARES)) * SCATTER_SEMS + 2 * KV_PIECES
    return pl.pallas_call(
        scatter_kernel,
        out_shape=(
            jax.ShapeDtypeStruct((rows, width), single),
            jax.ShapeDtypeStruct((rows, edge), single),
            jax.ShapeDtypeStruct((rows, wide), single),
            jax.ShapeDtypeStruct((local, width), single),
            jax.ShapeDtypeStruct((BLOCKS, cols), single),
            jax.ShapeDtypeStruct((NOTE_ROWS, LANES), single),
            jax.ShapeDtypeStruct((BLOCKS, 1, 2 * LANES), single),
            jax.ShapeDtypeStruct(cuts, bfloat),
            jax.ShapeDtypeStruct((2, 2, 2, 2, rows, wide), bfloat),
        ),
        in_specs=[IN_HBM] * 10 + [IN_VMEM] * 6,
        out_specs=(IN_VMEM,) * 8 + (IN_HBM,),
        scratch_shapes=scatter_scratch(rows, width)
        + scatter_scratch(rows, width)
        + scatter_scratch(rows, edge)
        + scatter_scratch(rows, wide)
        + [
            pltpu.VMEM((2, local, kv_wide), bfloat),
            pltpu.VMEM((local, kv_wide), bfloat),
            pltpu.VMEM((2, local // KV_PIECES, kv_wide), bfloat),
            pltpu.VMEM((2, 2, 2, 2, 2, max(SHARES), width), bfloat),
            pltpu.VMEM((rows, width), single),
            pltpu.VMEM(cuts, bfloat),
            pltpu.VMEM((width, wide), bfloat),
            pltpu.VMEM((2, LANES, width), bfloat),
            pltpu.VMEM((2, LANES, width), single),
            pltpu.VMEM((width, wide), bfloat),
            pltpu.VMEM((local, wide), bfloat),
            pltpu.VMEM((NOTE_ROWS, width + LANES), single),
            pltpu.VMEM((1, 6 * width), single),
            pltpu.VMEM((count, NOTE_ROWS, LANES), single),
            pltpu.VMEM((PLANES, 1, cols), single),
            pltpu.VMEM((count, NOTE_ROWS, LANES), single),
            pltpu.VMEM((count, 1, cols), single),
            pltpu.VMEM((BLOCKS, 1, 2 * LANES), single),
            pltpu.VMEM((count, 1, 2 * LANES), single),
            pltpu.SemaphoreType.DMA((PLANES,)),
            pltpu.SemaphoreType.DMA((PLANES,)),
            pltpu.SemaphoreType.DMA((4,)),
            pltpu.SemaphoreType.DMA((BLOCKS,)),
        ]
        + [pltpu.SemaphoreType.DMA((count,))] * 6
        + [pltpu.SemaphoreType.DMA((sems,))] * 2,
        compiler_params=pltpu.CompilerParams(
            collective_id=4, has_side_effects=True, vmem_limit_bytes=63 * 1024 * 1024
        ),
        cost_estimate=cost(12 * local * width * width, 300 * rows * width),
        name="scatter",
    )(
        kv_far,
        kv_near,
        down_far.reshape(cube),
        down_near.reshape(cube),
        up_far.reshape(cube),
        up_near.reshape(cube),
        wo_far.reshape(wo_cube),
        weight,
        tokens,
        middle_grad,
        wo_near.reshape(wo_cube),
        first_in,
        query_grad,
        mods,
        row_grads,
        ada_master,
    )


def whole(shape):
    return pl.BlockSpec(shape, lambda *_: (0,) * len(shape))


def qkv_kernel(cols, x_ref, shift_ref, scale_ref, bias_ref, w_ref, a_ref, q_ref, kv_ref, acc):
    step = pl.program_id(0)
    width = x_ref.shape[1]

    @pl.when(step == 0)
    def _():
        values = x_ref[...].astype(single)
        a_ref[...] = modulate(values, shift_ref[...], scale_ref[...]).astype(bfloat)

    wide = -(-cols // LANES) * LANES
    part = dot_nn(a_ref[...], w_ref[0, :, :wide])[:, :cols]
    for index in range(PLANES):

        @pl.when(step == index)
        def _():
            acc[:, index * cols : (index + 1) * cols] = part

    @pl.when(step == PLANES - 1)
    def _():
        q_ref[...] = (acc[:, :width] + bias_ref[:, :width]).astype(bfloat)
        kv_ref[...] = (acc[:, width:] + bias_ref[:, width:]).astype(bfloat)


def project_qkv(tokens, shift_row, scale_row, bias_row, weight):
    rows, width = tokens.shape
    cols = 3 * width // PLANES
    return pl.pallas_call(
        functools.partial(qkv_kernel, cols),
        grid=(PLANES,),
        out_shape=(
            jax.ShapeDtypeStruct((rows, width), bfloat),
            jax.ShapeDtypeStruct((rows, width), bfloat),
            jax.ShapeDtypeStruct((rows, 2 * width), bfloat),
        ),
        in_specs=[
            whole((rows, width)),
            whole((1, width)),
            whole((1, width)),
            whole((1, 3 * width)),
            pl.BlockSpec((1,) + weight.shape[1:], lambda s: (s, 0, 0)),
        ],
        out_specs=(whole((rows, width)), whole((rows, width)), whole((rows, 2 * width))),
        scratch_shapes=[pltpu.VMEM((rows, 3 * width), single)],
        compiler_params=params("arbitrary"),
        cost_estimate=cost(6 * rows * width * width, 8 * width * width),
        name="project_qkv",
    )(tokens, shift_row, scale_row, bias_row, weight)


def image_of(len_ref, position):
    start, length, end = jnp.int32(0), jnp.int32(0), jnp.int32(0)
    for index in range(len_ref.shape[1]):
        here = len_ref[0, index]
        inside = jnp.logical_and(position >= end, position < end + here)
        start = jnp.where(inside, end, start)
        length = jnp.where(inside, here, length)
        end = end + here
    return start, length


def head_windows(heads, size):
    for head in range(heads):
        low, high = head * size, (head + 1) * size
        yield head, low // LANES * LANES, -(-high // LANES) * LANES, low, high


def head_mask(low, high, left, right):
    lane = lax.broadcasted_iota(jnp.int32, (1, high - low), 1) + low
    return jnp.logical_and(lane >= left, lane < right)


LONG, SHORT = 1024, 256


def head_row(table_ref, bucket_ref, width):
    heads = table_ref.shape[1]
    size = width // heads
    lane = lax.broadcasted_iota(jnp.int32, (1, width), 1)
    row = jnp.zeros((1, width), jnp.int32)
    for head in range(heads):
        inside = jnp.logical_and(lane >= head * size, lane < (head + 1) * size)
        row = jnp.where(inside, table_ref[bucket_ref[0], head], row)
    return row.astype(single)


def attend_kernel(heads, len_ref, table_ref, bucket_ref, q_ref, kv, ob_ref, log_ref, out):
    rows, width = q_ref.shape
    size = width // heads
    my_seq = lax.axis_index("seq")
    factor = size ** (-0.5) * LOG2E

    def run(tile_start, start, span):
        tile = pl.ds(tile_start, TILE)
        keys = pl.ds(start, span)
        logs = jnp.zeros((TILE, LANES), single)
        lane = lax.broadcasted_iota(jnp.int32, (TILE, LANES), 1)
        for head, low, high, left, right in head_windows(heads, size):
            mask = head_mask(low, high, left, right)
            query = q_ref[tile, low:high] * mask.astype(single).astype(bfloat)
            scores = dot_nt(query, kv[keys, low:high])
            top = jnp.max(scores, axis=-1, keepdims=True)
            expo = jnp.exp2((scores - top) * factor)
            total = jnp.sum(expo, axis=-1, keepdims=True)
            part = dot_nn(expo.astype(bfloat), kv[keys, width + low : width + high]) / total
            out[tile, low:high] = jnp.where(mask, part, out[tile, low:high])
            logs = jnp.where(lane == head, top * factor + jnp.log2(total), logs)
        log_ref[:, tile] = logs.T[:heads, :]

    @pl.loop(0, rows // TILE)
    def _(index):
        tile_start = pl.multiple_of(index * TILE, TILE)
        start, length = image_of(len_ref, my_seq * rows + tile_start)
        start = pl.multiple_of(start, SHORT)

        @pl.when(length > SHORT)
        def _():
            run(tile_start, start, LONG)

        @pl.when(length <= SHORT)
        def _():
            run(tile_start, start, SHORT)

    ob_ref[...] = (out[...] * head_row(table_ref, bucket_ref, width)).astype(bfloat)


def attend(lengths, head_table, bucket_ids, query, kv, heads):
    rows, width = query.shape
    group = kv.shape[0]
    return pl.pallas_call(
        functools.partial(attend_kernel, heads),
        out_shape=(
            jax.ShapeDtypeStruct((rows, width), bfloat),
            jax.ShapeDtypeStruct((heads, rows), single),
        ),
        in_specs=[IN_SMEM] * 3 + [IN_VMEM] * 2,
        out_specs=(IN_VMEM,) * 2,
        scratch_shapes=[pltpu.VMEM((rows, width), single)],
        compiler_params=params(),
        cost_estimate=cost(16 * rows * LONG * width, 10 * group * width, heads * rows * LONG),
        name="attend",
    )(lengths, head_table, bucket_ids, query, kv)


def out_copies(source, layout, plane, buffer, seq_bits, far_ref, near_ref, sem):
    my_bucket, my_seq = place_in_kernel()
    rows = far_ref.shape[1]
    copies = []
    for index in range(BLOCKS):
        if layout == "rows":
            bits, part = index % PLANES, index // PLANES
            seq = my_seq ^ bits
            bucket = plane * (BLOCKS // PLANES) + part
            start = pl.multiple_of((part * PLANES + seq) * rows, 16)
            side = bits % 2
        else:
            bits, bucket, start, side = seq_bits, index, index * rows, seq_bits_side(seq_bits)
        target = far_ref if side else near_ref
        slot = slot_of(bucket ^ my_bucket, bits if layout == "rows" else seq_bits[0])
        copies.append(
            pltpu.make_async_copy(
                source.at[buffer, pl.ds(start, rows), :], target.at[slot], sem.at[buffer, index]
            )
        )
    return copies


def seq_bits_side(seq_bits):
    return seq_bits[1]


def middle_kernel(
    heads,
    bucket_ref,
    table_ref,
    ob_ref,
    x_ref,
    c_ref,
    keep_ref,
    mod_ref,
    out_bias,
    down_bias,
    chan_ref,
    up_bias,
    pair_ref,
    up_ref,
    down_ref,
    out_ref,
    mid_ref,
    up_far,
    up_near,
    down_far,
    down_near,
    wo_far,
    wo_near,
    do_ref,
    delta_ref,
    row_ref,
    db_ref,
    up,
    down,
    up_grad,
    down_grad,
    total,
    da,
    result,
    second,
    df,
    dr,
    wo_sem,
    up_sem,
    down_sem,
    up_out,
    down_out,
    wo_out,
):
    local, width = x_ref.shape
    my_seq = place_in_kernel()[1]
    cols, edge = width // PLANES, dr.shape[2]

    def wo_load(plane, target):
        source = pair_ref.at[plane, :, pl.ds(width - edge, edge)]
        return pltpu.make_async_copy(source, target, wo_sem.at[plane])

    def wo_stage(plane):
        return up_grad.at[plane % 2, :, pl.ds(plane // 2 * edge, edge)]

    def loads(bits):
        plane = my_seq ^ bits
        rows = pl.ds(pl.multiple_of(plane * width, LANES), width)
        return (
            pltpu.make_async_copy(up_ref.at[plane], up.at[plane], up_sem.at[bits]),
            pltpu.make_async_copy(down_ref.at[rows, :], down.at[rows, :], down_sem.at[bits]),
        )

    for plane in range(PLANES):
        wo_load(plane, wo_stage(plane)).start()
    for bits in (1, 3, 0, 2):
        for copy in loads(bits):
            copy.start()
    total[...] = jnp.zeros_like(total)
    da[...] = jnp.zeros_like(da)
    row_ref[...] = jnp.zeros_like(row_ref)
    for plane in range(PLANES):
        wo_load(plane, wo_stage(plane)).wait()
        stage = up_grad[plane % 2, :, plane // 2 * edge : (plane // 2 + 1) * edge]
        result[:, plane * cols : (plane + 1) * cols] = dot_nn(ob_ref[...], stage)[:, -cols:]

    @pl.loop(0, local, step=LANES)
    def _(tile):
        span = pl.ds(pl.multiple_of(tile, LANES), LANES)
        branch = result[span, :] + out_bias[...]
        result[span, :] = branch
        middle = x_ref[span, :].astype(single) + mod_ref[2:3, :] * branch
        mid_ref[span, :] = middle
        second[span, :] = modulate(middle, mod_ref[3:4, :], mod_ref[4:5, :]).astype(bfloat)
        upstream = c_ref[span, :].astype(single)
        df[span, :] = (mod_ref[5:6, :] * keep_ref[span, :] * upstream).astype(bfloat)

    def one(plane, low, high, buffer):
        first, grad = second[...], df[...]
        hidden_rows = pl.ds(pl.multiple_of(plane * width + low, LANES), high - low)
        keep = chan_ref[pl.ds(bucket_ref[0], 1), hidden_rows].astype(single)
        pre = dot_nn(first, up[plane, :, low:high]) + up_bias[plane, :, low:high]
        root = math.sqrt(2.0 / math.pi)
        square = pre * pre
        half = 0.5 + 0.5 * jnp.tanh(pre * (root + (root * 0.044715) * square))
        kept = half * keep
        hidden = (pre * kept).astype(bfloat)
        bend = pre * (1.0 - half) * (2.0 * root + (2.0 * root * 0.134145) * square)
        back = (dot_nt(grad, down[hidden_rows, :]) * (kept + kept * bend)).astype(bfloat)
        total[...] += dot_nn(hidden, down[hidden_rows, :])
        da[...] += dot_nt(back, up[plane, :, low:high])
        up_grad[buffer, :, low:high] = dot_tn(first, back).astype(bfloat)
        down_grad[buffer, low:high, :] = dot_tn(hidden, grad).astype(bfloat)
        db_ref[plane, :, low:high] = column_sum(back.astype(single))

    cut = -(-width // 2 // LANES) * LANES

    def sends(plane, buffer, side_bits, far_side):
        return out_copies(
            up_grad, "planes", plane, buffer, (side_bits, far_side), up_far, up_near, up_out
        ) + out_copies(down_grad, "rows", plane, buffer, None, down_far, down_near, down_out)

    for far_side in (1, 0):

        @pl.loop(0, 2)
        def _(above):
            bits = above * 2 + far_side
            plane = my_seq ^ bits
            if not far_side:
                for copy in sends(plane, above, bits, far_side):
                    copy.wait()
            for copy in loads(bits):
                copy.wait()
            one(plane, 0, cut, above)
            one(plane, cut, width, above)
            for copy in sends(plane, above, bits, far_side):
                copy.start()

    def wo_end(plane):
        return down.at[pl.ds(plane * width, width), pl.ds(0, edge)]

    for plane in range(PLANES):
        wo_load(plane, wo_end(plane)).start()
    gate_one, scale, gate_two = mod_ref[2:3, :], mod_ref[4:5, :], mod_ref[5:6, :]

    @pl.loop(0, local, step=LANES)
    def _(tile):
        span = pl.ds(pl.multiple_of(tile, LANES), LANES)
        keep = keep_ref[span, :]
        upstream = c_ref[span, :].astype(single)
        middle = mid_ref[span, :]
        mlp = total[span, :] + down_bias[...]
        out_ref[span, :] = (middle + gate_two * keep * mlp).astype(bfloat)
        grad = da[span, :]
        back, normed = norm_back(middle, grad, scale)
        dmid = upstream + back
        mid_ref[span, :] = dmid
        branch = (gate_one * dmid).astype(bfloat).astype(single)
        for plane in range(PLANES):
            dr[plane, span, : edge - cols] = jnp.zeros((LANES, edge - cols), bfloat)
            dr[plane, span, edge - cols :] = branch[:, plane * cols : (plane + 1) * cols].astype(
                bfloat
            )
        row_ref[0:1, :] += column_sum(dmid * result[span, :])
        row_ref[1:2, :] += column_sum(grad)
        row_ref[2:3, :] += column_sum(grad * normed)
        row_ref[3:4, :] += column_sum(keep * upstream * mlp)
        row_ref[4:5, :] += column_sum(branch)
        row_ref[5:6, :] += column_sum(df[span, :].astype(single))

    for above in range(2):
        for copy in sends(my_seq ^ (above * 2), above, above * 2, 0):
            copy.wait()
    stage = up_grad.at[:, :, pl.ds(0, edge)]
    for far_side in (1, 0):
        for above in range(2):
            bits = above * 2 + far_side
            plane = my_seq ^ bits
            copies = out_copies(
                stage, "planes", plane, above, (bits, far_side), wo_far, wo_near, wo_out
            )
            if not far_side:
                for copy in copies:
                    copy.wait()
            up_grad[above, :, :edge] = dot_tn(ob_ref[...], dr[plane]).astype(bfloat)
            for copy in copies:
                copy.start()
    for plane in range(PLANES):
        wo_load(plane, wo_end(plane)).wait()
        part = dot_nt(dr[plane], down[plane * width : (plane + 1) * width, :edge])
        if plane == 0:
            total[...] = part
        else:
            total[...] += part
    size = width // heads
    grad = (total[...] * head_row(table_ref, bucket_ref, width)).astype(bfloat)
    do_ref[...] = grad
    terms = grad.astype(single) * ob_ref[...].astype(single)
    head = lax.broadcasted_iota(jnp.int32, (heads, width), 0)
    lane = lax.broadcasted_iota(jnp.int32, (heads, width), 1)
    chosen = jnp.logical_and(lane >= head * size, lane < (head + 1) * size)
    delta_ref[...] = lax.dot_general(
        chosen.astype(single),
        terms,
        (((1,), (1,)), ((), ())),
        preferred_element_type=single,
        precision=HIGHEST,
    )
    for above in range(2):
        for copy in out_copies(
            stage, "planes", my_seq ^ (above * 2), above, (above * 2, 0), wo_far, wo_near, wo_out
        ):
            copy.wait()


def middle(
    bucket_ids,
    head_table,
    branch,
    tokens,
    upstream,
    keep,
    mods,
    out_bias,
    down_bias,
    chan_table,
    up_bias,
    pair_weight,
    up_weight,
    down_weight,
):
    rows, width = branch.shape
    heads, hidden = head_table.shape[1], chan_table.shape[1]
    edge = 3 * LANES
    blocks = jax.ShapeDtypeStruct((BLOCKS * PLANES // 2, width // BLOCKS, width), bfloat)
    narrow = jax.ShapeDtypeStruct((BLOCKS * PLANES // 2, width // BLOCKS, edge), bfloat)
    square = pltpu.VMEM((rows, width), single)
    low_square = pltpu.VMEM((rows, width), bfloat)
    return pl.pallas_call(
        functools.partial(middle_kernel, heads),
        out_shape=(
            jax.ShapeDtypeStruct((rows, width), bfloat),
            jax.ShapeDtypeStruct((rows, width), single),
            blocks,
            blocks,
            blocks,
            blocks,
            narrow,
            narrow,
            jax.ShapeDtypeStruct((rows, width), bfloat),
            jax.ShapeDtypeStruct((heads, rows), single),
            jax.ShapeDtypeStruct((8, width), single),
            jax.ShapeDtypeStruct((PLANES, 1, width), single),
        ),
        in_specs=[IN_SMEM] * 2 + [IN_VMEM] * 9 + [IN_HBM] * 3,
        out_specs=(IN_VMEM,) * 2 + (IN_HBM,) * 6 + (IN_VMEM,) * 4,
        scratch_shapes=[
            pltpu.VMEM((PLANES, width, width), bfloat),
            pltpu.VMEM((hidden, width), bfloat),
            pltpu.VMEM((2, width, width), bfloat),
            pltpu.VMEM((2, width, width), bfloat),
            square,
            square,
            square,
            low_square,
            low_square,
            pltpu.VMEM((PLANES, rows, edge), bfloat),
            pltpu.SemaphoreType.DMA((PLANES,)),
            pltpu.SemaphoreType.DMA((PLANES,)),
            pltpu.SemaphoreType.DMA((PLANES,)),
            pltpu.SemaphoreType.DMA((2, BLOCKS)),
            pltpu.SemaphoreType.DMA((2, BLOCKS)),
            pltpu.SemaphoreType.DMA((2, BLOCKS)),
        ],
        compiler_params=pltpu.CompilerParams(vmem_limit_bytes=63 * 1024 * 1024),
        cost_estimate=cost(12 * rows * width * hidden, 8 * width * hidden, rows * hidden),
        name="middle",
    )(
        bucket_ids,
        head_table,
        branch,
        tokens,
        upstream,
        keep,
        mods,
        out_bias,
        down_bias,
        chan_table,
        up_bias.reshape(PLANES, 1, width),
        pair_weight,
        up_weight,
        down_weight,
    )


def attend_back_kernel(
    heads, len_ref, q_ref, do_ref, log_ref, delta_ref, kv, dq_ref, far_ref, near_ref, dq, dk, dv
):
    rows, width = q_ref.shape
    size = width // heads
    my_seq = lax.axis_index("seq")
    scale = size ** (-0.5)
    factor = scale * LOG2E
    dk[...] = jnp.zeros_like(dk)
    dv[...] = jnp.zeros_like(dv)

    def run(tile_start, start, span):
        tile = pl.ds(tile_start, TILE)
        keys = pl.ds(start, span)
        for head, low, high, left, right in head_windows(heads, size):
            mask = head_mask(low, high, left, right)
            chosen = mask.astype(single).astype(bfloat)
            query = q_ref[tile, low:high] * chosen
            grad = do_ref[tile, low:high] * chosen
            key = kv[keys, low:high]
            probs = jnp.exp2(dot_nt(key, query) * factor - log_ref[head : head + 1, tile])
            slope = dot_nt(kv[keys, width + low : width + high], grad)
            score_grad = (probs * (slope - delta_ref[head : head + 1, tile])).astype(bfloat)
            dv[keys, low:high] += dot_nn(probs.astype(bfloat), grad)
            dk[keys, low:high] += dot_nn(score_grad, query)
            part = dot_tn(score_grad, key)
            dq[tile, low:high] = jnp.where(mask, part, dq[tile, low:high])

    @pl.loop(0, rows // TILE)
    def _(index):
        tile_start = pl.multiple_of(index * TILE, TILE)
        start, length = image_of(len_ref, my_seq * rows + tile_start)
        start = pl.multiple_of(start, SHORT)

        @pl.when(length > SHORT)
        def _():
            run(tile_start, start, LONG)

        @pl.when(length <= SHORT)
        def _():
            run(tile_start, start, SHORT)

    dq_ref[...] = (dq[...] * scale).astype(bfloat)
    base = place_in_kernel()[1]
    for bits in range(PLANES):
        place = pl.ds(pl.multiple_of((base ^ bits) * rows, rows), rows)
        target = far_ref if bits % 2 else near_ref
        target[bits // 2, :, :width] = (dk[place, :] * scale).astype(bfloat)
        target[bits // 2, :, width:] = dv[place, :].astype(bfloat)


def attend_back(lengths, query, grad, logs, delta, kv, heads):
    rows, width = query.shape
    group = kv.shape[0]
    return pl.pallas_call(
        functools.partial(attend_back_kernel, heads),
        out_shape=(
            jax.ShapeDtypeStruct((rows, width), bfloat),
            jax.ShapeDtypeStruct((2, rows, 2 * width), bfloat),
            jax.ShapeDtypeStruct((2, rows, 2 * width), bfloat),
        ),
        in_specs=[pl.BlockSpec(memory_space=pltpu.SMEM)]
        + [IN_VMEM] * 5,
        out_specs=(IN_VMEM,) * 3,
        scratch_shapes=[
            pltpu.VMEM((rows, width), single),
            pltpu.VMEM((group, width), single),
            pltpu.VMEM((group, width), single),
        ],
        compiler_params=params(),
        cost_estimate=cost(40 * rows * LONG * width, 20 * group * width, heads * rows * LONG),
        name="attend_back",
    )(lengths, query, grad, logs, delta, kv)


def back_qkv_kernel(a_ref, dy_ref, w_ref, da_ref, far_ref, near_ref, stage, sem):
    my_seq = place_in_kernel()[1]
    wide = dy_ref.shape[2]
    da_ref[...] = jnp.zeros_like(da_ref)

    def sends(plane, buffer, bits, far_side):
        return out_copies(
            stage, "planes", plane, buffer, (bits, far_side), far_ref, near_ref, sem
        )

    for far_side in (1, 0):

        @pl.loop(0, 2)
        def _(above):
            bits = above * 2 + far_side
            plane = my_seq ^ bits
            if not far_side:
                for copy in sends(plane, above, bits, far_side):
                    copy.wait()
            da_ref[...] += dot_nt(dy_ref[plane], w_ref[plane, :, :wide])
            stage[above] = dot_tn(a_ref[...], dy_ref[plane]).astype(bfloat)
            for copy in sends(plane, above, bits, far_side):
                copy.start()

    for above in range(2):
        for copy in sends(my_seq ^ (above * 2), above, above * 2, 0):
            copy.wait()


def back_qkv(first_in, dy_planes, weight):
    rows, width = first_in.shape
    wide = dy_planes.shape[2]
    blocks = jax.ShapeDtypeStruct((BLOCKS * PLANES // 2, width // BLOCKS, wide), bfloat)
    return pl.pallas_call(
        back_qkv_kernel,
        out_shape=(jax.ShapeDtypeStruct((rows, width), single), blocks, blocks),
        in_specs=[IN_VMEM] * 3,
        out_specs=(IN_VMEM, IN_HBM, IN_HBM),
        scratch_shapes=[
            pltpu.VMEM((2, width, wide), bfloat),
            pltpu.SemaphoreType.DMA((2, BLOCKS)),
        ],
        compiler_params=params(),
        cost_estimate=cost(12 * rows * width * width, 4 * weight.size),
        name="back_qkv",
    )(first_in, dy_planes, weight)


def on_device(
    tokens,
    condition,
    cotangent,
    lengths,
    bucket_ids,
    keep_flags,
    head_table,
    chan_table,
    ada_master,
    ada_first,
    ada_second,
    ada_average,
    qkv_master,
    qkv_first,
    qkv_second,
    qkv_average,
    out_master,
    out_first,
    out_second,
    out_average,
    up_master,
    up_first,
    up_second,
    up_average,
    down_master,
    down_first,
    down_second,
    down_average,
    bias_master,
    bias_first,
    bias_second,
    bias_average,
):
    local_rows, width = tokens.shape
    heads = head_table.shape[1]
    head_size = width // heads
    hidden_width = chan_table.shape[1]
    hidden_ratio = hidden_width // width
    table_cols = 10 + hidden_ratio
    my_bucket, my_seq = lax.axis_index("bucket"), lax.axis_index("seq")
    buckets, seqs = lax.axis_size("bucket"), lax.axis_size("seq")
    group_rows = local_rows * seqs
    block_rows = qkv_master.shape[0]
    if cube_path():
        table = bias_master.reshape(-1, table_cols).T
        cut = down_master.astype(bfloat).reshape(seqs, -1, down_master.shape[1])
        (
            pair_weight,
            up_weight,
            down_weight,
            near,
            silu_rows,
            mods,
            bias_table,
            first_in,
            query,
        ) = gather(
            condition, table, ada_master, qkv_master, out_master, up_master, cut, tokens
        )
    else:
        pair_block = jnp.concatenate([qkv_master, out_master], axis=1).astype(bfloat)
        down_block = lax.all_to_all(
            down_master.astype(bfloat), "seq", split_axis=0, concat_axis=1, tiled=True
        )
        up_block = up_master.astype(bfloat)
        ada_low = ada_master.astype(bfloat)
        pair_weight = gather_all(pair_block, "planes")
        bias_low = lax.all_gather(
            bias_master.astype(bfloat), ("bucket", "seq"), axis=0, tiled=True
        )
        silu_low = jax.nn.silu(condition).astype(bfloat)
        silu_all = lax.all_gather(silu_low, "bucket", axis=0, tiled=True)
        silu_rows = lax.dynamic_slice_in_dim(silu_all, my_bucket * block_rows, block_rows, 1)
        mod_part = lax.psum_scatter(
            dot_nn(silu_rows, ada_low), "bucket", scatter_dimension=0, tiled=True
        )
        mod_row = lax.all_gather(mod_part, "seq", axis=1, tiled=True)
        bias_table = bias_low.astype(single).reshape(width, table_cols).T
        mods = jnp.pad(mod_row.reshape(6, width) + bias_table[:6], ((0, 2), (0, 0)))
        value_bias = bias_table[7:8]
        qkv_bias = jnp.concatenate(
            [bias_table[6:7], jnp.zeros_like(value_bias), value_bias], axis=1
        )
        first_in, query, key_value = project_qkv(
            tokens, mods[0:1], mods[1:2], qkv_bias, pair_weight
        )
        up_weight = gather_all(up_block, "planes")
        down_weight = gather_all(down_block, "rows")
        near = lax.all_gather(key_value, "seq", axis=0, tiled=True)

    out_bias = bias_table[8:9]
    up_bias = bias_table[9 : table_cols - 1].T.reshape(1, hidden_width)
    down_bias = bias_table[table_cols - 1 : table_cols]
    keep_float = keep_flags.astype(single)[:, None]
    branch_in, logs = attend(lengths, head_table, bucket_ids, query, near, heads)
    (
        output,
        middle_grad,
        up_far,
        up_near,
        down_far,
        down_near,
        wo_far,
        wo_near,
        attended_grad,
        delta,
        row_grads,
        up_bias_grad,
    ) = middle(
        bucket_ids,
        head_table,
        branch_in,
        tokens,
        cotangent,
        keep_float,
        mods,
        out_bias,
        down_bias,
        chan_table,
        up_bias,
        pair_weight,
        up_weight,
        down_weight,
    )
    up_bias_rows = up_bias_grad.reshape(width, hidden_ratio).T
    query_grad, kv_far, kv_near = attend_back(
        lengths, query, attended_grad, logs, delta, near, heads
    )
    qkv_cols = 3 * width // seqs
    if cube_path():
        rows_all = jnp.concatenate([row_grads[:5], up_bias_rows, row_grads[5:6]])
        rows_all = jnp.pad(rows_all, ((0, 16 - rows_all.shape[0]), (0, 0)))
        (
            up_new_grad,
            out_new_grad,
            pair_new_grad,
            token_grad,
            mod_all,
            bias_sum,
            silu_sum,
            down_cuts,
            _,
        ) = scatter(
            kv_far,
            kv_near,
            down_far,
            down_near,
            up_far,
            up_near,
            wo_far,
            wo_near,
            first_in,
            query_grad,
            pair_weight,
            tokens,
            middle_grad,
            mods,
            rows_all,
            ada_master,
        )
        down_mine = down_cuts.reshape(down_master.shape)
        bias_new_grad = bias_sum[:table_cols, : width // (buckets * seqs)].T.reshape(-1)
        silu_grad = silu_sum[:, 0, :block_rows].reshape(1, width)
    else:
        terms = jnp.stack([kv_near[0], kv_far[0], kv_near[1], kv_far[1]])
        kv_grad = lax.psum_scatter(terms, "seq", scatter_dimension=0)
        projected_grad = jnp.concatenate([query_grad, kv_grad], axis=1)
        dy_planes = jnp.pad(
            projected_grad.reshape(local_rows, seqs, qkv_cols).transpose(1, 0, 2),
            ((0, 0), (0, 0), (0, -qkv_cols % LANES)),
        )
        first_grad, pair_far, pair_near = back_qkv(first_in, dy_planes, pair_weight)
        out_new_grad = natural_sum(wo_far, wo_near, "planes")
        back, normed = norm_back(tokens.astype(single), first_grad, mods[1:2])
        token_grad = middle_grad + back
        up_new_grad = natural_sum(up_far, up_near, "planes")
        down_new_grad = natural_sum(down_far, down_near, "rows")
        pair_new_grad = natural_sum(pair_far, pair_near, "planes")
        mod_grads = jnp.concatenate(
            [column_sum(first_grad), column_sum(first_grad * normed), row_grads[:4]]
        )
        bias_grad = jnp.concatenate(
            [
                mod_grads,
                column_sum(query_grad.astype(single)),
                column_sum(kv_grad[:, width:].astype(single)),
                row_grads[4:5],
                up_bias_rows,
                row_grads[5:6],
            ]
        ).T.reshape(width * table_cols)
        mod_mine = lax.psum_scatter(
            mod_grads.reshape(seqs, 6 * width // seqs), "seq", scatter_dimension=0, tiled=True
        )
        mod_all = lax.all_gather(mod_mine, "bucket", axis=0, tiled=True)
        silu_part = lax.dot_general(
            mod_all,
            ada_low.astype(single),
            (((1,), (1,)), ((), ())),
            preferred_element_type=single,
            precision=HIGHEST,
        )
        silu_grad = lax.all_to_all(
            lax.psum(silu_part, "seq"), "bucket", split_axis=0, concat_axis=1, tiled=True
        )
        bias_new_grad = lax.psum_scatter(
            bias_grad, ("bucket", "seq"), scatter_dimension=0, tiled=True
        )
        down_mine = lax.all_to_all(
            down_new_grad.astype(bfloat), "seq", split_axis=1, concat_axis=0, tiled=True
        )
    ada_new_grad = lax.dot_general(
        silu_rows.astype(single),
        mod_all,
        (((0,), (0,)), ((), ())),
        preferred_element_type=single,
        precision=HIGHEST,
    )
    _, silu_back = jax.vjp(jax.nn.silu, condition)
    condition_grad = silu_back(silu_grad)[0]
    out_rate = (group_rows / (16.0 * width)) ** 0.5
    ada_new = adam_update(
        ada_master, ada_first, ada_second, ada_average, ada_new_grad, width ** (-0.5), MATRIX_DECAY
    )
    qkv_new = adam_update(
        qkv_master,
        qkv_first,
        qkv_second,
        qkv_average,
        pair_new_grad[:, :qkv_cols],
        width ** (-0.5),
        MATRIX_DECAY,
    )
    out_new = adam_update(
        out_master,
        out_first,
        out_second,
        out_average,
        out_new_grad[:, -out_master.shape[1] :],
        out_rate,
        MATRIX_DECAY,
    )
    up_new = adam_update(
        up_master, up_first, up_second, up_average, up_new_grad, width ** (-0.5), MATRIX_DECAY
    )
    down_new = adam_update(
        down_master.T,
        down_first.T,
        down_second.T,
        down_average.T,
        down_mine.T.astype(single),
        hidden_width ** (-0.5),
        MATRIX_DECAY,
    )
    down_new = [value.T for value in down_new]
    bias_new = adam_update(
        bias_master, bias_first, bias_second, bias_average, bias_new_grad, 0.3, 0.0
    )
    return (
        output,
        token_grad,
        condition_grad,
        *ada_new,
        *qkv_new,
        *out_new,
        *up_new,
        *down_new,
        *bias_new,
    )


def solution(mesh):
    in_specs = (
        P(("bucket", "seq"), None),
        P("bucket", None),
        P(("bucket", "seq"), None),
        P("bucket", None),
        P("bucket"),
        P(("bucket", "seq")),
        P(),
        P(),
        P("bucket", "seq"),
        P("bucket", "seq"),
        P("bucket", "seq"),
        P("bucket", "seq"),
        P("bucket", "seq"),
        P("bucket", "seq"),
        P("bucket", "seq"),
        P("bucket", "seq"),
        P("bucket", "seq"),
        P("bucket", "seq"),
        P("bucket", "seq"),
        P("bucket", "seq"),
        P("bucket", "seq"),
        P("bucket", "seq"),
        P("bucket", "seq"),
        P("bucket", "seq"),
        P("bucket", "seq"),
        P("bucket", "seq"),
        P("bucket", "seq"),
        P("bucket", "seq"),
        P(("bucket", "seq")),
        P(("bucket", "seq")),
        P(("bucket", "seq")),
        P(("bucket", "seq")),
    )
    out_specs = (
        P(("bucket", "seq"), None),
        P(("bucket", "seq"), None),
        P("bucket", None),
        P("bucket", "seq"),
        P("bucket", "seq"),
        P("bucket", "seq"),
        P("bucket", "seq"),
        P("bucket", "seq"),
        P("bucket", "seq"),
        P("bucket", "seq"),
        P("bucket", "seq"),
        P("bucket", "seq"),
        P("bucket", "seq"),
        P("bucket", "seq"),
        P("bucket", "seq"),
        P("bucket", "seq"),
        P("bucket", "seq"),
        P("bucket", "seq"),
        P("bucket", "seq"),
        P("bucket", "seq"),
        P("bucket", "seq"),
        P("bucket", "seq"),
        P("bucket", "seq"),
        P(("bucket", "seq")),
        P(("bucket", "seq")),
        P(("bucket", "seq")),
        P(("bucket", "seq")),
    )
    return jax.shard_map(
        on_device, mesh=mesh, in_specs=in_specs, out_specs=out_specs, check_vma=False
    )
```

```python
import functools
import math

import jax
import jax.numpy as jnp
from jax import lax
from jax.experimental import pallas as pl
from jax.experimental.pallas import tpu as pltpu
from jax.sharding import PartitionSpec as P

STEP = 10


EPSILON = 1e-06
BETA_FIRST = 0.5
BETA_SECOND = 0.5
ADAM_EPSILON = 1e-08
MATRIX_DECAY = 0.01
EMA_DECAY = 0.9999
HIGHEST = lax.Precision.HIGHEST
LOG2E = math.log2(math.e)
LANES = 128
TILE = 256
VMEM_LIMIT = 60 * 1024 * 1024
bfloat = jnp.bfloat16
single = jnp.float32


def layer_norm(values):
    centre = values - jnp.mean(values, axis=-1, keepdims=True)
    spread = jnp.mean(centre * centre, axis=-1, keepdims=True)
    return centre * lax.rsqrt(spread + EPSILON)


def modulate(values, shift_row, scale_row):
    return layer_norm(values) * (1.0 + scale_row) + shift_row


def dot_nn(left, right):
    return lax.dot_general(left, right, (((1,), (0,)), ((), ())), preferred_element_type=single)


def dot_nt(left, right):
    return lax.dot_general(left, right, (((1,), (1,)), ((), ())), preferred_element_type=single)


def dot_tn(left, right):
    return lax.dot_general(left, right, (((0,), (0,)), ((), ())), preferred_element_type=single)


def adam_update(master, moment_one, moment_two, average, gradient, step_rate, decay_rate):
    one_new = BETA_FIRST * moment_one + (1.0 - BETA_FIRST) * gradient
    two_new = BETA_SECOND * moment_two + (1.0 - BETA_SECOND) * gradient * gradient
    one_hat = one_new / (1.0 - BETA_FIRST**STEP)
    two_hat = two_new / (1.0 - BETA_SECOND**STEP)
    master_new = master - step_rate * (
        one_hat / (jnp.sqrt(two_hat) + ADAM_EPSILON) + decay_rate * master
    )
    average_decay = min(EMA_DECAY, (1.0 + STEP) / (10.0 + STEP))
    average_new = average_decay * average + (1.0 - average_decay) * master_new
    return (master_new, one_new, two_new, average_new)


def params(*semantics):
    return pltpu.CompilerParams(
        dimension_semantics=semantics or None, vmem_limit_bytes=VMEM_LIMIT
    )


def cost(flops, moved, exps=0):
    return pl.CostEstimate(flops=int(flops), bytes_accessed=int(moved), transcendentals=int(exps))


def exchange(values, axis, bit):
    count = lax.axis_size(axis)
    return lax.ppermute(values, axis, [(i, i ^ bit) for i in range(count)])


def pick(values, index, axis):
    return lax.dynamic_index_in_dim(values, index, axis, keepdims=False)


IN_VMEM = pl.BlockSpec(memory_space=pltpu.VMEM)
IN_HBM = pl.BlockSpec(memory_space=pl.ANY)
IN_SMEM = pl.BlockSpec(memory_space=pltpu.SMEM)


def cube_path():
    return lax.axis_size("bucket") == 8 and lax.axis_size("seq") == 4


BLOCKS, PLANES = 8, 4
X, Z0, Z1, CORE, Y = ("bucket", 1), ("bucket", 2), ("bucket", 4), ("seq", 1), ("seq", 2)
MIDDLE, FORWARD = ("bucket", 6), ("bucket", 2, "forward")


def gather_all(block, layout):
    width = block.shape[1]
    if layout == "rows":
        return lax.all_gather(block, ("bucket", "seq"), axis=0, tiled=True)
    tall = lax.all_gather(block, "bucket", axis=0, tiled=True)
    return lax.all_gather(tall, "seq", axis=0)


def place_in_kernel():
    if cube_path():
        return lax.axis_index("bucket"), lax.axis_index("seq")
    return 0, 0


DIMS = {"planes": (Y, CORE, Z1, Z0, X), "rows": (Z1, Z0, X, Y, CORE)}
MESH = pl.DeviceIdType.MESH


def my_coords():
    bucket, seq = lax.axis_index("bucket"), lax.axis_index("seq")
    return {
        (axis, amount): ((bucket if axis == "bucket" else seq) // amount) % 2
        for axis, amount in (X, Z0, Z1, CORE, Y)
    }


def partner(bit):
    bucket, seq = lax.axis_index("bucket"), lax.axis_index("seq")
    axis, amount = bit[:2]
    return (bucket ^ amount, seq) if axis == "bucket" else (bucket, seq ^ amount)


def peer_at(distance):
    bucket, seq = lax.axis_index("bucket"), lax.axis_index("seq")
    return bucket ^ (distance >> 2), seq ^ (distance & 3)


def greet(peers):
    barrier = pltpu.get_barrier_semaphore()
    for peer in peers:
        pl.semaphore_signal(barrier, inc=1, device_id=peer, device_id_type=MESH)
    pl.semaphore_wait(barrier, len(peers))


class Gathering:
    def __init__(self, own, out, layout, order, first, rows, send, recv, base):
        self.own, self.out, self.dims, self.order = own, out, DIMS[layout], order
        self.first, self.rows, self.send, self.recv, self.base = first, rows, send, recv, base
        self.me = my_coords()
        self.inner = self.me[Z0] != self.me[Z1]

    def view(self, free, flipped=None):
        index = tuple(
            slice(None)
            if dim in free
            else (1 - self.me[dim] if dim == flipped else self.me[dim])
            for dim in self.dims
        )
        return self.out.at[index + (pl.ds(self.first, self.rows), slice(None))]

    def copy(self, source, place, slot, bit):
        return pltpu.make_async_remote_copy(
            src_ref=source,
            dst_ref=place,
            send_sem=self.send.at[self.base + slot],
            recv_sem=self.recv.at[self.base + slot],
            device_id=partner(bit),
            device_id_type=MESH,
        )

    def dim(self, phase):
        return Z1 if self.order[phase] in (MIDDLE, FORWARD) else self.order[phase]

    def had(self, phase):
        return [self.dim(past) for past in range(phase) if self.order[past] != MIDDLE]

    def arrived(self, phase):
        return self.view(self.had(phase), self.dim(phase))

    def hop(self, phase):
        place = self.arrived(phase) if self.order[phase] == FORWARD else self.view(self.had(phase))
        source = self.own if phase == 0 else place
        return self.copy(source, place, phase, self.order[phase])

    def across(self, phase):
        if phase == 0:
            return self.copy(self.own, self.view(()), 5, CORE)
        place = self.arrived(phase - 1)
        return self.copy(place, place, 5 + phase, CORE)

    def keep(self):
        return pltpu.make_async_copy(self.own, self.view(()), self.send.at[self.base + 11])

    def begin(self):
        self.hop(0).start()
        self.across(0).start()
        self.keep().start()

    def sends(self, phase, act):
        if self.order[phase] in (MIDDLE, FORWARD):
            pl.when(self.inner)(act)
        else:
            act()

    def advance(self, phase):
        if phase == 0:
            self.keep().wait()
        kind = self.order[phase]
        if kind == MIDDLE:

            @pl.when(self.inner)
            def _():
                self.hop(phase).wait_recv()
                self.hop(phase + 1).start()

            return
        if kind == FORWARD:

            @pl.when(jnp.logical_not(self.inner))
            def _():
                self.hop(phase).wait_recv()

        else:
            self.hop(phase).wait_recv()
        if phase < 4:
            self.sends(phase + 1, lambda: self.hop(phase + 1).start())
        self.across(phase + 1).start()

    def collect(self):
        for phase in range(6):
            if phase == 0 or self.order[phase - 1] != MIDDLE:
                self.across(phase).wait_recv()

    def finish(self):
        for phase in range(5):
            self.sends(phase, lambda phase=phase: self.hop(phase).wait_send())
        for phase in range(6):
            if phase == 0 or self.order[phase - 1] != MIDDLE:
                self.across(phase).wait_send()


GATHER_SEMS = 12
SHARES = (32, 32, 32, 32, 16)
PAIR_PARTS = (
    (X, Z0, Y, MIDDLE, FORWARD),
    (Z0, MIDDLE, FORWARD, X, Y),
    (Z0, Y, MIDDLE, FORWARD, X),
    (Z0, MIDDLE, FORWARD, Y, X),
    (Z0, MIDDLE, FORWARD, Y, X),
)
UP_PARTS = (
    (Z0, X, Y, MIDDLE, FORWARD),
    (Z0, X, Y, MIDDLE, FORWARD),
    (Y, Z0, MIDDLE, FORWARD, X),
    (Y, Z0, MIDDLE, FORWARD, X),
    (Z0, X, MIDDLE, FORWARD, Y),
)
DOWN_PARTS = (
    (Z0, MIDDLE, FORWARD, Y, X),
    (Z0, Y, X, MIDDLE, FORWARD),
    (Z0, MIDDLE, FORWARD, Y, X),
    (Z0, X, Y, MIDDLE, FORWARD),
    (Z0, MIDDLE, FORWARD, X, Y),
)
BEGIN, PLANE, KV = -1, -2, -3
GATHER_STEPS = (
    (0, 0), (1, 0), (2, 0), (3, 0), (4, 0), (1, 1), (0, 1), (2, 1), (3, 1), (4, 1),
    (-1, 0), (1, 2), (3, 2), (0, 2), (2, 2), (4, 2), (7, 0), (5, 0), (8, 0), (6, 0),
    (9, 0), (1, 3), (10, 0), (11, 0), (5, 1), (3, 3), (12, 0), (13, 0), (14, 0), (6, 1),
    (4, 3), (9, 1), (0, 3), (2, 3), (10, 1), (7, 1), (12, 1), (14, 1), (8, 1), (1, 4),
    (3, 4), (9, 2), (11, 1), (13, 1), (7, 2), (5, 2), (4, 4), (0, 4), (8, 2), (10, 2),
    (6, 2), (12, 2), (14, 2), (13, 2), (9, 3), (2, 4), (-2, 0), (5, 3), (10, 3), (7, 3),
    (11, 2), (-2, 1), (14, 3), (12, 3), (-2, 2), (8, 3), (-2, 3), (-3, 0), (-3, 1), (-3, 2),
    (-3, 3), (6, 3), (9, 4), (10, 4), (14, 4), (5, 4), (13, 3), (7, 4), (6, 4), (11, 3),
    (12, 4), (13, 4), (8, 4), (11, 4),
)
NOTE, TAKE, ALL = -4, -5, -6
DOWN_SUM_PARTS = (
    (X, Z0, Y, Z1),
    (Z0, X, Y, Z1),
    (Z0, X, Y, Z1),
    (Y, Z0, Z1, X),
    (X, Z0, Z1, Y),
)
UP_SUM_PARTS = (
    (X, Z0, Z1, Y),
    (Y, X, Z0, Z1),
    (X, Y, Z0, Z1),
    (X, Y, Z0, Z1),
    (Z0, Y, X, Z1),
)
OUT_SHARES = (80, 64)
OUT_SUM_PARTS = (
    (Y, X, Z0, Z1),
    (X, Y, Z0, Z1),
)
PAIR_SUM_PARTS = (
    (Z0, Y, X, Z1),
    (X, Y, Z0, Z1),
    (X, Y, Z0, Z1),
    (Y, X, Z0, Z1),
    (X, Y, Z0, Z1),
)
SUM_STEPS = (
    (-3, 0), (-3, 1), (-3, 2), (-3, 3), (0, -1), (1, -1), (-5, 0), (2, -1), (3, -1), (4, -1),
    (5, -1), (-5, 1), (6, -1), (0, 0), (7, -1), (1, 0), (8, -1), (9, -1), (-5, 2), (4, 0),
    (10, -1), (11, -1), (-5, 3), (2, 0), (-2, 0), (5, 0), (0, 1), (-2, 1), (3, 0), (9, 0),
    (4, 1), (7, 0), (5, 1), (1, 1), (6, 0), (-6, 0), (-2, 2), (3, 1), (-2, 3), (4, 2),
    (8, 0), (10, 0), (12, -1), (13, -1), (14, -1), (15, -1), (16, -1), (5, 2), (0, 2), (9, 1),
    (-4, 0), (11, 0), (3, 2), (7, 1), (2, 1), (1, 2), (4, 3), (12, 0), (6, 1), (0, 3),
    (8, 1), (7, 2), (10, 1), (1, 3), (6, 2), (15, 0), (5, 3), (8, 2), (13, 0), (7, 3),
    (11, 1), (10, 2), (2, 2), (6, 3), (14, 0), (8, 3), (12, 1), (11, 2), (16, 0), (10, 3),
    (13, 1), (9, 2), (3, 3), (2, 3), (14, 1), (11, 3), (15, 1), (16, 1), (13, 2), (9, 3),
    (12, 2), (14, 2), (15, 2), (16, 2), (13, 3), (12, 3), (14, 3), (15, 3), (16, 3),
)
NOTE_STEP = 5
KV_PIECES = 4


def split_gatherings(block_ref, out_ref, layout, shares, orders, send, recv, base):
    moving, first = [], 0
    for index, (count, order) in enumerate(zip(shares, orders)):
        own = block_ref.at[pl.ds(first, count), :]
        slot = base + GATHER_SEMS * index
        moving.append(Gathering(own, out_ref, layout, order, first, count, send, recv, slot))
        first += count
    return moving


def kv_needed(piece, act):
    place = my_coords()
    quarter = KV_PIECES // 2
    last = jnp.logical_and(place[Y] == 1, place[CORE] == 1)
    first = jnp.logical_and(place[Y] == 0, place[CORE] == 0)
    skipped = first if piece < quarter else last
    pl.when(jnp.logical_not(skipped))(act)


def kv_expected(piece, act):
    place = my_coords()
    quarter = KV_PIECES // 2
    last = jnp.logical_and(place[Y] == 0, place[CORE] == 1)
    first = jnp.logical_and(place[Y] == 1, place[CORE] == 0)
    skipped = first if piece < quarter else last
    pl.when(jnp.logical_not(skipped))(act)


def kv_relayed(piece, act):
    place = my_coords()
    quarter = KV_PIECES // 2
    last = jnp.logical_and(place[Y] == 0, place[CORE] == 0)
    first = jnp.logical_and(place[Y] == 1, place[CORE] == 1)
    skipped = first if piece < quarter else last
    pl.when(jnp.logical_not(skipped))(act)


def gather_kernel(
    cond_ref,
    table_ref,
    ada_ref,
    qkv_master,
    out_master,
    up_master,
    cut_ref,
    x_ref,
    pair_out,
    up_out,
    down_out,
    kv_out,
    silu_ref,
    mod_ref,
    bias_ref,
    a_ref,
    q_ref,
    note_ref,
    pair_ref,
    up_ref,
    down_ref,
    cuts,
    inbox,
    parts,
    returns,
    row,
    weights,
    acc,
    kv,
    note_send,
    note_recv,
    mod_send,
    mod_recv,
    cut_send,
    cut_recv,
    weight_sem,
    send,
    recv,
):
    bucket, seq = lax.axis_index("bucket"), lax.axis_index("seq")
    place = my_coords()
    me = bucket * PLANES + seq
    count = BLOCKS * PLANES
    barrier = pltpu.get_barrier_semaphore()

    @pl.loop(1, count)
    def _(distance):
        pl.semaphore_signal(barrier, inc=1, device_id=peer_at(distance), device_id_type=MESH)

    rows, width = ada_ref.shape[0], x_ref.shape[1]
    cols = 3 * width // PLANES
    pair_ref[:, :cols] = qkv_master[...].astype(bfloat)
    pair_ref[:, cols:] = out_master[...].astype(bfloat)
    up_ref[...] = up_master[...].astype(bfloat)
    note_ref[...] = jnp.zeros_like(note_ref)
    for index in range(BLOCKS):
        start = index * rows
        note_ref[index, : NOTE_ROWS - 2, : table_ref.shape[1]] = table_ref[...]
        note_ref[index, NOTE_ROWS - 2 : NOTE_ROWS - 1, :] = cond_ref[:, start : start + LANES]
        note_ref[index, NOTE_ROWS - 1 :, : rows - LANES] = cond_ref[
            :, start + LANES : start + rows
        ]
    pl.semaphore_wait(barrier, count - 1)

    def cut(distance):
        return pltpu.make_async_remote_copy(
            src_ref=cut_ref.at[seq ^ distance],
            dst_ref=cuts.at[seq],
            send_sem=cut_send.at[distance],
            recv_sem=cut_recv.at[distance],
            device_id=(bucket, seq ^ distance),
            device_id_type=MESH,
        )

    def note(distance):
        peer = peer_at(distance)
        return pltpu.make_async_remote_copy(
            src_ref=note_ref.at[peer[0]],
            dst_ref=inbox.at[me],
            send_sem=note_send.at[distance],
            recv_sem=note_recv.at[distance],
            device_id=peer,
            device_id_type=MESH,
        )

    def answer(distance):
        peer = peer_at(distance)
        return pltpu.make_async_remote_copy(
            src_ref=parts.at[peer[0]],
            dst_ref=returns.at[me],
            send_sem=mod_send.at[distance],
            recv_sem=mod_recv.at[distance],
            device_id=peer,
            device_id_type=MESH,
        )

    @pl.loop(1, count)
    def _(distance):
        note(distance).start()

    inbox[me] = note_ref[bucket]
    cuts[seq] = cut_ref[seq]
    base = len(PAIR_PARTS) * GATHER_SEMS
    pairs = split_gatherings(pair_ref, pair_out, "planes", SHARES, PAIR_PARTS, send, recv, 0)
    rest = split_gatherings(up_ref, up_out, "planes", SHARES, UP_PARTS, send, recv, base)
    base += len(UP_PARTS) * GATHER_SEMS
    rest += split_gatherings(down_ref, down_out, "rows", SHARES, DOWN_PARTS, send, recv, base)
    base += len(DOWN_PARTS) * GATHER_SEMS
    moving = pairs + rest
    for part in pairs:
        part.begin()
    for distance in range(1, PLANES):
        cut(distance).start()

    local = x_ref.shape[0] // KV_PIECES

    def kv_copy(source, target, slot, bit):
        return pltpu.make_async_remote_copy(
            src_ref=source,
            dst_ref=target,
            send_sem=send.at[base + slot],
            recv_sem=recv.at[base + slot],
            device_id=partner(bit),
            device_id_type=MESH,
        )

    def kv_step(piece, kind):
        span = pl.ds(piece * local, local)
        mine = kv_out.at[place[Y], place[CORE], span, :]
        other = kv_out.at[1 - place[Y], place[CORE], span, :]
        if kind == "over":
            return kv_copy(kv.at[span, :], mine, 4 * piece, Y)
        if kind == "near":
            return kv_copy(kv.at[span, :], mine, 4 * piece + 1, CORE)
        if kind == "far":
            return kv_copy(other, other, 4 * piece + 2, CORE)
        return pltpu.make_async_copy(kv.at[span, :], mine, send.at[base + 4 * piece + 3])

    def load(plane):
        source = pair_out.at[plane // 2, plane % 2, :, :, :, :, pl.ds(0, weights.shape[5])]
        return pltpu.make_async_copy(source, weights.at[plane % 2], weight_sem.at[plane % 2])

    def modulations():
        @pl.loop(1, count)
        def _(distance):
            note(distance).wait_recv()

        head = jnp.concatenate(
            [inbox[PLANES * g, NOTE_ROWS - 2 : NOTE_ROWS - 1, :] for g in range(BLOCKS)]
        )
        tail = jnp.concatenate(
            [inbox[PLANES * g, NOTE_ROWS - 1 : NOTE_ROWS, :] for g in range(BLOCKS)]
        )
        head, tail = jax.nn.silu(head).astype(bfloat), jax.nn.silu(tail).astype(bfloat)
        silu_ref[:, :LANES] = head
        silu_ref[:, LANES:] = tail
        mods = dot_nn(head, ada_ref[:LANES, :].astype(bfloat)) + dot_nn(
            tail[:, : rows - LANES], ada_ref[LANES:, :].astype(bfloat)
        )
        for group in range(BLOCKS):
            parts[group] = mods[group : group + 1, :]
        returns[me] = parts[bucket]

        @pl.loop(1, count)
        def _(distance):
            answer(distance).start()

    def biases():
        each = width // count
        for device in range(count):
            heard = inbox[device].astype(bfloat).astype(single)
            bias_ref[:, device * each : (device + 1) * each] = heard[:, :each]

    def projection(plane):
        if plane == 0:
            for part in pairs:
                part.collect()
            load(0).start()
            load(1).start()

            @pl.loop(1, count)
            def _(distance):
                answer(distance).wait_recv()

            for index in range(PLANES):
                wide = returns.shape[2]
                row[:, index * wide : (index + 1) * wide] = sum(
                    returns[PLANES * g + index] for g in range(BLOCKS)
                )
            for index in range(6):
                mod_ref[index : index + 1, :] = (
                    row[:, index * width : (index + 1) * width] + bias_ref[index : index + 1, :]
                )
            a_ref[...] = modulate(
                x_ref[...].astype(single), mod_ref[0:1, :], mod_ref[1:2, :]
            ).astype(bfloat)
        load(plane).wait()
        weight = weights[plane % 2].reshape(width, weights.shape[5])
        acc[:, plane * cols : (plane + 1) * cols] = dot_nn(a_ref[...], weight)[:, :cols]
        if plane + 2 < PLANES:
            load(plane + 2).start()
        if plane == PLANES - 1:
            q_ref[...] = (acc[:, :width] + bias_ref[6:7, :]).astype(bfloat)
            kv[:, :width] = acc[:, width : 2 * width].astype(bfloat)
            kv[:, width:] = (acc[:, 2 * width :] + bias_ref[7:8, :]).astype(bfloat)

    def relay(piece):
        kv_step(piece, "over").wait_recv()
        kv_step(piece, "far").start()

    for step, (part, phase) in enumerate(GATHER_STEPS):
        if step == NOTE_STEP:
            modulations()
            biases()
        if part == BEGIN:
            for distance in range(1, PLANES):
                cut(distance).wait_recv()
            for index in range(PLANES):
                each = cuts.shape[2]
                down_ref[:, index * each : (index + 1) * each] = cuts[index]
            for moved in rest:
                moved.begin()
        elif part == PLANE:
            projection(phase)
        elif part == KV:
            kv_needed(phase, lambda: kv_step(phase, "over").start())
            for kind in ("near", "keep"):
                kv_step(phase, kind).start()
        else:
            moving[part].advance(phase)
        behind = len(GATHER_STEPS) - 1 - step
        if behind < 2 * KV_PIECES and behind % 2 == 0:
            piece = KV_PIECES - 1 - behind // 2
            kv_expected(piece, functools.partial(relay, piece))
    for part in rest:
        part.collect()
    for part in moving:
        part.finish()
    for piece in range(KV_PIECES):
        kv_step(piece, "near").wait_recv()
        kv_relayed(piece, lambda piece=piece: kv_step(piece, "far").wait_recv())
        kv_step(piece, "keep").wait()
        kv_step(piece, "near").wait_send()
        kv_needed(piece, lambda piece=piece: kv_step(piece, "over").wait_send())
        kv_expected(piece, lambda piece=piece: kv_step(piece, "far").wait_send())

    for distance in range(1, PLANES):
        cut(distance).wait_send()

    @pl.loop(1, count)
    def _(distance):
        note(distance).wait_send()
        answer(distance).wait_send()


NOTE_ROWS = 16


def gather(condition, table, ada_master, qkv_master, out_master, up_master, cut, tokens):
    rows, width = up_master.shape
    local = tokens.shape[0]
    count = BLOCKS * PLANES
    cols = ada_master.shape[1]
    block = pltpu.VMEM((rows, width), bfloat)
    wide = -(-3 * width // PLANES // LANES) * LANES
    blocks = jax.ShapeDtypeStruct((2, 2, 2, 2, 2, rows, width), bfloat)
    sems = 3 * len(SHARES) * GATHER_SEMS + 4 * KV_PIECES
    pair, up, down, kv, silu, mods, biases, first_in, query = pl.pallas_call(
        gather_kernel,
        out_shape=(
            blocks,
            blocks,
            blocks,
            jax.ShapeDtypeStruct((2, 2, local, 2 * width), bfloat),
            jax.ShapeDtypeStruct((BLOCKS, 2 * LANES), bfloat),
            jax.ShapeDtypeStruct((8, width), single),
            jax.ShapeDtypeStruct((NOTE_ROWS, width), single),
            jax.ShapeDtypeStruct((local, width), bfloat),
            jax.ShapeDtypeStruct((local, width), bfloat),
        ),
        in_specs=[IN_VMEM] * 8,
        out_specs=(IN_HBM,) * 4 + (IN_VMEM,) * 5,
        scratch_shapes=[
            pltpu.VMEM((BLOCKS, NOTE_ROWS, LANES), single),
            block,
            block,
            block,
            pltpu.VMEM(cut.shape, bfloat),
            pltpu.VMEM((count, NOTE_ROWS, LANES), single),
            pltpu.VMEM((BLOCKS, 1, cols), single),
            pltpu.VMEM((count, 1, cols), single),
            pltpu.VMEM((1, 6 * width), single),
            pltpu.VMEM((2, 2, 2, 2, rows, wide), bfloat),
            pltpu.VMEM((local, 3 * width), single),
            pltpu.VMEM((local, 2 * width), bfloat),
        ]
        + [pltpu.SemaphoreType.DMA((count,))] * 4
        + [pltpu.SemaphoreType.DMA((PLANES,))] * 2
        + [pltpu.SemaphoreType.DMA((2,))]
        + [pltpu.SemaphoreType.DMA((sems,))] * 2,
        compiler_params=pltpu.CompilerParams(
            collective_id=1, has_side_effects=True, vmem_limit_bytes=VMEM_LIMIT
        ),
        cost_estimate=cost(6 * local * width * width, 200 * rows * width),
        name="gather",
    )(condition, table, ada_master, qkv_master, out_master, up_master, cut, tokens)
    tall = BLOCKS * rows
    return (
        pair.reshape(PLANES, tall, width),
        up.reshape(PLANES, tall, width),
        down.reshape(PLANES * tall, width),
        kv.reshape(PLANES * local, 2 * width),
        silu[:, :rows],
        mods,
        biases,
        first_in,
        query,
    )


def slot_of(bucket_bits, seq_bits):
    slot = 0
    for axis, amount in SLOT_DIMS:
        bits = bucket_bits if axis == "bucket" else seq_bits
        slot = slot * 2 + ((bits >> amount.bit_length() - 1) & 1)
    return slot


def natural_sum(far, near, layout):
    width = far.shape[2]
    both = jnp.concatenate([near, far])
    index = {
        (b, s): slot_of(b, s) + near.shape[0] * (s % 2)
        for b in range(BLOCKS)
        for s in range(PLANES)
    }
    if layout == "rows":
        picked = [index[b, s] for b in range(BLOCKS) for s in range(PLANES)]
        gradient = jnp.stack([both[k] for k in picked]).reshape(-1, width)
        part = lax.psum_scatter(gradient, ("bucket", "seq"), scatter_dimension=0, tiled=True)
        return part.astype(single)
    picked = [index[b, s] for s in range(PLANES) for b in range(BLOCKS)]
    gradient = jnp.stack([both[k] for k in picked]).reshape(PLANES, -1, width)
    part = lax.psum_scatter(gradient, "seq", scatter_dimension=0)
    return lax.psum_scatter(part, "bucket", scatter_dimension=0, tiled=True).astype(single)


SLOT_DIMS = (Y, X, Z1, Z0)


class Scattering:
    def __init__(self, far, near, total, arrivals, out, order, first, rows, send, recv, base):
        self.far, self.near, self.total, self.arrivals = far, near, total, arrivals
        self.out, self.order, self.first, self.rows = out, order, first, rows
        self.send, self.recv, self.base = send, recv, base
        self.span = (pl.ds(first, rows), slice(None))
        self.near_span = None

    def copy(self, source, place, slot, bit):
        return pltpu.make_async_remote_copy(
            src_ref=source,
            dst_ref=place,
            send_sem=self.send.at[self.base + slot],
            recv_sem=self.recv.at[self.base + slot],
            device_id=partner(bit),
            device_id_type=MESH,
        )

    def across(self):
        index = (slice(None),) * 4 + self.span
        return self.copy(self.far.at[index], self.total.at[index], 4, CORE)

    def place(self, fixed):
        return tuple(fixed.get(dim, slice(None)) for dim in SLOT_DIMS)

    def hop(self, phase):
        fixed = {dim: 0 for dim in self.order[:phase]} | {self.order[phase]: 1}
        source = self.total.at[self.place(fixed) + self.span]
        place = self.arrivals[phase].at[(slice(None),) * (3 - phase) + self.span]
        return self.copy(source, place, phase, self.order[phase])

    def add(self, fixed, source, source_dims, source_span=None):
        free = [dim for dim in SLOT_DIMS if dim not in fixed]

        def one(step):
            index = dict(fixed)
            for place, dim in enumerate(free):
                index[dim] = (step >> place) & 1
            spot = tuple(index[dim] for dim in SLOT_DIMS) + self.span
            term = source[tuple(index[dim] for dim in source_dims) + (source_span or self.span)]
            self.total[spot] = (self.total[spot].astype(single) + term.astype(single)).astype(
                bfloat
            )

        if free:
            pl.loop(0, 2 ** len(free))(one)
        else:
            one(0)

    def advance(self, phase):
        span = None
        if phase < 0 and self.near is None:
            self.hop(0).start()
            return
        if phase < 0:
            self.across().wait_recv()
            source, dims, fixed, span = self.near, SLOT_DIMS, {}, self.near_span
        else:
            self.hop(phase).wait_recv()
            done = self.order[: phase + 1]
            dims = tuple(dim for dim in SLOT_DIMS if dim not in done)
            source, fixed = self.arrivals[phase], {dim: 0 for dim in done}
        if phase == 3:
            spot = (0,) * 4 + self.span
            self.out[self.span] = self.total[spot].astype(single) + source[self.span].astype(
                single
            )
            return
        ahead = self.order[phase + 1]
        self.add(fixed | {ahead: 1}, source, dims, span)
        self.hop(phase + 1).start()
        self.add(fixed | {ahead: 0}, source, dims, span)

    def finish(self):
        self.across().wait_send()
        for phase in range(4):
            self.hop(phase).wait_send()


SCATTER_SEMS = 5


def scatter_scratch(rows, width):
    return [
        pltpu.VMEM((2,) * free + (rows, width), bfloat) for free in (4, 3, 2, 1, 0)
    ]


def split_scatterings(far, near, scratch, out, shares, orders, send, recv, base):
    moving, first = [], 0
    for index, (count, order) in enumerate(zip(shares, orders)):
        slot = base + SCATTER_SEMS * index
        moving.append(
            Scattering(
                far, near, scratch[0], scratch[1:], out, order, first, count, send, recv, slot
            )
        )
        first += count
    return moving


def norm_back(values, grad, scale_row):
    centre = values - jnp.mean(values, axis=-1, keepdims=True)
    root = lax.rsqrt(jnp.mean(centre * centre, axis=-1, keepdims=True) + EPSILON)
    normed = centre * root
    scaled = grad * (1.0 + scale_row)
    inner = jnp.mean(scaled * normed, axis=-1, keepdims=True)
    return root * (scaled - jnp.mean(scaled, axis=-1, keepdims=True) - normed * inner), normed


def column_sum(values):
    return jnp.sum(values, axis=0, keepdims=True)


def scatter_kernel(
    kv_far,
    kv_near,
    down_far,
    down_near,
    up_far,
    up_near,
    wo_far,
    w_ref,
    x_ref,
    dmid_ref,
    wo_near,
    a_ref,
    dq_ref,
    mod_ref,
    row_ref,
    ada_ref,
    up_out,
    wo_sum,
    pair_out,
    grad_ref,
    mods_ref,
    bias_ref,
    silu_ref,
    cuts,
    far,
    *refs,
):
    down_scratch, up_scratch, refs = refs[:5], refs[5:10], refs[10:]
    wo_scratch, pair_scratch, refs = refs[:5], refs[5:10], refs[10:]
    kv_total, kv_arrival, kv_stage, stage, down_sum, cut_ref, plane_stage, refs = refs[:7] + (refs[7:],)
    x_tile, dmid_tile, weights, dy, table, line, bias_notes, mod_notes, bias_box, mod_box = refs[:10]
    parts, returns, cut_send, cut_recv, local_sem, far_sem = refs[10:16]
    bias_send, bias_recv, mod_send, mod_recv, back_send, back_recv, send, recv = refs[16:]
    bucket, seq = lax.axis_index("bucket"), lax.axis_index("seq")
    me = bucket * PLANES + seq
    count = BLOCKS * PLANES
    barrier = pltpu.get_barrier_semaphore()

    @pl.loop(1, count)
    def _(distance):
        pl.semaphore_signal(barrier, inc=1, device_id=peer_at(distance), device_id_type=MESH)

    pl.semaphore_wait(barrier, count - 1)

    def message(source, target, out_sem, in_sem, distance):
        return pltpu.make_async_remote_copy(
            src_ref=source,
            dst_ref=target,
            send_sem=out_sem.at[distance],
            recv_sem=in_sem.at[distance],
            device_id=peer_at(distance),
            device_id_type=MESH,
        )

    def bias_note(distance):
        peer = peer_at(distance)
        source = bias_notes.at[peer[0] * PLANES + peer[1]]
        return message(source, bias_box.at[me], bias_send, bias_recv, distance)

    def mod_note(distance):
        source = mod_notes.at[peer_at(distance)[1]]
        return message(source, mod_box.at[me], mod_send, mod_recv, distance)

    def answer(distance):
        source = parts.at[peer_at(distance)[0]]
        return message(source, returns.at[me], back_send, back_recv, distance)

    place = my_coords()
    base = 0

    def streams(far_ref, near_ref, scratch, out, shares, orders):
        nonlocal base
        start, base = base, base + len(orders) * SCATTER_SEMS
        return split_scatterings(far_ref, near_ref, scratch, out, shares, orders, send, recv, start)

    downs = streams(down_far, down_near, down_scratch, down_sum, SHARES, DOWN_SUM_PARTS)
    ups = streams(up_far, up_near, up_scratch, up_out, SHARES, UP_SUM_PARTS)
    wos = streams(wo_far, wo_near, wo_scratch, wo_sum, OUT_SHARES, OUT_SUM_PARTS)
    pairs = streams(far, None, pair_scratch, pair_out, SHARES, PAIR_SUM_PARTS)
    moving = downs + ups + wos + pairs
    piece_rows = kv_arrival.shape[0] // KV_PIECES

    def kv_copy(source, target, slot, bit):
        return pltpu.make_async_remote_copy(
            src_ref=source,
            dst_ref=target,
            send_sem=send.at[base + slot],
            recv_sem=recv.at[base + slot],
            device_id=partner(bit),
            device_id_type=MESH,
        )

    def kv_span(piece):
        return pl.ds(piece * piece_rows, piece_rows)

    def near_kv(piece):
        span = kv_span(piece)
        return kv_copy(kv_far.at[:, span, :], kv_total.at[:, span, :], 2 * piece, CORE)

    def over(piece):
        span = kv_span(piece)
        return kv_copy(kv_total.at[1, span, :], kv_arrival.at[span, :], 2 * piece + 1, Y)

    def kv_load(piece):
        return pltpu.make_async_copy(
            kv_near.at[:, kv_span(piece), :], kv_stage, local_sem.at[2]
        )

    def kv_add(piece, side):
        span = kv_span(piece)
        kv_total[side, span, :] = (
            kv_total[side, span, :].astype(single) + kv_stage[side].astype(single)
        ).astype(bfloat)

    def pass_over(piece):
        kv_add(piece, 1)
        over(piece).start()

    def take(piece):
        over(piece).wait_recv()
        span = kv_span(piece)
        kv_total[0, span, :] = (
            kv_total[0, span, :].astype(single) + kv_arrival[span, :].astype(single)
        ).astype(bfloat)

    staged = [part for part, phase in SUM_STEPS if phase < 0 and 0 <= part < len(downs + ups)]

    def stage_load(turn):
        part = moving[staged[turn]]
        spot = (slice(None),) * 4
        return pltpu.make_async_copy(
            part.near.at[spot + part.span],
            stage.at[(turn % 2,) + spot + (pl.ds(0, part.rows), slice(None))],
            local_sem.at[turn % 2],
        )

    kv_load(0).start()
    for piece in range(KV_PIECES):
        near_kv(piece).start()
    for part in downs + ups + wos:
        part.across().start()
    for turn in range(2):
        stage_load(turn).start()

    def cut(distance):
        return pltpu.make_async_remote_copy(
            src_ref=cut_ref.at[seq ^ distance],
            dst_ref=cuts.at[seq],
            send_sem=cut_send.at[distance],
            recv_sem=cut_recv.at[distance],
            device_id=(bucket, seq ^ distance),
            device_id_type=MESH,
        )

    def cut_down():
        for index in range(PLANES):
            each = cuts.shape[2]
            cut_ref[index] = down_sum[:, index * each : (index + 1) * each].astype(bfloat)
        cuts[seq] = cut_ref[seq]
        for distance in range(1, PLANES):
            cut(distance).start()

    local, width = dq_ref.shape
    rows = up_out.shape[0]
    cols = 3 * width // PLANES
    wide = dy.shape[1]
    order = (1, 3, 0, 2)

    def load(step):
        plane = seq ^ order[step]
        return pltpu.make_async_copy(
            w_ref.at[plane, :, pl.ds(0, wide)], weights, local_sem.at[3]
        )

    def gather_dy(index):
        low, high = index * cols, (index + 1) * cols
        pieces = []
        if low < width:
            pieces.append(dq_ref[:, low : min(high, width)])
        if high > width:
            pieces.append(kv_total[0, :, max(low - width, 0) : high - width])
        first = 0
        for piece in pieces:
            dy[:, first : first + piece.shape[1]] = piece
            first += piece.shape[1]

    def block_spot(block, bits):
        return (
            bits // 2,
            (block % 2) ^ place[X],
            (block // 4) ^ place[Z1],
            (block // 2 % 2) ^ place[Z0],
        )

    def far_copy(block, bits):
        return pltpu.make_async_copy(
            plane_stage.at[pl.ds(block * rows, rows), :],
            far.at[block_spot(block, bits)],
            far_sem.at[block],
        )

    def project(step):
        bits = order[step]
        plane = seq ^ bits
        if step == 0:
            load(0).start()
            dy[:, cols:] = jnp.zeros((local, wide - cols), bfloat)
            grad_ref[...] = jnp.zeros_like(grad_ref)
        for index in range(PLANES):

            @pl.when(plane == index)
            def _():
                gather_dy(index)

        if step == 1:
            for block in range(BLOCKS):
                far_copy(block, order[0]).wait()
        total = pair_scratch[0]
        for low, high in ((0, 4 * LANES), (4 * LANES, wide)):
            values = dot_tn(a_ref[...], dy[:, low:high])
            if step < 2:
                plane_stage[:, low:high] = values.astype(bfloat)
                continue
            for block in range(BLOCKS):
                spot = block_spot(block, bits) + (slice(None), slice(low, high))
                value = values[block * rows : (block + 1) * rows, :]
                total[spot] = (total[spot].astype(single) + value).astype(bfloat)
        if step < 2:
            for block in range(BLOCKS):
                far_copy(block, bits).start()
        load(step).wait()
        grad_ref[...] += dot_nt(dy[...], weights[...])
        if step + 1 < PLANES:
            load(step + 1).start()
        if step == 1:
            for block in range(BLOCKS):
                far_copy(block, bits).wait()
            for part in pairs:
                part.across().start()

    def tile_loads(tile):
        span = pl.ds(tile * LANES, LANES)
        return (
            pltpu.make_async_copy(x_ref.at[span, :], x_tile.at[tile % 2], far_sem.at[tile % 2]),
            pltpu.make_async_copy(
                dmid_ref.at[span, :], dmid_tile.at[tile % 2], far_sem.at[2 + tile % 2]
            ),
        )

    def notes():
        shift_sum, scale_sum = jnp.zeros((1, width), single), jnp.zeros((1, width), single)
        scale_row = mod_ref[1:2, :]
        tiles = local // LANES
        for copy in tile_loads(0):
            copy.start()
        for tile in range(tiles):
            if tile + 1 < tiles:
                for copy in tile_loads(tile + 1):
                    copy.start()
            for copy in tile_loads(tile):
                copy.wait()
            span = slice(tile * LANES, (tile + 1) * LANES)
            grad = grad_ref[span, :]
            back, normed = norm_back(x_tile[tile % 2].astype(single), grad, scale_row)
            shift_sum += column_sum(grad)
            scale_sum += column_sum(grad * normed)
            grad_ref[span, :] = dmid_tile[tile % 2] + back
        table[...] = jnp.zeros_like(table)
        line[:, :width] = shift_sum
        line[:, width : 2 * width] = scale_sum
        table[0:1, :width] = shift_sum
        table[1:2, :width] = scale_sum
        for index in range(4):
            line[:, (2 + index) * width : (3 + index) * width] = row_ref[index : index + 1, :]
        table[2:6, :width] = row_ref[0:4, :]
        table[6:7, :width] = column_sum(dq_ref[...].astype(single))
        table[7:8, :width] = column_sum(kv_total[0, :, width:].astype(single))
        table[8:14, :width] = row_ref[4:10, :]
        each = width // count
        for device in range(count):
            bias_notes[device] = table[:, device * each : device * each + LANES]

        part = mod_notes.shape[2]
        for index in range(PLANES):
            mod_notes[index] = line[:, index * part : (index + 1) * part]
        bias_box[me] = bias_notes[me]
        mod_box[me] = mod_notes[seq]

        @pl.loop(1, count)
        def _(distance):
            mod_note(distance).start()
            bias_note(distance).start()

    def answers():
        @pl.loop(1, count)
        def _(distance):
            mod_note(distance).wait_recv()

        sums = [sum(mod_box[PLANES * g + s] for s in range(PLANES)) for g in range(BLOCKS)]
        mods = jnp.concatenate(sums)
        mods_ref[...] = mods
        silu = lax.dot_general(
            mods,
            ada_ref[...].astype(bfloat).astype(single),
            (((1,), (1,)), ((), ())),
            preferred_element_type=single,
            precision=HIGHEST,
        )
        for group in range(BLOCKS):
            parts[group, :, :rows] = silu[group : group + 1, :]
            parts[group, :, rows:] = jnp.zeros((1, parts.shape[2] - rows), single)
        returns[me] = parts[bucket]

        @pl.loop(1, count)
        def _(distance):
            answer(distance).start()

    since, turn, left = 0, 0, len(downs)
    for part, phase in SUM_STEPS:
        if part == KV:
            near_kv(phase).wait_recv()
            kv_load(phase).wait()
            kv_expected(phase, functools.partial(pass_over, phase))
            kv_add(phase, 0)
            if phase + 1 < KV_PIECES:
                kv_load(phase + 1).start()
        elif part == TAKE:
            kv_needed(phase, functools.partial(take, phase))
        elif part == ALL:
            for moved in pairs:
                moved.across().wait_recv()
        elif part == PLANE:
            project(phase)
        elif part == NOTE:
            notes()
            since = 1
        else:
            mover = moving[part]
            if phase < 0 and part < len(downs + ups):
                stage_load(turn).wait()
                mover.near = stage.at[turn % 2]
                mover.near_span = (pl.ds(0, mover.rows), slice(None))
                mover.advance(phase)
                if turn + 2 < len(staged):
                    stage_load(turn + 2).start()
                turn += 1
            else:
                mover.advance(phase)
            if part < len(downs) and phase == 3:
                left -= 1
                if left == 0:
                    cut_down()
            since += since > 0
            if since == ANSWER_AFTER:
                answers()

    @pl.loop(1, count)
    def _(distance):
        bias_note(distance).wait_recv()

    bias_ref[...] = jnp.zeros_like(bias_ref)

    @pl.loop(0, count)
    def _(device):
        bias_ref[...] += bias_box[device]

    @pl.loop(1, count)
    def _(distance):
        answer(distance).wait_recv()

    for group in range(BLOCKS):
        silu_ref[group] = sum(returns[PLANES * group + s] for s in range(PLANES))
    for part in moving:
        part.finish()
    for piece in range(KV_PIECES):
        near_kv(piece).wait_send()
        kv_expected(piece, lambda piece=piece: over(piece).wait_send())
    for distance in range(1, PLANES):
        cut(distance).wait_recv()
        cut(distance).wait_send()

    @pl.loop(1, count)
    def _(distance):
        bias_note(distance).wait_send()
        mod_note(distance).wait_send()
        answer(distance).wait_send()


ANSWER_AFTER = 26


def scatter(
    kv_far,
    kv_near,
    down_far,
    down_near,
    up_far,
    up_near,
    wo_far,
    wo_near,
    first_in,
    query_grad,
    weight,
    tokens,
    middle_grad,
    mods,
    row_grads,
    ada_master,
):
    rows, width = up_far.shape[1:]
    edge = wo_far.shape[2]
    count = BLOCKS * PLANES
    cols = ada_master.shape[1]
    cuts = (PLANES, rows, width // PLANES)
    local, kv_wide = kv_far.shape[1:]
    wide = -(-3 * width // PLANES // LANES) * LANES
    cube, wo_cube = (2, 2, 2, 2, rows, width), (2, 2, 2, 2, rows, edge)
    sems = (3 * len(SHARES) + len(OUT_SHARES)) * SCATTER_SEMS + 2 * KV_PIECES
    return pl.pallas_call(
        scatter_kernel,
        out_shape=(
            jax.ShapeDtypeStruct((rows, width), single),
            jax.ShapeDtypeStruct((rows, edge), single),
            jax.ShapeDtypeStruct((rows, wide), single),
            jax.ShapeDtypeStruct((local, width), single),
            jax.ShapeDtypeStruct((BLOCKS, cols), single),
            jax.ShapeDtypeStruct((NOTE_ROWS, LANES), single),
            jax.ShapeDtypeStruct((BLOCKS, 1, 2 * LANES), single),
            jax.ShapeDtypeStruct(cuts, bfloat),
            jax.ShapeDtypeStruct((2, 2, 2, 2, rows, wide), bfloat),
        ),
        in_specs=[IN_HBM] * 10 + [IN_VMEM] * 6,
        out_specs=(IN_VMEM,) * 8 + (IN_HBM,),
        scratch_shapes=scatter_scratch(rows, width)
        + scatter_scratch(rows, width)
        + scatter_scratch(rows, edge)
        + scatter_scratch(rows, wide)
        + [
            pltpu.VMEM((2, local, kv_wide), bfloat),
            pltpu.VMEM((local, kv_wide), bfloat),
            pltpu.VMEM((2, local // KV_PIECES, kv_wide), bfloat),
            pltpu.VMEM((2, 2, 2, 2, 2, max(SHARES), width), bfloat),
            pltpu.VMEM((rows, width), single),
            pltpu.VMEM(cuts, bfloat),
            pltpu.VMEM((width, wide), bfloat),
            pltpu.VMEM((2, LANES, width), bfloat),
            pltpu.VMEM((2, LANES, width), single),
            pltpu.VMEM((width, wide), bfloat),
            pltpu.VMEM((local, wide), bfloat),
            pltpu.VMEM((NOTE_ROWS, width + LANES), single),
            pltpu.VMEM((1, 6 * width), single),
            pltpu.VMEM((count, NOTE_ROWS, LANES), single),
            pltpu.VMEM((PLANES, 1, cols), single),
            pltpu.VMEM((count, NOTE_ROWS, LANES), single),
            pltpu.VMEM((count, 1, cols), single),
            pltpu.VMEM((BLOCKS, 1, 2 * LANES), single),
            pltpu.VMEM((count, 1, 2 * LANES), single),
            pltpu.SemaphoreType.DMA((PLANES,)),
            pltpu.SemaphoreType.DMA((PLANES,)),
            pltpu.SemaphoreType.DMA((4,)),
            pltpu.SemaphoreType.DMA((BLOCKS,)),
        ]
        + [pltpu.SemaphoreType.DMA((count,))] * 6
        + [pltpu.SemaphoreType.DMA((sems,))] * 2,
        compiler_params=pltpu.CompilerParams(
            collective_id=4, has_side_effects=True, vmem_limit_bytes=63 * 1024 * 1024
        ),
        cost_estimate=cost(12 * local * width * width, 300 * rows * width),
        name="scatter",
    )(
        kv_far,
        kv_near,
        down_far.reshape(cube),
        down_near.reshape(cube),
        up_far.reshape(cube),
        up_near.reshape(cube),
        wo_far.reshape(wo_cube),
        weight,
        tokens,
        middle_grad,
        wo_near.reshape(wo_cube),
        first_in,
        query_grad,
        mods,
        row_grads,
        ada_master,
    )


def whole(shape):
    return pl.BlockSpec(shape, lambda *_: (0,) * len(shape))


def qkv_kernel(cols, x_ref, shift_ref, scale_ref, bias_ref, w_ref, a_ref, q_ref, kv_ref, acc):
    step = pl.program_id(0)
    width = x_ref.shape[1]

    @pl.when(step == 0)
    def _():
        values = x_ref[...].astype(single)
        a_ref[...] = modulate(values, shift_ref[...], scale_ref[...]).astype(bfloat)

    wide = -(-cols // LANES) * LANES
    part = dot_nn(a_ref[...], w_ref[0, :, :wide])[:, :cols]
    for index in range(PLANES):

        @pl.when(step == index)
        def _():
            acc[:, index * cols : (index + 1) * cols] = part

    @pl.when(step == PLANES - 1)
    def _():
        q_ref[...] = (acc[:, :width] + bias_ref[:, :width]).astype(bfloat)
        kv_ref[...] = (acc[:, width:] + bias_ref[:, width:]).astype(bfloat)


def project_qkv(tokens, shift_row, scale_row, bias_row, weight):
    rows, width = tokens.shape
    cols = 3 * width // PLANES
    return pl.pallas_call(
        functools.partial(qkv_kernel, cols),
        grid=(PLANES,),
        out_shape=(
            jax.ShapeDtypeStruct((rows, width), bfloat),
            jax.ShapeDtypeStruct((rows, width), bfloat),
            jax.ShapeDtypeStruct((rows, 2 * width), bfloat),
        ),
        in_specs=[
            whole((rows, width)),
            whole((1, width)),
            whole((1, width)),
            whole((1, 3 * width)),
            pl.BlockSpec((1,) + weight.shape[1:], lambda s: (s, 0, 0)),
        ],
        out_specs=(whole((rows, width)), whole((rows, width)), whole((rows, 2 * width))),
        scratch_shapes=[pltpu.VMEM((rows, 3 * width), single)],
        compiler_params=params("arbitrary"),
        cost_estimate=cost(6 * rows * width * width, 8 * width * width),
        name="project_qkv",
    )(tokens, shift_row, scale_row, bias_row, weight)


def image_of(len_ref, position):
    start, length, end = jnp.int32(0), jnp.int32(0), jnp.int32(0)
    for index in range(len_ref.shape[1]):
        here = len_ref[0, index]
        inside = jnp.logical_and(position >= end, position < end + here)
        start = jnp.where(inside, end, start)
        length = jnp.where(inside, here, length)
        end = end + here
    return start, length


def head_windows(heads, size):
    for head in range(heads):
        low, high = head * size, (head + 1) * size
        yield head, low // LANES * LANES, -(-high // LANES) * LANES, low, high


def head_mask(low, high, left, right):
    lane = lax.broadcasted_iota(jnp.int32, (1, high - low), 1) + low
    return jnp.logical_and(lane >= left, lane < right)


LONG, SHORT = 1024, 256


def head_row(table_ref, bucket_ref, width):
    heads = table_ref.shape[1]
    size = width // heads
    lane = lax.broadcasted_iota(jnp.int32, (1, width), 1)
    row = jnp.zeros((1, width), jnp.int32)
    for head in range(heads):
        inside = jnp.logical_and(lane >= head * size, lane < (head + 1) * size)
        row = jnp.where(inside, table_ref[bucket_ref[0], head], row)
    return row.astype(single)


def attend_kernel(heads, len_ref, table_ref, bucket_ref, q_ref, kv, ob_ref, log_ref, out):
    rows, width = q_ref.shape
    size = width // heads
    my_seq = lax.axis_index("seq")
    factor = size ** (-0.5) * LOG2E

    def run(tile_start, start, span):
        tile = pl.ds(tile_start, TILE)
        keys = pl.ds(start, span)
        logs = jnp.zeros((TILE, LANES), single)
        lane = lax.broadcasted_iota(jnp.int32, (TILE, LANES), 1)
        for head, low, high, left, right in head_windows(heads, size):
            mask = head_mask(low, high, left, right)
            query = q_ref[tile, low:high] * mask.astype(single).astype(bfloat)
            scores = dot_nt(query, kv[keys, low:high])
            top = jnp.max(scores, axis=-1, keepdims=True)
            expo = jnp.exp2((scores - top) * factor)
            total = jnp.sum(expo, axis=-1, keepdims=True)
            part = dot_nn(expo.astype(bfloat), kv[keys, width + low : width + high]) / total
            out[tile, low:high] = jnp.where(mask, part, out[tile, low:high])
            logs = jnp.where(lane == head, top * factor + jnp.log2(total), logs)
        log_ref[:, tile] = logs.T[:heads, :]

    @pl.loop(0, rows // TILE)
    def _(index):
        tile_start = pl.multiple_of(index * TILE, TILE)
        start, length = image_of(len_ref, my_seq * rows + tile_start)
        start = pl.multiple_of(start, SHORT)

        @pl.when(length > SHORT)
        def _():
            run(tile_start, start, LONG)

        @pl.when(length <= SHORT)
        def _():
            run(tile_start, start, SHORT)

    ob_ref[...] = (out[...] * head_row(table_ref, bucket_ref, width)).astype(bfloat)


def attend(lengths, head_table, bucket_ids, query, kv, heads):
    rows, width = query.shape
    group = kv.shape[0]
    return pl.pallas_call(
        functools.partial(attend_kernel, heads),
        out_shape=(
            jax.ShapeDtypeStruct((rows, width), bfloat),
            jax.ShapeDtypeStruct((heads, rows), single),
        ),
        in_specs=[IN_SMEM] * 3 + [IN_VMEM] * 2,
        out_specs=(IN_VMEM,) * 2,
        scratch_shapes=[pltpu.VMEM((rows, width), single)],
        compiler_params=params(),
        cost_estimate=cost(16 * rows * LONG * width, 10 * group * width, heads * rows * LONG),
        name="attend",
    )(lengths, head_table, bucket_ids, query, kv)


def out_copies(source, layout, plane, buffer, seq_bits, far_ref, near_ref, sem):
    my_bucket, my_seq = place_in_kernel()
    rows = far_ref.shape[1]
    copies = []
    for index in range(BLOCKS):
        if layout == "rows":
            bits, part = index % PLANES, index // PLANES
            seq = my_seq ^ bits
            bucket = plane * (BLOCKS // PLANES) + part
            start = pl.multiple_of((part * PLANES + seq) * rows, 16)
            side = bits % 2
        else:
            bits, bucket, start, side = seq_bits, index, index * rows, seq_bits_side(seq_bits)
        target = far_ref if side else near_ref
        slot = slot_of(bucket ^ my_bucket, bits if layout == "rows" else seq_bits[0])
        copies.append(
            pltpu.make_async_copy(
                source.at[buffer, pl.ds(start, rows), :], target.at[slot], sem.at[buffer, index]
            )
        )
    return copies


def seq_bits_side(seq_bits):
    return seq_bits[1]


def middle_kernel(
    heads,
    bucket_ref,
    table_ref,
    ob_ref,
    x_ref,
    c_ref,
    keep_ref,
    mod_ref,
    out_bias,
    down_bias,
    chan_ref,
    up_bias,
    pair_ref,
    up_ref,
    down_ref,
    out_ref,
    mid_ref,
    up_far,
    up_near,
    down_far,
    down_near,
    wo_far,
    wo_near,
    do_ref,
    delta_ref,
    row_ref,
    db_ref,
    up,
    down,
    up_grad,
    down_grad,
    total,
    da,
    result,
    second,
    df,
    dr,
    wo_sem,
    up_sem,
    down_sem,
    up_out,
    down_out,
    wo_out,
):
    local, width = x_ref.shape
    my_seq = place_in_kernel()[1]
    cols, edge = width // PLANES, dr.shape[2]

    def wo_load(plane, target):
        source = pair_ref.at[plane, :, pl.ds(width - edge, edge)]
        return pltpu.make_async_copy(source, target, wo_sem.at[plane])

    def wo_stage(plane):
        return up_grad.at[plane % 2, :, pl.ds(plane // 2 * edge, edge)]

    def loads(bits):
        plane = my_seq ^ bits
        rows = pl.ds(pl.multiple_of(plane * width, LANES), width)
        return (
            pltpu.make_async_copy(up_ref.at[plane], up.at[plane], up_sem.at[bits]),
            pltpu.make_async_copy(down_ref.at[rows, :], down.at[rows, :], down_sem.at[bits]),
        )

    for plane in range(PLANES):
        wo_load(plane, wo_stage(plane)).start()
    for bits in (1, 3, 0, 2):
        for copy in loads(bits):
            copy.start()
    total[...] = jnp.zeros_like(total)
    da[...] = jnp.zeros_like(da)
    row_ref[...] = jnp.zeros_like(row_ref)
    for plane in range(PLANES):
        wo_load(plane, wo_stage(plane)).wait()
        stage = up_grad[plane % 2, :, plane // 2 * edge : (plane // 2 + 1) * edge]
        result[:, plane * cols : (plane + 1) * cols] = dot_nn(ob_ref[...], stage)[:, -cols:]

    @pl.loop(0, local, step=LANES)
    def _(tile):
        span = pl.ds(pl.multiple_of(tile, LANES), LANES)
        branch = result[span, :] + out_bias[...]
        result[span, :] = branch
        middle = x_ref[span, :].astype(single) + mod_ref[2:3, :] * branch
        mid_ref[span, :] = middle
        second[span, :] = modulate(middle, mod_ref[3:4, :], mod_ref[4:5, :]).astype(bfloat)
        upstream = c_ref[span, :].astype(single)
        df[span, :] = (mod_ref[5:6, :] * keep_ref[span, :] * upstream).astype(bfloat)

    def one(plane, low, high, buffer):
        first, grad = second[...], df[...]
        hidden_rows = pl.ds(pl.multiple_of(plane * width + low, LANES), high - low)
        keep = chan_ref[pl.ds(bucket_ref[0], 1), hidden_rows].astype(single)
        pre = dot_nn(first, up[plane, :, low:high]) + up_bias[plane, :, low:high]
        root = math.sqrt(2.0 / math.pi)
        square = pre * pre
        half = 0.5 + 0.5 * jnp.tanh(pre * (root + (root * 0.044715) * square))
        kept = half * keep
        hidden = (pre * kept).astype(bfloat)
        bend = pre * (1.0 - half) * (2.0 * root + (2.0 * root * 0.134145) * square)
        back = (dot_nt(grad, down[hidden_rows, :]) * (kept + kept * bend)).astype(bfloat)
        total[...] += dot_nn(hidden, down[hidden_rows, :])
        da[...] += dot_nt(back, up[plane, :, low:high])
        up_grad[buffer, :, low:high] = dot_tn(first, back).astype(bfloat)
        down_grad[buffer, low:high, :] = dot_tn(hidden, grad).astype(bfloat)
        db_ref[plane, :, low:high] = column_sum(back.astype(single))

    cut = -(-width // 2 // LANES) * LANES

    def sends(plane, buffer, side_bits, far_side):
        return out_copies(
            up_grad, "planes", plane, buffer, (side_bits, far_side), up_far, up_near, up_out
        ) + out_copies(down_grad, "rows", plane, buffer, None, down_far, down_near, down_out)

    for far_side in (1, 0):

        @pl.loop(0, 2)
        def _(above):
            bits = above * 2 + far_side
            plane = my_seq ^ bits
            if not far_side:
                for copy in sends(plane, above, bits, far_side):
                    copy.wait()
            for copy in loads(bits):
                copy.wait()
            one(plane, 0, cut, above)
            one(plane, cut, width, above)
            for copy in sends(plane, above, bits, far_side):
                copy.start()

    def wo_end(plane):
        return down.at[pl.ds(plane * width, width), pl.ds(0, edge)]

    for plane in range(PLANES):
        wo_load(plane, wo_end(plane)).start()
    gate_one, scale, gate_two = mod_ref[2:3, :], mod_ref[4:5, :], mod_ref[5:6, :]

    @pl.loop(0, local, step=LANES)
    def _(tile):
        span = pl.ds(pl.multiple_of(tile, LANES), LANES)
        keep = keep_ref[span, :]
        upstream = c_ref[span, :].astype(single)
        middle = mid_ref[span, :]
        mlp = total[span, :] + down_bias[...]
        out_ref[span, :] = (middle + gate_two * keep * mlp).astype(bfloat)
        grad = da[span, :]
        back, normed = norm_back(middle, grad, scale)
        dmid = upstream + back
        mid_ref[span, :] = dmid
        branch = (gate_one * dmid).astype(bfloat).astype(single)
        for plane in range(PLANES):
            dr[plane, span, : edge - cols] = jnp.zeros((LANES, edge - cols), bfloat)
            dr[plane, span, edge - cols :] = branch[:, plane * cols : (plane + 1) * cols].astype(
                bfloat
            )
        row_ref[0:1, :] += column_sum(dmid * result[span, :])
        row_ref[1:2, :] += column_sum(grad)
        row_ref[2:3, :] += column_sum(grad * normed)
        row_ref[3:4, :] += column_sum(keep * upstream * mlp)
        row_ref[4:5, :] += column_sum(branch)
        row_ref[5:6, :] += column_sum(df[span, :].astype(single))

    for above in range(2):
        for copy in sends(my_seq ^ (above * 2), above, above * 2, 0):
            copy.wait()
    stage = up_grad.at[:, :, pl.ds(0, edge)]
    for far_side in (1, 0):
        for above in range(2):
            bits = above * 2 + far_side
            plane = my_seq ^ bits
            copies = out_copies(
                stage, "planes", plane, above, (bits, far_side), wo_far, wo_near, wo_out
            )
            if not far_side:
                for copy in copies:
                    copy.wait()
            up_grad[above, :, :edge] = dot_tn(ob_ref[...], dr[plane]).astype(bfloat)
            for copy in copies:
                copy.start()
    for plane in range(PLANES):
        wo_load(plane, wo_end(plane)).wait()
        part = dot_nt(dr[plane], down[plane * width : (plane + 1) * width, :edge])
        if plane == 0:
            total[...] = part
        else:
            total[...] += part
    size = width // heads
    grad = (total[...] * head_row(table_ref, bucket_ref, width)).astype(bfloat)
    do_ref[...] = grad
    terms = grad.astype(single) * ob_ref[...].astype(single)
    head = lax.broadcasted_iota(jnp.int32, (heads, width), 0)
    lane = lax.broadcasted_iota(jnp.int32, (heads, width), 1)
    chosen = jnp.logical_and(lane >= head * size, lane < (head + 1) * size)
    delta_ref[...] = lax.dot_general(
        chosen.astype(single),
        terms,
        (((1,), (1,)), ((), ())),
        preferred_element_type=single,
        precision=HIGHEST,
    )
    for above in range(2):
        for copy in out_copies(
            stage, "planes", my_seq ^ (above * 2), above, (above * 2, 0), wo_far, wo_near, wo_out
        ):
            copy.wait()


def middle(
    bucket_ids,
    head_table,
    branch,
    tokens,
    upstream,
    keep,
    mods,
    out_bias,
    down_bias,
    chan_table,
    up_bias,
    pair_weight,
    up_weight,
    down_weight,
):
    rows, width = branch.shape
    heads, hidden = head_table.shape[1], chan_table.shape[1]
    edge = 3 * LANES
    blocks = jax.ShapeDtypeStruct((BLOCKS * PLANES // 2, width // BLOCKS, width), bfloat)
    narrow = jax.ShapeDtypeStruct((BLOCKS * PLANES // 2, width // BLOCKS, edge), bfloat)
    square = pltpu.VMEM((rows, width), single)
    low_square = pltpu.VMEM((rows, width), bfloat)
    return pl.pallas_call(
        functools.partial(middle_kernel, heads),
        out_shape=(
            jax.ShapeDtypeStruct((rows, width), bfloat),
            jax.ShapeDtypeStruct((rows, width), single),
            blocks,
            blocks,
            blocks,
            blocks,
            narrow,
            narrow,
            jax.ShapeDtypeStruct((rows, width), bfloat),
            jax.ShapeDtypeStruct((heads, rows), single),
            jax.ShapeDtypeStruct((8, width), single),
            jax.ShapeDtypeStruct((PLANES, 1, width), single),
        ),
        in_specs=[IN_SMEM] * 2 + [IN_VMEM] * 9 + [IN_HBM] * 3,
        out_specs=(IN_VMEM,) * 2 + (IN_HBM,) * 6 + (IN_VMEM,) * 4,
        scratch_shapes=[
            pltpu.VMEM((PLANES, width, width), bfloat),
            pltpu.VMEM((hidden, width), bfloat),
            pltpu.VMEM((2, width, width), bfloat),
            pltpu.VMEM((2, width, width), bfloat),
            square,
            square,
            square,
            low_square,
            low_square,
            pltpu.VMEM((PLANES, rows, edge), bfloat),
            pltpu.SemaphoreType.DMA((PLANES,)),
            pltpu.SemaphoreType.DMA((PLANES,)),
            pltpu.SemaphoreType.DMA((PLANES,)),
            pltpu.SemaphoreType.DMA((2, BLOCKS)),
            pltpu.SemaphoreType.DMA((2, BLOCKS)),
            pltpu.SemaphoreType.DMA((2, BLOCKS)),
        ],
        compiler_params=pltpu.CompilerParams(vmem_limit_bytes=63 * 1024 * 1024),
        cost_estimate=cost(12 * rows * width * hidden, 8 * width * hidden, rows * hidden),
        name="middle",
    )(
        bucket_ids,
        head_table,
        branch,
        tokens,
        upstream,
        keep,
        mods,
        out_bias,
        down_bias,
        chan_table,
        up_bias.reshape(PLANES, 1, width),
        pair_weight,
        up_weight,
        down_weight,
    )


def attend_back_kernel(
    heads, len_ref, q_ref, do_ref, log_ref, delta_ref, kv, dq_ref, far_ref, near_ref, dq, dk, dv
):
    rows, width = q_ref.shape
    size = width // heads
    my_seq = lax.axis_index("seq")
    scale = size ** (-0.5)
    factor = scale * LOG2E
    dk[...] = jnp.zeros_like(dk)
    dv[...] = jnp.zeros_like(dv)

    def run(tile_start, start, span):
        tile = pl.ds(tile_start, TILE)
        keys = pl.ds(start, span)
        for head, low, high, left, right in head_windows(heads, size):
            mask = head_mask(low, high, left, right)
            chosen = mask.astype(single).astype(bfloat)
            query = q_ref[tile, low:high] * chosen
            grad = do_ref[tile, low:high] * chosen
            key = kv[keys, low:high]
            probs = jnp.exp2(dot_nt(key, query) * factor - log_ref[head : head + 1, tile])
            slope = dot_nt(kv[keys, width + low : width + high], grad)
            score_grad = (probs * (slope - delta_ref[head : head + 1, tile])).astype(bfloat)
            dv[keys, low:high] += dot_nn(probs.astype(bfloat), grad)
            dk[keys, low:high] += dot_nn(score_grad, query)
            part = dot_tn(score_grad, key)
            dq[tile, low:high] = jnp.where(mask, part, dq[tile, low:high])

    @pl.loop(0, rows // TILE)
    def _(index):
        tile_start = pl.multiple_of(index * TILE, TILE)
        start, length = image_of(len_ref, my_seq * rows + tile_start)
        start = pl.multiple_of(start, SHORT)

        @pl.when(length > SHORT)
        def _():
            run(tile_start, start, LONG)

        @pl.when(length <= SHORT)
        def _():
            run(tile_start, start, SHORT)

    dq_ref[...] = (dq[...] * scale).astype(bfloat)
    base = place_in_kernel()[1]
    for bits in range(PLANES):
        place = pl.ds(pl.multiple_of((base ^ bits) * rows, rows), rows)
        target = far_ref if bits % 2 else near_ref
        target[bits // 2, :, :width] = (dk[place, :] * scale).astype(bfloat)
        target[bits // 2, :, width:] = dv[place, :].astype(bfloat)


def attend_back(lengths, query, grad, logs, delta, kv, heads):
    rows, width = query.shape
    group = kv.shape[0]
    return pl.pallas_call(
        functools.partial(attend_back_kernel, heads),
        out_shape=(
            jax.ShapeDtypeStruct((rows, width), bfloat),
            jax.ShapeDtypeStruct((2, rows, 2 * width), bfloat),
            jax.ShapeDtypeStruct((2, rows, 2 * width), bfloat),
        ),
        in_specs=[pl.BlockSpec(memory_space=pltpu.SMEM)]
        + [IN_VMEM] * 5,
        out_specs=(IN_VMEM,) * 3,
        scratch_shapes=[
            pltpu.VMEM((rows, width), single),
            pltpu.VMEM((group, width), single),
            pltpu.VMEM((group, width), single),
        ],
        compiler_params=params(),
        cost_estimate=cost(40 * rows * LONG * width, 20 * group * width, heads * rows * LONG),
        name="attend_back",
    )(lengths, query, grad, logs, delta, kv)


def back_qkv_kernel(a_ref, dy_ref, w_ref, da_ref, far_ref, near_ref, stage, sem):
    my_seq = place_in_kernel()[1]
    wide = dy_ref.shape[2]
    da_ref[...] = jnp.zeros_like(da_ref)

    def sends(plane, buffer, bits, far_side):
        return out_copies(
            stage, "planes", plane, buffer, (bits, far_side), far_ref, near_ref, sem
        )

    for far_side in (1, 0):

        @pl.loop(0, 2)
        def _(above):
            bits = above * 2 + far_side
            plane = my_seq ^ bits
            if not far_side:
                for copy in sends(plane, above, bits, far_side):
                    copy.wait()
            da_ref[...] += dot_nt(dy_ref[plane], w_ref[plane, :, :wide])
            stage[above] = dot_tn(a_ref[...], dy_ref[plane]).astype(bfloat)
            for copy in sends(plane, above, bits, far_side):
                copy.start()

    for above in range(2):
        for copy in sends(my_seq ^ (above * 2), above, above * 2, 0):
            copy.wait()


def back_qkv(first_in, dy_planes, weight):
    rows, width = first_in.shape
    wide = dy_planes.shape[2]
    blocks = jax.ShapeDtypeStruct((BLOCKS * PLANES // 2, width // BLOCKS, wide), bfloat)
    return pl.pallas_call(
        back_qkv_kernel,
        out_shape=(jax.ShapeDtypeStruct((rows, width), single), blocks, blocks),
        in_specs=[IN_VMEM] * 3,
        out_specs=(IN_VMEM, IN_HBM, IN_HBM),
        scratch_shapes=[
            pltpu.VMEM((2, width, wide), bfloat),
            pltpu.SemaphoreType.DMA((2, BLOCKS)),
        ],
        compiler_params=params(),
        cost_estimate=cost(12 * rows * width * width, 4 * weight.size),
        name="back_qkv",
    )(first_in, dy_planes, weight)


def on_device(
    tokens,
    condition,
    cotangent,
    lengths,
    bucket_ids,
    keep_flags,
    head_table,
    chan_table,
    ada_master,
    ada_first,
    ada_second,
    ada_average,
    qkv_master,
    qkv_first,
    qkv_second,
    qkv_average,
    out_master,
    out_first,
    out_second,
    out_average,
    up_master,
    up_first,
    up_second,
    up_average,
    down_master,
    down_first,
    down_second,
    down_average,
    bias_master,
    bias_first,
    bias_second,
    bias_average,
):
    local_rows, width = tokens.shape
    heads = head_table.shape[1]
    head_size = width // heads
    hidden_width = chan_table.shape[1]
    hidden_ratio = hidden_width // width
    table_cols = 10 + hidden_ratio
    my_bucket, my_seq = lax.axis_index("bucket"), lax.axis_index("seq")
    buckets, seqs = lax.axis_size("bucket"), lax.axis_size("seq")
    group_rows = local_rows * seqs
    block_rows = qkv_master.shape[0]
    if cube_path():
        table = bias_master.reshape(-1, table_cols).T
        cut = down_master.astype(bfloat).reshape(seqs, -1, down_master.shape[1])
        (
            pair_weight,
            up_weight,
            down_weight,
            near,
            silu_rows,
            mods,
            bias_table,
            first_in,
            query,
        ) = gather(
            condition, table, ada_master, qkv_master, out_master, up_master, cut, tokens
        )
    else:
        pair_block = jnp.concatenate([qkv_master, out_master], axis=1).astype(bfloat)
        down_block = lax.all_to_all(
            down_master.astype(bfloat), "seq", split_axis=0, concat_axis=1, tiled=True
        )
        up_block = up_master.astype(bfloat)
        ada_low = ada_master.astype(bfloat)
        pair_weight = gather_all(pair_block, "planes")
        bias_low = lax.all_gather(
            bias_master.astype(bfloat), ("bucket", "seq"), axis=0, tiled=True
        )
        silu_low = jax.nn.silu(condition).astype(bfloat)
        silu_all = lax.all_gather(silu_low, "bucket", axis=0, tiled=True)
        silu_rows = lax.dynamic_slice_in_dim(silu_all, my_bucket * block_rows, block_rows, 1)
        mod_part = lax.psum_scatter(
            dot_nn(silu_rows, ada_low), "bucket", scatter_dimension=0, tiled=True
        )
        mod_row = lax.all_gather(mod_part, "seq", axis=1, tiled=True)
        bias_table = bias_low.astype(single).reshape(width, table_cols).T
        mods = jnp.pad(mod_row.reshape(6, width) + bias_table[:6], ((0, 2), (0, 0)))
        value_bias = bias_table[7:8]
        qkv_bias = jnp.concatenate(
            [bias_table[6:7], jnp.zeros_like(value_bias), value_bias], axis=1
        )
        first_in, query, key_value = project_qkv(
            tokens, mods[0:1], mods[1:2], qkv_bias, pair_weight
        )
        up_weight = gather_all(up_block, "planes")
        down_weight = gather_all(down_block, "rows")
        near = lax.all_gather(key_value, "seq", axis=0, tiled=True)

    out_bias = bias_table[8:9]
    up_bias = bias_table[9 : table_cols - 1].T.reshape(1, hidden_width)
    down_bias = bias_table[table_cols - 1 : table_cols]
    keep_float = keep_flags.astype(single)[:, None]
    branch_in, logs = attend(lengths, head_table, bucket_ids, query, near, heads)
    (
        output,
        middle_grad,
        up_far,
        up_near,
        down_far,
        down_near,
        wo_far,
        wo_near,
        attended_grad,
        delta,
        row_grads,
        up_bias_grad,
    ) = middle(
        bucket_ids,
        head_table,
        branch_in,
        tokens,
        cotangent,
        keep_float,
        mods,
        out_bias,
        down_bias,
        chan_table,
        up_bias,
        pair_weight,
        up_weight,
        down_weight,
    )
    up_bias_rows = up_bias_grad.reshape(width, hidden_ratio).T
    query_grad, kv_far, kv_near = attend_back(
        lengths, query, attended_grad, logs, delta, near, heads
    )
    qkv_cols = 3 * width // seqs
    if cube_path():
        rows_all = jnp.concatenate([row_grads[:5], up_bias_rows, row_grads[5:6]])
        rows_all = jnp.pad(rows_all, ((0, 16 - rows_all.shape[0]), (0, 0)))
        (
            up_new_grad,
            out_new_grad,
            pair_new_grad,
            token_grad,
            mod_all,
            bias_sum,
            silu_sum,
            down_cuts,
            _,
        ) = scatter(
            kv_far,
            kv_near,
            down_far,
            down_near,
            up_far,
            up_near,
            wo_far,
            wo_near,
            first_in,
            query_grad,
            pair_weight,
            tokens,
            middle_grad,
            mods,
            rows_all,
            ada_master,
        )
        down_mine = down_cuts.reshape(down_master.shape)
        bias_new_grad = bias_sum[:table_cols, : width // (buckets * seqs)].T.reshape(-1)
        silu_grad = silu_sum[:, 0, :block_rows].reshape(1, width)
    else:
        terms = jnp.stack([kv_near[0], kv_far[0], kv_near[1], kv_far[1]])
        kv_grad = lax.psum_scatter(terms, "seq", scatter_dimension=0)
        projected_grad = jnp.concatenate([query_grad, kv_grad], axis=1)
        dy_planes = jnp.pad(
            projected_grad.reshape(local_rows, seqs, qkv_cols).transpose(1, 0, 2),
            ((0, 0), (0, 0), (0, -qkv_cols % LANES)),
        )
        first_grad, pair_far, pair_near = back_qkv(first_in, dy_planes, pair_weight)
        out_new_grad = natural_sum(wo_far, wo_near, "planes")
        back, normed = norm_back(tokens.astype(single), first_grad, mods[1:2])
        token_grad = middle_grad + back
        up_new_grad = natural_sum(up_far, up_near, "planes")
        down_new_grad = natural_sum(down_far, down_near, "rows")
        pair_new_grad = natural_sum(pair_far, pair_near, "planes")
        mod_grads = jnp.concatenate(
            [column_sum(first_grad), column_sum(first_grad * normed), row_grads[:4]]
        )
        bias_grad = jnp.concatenate(
            [
                mod_grads,
                column_sum(query_grad.astype(single)),
                column_sum(kv_grad[:, width:].astype(single)),
                row_grads[4:5],
                up_bias_rows,
                row_grads[5:6],
            ]
        ).T.reshape(width * table_cols)
        mod_mine = lax.psum_scatter(
            mod_grads.reshape(seqs, 6 * width // seqs), "seq", scatter_dimension=0, tiled=True
        )
        mod_all = lax.all_gather(mod_mine, "bucket", axis=0, tiled=True)
        silu_part = lax.dot_general(
            mod_all,
            ada_low.astype(single),
            (((1,), (1,)), ((), ())),
            preferred_element_type=single,
            precision=HIGHEST,
        )
        silu_grad = lax.all_to_all(
            lax.psum(silu_part, "seq"), "bucket", split_axis=0, concat_axis=1, tiled=True
        )
        bias_new_grad = lax.psum_scatter(
            bias_grad, ("bucket", "seq"), scatter_dimension=0, tiled=True
        )
        down_mine = lax.all_to_all(
            down_new_grad.astype(bfloat), "seq", split_axis=1, concat_axis=0, tiled=True
        )
    ada_new_grad = lax.dot_general(
        silu_rows.astype(single),
        mod_all,
        (((0,), (0,)), ((), ())),
        preferred_element_type=single,
        precision=HIGHEST,
    )
    _, silu_back = jax.vjp(jax.nn.silu, condition)
    condition_grad = silu_back(silu_grad)[0]
    out_rate = (group_rows / (16.0 * width)) ** 0.5
    ada_new = adam_update(
        ada_master, ada_first, ada_second, ada_average, ada_new_grad, width ** (-0.5), MATRIX_DECAY
    )
    qkv_new = adam_update(
        qkv_master,
        qkv_first,
        qkv_second,
        qkv_average,
        pair_new_grad[:, :qkv_cols],
        width ** (-0.5),
        MATRIX_DECAY,
    )
    out_new = adam_update(
        out_master,
        out_first,
        out_second,
        out_average,
        out_new_grad[:, -out_master.shape[1] :],
        out_rate,
        MATRIX_DECAY,
    )
    up_new = adam_update(
        up_master, up_first, up_second, up_average, up_new_grad, width ** (-0.5), MATRIX_DECAY
    )
    down_new = adam_update(
        down_master.T,
        down_first.T,
        down_second.T,
        down_average.T,
        down_mine.T.astype(single),
        hidden_width ** (-0.5),
        MATRIX_DECAY,
    )
    down_new = [value.T for value in down_new]
    bias_new = adam_update(
        bias_master, bias_first, bias_second, bias_average, bias_new_grad, 0.3, 0.0
    )
    return (
        output,
        token_grad,
        condition_grad,
        *ada_new,
        *qkv_new,
        *out_new,
        *up_new,
        *down_new,
        *bias_new,
    )


def solution(mesh):
    in_specs = (
        P(("bucket", "seq"), None),
        P("bucket", None),
        P(("bucket", "seq"), None),
        P("bucket", None),
        P("bucket"),
        P(("bucket", "seq")),
        P(),
        P(),
        P("bucket", "seq"),
        P("bucket", "seq"),
        P("bucket", "seq"),
        P("bucket", "seq"),
        P("bucket", "seq"),
        P("bucket", "seq"),
        P("bucket", "seq"),
        P("bucket", "seq"),
        P("bucket", "seq"),
        P("bucket", "seq"),
        P("bucket", "seq"),
        P("bucket", "seq"),
        P("bucket", "seq"),
        P("bucket", "seq"),
        P("bucket", "seq"),
        P("bucket", "seq"),
        P("bucket", "seq"),
        P("bucket", "seq"),
        P("bucket", "seq"),
        P("bucket", "seq"),
        P(("bucket", "seq")),
        P(("bucket", "seq")),
        P(("bucket", "seq")),
        P(("bucket", "seq")),
    )
    out_specs = (
        P(("bucket", "seq"), None),
        P(("bucket", "seq"), None),
        P("bucket", None),
        P("bucket", "seq"),
        P("bucket", "seq"),
        P("bucket", "seq"),
        P("bucket", "seq"),
        P("bucket", "seq"),
        P("bucket", "seq"),
        P("bucket", "seq"),
        P("bucket", "seq"),
        P("bucket", "seq"),
        P("bucket", "seq"),
        P("bucket", "seq"),
        P("bucket", "seq"),
        P("bucket", "seq"),
        P("bucket", "seq"),
        P("bucket", "seq"),
        P("bucket", "seq"),
        P("bucket", "seq"),
        P("bucket", "seq"),
        P("bucket", "seq"),
        P("bucket", "seq"),
        P(("bucket", "seq")),
        P(("bucket", "seq")),
        P(("bucket", "seq")),
        P(("bucket", "seq")),
    )
    return jax.shard_map(
        on_device, mesh=mesh, in_specs=in_specs, out_specs=out_specs, check_vma=False
    )
```
